32 devices in a mesh: blk: 2 (over y), grid: 16 (over z, x, core).
Axes of the slice: x: 2, y: 2, z: 4, core: 2. Of those that a mesh axis runs over, the one named last changes fastest.
Arguments:
- density: bfloat16 [1536, 1536], P('blk', 'grid')
- points: float32 [512, 4, 256], P('grid')
- sig_blocks: int32 [512, 2], P('grid'), may hold values from 0 to 11, as said below
- migration: int32 [512], P('grid'), may hold values from -1 to 255, as said below
- atom_coords: float32 [3, 256], replicated, may hold values from 0 to 4
- exponents: float32 [1536], replicated, may hold values from 0.1 to 1
- shape_coef: float32 [3, 1536], replicated, may hold values from -3 to 3
- func_atom: int32 [1536], replicated, may hold values from 0 to 255
Outputs:
- batch_energy: float32 [256], P('grid')
- forces: float32 [3, 256], replicated
The draws below stay inside these ranges and needn't reach their ends.
Inputs may be any that keep to these rules, and one draw needn't show every extreme that they name: `sig_blocks`: entry i of a slot's list is one of the blocks of blk index i, in [i * 6, (i + 1) * 6); empty slots hold such lists too. `migration`: the live slots of a grid index come first; live entries are distinct and cover every destination once; destination d belongs to grid index d // 16; at most 2 live slots of one grid index go to any one grid index, and some grid index holds 32 live slots.
All inputs are finite; a program needn't handle non-finite values.
Results may differ from the reference program's by a relative error of at most 0.0003.
Values may be sent and summed in bfloat16 or wider, within the bound.
No kernel may reach another device: no remote copies, remote signals or barrier semaphores. Data moves between devices by JAX's collectives and lax.ppermute only.
A program may use at most 64 MiB of HBM per device.

```python
import math
import jax
import jax.numpy as jnp
from jax import lax

BLOCK = 128
PTS = 256
BPD = 6
BAT_AVG = 16
NATOM = 256
NBLK = 12
NB = 1536
BAT_MAX = 32
N_BLK = 2
N_GRID = 16


def draw_density(key, part):
    size_all = NBLK * BLOCK
    first_key, second_key = jax.random.split(key)
    noise = jax.random.normal(first_key, (size_all, size_all), jnp.float32)
    diagonal = jax.random.uniform(second_key, (size_all,), jnp.float32, 0.5, 1.5)
    symmetric = 0.5 * (noise + noise.T)
    identity = (jnp.arange(size_all)[:, None] == jnp.arange(size_all)[None, :]).astype(jnp.float32)
    factor = 4.0 / (N_BLK * BLOCK)
    spread = 1.0 / math.sqrt(N_BLK * BLOCK)
    return ((identity * diagonal[None, :] + symmetric * spread) * factor).astype(jnp.bfloat16)


def draw_points(key, part):
    slot_total = BAT_MAX * N_GRID
    first_key, second_key = jax.random.split(key)
    coords = jax.random.uniform(first_key, (slot_total, 3, PTS), jnp.float32, 0.0, 4.0)
    weight = jax.random.uniform(second_key, (slot_total, 1, PTS), jnp.float32, 0.5, 1.5) * (4.0 / PTS)
    return jnp.concatenate([coords, weight], axis=1)


def draw_sig_blocks(key, part):
    slot_total = BAT_MAX * N_GRID
    picked_blocks = jax.random.randint(key, (slot_total, N_BLK), 0, BPD)
    return (picked_blocks + (jnp.arange(N_BLK, dtype=jnp.int32) * BPD)[None, :]).astype(jnp.int32)


def draw_migration(key, part):
    key_list = jax.random.split(jax.random.fold_in(key, 7), 4)
    total = BAT_AVG * N_GRID
    half_count = N_GRID // 2
    ordering = jax.random.permutation(key_list[0], N_GRID)
    moved = jax.random.randint(key_list[1], (half_count,), 0, BAT_AVG + 1)
    moved = moved.at[0].set(BAT_AVG)
    counts = jnp.full((N_GRID,), BAT_AVG, jnp.int32)
    counts = counts.at[ordering[:half_count]].add(moved)
    counts = counts.at[ordering[half_count:2 * half_count]].add(-moved)
    starts = jnp.cumsum(counts) - counts
    slots = jnp.arange(BAT_MAX, dtype=jnp.int32)
    offset = jax.random.randint(key_list[2], (), 0, total)
    place = (starts[:, None] + slots[None, :] + offset) % total
    target = jax.random.permutation(key_list[3], N_GRID)
    destination = target[place % N_GRID] * BAT_AVG + place // N_GRID
    return jnp.where(slots[None, :] < counts[:, None], destination, -1).reshape(-1).astype(jnp.int32)


def place_ends(entries, rng, least, largest):
    shape = entries.shape
    spot = [jax.random.randint(jax.random.fold_in(rng, axis), (), 0, shape[axis]) for axis in range(len(shape))]
    entries = entries.at[tuple(spot)].set(least)
    longest = shape.index(max(shape))
    spot[longest] = (spot[longest] + 1) % shape[longest]
    return entries.at[tuple(spot)].set(largest)


def centred(stream_key, dims, width, most, held_as=jnp.bfloat16):
    drawn = width * jax.random.normal(stream_key, dims, jnp.float32)
    return jnp.clip(drawn, min=-most, max=most).astype(held_as)


def setup_inputs(seed: int = 0) -> dict:
    streams_of = jax.random.split(jax.random.key(seed), 9)
    density = draw_density(jax.random.fold_in(streams_of[8], 71), 0)
    points = draw_points(jax.random.fold_in(streams_of[8], 71), 0)
    sig_blocks = draw_sig_blocks(jax.random.fold_in(streams_of[8], 71), 0)
    migration = draw_migration(jax.random.fold_in(streams_of[8], 71), 0)
    atom_coords = jnp.clip(jax.random.uniform(streams_of[4], (3, NATOM), jnp.float32, 0.0, 4.0), 0.0, 4.0)
    exponents = jnp.clip(jnp.exp(jax.random.uniform(streams_of[5], (NB,), jnp.float32, math.log(0.1), math.log(1.0))), 0.1, 1.0)
    shape_coef = centred(streams_of[6], (3, NB), 0.5, 3.0, jnp.float32)
    func_atom = place_ends(jax.random.randint(streams_of[7], (NB,), 0, NATOM), jax.random.fold_in(streams_of[7], 1), 0, NATOM - 1).astype(jnp.int32)
    return dict(density=density, points=points, sig_blocks=sig_blocks, migration=migration, atom_coords=atom_coords, exponents=exponents, shape_coef=shape_coef, func_atom=func_atom)


SLATER = 0.7386
RHO_SOFT = 0.05

def basis_parts(coords, center, expo, coef):
    offset = coords[:, None, :] - center[:, :, None]
    squared = lax.optimization_barrier(jnp.sum(offset * offset, axis=0))
    radial = jnp.exp(-expo[:, None] * squared)
    linear = 1.0 + lax.optimization_barrier(jnp.sum(coef[:, :, None] * offset, axis=0))
    return (offset, radial, linear)

def reference(density, points, sig_blocks, migration, atom_coords, exponents, shape_coef, func_atom):
    source_count = migration.shape[0]
    batch_total = BAT_AVG * N_GRID
    live_slots = migration >= 0
    slot_index = jnp.where(live_slots, migration, batch_total).astype(jnp.int32)
    sources = jnp.zeros((batch_total + 1,), jnp.int32).at[slot_index].set(jnp.arange(source_count, dtype=jnp.int32))[:batch_total]
    func_center = atom_coords[:, func_atom]
    blocks = density.reshape(NBLK, BLOCK, NBLK, BLOCK)
    atom_ids = jnp.arange(NATOM, dtype=jnp.int32)
    within = jnp.arange(BLOCK, dtype=jnp.int32)

    def per_batch(source):
        listed = sig_blocks[source]
        functions = (listed[:, None] * BLOCK + within[None, :]).reshape(-1)
        coords = points[source, 0:3]
        weight = points[source, 3]
        expo = exponents[functions]
        coef = shape_coef[:, functions]
        offset, radial, linear = basis_parts(coords, func_center[:, functions], expo, coef)
        basis_vals = (linear * radial).astype(jnp.bfloat16)
        sub_density = blocks[listed][:, :, listed, :].reshape(N_BLK * BLOCK, N_BLK * BLOCK)
        contracted = jnp.dot(sub_density, basis_vals, preferred_element_type=jnp.float32)
        density_pts = lax.optimization_barrier(jnp.sum(basis_vals.astype(jnp.float32) * contracted, axis=0))
        softened = jnp.sqrt(density_pts * density_pts + RHO_SOFT * RHO_SOFT)
        energy = jnp.sum(weight * -SLATER * softened ** (4.0 / 3.0))
        potential = weight * (-(4.0 / 3.0) * SLATER) * softened ** (1.0 / 3.0) * density_pts / softened
        gradient = coef[:, :, None] * radial[None] - 2.0 * expo[None, :, None] * offset * (linear * radial)[None]
        force_terms = 2.0 * lax.optimization_barrier(jnp.sum(gradient * (contracted * potential[None, :])[None], axis=2))
        onehot = (func_atom[functions][:, None] == atom_ids[None, :]).astype(jnp.float32)
        return (energy, jnp.dot(force_terms, onehot, precision=lax.Precision.HIGHEST))
    energies, partials = lax.map(per_batch, sources, batch_size=8)
    return (energies, lax.optimization_barrier(jnp.sum(partials, axis=0)))
```

```python
import functools

import jax
import jax.numpy as jnp
from jax import lax
from jax.experimental import pallas as pl
from jax.experimental.pallas import tpu as pltpu
from jax.sharding import PartitionSpec as P

BLOCK = 128
BPD = 6
NATOM = 256
LANES = 128
ROWS = 32

SLATER = 0.7386
RHO_SOFT = 0.05

VMEM = pltpu.MemorySpace.VMEM
SMEM = pltpu.MemorySpace.SMEM


def aligned(start, size):
    return pl.ds(pl.multiple_of(start, size), size)


def live_count(mig_ref):
    return lax.fori_loop(
        0,
        mig_ref.shape[0],
        lambda s, n: n + jnp.where(mig_ref[s] >= 0, 1, 0),
        jnp.int32(0),
    )


def table_kernel(atom_ref, expo_ref, coef_ref, coords_ref, table_ref, coords_pad, rows):
    coords_pad[...] = jnp.zeros_like(coords_pad)
    coords_pad[0:3, :] = coords_ref[...]
    coords = coords_pad[...]
    high = coords.astype(jnp.bfloat16)
    rest = coords - high.astype(jnp.float32)
    mid = rest.astype(jnp.bfloat16)
    low = (rest - mid.astype(jnp.float32)).astype(jnp.bfloat16)
    rows[...] = jnp.zeros_like(rows)

    def one_block(k, carry):
        cols = aligned(k * BLOCK, BLOCK)
        atom = atom_ref[0:1, cols]
        onehot = jnp.where(
            lax.broadcasted_iota(jnp.int32, (NATOM, BLOCK), 0) == atom, 1.0, 0.0
        ).astype(jnp.bfloat16)
        picked = [
            jnp.dot(part, onehot, preferred_element_type=jnp.float32) for part in (high, mid, low)
        ]
        center = (picked[0] + picked[1]) + picked[2]
        rows[0:3, :] = center[0:3, :]
        rows[3:6, :] = coef_ref[:, cols]
        rows[6:7, :] = expo_ref[0:1, cols]
        rows[7:8, :] = atom.astype(jnp.float32)
        columns = rows[...].T
        for p in range(8):
            table_ref[k, p] = jnp.broadcast_to(columns[:, p : p + 1], (BLOCK, LANES))
        return carry

    lax.fori_loop(0, table_ref.shape[0], one_block, 0)


def phi_kernel(lists_ref, mig_ref, points_ref, table_ref, phi_ref, radial_ref, basis_ref):
    blk = lax.axis_index("blk")
    length = lists_ref.shape[1]
    point_count = points_ref.shape[2]

    def one_slot(s, carry):
        for j in range(length):
            k = lists_ref[s, lax.rem(blk + j, length)]
            for h in range(0, point_count, LANES):
                lanes = slice(h, h + LANES)
                x = points_ref[s, 0:1, lanes]
                y = points_ref[s, 1:2, lanes]
                z = points_ref[s, 2:3, lanes]
                for r in range(0, BLOCK, ROWS):
                    sub = slice(r, r + ROWS)
                    ox = x - table_ref[k, 0, sub]
                    oy = y - table_ref[k, 1, sub]
                    oz = z - table_ref[k, 2, sub]
                    squared = ox * ox + oy * oy + oz * oz
                    radial = jnp.exp(-table_ref[k, 6, sub] * squared)
                    linear = 1.0 + (
                        table_ref[k, 3, sub] * ox
                        + table_ref[k, 4, sub] * oy
                        + table_ref[k, 5, sub] * oz
                    )
                    basis = linear * radial
                    phi_ref[s, j, sub, lanes] = basis.astype(jnp.bfloat16)
                    if j == 0:
                        radial_ref[s, sub, lanes] = radial
                        basis_ref[s, sub, lanes] = basis
        return carry

    lax.fori_loop(0, live_count(mig_ref), one_slot, 0)


def rho_kernel(slab_count, lists_ref, mig_ref, phi_ref, *refs):
    slabs = refs[:slab_count]
    chi_ref, rho_ref, tiles, sems = refs[slab_count:]
    blk = lax.axis_index("blk")
    me = lax.axis_index("grid")
    length = lists_ref.shape[1]
    depth = slabs[0].shape[0]
    copies = []
    for e in range(slab_count):
        place = aligned(jnp.bitwise_xor(me, e) * depth, depth)
        copies.append(pltpu.make_async_copy(slabs[e], tiles.at[place], sems.at[e]))
    for copy in copies:
        copy.start()
    rho_ref[...] = jnp.zeros_like(rho_ref)
    for copy in copies:
        copy.wait()

    def one_slot(s, carry):
        own = lists_ref[s, blk] - blk * BPD
        cols = aligned(own * BLOCK, BLOCK)
        chi = None
        for j in range(length):
            k = lists_ref[s, lax.rem(blk + j, length)]
            tile = tiles[aligned(k * BLOCK, BLOCK), cols]
            part = lax.dot_general(
                tile,
                phi_ref[s, j],
                (((0,), (0,)), ((), ())),
                preferred_element_type=jnp.float32,
            )
            chi = part if chi is None else chi + part
        chi_ref[s] = chi
        rho_ref[pl.ds(s, 1), :] = jnp.sum(
            phi_ref[s, 0].astype(jnp.float32) * chi, axis=0, keepdims=True
        )
        return carry

    lax.fori_loop(0, live_count(mig_ref), one_slot, 0)


def force_kernel(
    lists_ref,
    mig_ref,
    points_ref,
    rho_a_ref,
    rho_b_ref,
    chi_ref,
    radial_ref,
    basis_ref,
    table_ref,
    out_ref,
    pot_ref,
    acc,
    energy_rows,
):
    blk = lax.axis_index("blk")
    slots, _, point_count = points_ref.shape
    dests = energy_rows.shape[1]
    live = live_count(mig_ref)
    rho = rho_a_ref[...] + rho_b_ref[...]
    weight = points_ref[:, 3, :]
    log_sq = jnp.log(rho * rho + RHO_SOFT * RHO_SOFT)
    pot_ref[...] = weight * (-(4.0 / 3.0) * SLATER) * rho * jnp.exp(log_sq * (-1.0 / 3.0))
    energies = jnp.sum(weight * -SLATER * jnp.exp(log_sq * (2.0 / 3.0)), axis=1, keepdims=True)
    energy_rows[...] = jnp.zeros_like(energy_rows)
    acc[...] = jnp.zeros_like(acc)
    dest_ids = lax.broadcasted_iota(jnp.int32, (1, dests), 1)

    def one_slot(s, carry):
        energy_rows[pl.ds(s, 1), :] = jnp.where(dest_ids == mig_ref[s], 1.0, 0.0)
        own = lists_ref[s, blk] - blk * BPD
        pot = pot_ref[pl.ds(s, 1), :]
        for r in range(0, BLOCK, ROWS):
            sub = slice(r, r + ROWS)
            sums = None
            for h in range(0, point_count, LANES):
                lanes = slice(h, h + LANES)
                u = chi_ref[s, sub, lanes] * pot[:, lanes]
                ub = u * basis_ref[s, sub, lanes]
                terms = (
                    u * radial_ref[s, sub, lanes],
                    ub,
                    ub * points_ref[s, 0:1, lanes],
                    ub * points_ref[s, 1:2, lanes],
                    ub * points_ref[s, 2:3, lanes],
                )
                sums = terms if sums is None else [a + b for a, b in zip(sums, terms)]
            for q in range(5):
                acc[own, q, sub] += sums[q]
        return carry

    lax.fori_loop(0, live, one_slot, 0)

    lane_ids = lax.broadcasted_iota(jnp.int32, (1, LANES), 1).astype(jnp.float32)

    def one_block(b, totals):
        k = blk * BPD + b
        totals = list(totals)
        for r in range(0, BLOCK, ROWS):
            sub = slice(r, r + ROWS)
            doubled = 2.0 * table_ref[k, 6, sub]
            plain = acc[b, 1, sub]
            atom = table_ref[k, 7, sub]
            for c in range(3):
                force = table_ref[k, 3 + c, sub] * acc[b, 0, sub] - doubled * (
                    acc[b, 2 + c, sub] - table_ref[k, c, sub] * plain
                )
                column = 2.0 * jnp.sum(force, axis=1, keepdims=True)
                for h in range(NATOM // LANES):
                    hit = jnp.where(atom == lane_ids + float(h * LANES), column, 0.0)
                    i = c * (NATOM // LANES) + h
                    totals[i] = totals[i] + sum(hit[i8 : i8 + 8] for i8 in range(0, ROWS, 8))
        return tuple(totals)

    zero = jnp.zeros((8, LANES), jnp.float32)
    count = 3 * NATOM // LANES
    totals = lax.fori_loop(0, BPD, one_block, (zero,) * count)
    rows = [jnp.sum(t, axis=0, keepdims=True) for t in totals]
    moved = jnp.sum(energy_rows[...] * energies, axis=0, keepdims=True)
    rows += [moved[:, h : h + LANES] for h in range(0, dests, LANES)]
    for i, row in enumerate(rows):
        out_ref[:, i, :] = jnp.broadcast_to(row, (out_ref.shape[0], LANES))


def sum_kernel(copies, arrived_ref, energy_ref, forces_ref):
    me = lax.axis_index("grid")
    total = jnp.sum(arrived_ref[...], axis=0)
    per = NATOM // LANES
    for c in range(3):
        for h in range(per):
            forces_ref[c : c + 1, h * LANES : (h + 1) * LANES] = total[c * per + h : c * per + h + 1]
    width = energy_ref.shape[1]
    first = me * width
    energy = jnp.zeros((1, LANES), jnp.float32)
    for i in range(3 * per, total.shape[0]):
        chosen = lax.div(first, LANES) == i - 3 * per
        energy = jnp.where(chosen, total[i : i + 1], energy)
    energy = pltpu.roll(jnp.broadcast_to(energy, (8, LANES)), lax.rem(LANES - lax.rem(first, LANES), LANES), 1)
    energy_ref[...] = energy[0:1, 0:width] * (1.0 / copies)


def gather_slabs(slab, grid_count):
    held = {0: slab}
    step = grid_count // 2
    while step:
        perm = [(i, i ^ step) for i in range(grid_count)]
        held.update({e ^ step: lax.ppermute(held[e], "grid", perm) for e in list(held)})
        step //= 2
    return [held[e] for e in range(grid_count)]


def spec(space):
    return pl.BlockSpec(memory_space=space)


def params():
    return pltpu.CompilerParams(vmem_limit_bytes=48 * 1024 * 1024)


def f32(*shape):
    return jax.ShapeDtypeStruct(shape, jnp.float32)


def local(density, points, sig_blocks, migration, atom_coords, exponents, shape_coef, func_atom):
    grid_count = lax.axis_size("grid")
    blk_count = lax.axis_size("blk")
    slots, _, point_count = points.shape
    length = sig_blocks.shape[1]
    functions = exponents.shape[0]
    blocks = functions // BLOCK
    dests = grid_count * (slots // 2)
    slab = density.T
    slabs = gather_slabs(slab, grid_count)

    table = pl.pallas_call(
        table_kernel,
        out_shape=f32(blocks, 8, BLOCK, LANES),
        in_specs=[spec(VMEM)] * 4,
        out_specs=spec(VMEM),
        scratch_shapes=[
            pltpu.VMEM((8, NATOM), jnp.float32),
            pltpu.VMEM((BLOCK, LANES), jnp.float32),
        ],
        compiler_params=params(),
        name="param_table",
    )(func_atom.reshape(1, functions), exponents.reshape(1, functions), shape_coef, atom_coords)

    phi, radial, basis = pl.pallas_call(
        phi_kernel,
        out_shape=[
            jax.ShapeDtypeStruct((slots, length, BLOCK, point_count), jnp.bfloat16),
            f32(slots, BLOCK, point_count),
            f32(slots, BLOCK, point_count),
        ],
        in_specs=[spec(SMEM), spec(SMEM), spec(VMEM), spec(VMEM)],
        out_specs=[spec(VMEM)] * 3,
        compiler_params=params(),
        name="basis_values",
    )(sig_blocks, migration, points, table)

    chi, rho = pl.pallas_call(
        functools.partial(rho_kernel, grid_count),
        out_shape=[f32(slots, BLOCK, point_count), f32(slots, point_count)],
        in_specs=[spec(SMEM), spec(SMEM), spec(VMEM)] + [spec(pl.ANY)] * grid_count,
        out_specs=[spec(VMEM)] * 2,
        scratch_shapes=[
            pltpu.VMEM((functions, BPD * BLOCK), jnp.bfloat16),
            pltpu.SemaphoreType.DMA((grid_count,)),
        ],
        compiler_params=params(),
        name="density_at_points",
    )(sig_blocks, migration, phi, *slabs)

    if blk_count == 2:
        other = lax.ppermute(rho, "blk", [(0, 1), (1, 0)])
    else:
        other = lax.psum(rho, "blk") - rho

    rows = 3 * NATOM // LANES + dests // LANES
    outgoing = pl.pallas_call(
        force_kernel,
        out_shape=f32(blk_count * grid_count, rows, LANES),
        in_specs=[spec(SMEM), spec(SMEM)] + [spec(VMEM)] * 7,
        out_specs=spec(VMEM),
        scratch_shapes=[
            pltpu.VMEM((slots, point_count), jnp.float32),
            pltpu.VMEM((BPD, 5, BLOCK, LANES), jnp.float32),
            pltpu.VMEM((slots, dests), jnp.float32),
        ],
        compiler_params=params(),
        name="forces_and_energies",
    )(sig_blocks, migration, points, rho, other, chi, radial, basis, table)

    arrived = lax.all_to_all(outgoing, ("blk", "grid"), split_axis=0, concat_axis=0, tiled=True)

    energy, forces = pl.pallas_call(
        functools.partial(sum_kernel, blk_count),
        out_shape=[f32(1, dests // grid_count), f32(3, NATOM)],
        in_specs=[spec(VMEM)],
        out_specs=[spec(VMEM)] * 2,
        compiler_params=params(),
        name="final_sums",
    )(arrived)
    return (energy.reshape(dests // grid_count), forces)


def solution(mesh):
    in_specs = (
        P("blk", "grid"),
        P("grid", None, None),
        P("grid", None),
        P("grid"),
        P(),
        P(),
        P(),
        P(),
    )
    out_specs = (P("grid"), P())
    return jax.shard_map(local, mesh=mesh, in_specs=in_specs, out_specs=out_specs, check_vma=False)
```

```python
import functools

import jax
import jax.numpy as jnp
from jax import lax
from jax.experimental import pallas as pl
from jax.experimental.pallas import tpu as pltpu
from jax.sharding import PartitionSpec as P

BLOCK = 128
BPD = 6
NATOM = 256
LANES = 128
ROWS = 32
UNROLL = 4
CHUNKS = 2

SLATER = 0.7386
RHO_SOFT = 0.05

VMEM = pltpu.MemorySpace.VMEM
SMEM = pltpu.MemorySpace.SMEM


def aligned(start, size):
    return pl.ds(pl.multiple_of(start, size), size)


def live_count(mig_ref):
    return lax.fori_loop(
        0,
        mig_ref.shape[0],
        lambda s, n: n + jnp.where(mig_ref[s] >= 0, 1, 0),
        jnp.int32(0),
    )


def table_kernel(mig_ref, atom_ref, expo_ref, coef_ref, coords_ref, table_ref, dest_ref):
    coords = coords_ref[...]
    high = coords.astype(jnp.bfloat16)
    rest = coords - high.astype(jnp.float32)
    mid = rest.astype(jnp.bfloat16)
    low = (rest - mid.astype(jnp.float32)).astype(jnp.bfloat16)

    def one_block(k):
        cols = aligned(k * BLOCK, BLOCK)
        atom = atom_ref[0:1, cols]
        onehot = jnp.where(
            lax.broadcasted_iota(jnp.int32, (NATOM, BLOCK), 0) == atom, 1.0, 0.0
        ).astype(jnp.bfloat16)
        picked = [
            jnp.dot(part, onehot, preferred_element_type=jnp.float32) for part in (high, mid, low)
        ]
        center = (picked[0] + picked[1]) + picked[2]
        rows = jnp.concatenate(
            [center, coef_ref[:, cols], expo_ref[0:1, cols], atom.astype(jnp.float32)], axis=0
        )
        columns = rows.T
        for p in range(8):
            table_ref[k, p] = jnp.broadcast_to(columns[:, p : p + 1], (BLOCK, LANES))

    def some_blocks(i, carry):
        for u in range(BPD):
            one_block(i * BPD + u)
        return carry

    lax.fori_loop(0, table_ref.shape[0] // BPD, some_blocks, 0)

    dest_ids = lax.broadcasted_iota(jnp.int32, (1, dest_ref.shape[1]), 1)

    for s in range(mig_ref.shape[0]):
        dest_ref[s : s + 1, :] = jnp.where(dest_ids == mig_ref[s], 1.0, 0.0)


def chunk_steps(mig_ref, first, size):
    left = jnp.clip(live_count(mig_ref) - first, 0, size)
    return lax.div(left + (UNROLL - 1), UNROLL)


def phi_kernel(first, lists_ref, mig_ref, points_ref, table_ref, phi_ref, radial_ref, basis_ref):
    blk = lax.axis_index("blk")
    length = lists_ref.shape[1]
    point_count = points_ref.shape[2]

    def one_slot(s):
        for j in range(length):
            k = lists_ref[first + s, lax.rem(blk + j, length)]
            for r in range(0, BLOCK, ROWS):
                sub = slice(r, r + ROWS)
                cx, cy, cz, sx, sy, sz, expo = [table_ref[k, p, sub] for p in range(7)]
                for h in range(0, point_count, LANES):
                    lanes = slice(h, h + LANES)
                    ox = points_ref[first + s, 0:1, lanes] - cx
                    oy = points_ref[first + s, 1:2, lanes] - cy
                    oz = points_ref[first + s, 2:3, lanes] - cz
                    squared = ox * ox + oy * oy + oz * oz
                    radial = jnp.exp(-expo * squared)
                    linear = 1.0 + (sx * ox + sy * oy + sz * oz)
                    basis = linear * radial
                    phi_ref[s, j, sub, lanes] = basis.astype(jnp.bfloat16)
                    if j == 0:
                        radial_ref[s, sub, lanes] = radial
                        basis_ref[s, sub, lanes] = basis

    def some_slots(i, carry):
        for u in range(2):
            one_slot(i * 2 + u)
        return carry

    steps = chunk_steps(mig_ref, first, phi_ref.shape[0]) * (UNROLL // 2)
    lax.fori_loop(0, steps, some_slots, 0)


def rho_kernel(slab_count, chunks, lists_ref, mig_ref, *refs):
    phis = refs[:chunks]
    slabs = refs[chunks : chunks + slab_count]
    chi_ref, rho_ref, tiles, sems = refs[chunks + slab_count :]
    blk = lax.axis_index("blk")
    me = lax.axis_index("grid")
    length = lists_ref.shape[1]
    depth = slabs[0].shape[0]
    copies = []
    for e in range(slab_count):
        place = aligned(jnp.bitwise_xor(me, e) * depth, depth)
        copies.append(pltpu.make_async_copy(slabs[e], tiles.at[place], sems.at[e]))
    for copy in copies:
        copy.start()
    rho_ref[...] = jnp.zeros_like(rho_ref)
    for copy in copies:
        copy.wait()

    for c, phi_ref in enumerate(phis):
        size = phi_ref.shape[0]

        def one_slot(s, c=c, phi_ref=phi_ref, size=size):
            slot = c * size + s
            own = lists_ref[slot, blk]
            cols = aligned((own - blk * BPD) * BLOCK, BLOCK)
            phi = phi_ref[s, 0]
            chi = jnp.dot(
                tiles[aligned(own * BLOCK, BLOCK), cols], phi, preferred_element_type=jnp.float32
            )
            for j in range(1, length):
                k = lists_ref[slot, lax.rem(blk + j, length)]
                chi += lax.dot_general(
                    tiles[aligned(k * BLOCK, BLOCK), cols],
                    phi_ref[s, j],
                    (((0,), (0,)), ((), ())),
                    preferred_element_type=jnp.float32,
                )
            chi_ref[slot] = chi
            rho_ref[pl.ds(slot, 1), :] = jnp.sum(
                phi.astype(jnp.float32) * chi, axis=0, keepdims=True
            )

        def some_slots(i, carry, one_slot=one_slot):
            for u in range(UNROLL):
                one_slot(i * UNROLL + u)
            return carry

        lax.fori_loop(0, chunk_steps(mig_ref, c * size, size), some_slots, 0)


def force_kernel(chunks, lists_ref, mig_ref, points_ref, rho_a_ref, rho_b_ref, chi_ref, *refs):
    radials = refs[:chunks]
    bases = refs[chunks : 2 * chunks]
    table_ref, dest_ref, out_ref, pot_ref, *accs = refs[2 * chunks :]
    blk = lax.axis_index("blk")
    slots, _, point_count = points_ref.shape
    dests = dest_ref.shape[1]
    live = live_count(mig_ref)
    rho = rho_a_ref[...] + rho_b_ref[...]
    weight = points_ref[:, 3, :]
    log_sq = jnp.log(rho * rho + RHO_SOFT * RHO_SOFT)
    pot = weight * (-(4.0 / 3.0) * SLATER) * rho * jnp.exp(log_sq * (-1.0 / 3.0))
    slot_ids = lax.broadcasted_iota(jnp.int32, (slots, 1), 0)
    pot_ref[...] = jnp.where(slot_ids < live, pot, 0.0)
    energies = jnp.sum(weight * -SLATER * jnp.exp(log_sq * (2.0 / 3.0)), axis=1, keepdims=True)
    for acc in accs:
        acc[...] = jnp.zeros_like(acc)

    for c in range(chunks):
        radial_ref, basis_ref = radials[c], bases[c]
        size = radial_ref.shape[0]

        def one_slot(s, acc, c=c, radial_ref=radial_ref, basis_ref=basis_ref, size=size):
            slot = c * size + s
            own = lists_ref[slot, blk] - blk * BPD
            pots = pot_ref[pl.ds(slot, 1), :]
            for r in range(0, BLOCK, ROWS):
                sub = slice(r, r + ROWS)
                sums = None
                for h in range(0, point_count, LANES):
                    lanes = slice(h, h + LANES)
                    u = chi_ref[slot, sub, lanes] * pots[:, lanes]
                    ub = u * basis_ref[s, sub, lanes]
                    terms = (
                        u * radial_ref[s, sub, lanes],
                        ub,
                        ub * points_ref[slot, 0:1, lanes],
                        ub * points_ref[slot, 1:2, lanes],
                        ub * points_ref[slot, 2:3, lanes],
                    )
                    sums = terms if sums is None else [a + b for a, b in zip(sums, terms)]
                for q in range(5):
                    acc[own, q, sub] += sums[q]

        def some_slots(i, carry, one_slot=one_slot):
            for u in range(UNROLL):
                one_slot(i * UNROLL + u, accs[u % len(accs)])
            return carry

        lax.fori_loop(0, chunk_steps(mig_ref, c * size, size), some_slots, 0)

    lane_ids = lax.broadcasted_iota(jnp.int32, (1, LANES), 1).astype(jnp.float32)

    def one_block(b, totals):
        k = blk * BPD + b
        totals = list(totals)
        for r in range(0, BLOCK, ROWS):
            sub = slice(r, r + ROWS)
            parts = [sum(acc[b, q, sub] for acc in accs) for q in range(5)]
            doubled = 2.0 * table_ref[k, 6, sub]
            atom = table_ref[k, 7, sub]
            for c in range(3):
                force = table_ref[k, 3 + c, sub] * parts[0] - doubled * (
                    parts[2 + c] - table_ref[k, c, sub] * parts[1]
                )
                column = 2.0 * jnp.sum(force, axis=1, keepdims=True)
                for h in range(NATOM // LANES):
                    hit = jnp.where(atom == lane_ids + float(h * LANES), column, 0.0)
                    i = c * (NATOM // LANES) + h
                    totals[i] = totals[i] + sum(hit[i8 : i8 + 8] for i8 in range(0, ROWS, 8))
        return tuple(totals)

    zero = jnp.zeros((8, LANES), jnp.float32)
    count = 3 * NATOM // LANES
    totals = lax.fori_loop(0, BPD, one_block, (zero,) * count)
    rows = [jnp.sum(t, axis=0, keepdims=True) for t in totals]
    moved = jnp.sum(dest_ref[...] * energies, axis=0, keepdims=True)
    rows += [moved[:, h : h + LANES] for h in range(0, dests, LANES)]
    for i, row in enumerate(rows):
        out_ref[:, i, :] = jnp.broadcast_to(row, (out_ref.shape[0], LANES))


def sum_kernel(copies, arrived_ref, energy_ref, forces_ref):
    me = lax.axis_index("grid")
    total = jnp.sum(arrived_ref[...], axis=0)
    per = NATOM // LANES
    for c in range(3):
        for h in range(per):
            forces_ref[c : c + 1, h * LANES : (h + 1) * LANES] = total[c * per + h : c * per + h + 1]
    width = energy_ref.shape[1]
    first = me * width
    energy = jnp.zeros((1, LANES), jnp.float32)
    for i in range(3 * per, total.shape[0]):
        chosen = lax.div(first, LANES) == i - 3 * per
        energy = jnp.where(chosen, total[i : i + 1], energy)
    energy = pltpu.roll(jnp.broadcast_to(energy, (8, LANES)), lax.rem(LANES - lax.rem(first, LANES), LANES), 1)
    energy_ref[...] = energy[0:1, 0:width] * (1.0 / copies)


def swap(array, offset):
    count = lax.axis_size("grid")
    return lax.ppermute(array, "grid", [(i, i ^ offset) for i in range(count)])


def spec(space):
    return pl.BlockSpec(memory_space=space)


def params():
    return pltpu.CompilerParams(vmem_limit_bytes=12 * 1024 * 1024)


def cost(nominal_us):
    return pl.CostEstimate(
        flops=0, bytes_accessed=int(nominal_us * 3.69e6), transcendentals=0
    )


def f32(*shape):
    return jax.ShapeDtypeStruct(shape, jnp.float32)


def local(density, points, sig_blocks, migration, atom_coords, exponents, shape_coef, func_atom):
    grid_count = lax.axis_size("grid")
    blk_count = lax.axis_size("blk")
    slots, _, point_count = points.shape
    length = sig_blocks.shape[1]
    functions = exponents.shape[0]
    blocks = functions // BLOCK
    dests = grid_count * (slots // 2)
    size = slots // CHUNKS
    slab = density.T
    tied = lax.optimization_barrier

    held = {0: slab}
    side = 2
    far = [e for e in range(2 * side, grid_count, 2 * side)]
    for e in far + [side, 1]:
        held[e] = swap(slab, e)

    table, dest_mask = pl.pallas_call(
        table_kernel,
        out_shape=[f32(blocks, 8, BLOCK, LANES), f32(slots, dests)],
        in_specs=[spec(SMEM)] + [spec(VMEM)] * 4,
        out_specs=[spec(VMEM)] * 2,
        compiler_params=params(),
        cost_estimate=cost(4),
        name="param_table",
    )(migration, func_atom.reshape(1, functions), exponents.reshape(1, functions), shape_coef, atom_coords)

    def basis_chunk(c, points):
        return pl.pallas_call(
            functools.partial(phi_kernel, c * size),
            out_shape=[
                jax.ShapeDtypeStruct((size, length, BLOCK, point_count), jnp.bfloat16),
                f32(size, BLOCK, point_count),
                f32(size, BLOCK, point_count),
            ],
            in_specs=[spec(SMEM), spec(SMEM), spec(VMEM), spec(VMEM)],
            out_specs=[spec(VMEM)] * 3,
            compiler_params=params(),
            cost_estimate=cost(5),
            name="basis_values",
        )(sig_blocks, migration, points, table)

    first = basis_chunk(0, points)
    held, first, points = tied((held, first, points))
    for e in far:
        held[e ^ side] = swap(held[e], side)
    for e in far + [side]:
        held[e ^ 1] = swap(held[e], 1)
    second = basis_chunk(1, points)
    held, second, points = tied((held, second, points))
    for e in far:
        held[e ^ side ^ 1] = swap(held[e ^ side], 1)
    slabs = [held[e] for e in range(grid_count)]
    phis, radials, bases = zip(first, second)

    chi, rho = pl.pallas_call(
        functools.partial(rho_kernel, grid_count, CHUNKS),
        out_shape=[f32(slots, BLOCK, point_count), f32(slots, point_count)],
        in_specs=[spec(SMEM), spec(SMEM)]
        + [spec(VMEM)] * CHUNKS
        + [spec(pl.ANY)] * grid_count,
        out_specs=[spec(VMEM)] * 2,
        scratch_shapes=[
            pltpu.VMEM((functions, BPD * BLOCK), jnp.bfloat16),
            pltpu.SemaphoreType.DMA((grid_count,)),
        ],
        compiler_params=params(),
        cost_estimate=cost(5),
        name="density_at_points",
    )(sig_blocks, migration, *phis, *slabs)

    if blk_count == 2:
        other = lax.ppermute(rho, "blk", [(0, 1), (1, 0)])
    else:
        other = lax.psum(rho, "blk") - rho

    rows = 3 * NATOM // LANES + dests // LANES
    outgoing = pl.pallas_call(
        functools.partial(force_kernel, CHUNKS),
        out_shape=f32(blk_count * grid_count, rows, LANES),
        in_specs=[spec(SMEM), spec(SMEM)] + [spec(VMEM)] * (6 + 2 * CHUNKS),
        out_specs=spec(VMEM),
        scratch_shapes=[
            pltpu.VMEM((slots, point_count), jnp.float32),
            pltpu.VMEM((BPD, 5, BLOCK, LANES), jnp.float32),
            pltpu.VMEM((BPD, 5, BLOCK, LANES), jnp.float32),
        ],
        compiler_params=params(),
        cost_estimate=cost(5),
        name="forces_and_energies",
    )(sig_blocks, migration, points, rho, other, chi, *radials, *bases, table, dest_mask)

    arrived = lax.all_to_all(outgoing, ("blk", "grid"), split_axis=0, concat_axis=0, tiled=True)

    energy, forces = pl.pallas_call(
        functools.partial(sum_kernel, blk_count),
        out_shape=[f32(1, dests // grid_count), f32(3, NATOM)],
        in_specs=[spec(VMEM)],
        out_specs=[spec(VMEM)] * 2,
        compiler_params=params(),
        name="final_sums",
    )(arrived)
    return (energy.reshape(dests // grid_count), forces)


def solution(mesh):
    in_specs = (
        P("blk", "grid"),
        P("grid", None, None),
        P("grid", None),
        P("grid"),
        P(),
        P(),
        P(),
        P(),
    )
    out_specs = (P("grid"), P())
    return jax.shard_map(local, mesh=mesh, in_specs=in_specs, out_specs=out_specs, check_vma=False)
```

```python
import functools

import jax
import jax.numpy as jnp
from jax import lax
from jax.experimental import pallas as pl
from jax.experimental.pallas import tpu as pltpu
from jax.sharding import PartitionSpec as P

BLOCK = 128
BPD = 6
NATOM = 256
LANES = 128
ROWS = 32
UNROLL = 4
CHUNKS = 2

SLATER = 0.7386
RHO_SOFT = 0.05

VMEM = pltpu.MemorySpace.VMEM
SMEM = pltpu.MemorySpace.SMEM


def aligned(start, size):
    return pl.ds(pl.multiple_of(start, size), size)


def live_count(mig_ref):
    slots = mig_ref.shape[0]
    step = 1
    while step * 2 <= slots:
        step *= 2
    count = jnp.int32(0)
    while step:
        more = count + step
        found = mig_ref[jnp.minimum(more, slots) - 1] >= 0
        count = jnp.where(jnp.logical_and(more <= slots, found), more, count)
        step //= 2
    return count


def start_copies(pairs, sems):
    copies = [pltpu.make_async_copy(src, dst, sems.at[i]) for i, (src, dst) in enumerate(pairs)]
    for copy in copies:
        copy.start()
    return copies


def start_slabs(offsets, slabs, tiles, sems):
    me = lax.axis_index("grid")
    depth = slabs[0].shape[0] if slabs else 0
    places = [aligned(jnp.bitwise_xor(me, e) * depth, depth) for e in offsets]
    return start_copies([(slab, tiles.at[place]) for slab, place in zip(slabs, places)], sems)


def table_kernel(
    mig_hbm,
    atom_hbm,
    expo_hbm,
    coef_hbm,
    coords_hbm,
    points_hbm,
    lists_hbm,
    table_ref,
    dest_ref,
    points_out,
    lists_out,
    mig_out,
    mig_ref,
    atom_ref,
    expo_ref,
    coef_ref,
    coords_ref,
    sems,
):
    copies = start_copies(
        [
            (mig_hbm, mig_ref),
            (atom_hbm, atom_ref),
            (expo_hbm, expo_ref),
            (coef_hbm, coef_ref),
            (coords_hbm, coords_ref),
            (points_hbm, points_out),
            (lists_hbm, lists_out),
            (mig_hbm, mig_out),
        ],
        sems,
    )
    for copy in copies[:5]:
        copy.wait()
    coords = coords_ref[...]
    high = coords.astype(jnp.bfloat16)
    rest = coords - high.astype(jnp.float32)
    mid = rest.astype(jnp.bfloat16)
    low = (rest - mid.astype(jnp.float32)).astype(jnp.bfloat16)
    blocks = table_ref.shape[0]
    atoms = atom_ref[...].reshape(blocks, BLOCK)
    expos = expo_ref[...].reshape(blocks, BLOCK)

    for k in range(blocks):
        atom = atoms[k : k + 1]
        onehot = jnp.where(
            lax.broadcasted_iota(jnp.int32, (NATOM, BLOCK), 0) == atom, 1.0, 0.0
        ).astype(jnp.bfloat16)
        picked = [
            jnp.dot(part, onehot, preferred_element_type=jnp.float32) for part in (high, mid, low)
        ]
        center = (picked[0] + picked[1]) + picked[2]
        coef = coef_ref[:, k * BLOCK : (k + 1) * BLOCK]
        rows = jnp.concatenate(
            [center, coef, expos[k : k + 1], atom.astype(jnp.float32)], axis=0
        )
        columns = rows.T
        for p in range(8):
            table_ref[k, p] = jnp.broadcast_to(columns[:, p : p + 1], (BLOCK, LANES))

    dest_ids = lax.broadcasted_iota(jnp.int32, (1, dest_ref.shape[1]), 1)
    for s in range(mig_ref.shape[0]):
        dest_ref[s : s + 1, :] = jnp.where(dest_ids == mig_ref[s], 1.0, 0.0)
    for copy in copies[5:]:
        copy.wait()


def chunk_steps(mig_ref, first, size):
    left = jnp.clip(live_count(mig_ref) - first, 0, size)
    return lax.div(left + (UNROLL - 1), UNROLL)


def phi_kernel(first, offsets, placed, lists_ref, mig_ref, points_ref, table_ref, *refs):
    slabs = refs[: len(offsets)]
    phi_ref, radial_ref, basis_ref, *scratch = refs[len(offsets) + placed :]
    copies = start_slabs(offsets, slabs, *scratch) if offsets else []
    blk = lax.axis_index("blk")
    length = lists_ref.shape[0]
    point_count = points_ref.shape[2]

    def one_slot(s):
        for j in range(length):
            k = lists_ref[lax.rem(blk + j, length), first + s]
            for r in range(0, BLOCK, ROWS):
                sub = slice(r, r + ROWS)
                cx, cy, cz, sx, sy, sz, expo = [table_ref[k, p, sub] for p in range(7)]
                for h in range(0, point_count, LANES):
                    lanes = slice(h, h + LANES)
                    ox = points_ref[first + s, 0:1, lanes] - cx
                    oy = points_ref[first + s, 1:2, lanes] - cy
                    oz = points_ref[first + s, 2:3, lanes] - cz
                    squared = ox * ox + oy * oy + oz * oz
                    radial = jnp.exp(-expo * squared)
                    linear = 1.0 + (sx * ox + sy * oy + sz * oz)
                    basis = linear * radial
                    phi_ref[s, j, sub, lanes] = basis.astype(jnp.bfloat16)
                    if j == 0:
                        radial_ref[s, sub, lanes] = radial
                        basis_ref[s, sub, lanes] = basis

    def some_slots(i, carry):
        for u in range(2):
            one_slot(i * 2 + u)
        return carry

    steps = chunk_steps(mig_ref, first, phi_ref.shape[0]) * (UNROLL // 2)
    lax.fori_loop(0, steps, some_slots, 0)
    for copy in copies:
        copy.wait()


def rho_kernel(offsets, chunks, lists_ref, mig_ref, *refs):
    phis = refs[:chunks]
    slabs = refs[chunks : chunks + len(offsets)]
    tiles, chi_ref, rho_ref, *scratch = refs[chunks + len(offsets) :]
    if offsets:
        tiles = scratch[0]
    copies = start_slabs(offsets, slabs, *scratch) if offsets else []
    blk = lax.axis_index("blk")
    length = lists_ref.shape[0]
    rho_ref[...] = jnp.zeros_like(rho_ref)
    for copy in copies:
        copy.wait()

    for c, phi_ref in enumerate(phis):
        size = phi_ref.shape[0]

        def one_slot(s, c=c, phi_ref=phi_ref, size=size):
            slot = c * size + s
            own = lists_ref[blk, slot]
            cols = aligned((own - blk * BPD) * BLOCK, BLOCK)
            phi = phi_ref[s, 0]
            chi = jnp.dot(
                tiles[aligned(own * BLOCK, BLOCK), cols], phi, preferred_element_type=jnp.float32
            )
            for j in range(1, length):
                k = lists_ref[lax.rem(blk + j, length), slot]
                chi += lax.dot_general(
                    tiles[aligned(k * BLOCK, BLOCK), cols],
                    phi_ref[s, j],
                    (((0,), (0,)), ((), ())),
                    preferred_element_type=jnp.float32,
                )
            chi_ref[slot] = chi
            rho_ref[pl.ds(slot, 1), :] = jnp.sum(
                phi.astype(jnp.float32) * chi, axis=0, keepdims=True
            )

        def some_slots(i, carry, one_slot=one_slot):
            for u in range(UNROLL):
                one_slot(i * UNROLL + u)
            return carry

        lax.fori_loop(0, chunk_steps(mig_ref, c * size, size), some_slots, 0)


def force_kernel(chunks, lists_ref, mig_ref, points_ref, rho_a_ref, rho_b_ref, chi_ref, *refs):
    radials = refs[:chunks]
    bases = refs[chunks : 2 * chunks]
    table_ref, dest_ref, out_ref, pot_ref, acc = refs[2 * chunks :]
    blk = lax.axis_index("blk")
    slots, _, point_count = points_ref.shape
    dests = dest_ref.shape[1]
    live = live_count(mig_ref)
    rho = rho_a_ref[...] + rho_b_ref[...]
    weight = points_ref[:, 3, :]
    log_sq = jnp.log(rho * rho + RHO_SOFT * RHO_SOFT)
    pot = weight * (-(4.0 / 3.0) * SLATER) * rho * jnp.exp(log_sq * (-1.0 / 3.0))
    slot_ids = lax.broadcasted_iota(jnp.int32, (slots, 1), 0)
    pot_ref[...] = jnp.where(slot_ids < live, pot, 0.0)
    energies = jnp.sum(weight * -SLATER * jnp.exp(log_sq * (2.0 / 3.0)), axis=1, keepdims=True)
    acc[...] = jnp.zeros_like(acc)

    for c in range(chunks):
        radial_ref, basis_ref = radials[c], bases[c]
        size = radial_ref.shape[0]

        def one_slot(s, c=c, radial_ref=radial_ref, basis_ref=basis_ref, size=size):
            slot = c * size + s
            own = lists_ref[blk, slot] - blk * BPD
            pots = pot_ref[pl.ds(slot, 1), :]
            for r in range(0, BLOCK, ROWS):
                sub = slice(r, r + ROWS)
                sums = None
                for h in range(0, point_count, LANES):
                    lanes = slice(h, h + LANES)
                    u = chi_ref[slot, sub, lanes] * pots[:, lanes]
                    ub = u * basis_ref[s, sub, lanes]
                    terms = (
                        u * radial_ref[s, sub, lanes],
                        ub,
                        ub * points_ref[slot, 0:1, lanes],
                        ub * points_ref[slot, 1:2, lanes],
                        ub * points_ref[slot, 2:3, lanes],
                    )
                    sums = terms if sums is None else [a + b for a, b in zip(sums, terms)]
                for q in range(5):
                    acc[own, q, sub] += sums[q]

        def some_slots(i, carry, one_slot=one_slot):
            for u in range(UNROLL):
                one_slot(i * UNROLL + u)
            return carry

        lax.fori_loop(0, chunk_steps(mig_ref, c * size, size), some_slots, 0)

    lane_ids = lax.broadcasted_iota(jnp.int32, (1, LANES), 1).astype(jnp.float32)

    def one_block(b, totals):
        k = blk * BPD + b
        totals = list(totals)
        for r in range(0, BLOCK, ROWS):
            sub = slice(r, r + ROWS)
            parts = [acc[b, q, sub] for q in range(5)]
            doubled = 2.0 * table_ref[k, 6, sub]
            atom = table_ref[k, 7, sub]
            for c in range(3):
                force = table_ref[k, 3 + c, sub] * parts[0] - doubled * (
                    parts[2 + c] - table_ref[k, c, sub] * parts[1]
                )
                column = 2.0 * jnp.sum(force, axis=1, keepdims=True)
                for h in range(NATOM // LANES):
                    hit = jnp.where(atom == lane_ids + float(h * LANES), column, 0.0)
                    i = c * (NATOM // LANES) + h
                    totals[i] = totals[i] + sum(hit[i8 : i8 + 8] for i8 in range(0, ROWS, 8))
        return tuple(totals)

    zero = jnp.zeros((8, LANES), jnp.float32)
    count = 3 * NATOM // LANES
    totals = lax.fori_loop(0, BPD, one_block, (zero,) * count)
    rows = [jnp.sum(t, axis=0, keepdims=True) for t in totals]
    moved = jnp.sum(dest_ref[...] * energies, axis=0, keepdims=True)
    rows += [moved[:, h : h + LANES] for h in range(0, dests, LANES)]
    packed = jnp.concatenate(rows, axis=0)
    for i in range(out_ref.shape[0]):
        out_ref[i] = packed


def sum_kernel(copies, arrived_ref, energy_ref, forces_ref):
    me = lax.axis_index("grid")
    total = jnp.sum(arrived_ref[...], axis=0)
    per = NATOM // LANES
    for c in range(3):
        for h in range(per):
            forces_ref[c : c + 1, h * LANES : (h + 1) * LANES] = total[c * per + h : c * per + h + 1]
    width = energy_ref.shape[1]
    first = me * width
    energy = jnp.zeros((1, LANES), jnp.float32)
    for i in range(3 * per, total.shape[0]):
        chosen = lax.div(first, LANES) == i - 3 * per
        energy = jnp.where(chosen, total[i : i + 1], energy)
    energy = pltpu.roll(jnp.broadcast_to(energy, (8, LANES)), lax.rem(LANES - lax.rem(first, LANES), LANES), 1)
    energy_ref[...] = energy[0:1, 0:width] * (1.0 / copies)


def swap(array, offset):
    count = lax.axis_size("grid")
    return lax.ppermute(array, "grid", [(i, i ^ offset) for i in range(count)])


def gather_stages(grid_count):
    evens = {}
    for e in range(2, grid_count, 2):
        evens.setdefault(e.bit_count(), []).append(e)
    odds = sorted(range(1, grid_count, 2), key=lambda e: (e.bit_count(), -e))
    stages, done = [], {0}
    while len(done) < grid_count:
        stage = sorted(evens.get(len(stages) + 1, []), reverse=True)
        for e in list(odds):
            if e - 1 in done and len(stage) < 4:
                stage.append(e)
                odds.remove(e)
        stages.append(stage)
        done.update(stage)
    return stages


def in_hbm(array):
    return pltpu.with_memory_space_constraint(array, pltpu.HBM)


def spec(space):
    return pl.BlockSpec(memory_space=space)


def params(blocks):
    return pltpu.CompilerParams(vmem_limit_bytes=blocks * 1024 * 1024)


def cost(nominal_us):
    return pl.CostEstimate(
        flops=0, bytes_accessed=int(nominal_us * 3.69e6), transcendentals=0
    )


def f32(*shape):
    return jax.ShapeDtypeStruct(shape, jnp.float32)


def local(density, points, sig_blocks, migration, atom_coords, exponents, shape_coef, func_atom):
    grid_count = lax.axis_size("grid")
    blk_count = lax.axis_size("blk")
    slots, _, point_count = points.shape
    length = sig_blocks.shape[1]
    functions = exponents.shape[0]
    blocks = functions // BLOCK
    dests = grid_count * (slots // 2)
    size = slots // CHUNKS
    slab = density.T
    tied = lax.optimization_barrier
    lists = sig_blocks.T

    table, dest_mask, points, lists, migration = pl.pallas_call(
        table_kernel,
        out_shape=[
            f32(blocks, 8, BLOCK, LANES),
            f32(slots, dests),
            f32(*points.shape),
            jax.ShapeDtypeStruct(lists.shape, jnp.int32),
            jax.ShapeDtypeStruct(migration.shape, jnp.int32),
        ],
        in_specs=[spec(pltpu.HBM)] * 7,
        out_specs=[spec(VMEM)] * 5,
        scratch_shapes=[
            pltpu.SMEM((slots,), jnp.int32),
            pltpu.VMEM((functions,), jnp.int32),
            pltpu.VMEM((functions,), jnp.float32),
            pltpu.VMEM((3, functions), jnp.float32),
            pltpu.VMEM((3, NATOM), jnp.float32),
            pltpu.SemaphoreType.DMA((8,)),
        ],
        compiler_params=params(blocks),
        cost_estimate=cost(4),
        name="param_table",
    )(
        *[
            in_hbm(a)
            for a in (migration, func_atom, exponents, shape_coef, atom_coords, points, lists)
        ]
    )

    tile_shape = jax.ShapeDtypeStruct((functions, BPD * BLOCK), jnp.bfloat16)

    def basis_chunk(c, points, table, offsets=(), tiles=None):
        some = 1 if offsets else 0
        placed = 0 if tiles is None else 1
        return pl.pallas_call(
            functools.partial(phi_kernel, c * size, offsets, placed),
            out_shape=[
                jax.ShapeDtypeStruct((size, length, BLOCK, point_count), jnp.bfloat16),
                f32(size, BLOCK, point_count),
                f32(size, BLOCK, point_count),
            ]
            + [tile_shape] * some,
            in_specs=[spec(SMEM), spec(SMEM), spec(VMEM), spec(VMEM)]
            + [spec(pl.ANY)] * len(offsets)
            + [spec(pl.ANY)] * placed,
            out_specs=[spec(VMEM)] * 3 + [spec(pl.ANY)] * some,
            scratch_shapes=[pltpu.SemaphoreType.DMA((len(offsets),))] * some,
            input_output_aliases={4 + len(offsets): 3} if placed else {},
            compiler_params=params(blocks),
            cost_estimate=cost(5),
            name="basis_values",
        )(
            lists,
            migration,
            points,
            table,
            *[held[e] if e else in_hbm(slab) for e in offsets],
            *([tiles] * placed),
        )

    held = {0: slab}
    if grid_count <= 16:
        stages = gather_stages(grid_count)
        for e in stages[0]:
            held[e] = swap(slab, e)
        held, table = tied((held, table))
        ready = list(held)
        for e in stages[1]:
            held[e] = swap(held[e & (e - 1)], e & -e)
        *first, tiles = basis_chunk(0, points, table, ready, None)
        held, first, tiles, points = tied((held, first, tiles, points))
        for e in stages[2]:
            held[e] = swap(held[e & (e - 1)], e & -e)
        *second, tiles = basis_chunk(1, points, table, stages[1], tiles)
        held, second, tiles = tied((held, second, tiles))
        for stage in stages[3:]:
            for e in stage:
                held[e] = swap(held[e & (e - 1)], e & -e)
        late = [e for stage in stages[2:] for e in stage]
    else:
        tiles = lax.all_gather(slab, "grid", axis=0, tiled=True)
        first = basis_chunk(0, points, table)
        second = basis_chunk(1, points, table)
        late = []
    phis, radials, bases = zip(first, second)

    some = 1 if late else 0
    chi, rho, *_ = pl.pallas_call(
        functools.partial(rho_kernel, late, CHUNKS),
        out_shape=[f32(slots, BLOCK, point_count), f32(slots, point_count)] + [tile_shape] * some,
        in_specs=[spec(SMEM), spec(SMEM)]
        + [spec(VMEM)] * CHUNKS
        + [spec(pl.ANY)] * len(late)
        + [spec(VMEM)],
        out_specs=[spec(VMEM)] * (2 + some),
        scratch_shapes=[pltpu.SemaphoreType.DMA((len(late),))] * some,
        input_output_aliases={2 + CHUNKS + len(late): 2} if late else {},
        compiler_params=params(blocks),
        cost_estimate=cost(5),
        name="density_at_points",
    )(lists, migration, *phis, *[held[e] for e in late], tiles)

    if blk_count == 2:
        other = lax.ppermute(rho, "blk", [(0, 1), (1, 0)])
    else:
        other = lax.psum(rho, "blk") - rho

    rows = 3 * NATOM // LANES + dests // LANES
    outgoing = pl.pallas_call(
        functools.partial(force_kernel, CHUNKS),
        out_shape=f32(blk_count * grid_count, rows, LANES),
        in_specs=[spec(SMEM), spec(SMEM)] + [spec(VMEM)] * (6 + 2 * CHUNKS),
        out_specs=spec(VMEM),
        scratch_shapes=[
            pltpu.VMEM((slots, point_count), jnp.float32),
            pltpu.VMEM((BPD, 5, BLOCK, LANES), jnp.float32),
        ],
        compiler_params=params(blocks),
        cost_estimate=cost(5),
        name="forces_and_energies",
    )(lists, migration, points, rho, other, chi, *radials, *bases, table, dest_mask)

    arrived = lax.all_to_all(outgoing, ("blk", "grid"), split_axis=0, concat_axis=0, tiled=True)

    energy, forces = pl.pallas_call(
        functools.partial(sum_kernel, blk_count),
        out_shape=[f32(1, dests // grid_count), f32(3, NATOM)],
        in_specs=[spec(VMEM)],
        out_specs=[spec(VMEM)] * 2,
        compiler_params=params(blocks),
        name="final_sums",
    )(arrived)
    return (energy.reshape(dests // grid_count), forces)


def solution(mesh):
    in_specs = (
        P("blk", "grid"),
        P("grid", None, None),
        P("grid", None),
        P("grid"),
        P(),
        P(),
        P(),
        P(),
    )
    out_specs = (P("grid"), P())
    return jax.shard_map(local, mesh=mesh, in_specs=in_specs, out_specs=out_specs, check_vma=False)
```

```python
import functools

import jax
import jax.numpy as jnp
from jax import lax
from jax.experimental import pallas as pl
from jax.experimental.pallas import tpu as pltpu
from jax.sharding import PartitionSpec as P

BLOCK = 128
BPD = 6
NATOM = 256
LANES = 128
ROWS = 32
UNROLL = 4

SLATER = 0.7386
RHO_SOFT = 0.05

VMEM = pltpu.MemorySpace.VMEM
SMEM = pltpu.MemorySpace.SMEM


def aligned(start, size):
    return pl.ds(pl.multiple_of(start, size), size)


def live_count(mig_ref):
    slots = mig_ref.shape[0]
    step = 1
    while step * 2 <= slots:
        step *= 2
    count = jnp.int32(0)
    while step:
        more = count + step
        found = mig_ref[jnp.minimum(more, slots) - 1] >= 0
        count = jnp.where(jnp.logical_and(more <= slots, found), more, count)
        step //= 2
    return count


def start_copies(pairs, sems):
    copies = [pltpu.make_async_copy(src, dst, sems.at[i]) for i, (src, dst) in enumerate(pairs)]
    for copy in copies:
        copy.start()
    return copies


def place_slabs(offsets, slabs, tiles):
    me = lax.axis_index("grid")
    for e, slab in zip(offsets, slabs):
        depth = slab.shape[0]
        tiles[aligned(jnp.bitwise_xor(me, e) * depth, depth), :] = slab[...]


def table_kernel(
    mig_hbm,
    atom_hbm,
    expo_hbm,
    coef_hbm,
    coords_hbm,
    points_hbm,
    lists_hbm,
    table_ref,
    dest_ref,
    points_out,
    lists_out,
    mig_out,
    mig_ref,
    atom_ref,
    expo_ref,
    coef_ref,
    coords_ref,
    sems,
):
    copies = start_copies(
        [
            (mig_hbm, mig_ref),
            (atom_hbm, atom_ref),
            (expo_hbm, expo_ref),
            (coef_hbm, coef_ref),
            (coords_hbm, coords_ref),
            (points_hbm, points_out),
            (lists_hbm, lists_out),
            (mig_hbm, mig_out),
        ],
        sems,
    )
    for copy in copies[:5]:
        copy.wait()
    coords = coords_ref[...]
    high = coords.astype(jnp.bfloat16)
    rest = coords - high.astype(jnp.float32)
    mid = rest.astype(jnp.bfloat16)
    low = (rest - mid.astype(jnp.float32)).astype(jnp.bfloat16)
    blocks = table_ref.shape[0]
    atoms = atom_ref[...].reshape(blocks, BLOCK)
    expos = expo_ref[...].reshape(blocks, BLOCK)

    for k in range(blocks):
        atom = atoms[k : k + 1]
        onehot = jnp.where(
            lax.broadcasted_iota(jnp.int32, (NATOM, BLOCK), 0) == atom, 1.0, 0.0
        ).astype(jnp.bfloat16)
        picked = [
            jnp.dot(part, onehot, preferred_element_type=jnp.float32) for part in (high, mid, low)
        ]
        center = (picked[0] + picked[1]) + picked[2]
        coef = coef_ref[:, k * BLOCK : (k + 1) * BLOCK]
        rows = jnp.concatenate(
            [center, coef, expos[k : k + 1], atom.astype(jnp.float32)], axis=0
        )
        columns = rows.T
        for p in range(8):
            table_ref[k, p] = jnp.broadcast_to(columns[:, p : p + 1], (BLOCK, LANES))

    dest_ids = lax.broadcasted_iota(jnp.int32, (1, dest_ref.shape[1]), 1)
    for s in range(mig_ref.shape[0]):
        dest_ref[s : s + 1, :] = jnp.where(dest_ids == mig_ref[s], 1.0, 0.0)
    for copy in copies[5:]:
        copy.wait()


def chunk_steps(mig_ref, first, size):
    left = jnp.clip(live_count(mig_ref) - first, 0, size)
    return lax.div(left + (UNROLL - 1), UNROLL)


def phi_kernel(first, offsets, placed, lists_ref, mig_ref, points_ref, table_ref, *refs):
    slabs = refs[: len(offsets)]
    phi_ref, radial_ref, basis_ref, *tiles = refs[len(offsets) + placed :]
    if offsets:
        place_slabs(offsets, slabs, tiles[0])
    blk = lax.axis_index("blk")
    length = lists_ref.shape[0]
    point_count = points_ref.shape[2]

    def one_slot(s):
        for j in range(length):
            k = lists_ref[lax.rem(blk + j, length), first + s]
            for r in range(0, BLOCK, ROWS):
                sub = slice(r, r + ROWS)
                cx, cy, cz, sx, sy, sz, expo = [table_ref[k, p, sub] for p in range(7)]
                for h in range(0, point_count, LANES):
                    lanes = slice(h, h + LANES)
                    ox = points_ref[first + s, 0:1, lanes] - cx
                    oy = points_ref[first + s, 1:2, lanes] - cy
                    oz = points_ref[first + s, 2:3, lanes] - cz
                    squared = ox * ox + oy * oy + oz * oz
                    radial = jnp.exp(-expo * squared)
                    linear = 1.0 + (sx * ox + sy * oy + sz * oz)
                    basis = linear * radial
                    phi_ref[s, j, sub, lanes] = basis.astype(jnp.bfloat16)
                    if j == 0:
                        radial_ref[s, sub, lanes] = radial
                        basis_ref[s, sub, lanes] = basis

    def some_slots(i, carry):
        for u in range(2):
            one_slot(i * 2 + u)
        return carry

    steps = chunk_steps(mig_ref, first, phi_ref.shape[0]) * (UNROLL // 2)
    lax.fori_loop(0, steps, some_slots, 0)


def rho_kernel(offsets, starts, lists_ref, mig_ref, *refs):
    chunks = len(starts)
    phis = refs[:chunks]
    slabs = refs[chunks : chunks + len(offsets)]
    tiles, chi_ref, rho_ref, *placed = refs[chunks + len(offsets) :]
    if offsets:
        tiles = placed[0]
        place_slabs(offsets, slabs, tiles)
    blk = lax.axis_index("blk")
    length = lists_ref.shape[0]
    rho_ref[...] = jnp.zeros_like(rho_ref)

    for c, phi_ref in enumerate(phis):
        size = phi_ref.shape[0]

        def one_slot(s, first=starts[c], phi_ref=phi_ref):
            slot = first + s
            own = lists_ref[blk, slot]
            cols = aligned((own - blk * BPD) * BLOCK, BLOCK)
            phi = phi_ref[s, 0]
            chi = jnp.dot(
                tiles[aligned(own * BLOCK, BLOCK), cols], phi, preferred_element_type=jnp.float32
            )
            for j in range(1, length):
                k = lists_ref[lax.rem(blk + j, length), slot]
                chi += lax.dot_general(
                    tiles[aligned(k * BLOCK, BLOCK), cols],
                    phi_ref[s, j],
                    (((0,), (0,)), ((), ())),
                    preferred_element_type=jnp.float32,
                )
            chi_ref[slot] = chi
            rho_ref[pl.ds(slot, 1), :] = jnp.sum(
                phi.astype(jnp.float32) * chi, axis=0, keepdims=True
            )

        def some_slots(i, carry, one_slot=one_slot):
            for u in range(UNROLL):
                one_slot(i * UNROLL + u)
            return carry

        lax.fori_loop(0, chunk_steps(mig_ref, starts[c], size), some_slots, 0)


def force_kernel(starts, lists_ref, mig_ref, points_ref, rho_a_ref, rho_b_ref, chi_ref, *refs):
    chunks = len(starts)
    radials = refs[:chunks]
    bases = refs[chunks : 2 * chunks]
    table_ref, dest_ref, out_ref, pot_ref, acc = refs[2 * chunks :]
    blk = lax.axis_index("blk")
    slots, _, point_count = points_ref.shape
    dests = dest_ref.shape[1]
    live = live_count(mig_ref)
    rho = rho_a_ref[...] + rho_b_ref[...]
    weight = points_ref[:, 3, :]
    log_sq = jnp.log(rho * rho + RHO_SOFT * RHO_SOFT)
    pot = weight * (-(4.0 / 3.0) * SLATER) * rho * jnp.exp(log_sq * (-1.0 / 3.0))
    slot_ids = lax.broadcasted_iota(jnp.int32, (slots, 1), 0)
    pot_ref[...] = jnp.where(slot_ids < live, pot, 0.0)
    energies = jnp.sum(weight * -SLATER * jnp.exp(log_sq * (2.0 / 3.0)), axis=1, keepdims=True)
    acc[...] = jnp.zeros_like(acc)

    for c in range(chunks):
        radial_ref, basis_ref = radials[c], bases[c]
        size = radial_ref.shape[0]

        def one_slot(s, first=starts[c], radial_ref=radial_ref, basis_ref=basis_ref):
            slot = first + s
            own = lists_ref[blk, slot] - blk * BPD
            pots = pot_ref[pl.ds(slot, 1), :]
            for r in range(0, BLOCK, ROWS):
                sub = slice(r, r + ROWS)
                sums = None
                for h in range(0, point_count, LANES):
                    lanes = slice(h, h + LANES)
                    u = chi_ref[slot, sub, lanes] * pots[:, lanes]
                    ub = u * basis_ref[s, sub, lanes]
                    terms = (
                        u * radial_ref[s, sub, lanes],
                        ub,
                        ub * points_ref[slot, 0:1, lanes],
                        ub * points_ref[slot, 1:2, lanes],
                        ub * points_ref[slot, 2:3, lanes],
                    )
                    sums = terms if sums is None else [a + b for a, b in zip(sums, terms)]
                for q in range(5):
                    acc[own, q, sub] += sums[q]

        def some_slots(i, carry, one_slot=one_slot):
            for u in range(UNROLL):
                one_slot(i * UNROLL + u)
            return carry

        lax.fori_loop(0, chunk_steps(mig_ref, starts[c], size), some_slots, 0)

    lane_ids = lax.broadcasted_iota(jnp.int32, (1, LANES), 1).astype(jnp.float32)

    def one_block(b, totals):
        k = blk * BPD + b
        totals = list(totals)
        for r in range(0, BLOCK, ROWS):
            sub = slice(r, r + ROWS)
            parts = [acc[b, q, sub] for q in range(5)]
            doubled = 2.0 * table_ref[k, 6, sub]
            atom = table_ref[k, 7, sub]
            for c in range(3):
                force = table_ref[k, 3 + c, sub] * parts[0] - doubled * (
                    parts[2 + c] - table_ref[k, c, sub] * parts[1]
                )
                column = 2.0 * jnp.sum(force, axis=1, keepdims=True)
                for h in range(NATOM // LANES):
                    hit = jnp.where(atom == lane_ids + float(h * LANES), column, 0.0)
                    i = c * (NATOM // LANES) + h
                    totals[i] = totals[i] + sum(hit[i8 : i8 + 8] for i8 in range(0, ROWS, 8))
        return tuple(totals)

    zero = jnp.zeros((8, LANES), jnp.float32)
    count = 3 * NATOM // LANES
    totals = lax.fori_loop(0, BPD, one_block, (zero,) * count)
    rows = [jnp.sum(t, axis=0, keepdims=True) for t in totals]
    moved = jnp.sum(dest_ref[...] * energies, axis=0, keepdims=True)
    rows += [moved[:, h : h + LANES] for h in range(0, dests, LANES)]
    packed = jnp.concatenate(rows, axis=0)
    if len(out_ref.shape) == 2:
        out_ref[...] = packed
    else:
        for i in range(out_ref.shape[0]):
            out_ref[i] = packed


def group_kernel(own_ref, core_ref, blk_ref, both_ref, out_ref):
    total = (own_ref[...] + core_ref[...]) + (blk_ref[...] + both_ref[...])
    for i in range(out_ref.shape[0]):
        out_ref[i] = total


def sum_kernel(copies, arrived_ref, energy_ref, forces_ref):
    me = lax.axis_index("grid")
    total = jnp.sum(arrived_ref[...], axis=0)
    per = NATOM // LANES
    for c in range(3):
        for h in range(per):
            forces_ref[c : c + 1, h * LANES : (h + 1) * LANES] = total[c * per + h : c * per + h + 1]
    width = energy_ref.shape[1]
    first = me * width
    energy = jnp.zeros((1, LANES), jnp.float32)
    for i in range(3 * per, total.shape[0]):
        chosen = lax.div(first, LANES) == i - 3 * per
        energy = jnp.where(chosen, total[i : i + 1], energy)
    energy = pltpu.roll(jnp.broadcast_to(energy, (8, LANES)), lax.rem(LANES - lax.rem(first, LANES), LANES), 1)
    energy_ref[...] = energy[0:1, 0:width] * (1.0 / copies)


def swap(array, offset):
    count = lax.axis_size("grid")
    return lax.ppermute(array, "grid", [(i, i ^ offset) for i in range(count)])


def gather_stages(grid_count):
    del grid_count
    return [
        [(8, 0), (4, 0), (2, 0), (1, 0)],
        [(12, 8), (10, 8), (9, 8), (5, 4)],
        [(14, 10), (6, 4), (13, 12), (11, 10), (3, 2)],
        [(15, 14), (7, 6)],
    ]


def in_hbm(array):
    return pltpu.with_memory_space_constraint(array, pltpu.HBM)


def spec(space):
    return pl.BlockSpec(memory_space=space)


def params(blocks):
    return pltpu.CompilerParams(vmem_limit_bytes=blocks * 1024 * 1024)


def cost(nominal_us):
    return pl.CostEstimate(
        flops=0, bytes_accessed=int(nominal_us * 3.69e6), transcendentals=0
    )


def f32(*shape):
    return jax.ShapeDtypeStruct(shape, jnp.float32)


def local(density, points, sig_blocks, migration, atom_coords, exponents, shape_coef, func_atom):
    grid_count = lax.axis_size("grid")
    blk_count = lax.axis_size("blk")
    slots, _, point_count = points.shape
    length = sig_blocks.shape[1]
    functions = exponents.shape[0]
    blocks = functions // BLOCK
    dests = grid_count * (slots // 2)
    sizes = [slots // 4, slots // 2, slots // 4]
    starts = [0, slots // 4, slots // 4 * 3]
    slab = density.T
    tied = lax.optimization_barrier
    lists = sig_blocks.T

    table, dest_mask, points, lists, migration = pl.pallas_call(
        table_kernel,
        out_shape=[
            f32(blocks, 8, BLOCK, LANES),
            f32(slots, dests),
            f32(*points.shape),
            jax.ShapeDtypeStruct(lists.shape, jnp.int32),
            jax.ShapeDtypeStruct(migration.shape, jnp.int32),
        ],
        in_specs=[spec(pltpu.HBM)] * 7,
        out_specs=[spec(VMEM)] * 5,
        scratch_shapes=[
            pltpu.SMEM((slots,), jnp.int32),
            pltpu.VMEM((functions,), jnp.int32),
            pltpu.VMEM((functions,), jnp.float32),
            pltpu.VMEM((3, functions), jnp.float32),
            pltpu.VMEM((3, NATOM), jnp.float32),
            pltpu.SemaphoreType.DMA((8,)),
        ],
        compiler_params=params(blocks),
        cost_estimate=cost(4),
        name="param_table",
    )(
        *[
            in_hbm(a)
            for a in (migration, func_atom, exponents, shape_coef, atom_coords, points, lists)
        ]
    )

    tile_shape = jax.ShapeDtypeStruct((functions, BPD * BLOCK), jnp.bfloat16)

    def basis_chunk(c, points, table, offsets=(), tiles=None):
        size = sizes[c]
        some = 1 if offsets else 0
        placed = 0 if tiles is None else 1
        return pl.pallas_call(
            functools.partial(phi_kernel, starts[c], offsets, placed),
            out_shape=[
                jax.ShapeDtypeStruct((size, length, BLOCK, point_count), jnp.bfloat16),
                f32(size, BLOCK, point_count),
                f32(size, BLOCK, point_count),
            ]
            + [tile_shape] * some,
            in_specs=[spec(SMEM), spec(SMEM), spec(VMEM), spec(VMEM)]
            + [spec(VMEM)] * (len(offsets) + placed),
            out_specs=[spec(VMEM)] * (3 + some),
            input_output_aliases={4 + len(offsets): 3} if placed else {},
            compiler_params=params(blocks),
            cost_estimate=cost(5),
            name="basis_values",
        )(
            lists,
            migration,
            points,
            table,
            *[held[e] for e in offsets],
            *([tiles] * placed),
        )

    held = {0: slab}
    late = []
    if grid_count == 16:
        stages = gather_stages(grid_count)
        chunks = []
        tiles = None
        for i, stage in enumerate(stages):
            held.update({e: swap(held[source], e ^ source) for e, source in stage})
            if i < len(starts):
                chunk = basis_chunk(i, points, table, late, tiles)
                tiles = chunk[3] if late else None
                late = [e for e, _ in stage] + ([] if i else [0])
                chunks.append(chunk[:3])
                held, chunks, tiles = tied((held, chunks, tiles))
        late = [e for stage in stages[2:] for e, _ in stage]
    else:
        tiles = lax.all_gather(slab, "grid", axis=0, tiled=True)
        chunks = [basis_chunk(i, points, table) for i in range(len(starts))]
    phis, radials, bases = zip(*chunks)

    some = 1 if late else 0
    chi, rho, *_ = pl.pallas_call(
        functools.partial(rho_kernel, late, starts),
        out_shape=[f32(slots, BLOCK, point_count), f32(slots, point_count)] + [tile_shape] * some,
        in_specs=[spec(SMEM), spec(SMEM)]
        + [spec(VMEM)] * (len(starts) + len(late) + 1),
        out_specs=[spec(VMEM)] * (2 + some),
        input_output_aliases={2 + len(starts) + len(late): 2} if late else {},
        compiler_params=params(blocks),
        cost_estimate=cost(5),
        name="density_at_points",
    )(lists, migration, *phis, *[held[e] for e in late], tiles)

    if blk_count == 2:
        other = lax.ppermute(rho, "blk", [(0, 1), (1, 0)])
    else:
        other = lax.psum(rho, "blk") - rho

    rows = 3 * NATOM // LANES + dests // LANES
    grouped = blk_count == 2
    outgoing = pl.pallas_call(
        functools.partial(force_kernel, starts),
        out_shape=f32(rows, LANES) if grouped else f32(blk_count * grid_count, rows, LANES),
        in_specs=[spec(SMEM), spec(SMEM)] + [spec(VMEM)] * (6 + 2 * len(starts)),
        out_specs=spec(VMEM),
        scratch_shapes=[
            pltpu.VMEM((slots, point_count), jnp.float32),
            pltpu.VMEM((BPD, 5, BLOCK, LANES), jnp.float32),
        ],
        compiler_params=params(blocks),
        cost_estimate=cost(5),
        name="forces_and_energies",
    )(lists, migration, points, rho, other, chi, *radials, *bases, table, dest_mask)

    if grouped:
        everyone = blk_count * grid_count
        others = [
            lax.ppermute(outgoing, ("blk", "grid"), [(i, i ^ e) for i in range(everyone)])
            for e in (1, grid_count, grid_count ^ 1)
        ]
        outgoing = pl.pallas_call(
            group_kernel,
            out_shape=f32(grid_count // 2, rows, LANES),
            in_specs=[spec(VMEM)] * 4,
            out_specs=spec(VMEM),
            compiler_params=params(blocks),
            name="group_sums",
        )(outgoing, *others)
        arrived = lax.all_to_all(
            outgoing,
            "grid",
            split_axis=0,
            concat_axis=0,
            tiled=True,
            axis_index_groups=[list(range(c, grid_count, 2)) for c in range(2)],
        )
    else:
        arrived = lax.all_to_all(outgoing, ("blk", "grid"), split_axis=0, concat_axis=0, tiled=True)

    energy, forces = pl.pallas_call(
        functools.partial(sum_kernel, blk_count),
        out_shape=[f32(1, dests // grid_count), f32(3, NATOM)],
        in_specs=[spec(VMEM)],
        out_specs=[spec(VMEM)] * 2,
        compiler_params=params(blocks),
        name="final_sums",
    )(arrived)
    return (energy.reshape(dests // grid_count), forces)


def solution(mesh):
    in_specs = (
        P("blk", "grid"),
        P("grid", None, None),
        P("grid", None),
        P("grid"),
        P(),
        P(),
        P(),
        P(),
    )
    out_specs = (P("grid"), P())
    return jax.shard_map(local, mesh=mesh, in_specs=in_specs, out_specs=out_specs, check_vma=False)
```

```python
import functools

import jax
import jax.numpy as jnp
from jax import lax
from jax.experimental import pallas as pl
from jax.experimental.pallas import tpu as pltpu
from jax.sharding import PartitionSpec as P

BLOCK = 128
BPD = 6
NATOM = 256
LANES = 128
ROWS = 32
UNROLL = 4

SLATER = 0.7386
RHO_SOFT = 0.05

VMEM = pltpu.MemorySpace.VMEM
SMEM = pltpu.MemorySpace.SMEM


def aligned(start, size):
    return pl.ds(pl.multiple_of(start, size), size)


def live_count(mig_ref):
    slots = mig_ref.shape[0]
    step = 1
    while step * 2 <= slots:
        step *= 2
    count = jnp.int32(0)
    while step:
        more = count + step
        found = mig_ref[jnp.minimum(more, slots) - 1] >= 0
        count = jnp.where(jnp.logical_and(more <= slots, found), more, count)
        step //= 2
    return count


def start_copies(pairs, sems):
    copies = [pltpu.make_async_copy(src, dst, sems.at[i]) for i, (src, dst) in enumerate(pairs)]
    for copy in copies:
        copy.start()
    return copies


def place_slabs(offsets, slabs, tiles):
    me = lax.axis_index("grid")
    depth = slabs[0].shape[-2]

    def place(e, slab):
        tiles[aligned(jnp.bitwise_xor(me, e) * depth, depth), :] = slab

    for e, slab in zip(offsets, slabs):
        if isinstance(e, tuple):
            for i, one in enumerate(e):
                place(one, slab[i])
        else:
            place(e, slab[...])


def pack_kernel(*refs):
    *slabs, out_ref = refs
    for i, slab in enumerate(slabs):
        out_ref[i] = slab[...]


def table_kernel(
    mig_hbm,
    atom_hbm,
    expo_hbm,
    coef_hbm,
    coords_hbm,
    points_hbm,
    lists_hbm,
    table_ref,
    dest_ref,
    points_out,
    lists_out,
    mig_out,
    mig_ref,
    atom_ref,
    expo_ref,
    coef_ref,
    coords_ref,
    sems,
):
    copies = start_copies(
        [
            (mig_hbm, mig_ref),
            (atom_hbm, atom_ref),
            (expo_hbm, expo_ref),
            (coef_hbm, coef_ref),
            (coords_hbm, coords_ref),
            (points_hbm, points_out),
            (lists_hbm, lists_out),
            (mig_hbm, mig_out),
        ],
        sems,
    )
    for copy in copies[:5]:
        copy.wait()
    coords = coords_ref[...]
    high = coords.astype(jnp.bfloat16)
    rest = coords - high.astype(jnp.float32)
    mid = rest.astype(jnp.bfloat16)
    low = (rest - mid.astype(jnp.float32)).astype(jnp.bfloat16)
    blocks = table_ref.shape[0]
    atoms = atom_ref[...].reshape(blocks, BLOCK)
    expos = expo_ref[...].reshape(blocks, BLOCK)

    for k in range(blocks):
        atom = atoms[k : k + 1]
        onehot = jnp.where(
            lax.broadcasted_iota(jnp.int32, (NATOM, BLOCK), 0) == atom, 1.0, 0.0
        ).astype(jnp.bfloat16)
        picked = [
            jnp.dot(part, onehot, preferred_element_type=jnp.float32) for part in (high, mid, low)
        ]
        center = (picked[0] + picked[1]) + picked[2]
        coef = coef_ref[:, k * BLOCK : (k + 1) * BLOCK]
        rows = jnp.concatenate(
            [center, coef, expos[k : k + 1], atom.astype(jnp.float32)], axis=0
        )
        columns = rows.T
        for p in range(8):
            table_ref[k, p] = jnp.broadcast_to(columns[:, p : p + 1], (BLOCK, LANES))

    dest_ids = lax.broadcasted_iota(jnp.int32, (1, dest_ref.shape[1]), 1)
    for s in range(mig_ref.shape[0]):
        dest_ref[s : s + 1, :] = jnp.where(dest_ids == mig_ref[s], 1.0, 0.0)
    for copy in copies[5:]:
        copy.wait()


def chunk_steps(mig_ref, first, size):
    left = jnp.clip(live_count(mig_ref) - first, 0, size)
    return lax.div(left + (UNROLL - 1), UNROLL)


def phi_kernel(first, offsets, packed, lists_ref, mig_ref, points_ref, table_ref, *refs):
    slabs = refs[: len(offsets)]
    phi_ref, radial_ref, basis_ref, *more = refs[len(offsets) :]
    if offsets:
        place_slabs(offsets, slabs, more[0])
        pack_kernel(*[slabs[offsets.index(e)] for e in packed], more[1])
    blk = lax.axis_index("blk")
    length = lists_ref.shape[0]
    point_count = points_ref.shape[2]

    def one_slot(s):
        for j in range(length):
            k = lists_ref[lax.rem(blk + j, length), first + s]
            for r in range(0, BLOCK, ROWS):
                sub = slice(r, r + ROWS)
                cx, cy, cz, sx, sy, sz, expo = [table_ref[k, p, sub] for p in range(7)]
                for h in range(0, point_count, LANES):
                    lanes = slice(h, h + LANES)
                    ox = points_ref[first + s, 0:1, lanes] - cx
                    oy = points_ref[first + s, 1:2, lanes] - cy
                    oz = points_ref[first + s, 2:3, lanes] - cz
                    squared = ox * ox + oy * oy + oz * oz
                    radial = jnp.exp(-expo * squared)
                    linear = 1.0 + (sx * ox + sy * oy + sz * oz)
                    basis = linear * radial
                    phi_ref[s, j, sub, lanes] = basis.astype(jnp.bfloat16)
                    if j == 0:
                        radial_ref[s, sub, lanes] = radial
                        basis_ref[s, sub, lanes] = basis

    def some_slots(i, carry):
        for u in range(2):
            one_slot(i * 2 + u)
        return carry

    steps = chunk_steps(mig_ref, first, phi_ref.shape[0]) * (UNROLL // 2)
    lax.fori_loop(0, steps, some_slots, 0)


def rho_kernel(offsets, starts, lists_ref, mig_ref, *refs):
    chunks = len(starts)
    phis = refs[:chunks]
    slabs = refs[chunks : chunks + len(offsets)]
    tiles, chi_ref, rho_ref, *placed = refs[chunks + len(offsets) :]
    if offsets:
        tiles = placed[0]
        place_slabs(offsets, slabs, tiles)
    blk = lax.axis_index("blk")
    length = lists_ref.shape[0]
    rho_ref[...] = jnp.zeros_like(rho_ref)

    for c, phi_ref in enumerate(phis):
        size = phi_ref.shape[0]

        def one_slot(s, first=starts[c], phi_ref=phi_ref):
            slot = first + s
            own = lists_ref[blk, slot]
            cols = aligned((own - blk * BPD) * BLOCK, BLOCK)
            phi = phi_ref[s, 0]
            chi = jnp.dot(
                tiles[aligned(own * BLOCK, BLOCK), cols], phi, preferred_element_type=jnp.float32
            )
            for j in range(1, length):
                k = lists_ref[lax.rem(blk + j, length), slot]
                chi += lax.dot_general(
                    tiles[aligned(k * BLOCK, BLOCK), cols],
                    phi_ref[s, j],
                    (((0,), (0,)), ((), ())),
                    preferred_element_type=jnp.float32,
                )
            chi_ref[slot] = chi
            rho_ref[pl.ds(slot, 1), :] = jnp.sum(
                phi.astype(jnp.float32) * chi, axis=0, keepdims=True
            )

        def some_slots(i, carry, one_slot=one_slot):
            for u in range(UNROLL):
                one_slot(i * UNROLL + u)
            return carry

        lax.fori_loop(0, chunk_steps(mig_ref, starts[c], size), some_slots, 0)


def force_kernel(starts, lists_ref, mig_ref, points_ref, rho_a_ref, rho_b_ref, chi_ref, *refs):
    chunks = len(starts)
    radials = refs[:chunks]
    bases = refs[chunks : 2 * chunks]
    table_ref, dest_ref, out_ref, pot_ref, acc = refs[2 * chunks :]
    blk = lax.axis_index("blk")
    slots, _, point_count = points_ref.shape
    dests = dest_ref.shape[1]
    live = live_count(mig_ref)
    rho = rho_a_ref[...] + rho_b_ref[...]
    weight = points_ref[:, 3, :]
    log_sq = jnp.log(rho * rho + RHO_SOFT * RHO_SOFT)
    pot = weight * (-(4.0 / 3.0) * SLATER) * rho * jnp.exp(log_sq * (-1.0 / 3.0))
    slot_ids = lax.broadcasted_iota(jnp.int32, (slots, 1), 0)
    pot_ref[...] = jnp.where(slot_ids < live, pot, 0.0)
    energies = jnp.sum(weight * -SLATER * jnp.exp(log_sq * (2.0 / 3.0)), axis=1, keepdims=True)
    acc[...] = jnp.zeros_like(acc)

    for c in range(chunks):
        radial_ref, basis_ref = radials[c], bases[c]
        size = radial_ref.shape[0]

        def one_slot(s, first=starts[c], radial_ref=radial_ref, basis_ref=basis_ref):
            slot = first + s
            own = lists_ref[blk, slot] - blk * BPD
            pots = pot_ref[pl.ds(slot, 1), :]
            for r in range(0, BLOCK, ROWS):
                sub = slice(r, r + ROWS)
                sums = None
                for h in range(0, point_count, LANES):
                    lanes = slice(h, h + LANES)
                    u = chi_ref[slot, sub, lanes] * pots[:, lanes]
                    ub = u * basis_ref[s, sub, lanes]
                    terms = (
                        u * radial_ref[s, sub, lanes],
                        ub,
                        ub * points_ref[slot, 0:1, lanes],
                        ub * points_ref[slot, 1:2, lanes],
                        ub * points_ref[slot, 2:3, lanes],
                    )
                    sums = terms if sums is None else [a + b for a, b in zip(sums, terms)]
                for q in range(5):
                    acc[own, q, sub] += sums[q]

        def some_slots(i, carry, one_slot=one_slot):
            for u in range(UNROLL):
                one_slot(i * UNROLL + u)
            return carry

        lax.fori_loop(0, chunk_steps(mig_ref, starts[c], size), some_slots, 0)

    lane_ids = lax.broadcasted_iota(jnp.int32, (1, LANES), 1).astype(jnp.float32)

    totals = [jnp.zeros((8, LANES), jnp.float32)] * (3 * NATOM // LANES)
    for b in range(BPD):
        k = blk * BPD + b
        for r in range(0, BLOCK, ROWS):
            sub = slice(r, r + ROWS)
            parts = [acc[b, q, sub] for q in range(5)]
            doubled = 2.0 * table_ref[k, 6, sub]
            atom = table_ref[k, 7, sub]
            for c in range(3):
                force = table_ref[k, 3 + c, sub] * parts[0] - doubled * (
                    parts[2 + c] - table_ref[k, c, sub] * parts[1]
                )
                column = 2.0 * jnp.sum(force, axis=1, keepdims=True)
                for h in range(NATOM // LANES):
                    hit = jnp.where(atom == lane_ids + float(h * LANES), column, 0.0)
                    i = c * (NATOM // LANES) + h
                    totals[i] = totals[i] + sum(hit[i8 : i8 + 8] for i8 in range(0, ROWS, 8))
    rows = [jnp.sum(t, axis=0, keepdims=True) for t in totals]
    moved = jnp.sum(dest_ref[...] * energies, axis=0, keepdims=True)
    rows += [moved[:, h : h + LANES] for h in range(0, dests, LANES)]
    packed = jnp.concatenate(rows, axis=0)
    if len(out_ref.shape) == 2:
        out_ref[...] = packed
    else:
        for i in range(out_ref.shape[0]):
            out_ref[i] = packed


def tree_sum(parts):
    while len(parts) > 1:
        parts = [a + b for a, b in zip(parts[::2], parts[1::2])]
    return parts[0]


def group_kernel(*refs):
    *parts, out_ref = refs
    out_ref[...] = tree_sum([part[...] for part in parts])


def sum_kernel(copies, *refs):
    *arrived, energy_ref, forces_ref = refs
    me = lax.axis_index("grid")
    if len(arrived) == 1:
        total = jnp.sum(arrived[0][...], axis=0)
    else:
        total = tree_sum([part[...] for part in arrived])
    per = NATOM // LANES
    for c in range(3):
        for h in range(per):
            forces_ref[c : c + 1, h * LANES : (h + 1) * LANES] = total[c * per + h : c * per + h + 1]
    width = energy_ref.shape[1]
    first = me * width
    energy = jnp.zeros((1, LANES), jnp.float32)
    for i in range(3 * per, total.shape[0]):
        chosen = lax.div(first, LANES) == i - 3 * per
        energy = jnp.where(chosen, total[i : i + 1], energy)
    energy = pltpu.roll(jnp.broadcast_to(energy, (8, LANES)), lax.rem(LANES - lax.rem(first, LANES), LANES), 1)
    energy_ref[...] = energy[0:1, 0:width] * (1.0 / copies)


def swap(array, offset):
    count = lax.axis_size("grid")
    return lax.ppermute(array, "grid", [(i, i ^ offset) for i in range(count)])


STAGES = (((8, 0), (4, 0), (2, 0)), ((12, 8), (10, 8)), ((14, 10), (6, 4)))
PACKS = ((0, 8, 4, 2), (12, 10, 14, 6))


def in_hbm(array):
    return pltpu.with_memory_space_constraint(array, pltpu.HBM)


def spec(space):
    return pl.BlockSpec(memory_space=space)


def params(blocks):
    return pltpu.CompilerParams(vmem_limit_bytes=blocks * 1024 * 1024)


def cost(nominal_us):
    return pl.CostEstimate(
        flops=0, bytes_accessed=int(nominal_us * 3.69e6), transcendentals=0
    )


def f32(*shape):
    return jax.ShapeDtypeStruct(shape, jnp.float32)


def local(density, points, sig_blocks, migration, atom_coords, exponents, shape_coef, func_atom):
    grid_count = lax.axis_size("grid")
    blk_count = lax.axis_size("blk")
    slots, _, point_count = points.shape
    length = sig_blocks.shape[1]
    functions = exponents.shape[0]
    blocks = functions // BLOCK
    dests = grid_count * (slots // 2)
    sizes = [slots // 4, slots // 2, slots // 4]
    starts = [0, slots // 4, slots // 4 * 3]
    slab = density.T
    tied = lax.optimization_barrier
    lists = sig_blocks.T

    table, dest_mask, points, lists, migration = pl.pallas_call(
        table_kernel,
        out_shape=[
            f32(blocks, 8, BLOCK, LANES),
            f32(slots, dests),
            f32(*points.shape),
            jax.ShapeDtypeStruct(lists.shape, jnp.int32),
            jax.ShapeDtypeStruct(migration.shape, jnp.int32),
        ],
        in_specs=[spec(pltpu.HBM)] * 7,
        out_specs=[spec(VMEM)] * 5,
        scratch_shapes=[
            pltpu.SMEM((slots,), jnp.int32),
            pltpu.VMEM((functions,), jnp.int32),
            pltpu.VMEM((functions,), jnp.float32),
            pltpu.VMEM((3, functions), jnp.float32),
            pltpu.VMEM((3, NATOM), jnp.float32),
            pltpu.SemaphoreType.DMA((8,)),
        ],
        compiler_params=params(blocks),
        cost_estimate=cost(4),
        name="param_table",
    )(
        *[
            in_hbm(a)
            for a in (migration, func_atom, exponents, shape_coef, atom_coords, points, lists)
        ]
    )

    tile_shape = jax.ShapeDtypeStruct((functions, BPD * BLOCK), jnp.bfloat16)

    def basis_chunk(c, points, offsets=(), packed=()):
        some = 1 if offsets else 0
        return pl.pallas_call(
            functools.partial(phi_kernel, starts[c], offsets, packed),
            out_shape=[
                jax.ShapeDtypeStruct((sizes[c], length, BLOCK, point_count), jnp.bfloat16),
                f32(sizes[c], BLOCK, point_count),
                f32(sizes[c], BLOCK, point_count),
            ]
            + [tile_shape, jax.ShapeDtypeStruct((len(packed), *slab.shape), slab.dtype)] * some,
            in_specs=[spec(SMEM), spec(SMEM)] + [spec(VMEM)] * (2 + len(offsets)),
            out_specs=[spec(VMEM)] * (3 + 2 * some),
            compiler_params=params(blocks),
            cost_estimate=cost(5),
            name="basis_values",
        )(lists, migration, points, table, *[held[e] for e in offsets])

    held = {0: slab}
    late, slabs = [], []
    if grid_count == 16:
        held.update({e: swap(held[source], e ^ source) for e, source in STAGES[0]})
        first = basis_chunk(0, points)
        held, first, points = tied((held, first, points))
        held.update({e: swap(held[source], e ^ source) for e, source in STAGES[1]})
        *second, tiles, pack = basis_chunk(1, points, PACKS[0], PACKS[0])
        held, second, tiles, pack, points = tied((held, second, tiles, pack, points))
        held.update({e: swap(held[source], e ^ source) for e, source in STAGES[2]})
        crossed = swap(pack, 1)
        third = basis_chunk(2, points)
        held, crossed, third = tied((held, crossed, third))
        pack = pl.pallas_call(
            pack_kernel,
            out_shape=jax.ShapeDtypeStruct((len(PACKS[1]), *slab.shape), slab.dtype),
            in_specs=[spec(VMEM)] * len(PACKS[1]),
            out_specs=spec(VMEM),
            compiler_params=params(blocks),
            name="pack",
        )(*[held[e] for e in PACKS[1]])
        chunks = [first, second, third]
        late = [*PACKS[1], *[tuple(e ^ 1 for e in offsets) for offsets in PACKS]]
        slabs = [*[held[e] for e in PACKS[1]], crossed, swap(pack, 1)]
    else:
        tiles = lax.all_gather(slab, "grid", axis=0, tiled=True)
        chunks = [basis_chunk(i, points) for i in range(len(starts))]
    phis, radials, bases = zip(*chunks)

    some = 1 if late else 0
    chi, rho, *_ = pl.pallas_call(
        functools.partial(rho_kernel, late, starts),
        out_shape=[f32(slots, BLOCK, point_count), f32(slots, point_count)] + [tile_shape] * some,
        in_specs=[spec(SMEM), spec(SMEM)]
        + [spec(VMEM)] * (len(starts) + len(late) + 1),
        out_specs=[spec(VMEM)] * (2 + some),
        input_output_aliases={2 + len(starts) + len(late): 2} if late else {},
        compiler_params=params(blocks),
        cost_estimate=cost(5),
        name="density_at_points",
    )(lists, migration, *phis, *slabs, tiles)

    if blk_count == 2:
        other = lax.ppermute(rho, "blk", [(0, 1), (1, 0)])
    else:
        other = lax.psum(rho, "blk") - rho

    rows = 3 * NATOM // LANES + dests // LANES
    grouped = (blk_count, grid_count) == (2, 16)
    outgoing = pl.pallas_call(
        functools.partial(force_kernel, starts),
        out_shape=f32(rows, LANES) if grouped else f32(blk_count * grid_count, rows, LANES),
        in_specs=[spec(SMEM), spec(SMEM)] + [spec(VMEM)] * (6 + 2 * len(starts)),
        out_specs=spec(VMEM),
        scratch_shapes=[
            pltpu.VMEM((slots, point_count), jnp.float32),
            pltpu.VMEM((BPD, 5, BLOCK, LANES), jnp.float32),
        ],
        compiler_params=params(blocks),
        cost_estimate=cost(5),
        name="forces_and_energies",
    )(lists, migration, points, rho, other, chi, *radials, *bases, table, dest_mask)

    if grouped:
        def exchanged(part, offsets):
            everyone = blk_count * grid_count
            return [part] + [
                lax.ppermute(part, ("blk", "grid"), [(i, i ^ e) for i in range(everyone)])
                for e in offsets[1:]
            ]

        near = [high + low for high in (0, grid_count) for low in range(4)]
        outgoing = pl.pallas_call(
            group_kernel,
            out_shape=f32(rows, LANES),
            in_specs=[spec(VMEM)] * len(near),
            out_specs=spec(VMEM),
            compiler_params=params(blocks),
            name="group_sums",
        )(*exchanged(outgoing, near))
        arrived = exchanged(outgoing, range(0, grid_count, 4))
    else:
        arrived = [
            lax.all_to_all(outgoing, ("blk", "grid"), split_axis=0, concat_axis=0, tiled=True)
        ]

    energy, forces = pl.pallas_call(
        functools.partial(sum_kernel, blk_count),
        out_shape=[f32(1, dests // grid_count), f32(3, NATOM)],
        in_specs=[spec(VMEM)] * len(arrived),
        out_specs=[spec(VMEM)] * 2,
        compiler_params=params(blocks),
        name="final_sums",
    )(*arrived)
    return (energy.reshape(dests // grid_count), forces)


def solution(mesh):
    in_specs = (
        P("blk", "grid"),
        P("grid", None, None),
        P("grid", None),
        P("grid"),
        P(),
        P(),
        P(),
        P(),
    )
    out_specs = (P("grid"), P())
    return jax.shard_map(local, mesh=mesh, in_specs=in_specs, out_specs=out_specs, check_vma=False)
```

```python
import functools

import jax
import jax.numpy as jnp
from jax import lax
from jax.experimental import pallas as pl
from jax.experimental.pallas import tpu as pltpu
from jax.sharding import PartitionSpec as P

BLOCK = 128
BPD = 6
NATOM = 256
LANES = 128
ROWS = 32
UNROLL = 4

SLATER = 0.7386
RHO_SOFT = 0.05

VMEM = pltpu.MemorySpace.VMEM
SMEM = pltpu.MemorySpace.SMEM


def aligned(start, size):
    return pl.ds(pl.multiple_of(start, size), size)


def live_count(mig_ref):
    slots = mig_ref.shape[0]
    step = 1
    while step * 2 <= slots:
        step *= 2
    count = jnp.int32(0)
    while step:
        more = count + step
        found = mig_ref[jnp.minimum(more, slots) - 1] >= 0
        count = jnp.where(jnp.logical_and(more <= slots, found), more, count)
        step //= 2
    return count


def start_copies(pairs, sems):
    copies = [pltpu.make_async_copy(src, dst, sems.at[i]) for i, (src, dst) in enumerate(pairs)]
    for copy in copies:
        copy.start()
    return copies


def place_slabs(offsets, slabs, tiles):
    me = lax.axis_index("grid")
    depth = slabs[0].shape[-2]

    def place(e, slab):
        tiles[aligned(jnp.bitwise_xor(me, e) * depth, depth), :] = slab

    for e, slab in zip(offsets, slabs):
        if isinstance(e, tuple):
            for i, one in enumerate(e):
                place(one, slab[i])
        else:
            place(e, slab[...])


def pack_kernel(*refs):
    *slabs, out_ref = refs
    for i, slab in enumerate(slabs):
        out_ref[i] = slab[...]


def table_kernel(
    mig_hbm,
    atom_hbm,
    expo_hbm,
    coef_hbm,
    coords_hbm,
    points_hbm,
    lists_hbm,
    table_ref,
    dest_ref,
    points_out,
    lists_out,
    mig_out,
    mig_ref,
    atom_ref,
    expo_ref,
    coef_ref,
    coords_ref,
    sems,
):
    copies = start_copies(
        [
            (mig_hbm, mig_ref),
            (atom_hbm, atom_ref),
            (expo_hbm, expo_ref),
            (coef_hbm, coef_ref),
            (coords_hbm, coords_ref),
            (points_hbm, points_out),
            (lists_hbm, lists_out),
            (mig_hbm, mig_out),
        ],
        sems,
    )
    for copy in copies[:5]:
        copy.wait()
    coords = coords_ref[...]
    high = coords.astype(jnp.bfloat16)
    rest = coords - high.astype(jnp.float32)
    mid = rest.astype(jnp.bfloat16)
    low = (rest - mid.astype(jnp.float32)).astype(jnp.bfloat16)
    blocks = table_ref.shape[0]
    atoms = atom_ref[...].reshape(blocks, BLOCK)
    expos = expo_ref[...].reshape(blocks, BLOCK)

    for k in range(blocks):
        atom = atoms[k : k + 1]
        onehot = jnp.where(
            lax.broadcasted_iota(jnp.int32, (NATOM, BLOCK), 0) == atom, 1.0, 0.0
        ).astype(jnp.bfloat16)
        picked = [
            jnp.dot(part, onehot, preferred_element_type=jnp.float32) for part in (high, mid, low)
        ]
        center = (picked[0] + picked[1]) + picked[2]
        coef = coef_ref[:, k * BLOCK : (k + 1) * BLOCK]
        rows = jnp.concatenate(
            [center, coef, expos[k : k + 1], atom.astype(jnp.float32)], axis=0
        )
        columns = rows.T
        for p in range(8):
            table_ref[k, p] = jnp.broadcast_to(columns[:, p : p + 1], (BLOCK, LANES))

    dest_ids = lax.broadcasted_iota(jnp.int32, (1, dest_ref.shape[1]), 1)
    for s in range(mig_ref.shape[0]):
        dest_ref[s : s + 1, :] = jnp.where(dest_ids == mig_ref[s], 1.0, 0.0)
    for copy in copies[5:]:
        copy.wait()


def chunk_steps(mig_ref, first, size):
    left = jnp.clip(live_count(mig_ref) - first, 0, size)
    return lax.div(left + (UNROLL - 1), UNROLL)


def phi_kernel(first, offsets, packed, lists_ref, mig_ref, points_ref, table_ref, *refs):
    slabs = refs[: len(offsets)]
    phi_ref, radial_ref, basis_ref, *more = refs[len(offsets) :]
    if offsets:
        place_slabs(offsets, slabs, more[0])
        pack_kernel(*[slabs[offsets.index(e)] for e in packed], more[1])
    blk = lax.axis_index("blk")
    length = lists_ref.shape[0]
    point_count = points_ref.shape[2]

    def one_slot(s):
        for j in range(length):
            k = lists_ref[lax.rem(blk + j, length), first + s]
            for r in range(0, BLOCK, ROWS):
                sub = slice(r, r + ROWS)
                cx, cy, cz, sx, sy, sz, expo = [table_ref[k, p, sub] for p in range(7)]
                for h in range(0, point_count, LANES):
                    lanes = slice(h, h + LANES)
                    ox = points_ref[first + s, 0:1, lanes] - cx
                    oy = points_ref[first + s, 1:2, lanes] - cy
                    oz = points_ref[first + s, 2:3, lanes] - cz
                    squared = ox * ox + oy * oy + oz * oz
                    radial = jnp.exp(-expo * squared)
                    linear = 1.0 + (sx * ox + sy * oy + sz * oz)
                    basis = linear * radial
                    phi_ref[s, j, sub, lanes] = basis.astype(jnp.bfloat16)
                    if j == 0:
                        radial_ref[s, sub, lanes] = radial
                        basis_ref[s, sub, lanes] = basis

    def some_slots(i, carry):
        for u in range(2):
            one_slot(i * 2 + u)
        return carry

    steps = chunk_steps(mig_ref, first, phi_ref.shape[0]) * (UNROLL // 2)
    lax.fori_loop(0, steps, some_slots, 0)


def rho_kernel(offsets, starts, lists_ref, mig_ref, *refs):
    chunks = len(starts)
    phis = refs[:chunks]
    slabs = refs[chunks : chunks + len(offsets)]
    tiles, chi_ref, rho_ref, *placed = refs[chunks + len(offsets) :]
    if offsets:
        tiles = placed[0]
        place_slabs(offsets, slabs, tiles)
    blk = lax.axis_index("blk")
    length = lists_ref.shape[0]
    rho_ref[...] = jnp.zeros_like(rho_ref)

    for c, phi_ref in enumerate(phis):
        size = phi_ref.shape[0]

        def one_slot(s, first=starts[c], phi_ref=phi_ref):
            slot = first + s
            own = lists_ref[blk, slot]
            cols = aligned((own - blk * BPD) * BLOCK, BLOCK)
            phi = phi_ref[s, 0]
            chi = jnp.dot(
                tiles[aligned(own * BLOCK, BLOCK), cols], phi, preferred_element_type=jnp.float32
            )
            for j in range(1, length):
                k = lists_ref[lax.rem(blk + j, length), slot]
                chi += lax.dot_general(
                    tiles[aligned(k * BLOCK, BLOCK), cols],
                    phi_ref[s, j],
                    (((0,), (0,)), ((), ())),
                    preferred_element_type=jnp.float32,
                )
            chi_ref[slot] = chi
            rho_ref[pl.ds(slot, 1), :] = jnp.sum(
                phi.astype(jnp.float32) * chi, axis=0, keepdims=True
            )

        def some_slots(i, carry, one_slot=one_slot):
            for u in range(UNROLL):
                one_slot(i * UNROLL + u)
            return carry

        lax.fori_loop(0, chunk_steps(mig_ref, starts[c], size), some_slots, 0)


def force_kernel(starts, lists_ref, mig_ref, points_ref, rho_a_ref, rho_b_ref, chi_ref, *refs):
    chunks = len(starts)
    radials = refs[:chunks]
    bases = refs[chunks : 2 * chunks]
    table_ref, dest_ref, out_ref, pot_ref, acc = refs[2 * chunks :]
    blk = lax.axis_index("blk")
    slots, _, point_count = points_ref.shape
    dests = dest_ref.shape[1]
    live = live_count(mig_ref)
    rho = rho_a_ref[...] + rho_b_ref[...]
    weight = points_ref[:, 3, :]
    log_sq = jnp.log(rho * rho + RHO_SOFT * RHO_SOFT)
    pot = weight * (-(4.0 / 3.0) * SLATER) * rho * jnp.exp(log_sq * (-1.0 / 3.0))
    slot_ids = lax.broadcasted_iota(jnp.int32, (slots, 1), 0)
    pot_ref[...] = jnp.where(slot_ids < live, pot, 0.0)
    energies = jnp.sum(weight * -SLATER * jnp.exp(log_sq * (2.0 / 3.0)), axis=1, keepdims=True)
    acc[...] = jnp.zeros_like(acc)

    for c in range(chunks):
        radial_ref, basis_ref = radials[c], bases[c]
        size = radial_ref.shape[0]

        def one_slot(s, first=starts[c], radial_ref=radial_ref, basis_ref=basis_ref):
            slot = first + s
            own = lists_ref[blk, slot] - blk * BPD
            pots = pot_ref[pl.ds(slot, 1), :]
            for r in range(0, BLOCK, ROWS):
                sub = slice(r, r + ROWS)
                sums = None
                for h in range(0, point_count, LANES):
                    lanes = slice(h, h + LANES)
                    u = chi_ref[slot, sub, lanes] * pots[:, lanes]
                    ub = u * basis_ref[s, sub, lanes]
                    terms = (
                        u * radial_ref[s, sub, lanes],
                        ub,
                        ub * points_ref[slot, 0:1, lanes],
                        ub * points_ref[slot, 1:2, lanes],
                        ub * points_ref[slot, 2:3, lanes],
                    )
                    sums = terms if sums is None else [a + b for a, b in zip(sums, terms)]
                for q in range(5):
                    acc[own, q, sub] += sums[q]

        def some_slots(i, carry, one_slot=one_slot):
            for u in range(UNROLL):
                one_slot(i * UNROLL + u)
            return carry

        lax.fori_loop(0, chunk_steps(mig_ref, starts[c], size), some_slots, 0)

    lane_ids = lax.broadcasted_iota(jnp.int32, (1, LANES), 1).astype(jnp.float32)

    totals = [jnp.zeros((8, LANES), jnp.float32)] * (3 * NATOM // LANES)
    for b in range(BPD):
        k = blk * BPD + b
        for r in range(0, BLOCK, ROWS):
            sub = slice(r, r + ROWS)
            parts = [acc[b, q, sub] for q in range(5)]
            doubled = 2.0 * table_ref[k, 6, sub]
            atom = table_ref[k, 7, sub]
            for c in range(3):
                force = table_ref[k, 3 + c, sub] * parts[0] - doubled * (
                    parts[2 + c] - table_ref[k, c, sub] * parts[1]
                )
                column = 2.0 * jnp.sum(force, axis=1, keepdims=True)
                for h in range(NATOM // LANES):
                    hit = jnp.where(atom == lane_ids + float(h * LANES), column, 0.0)
                    i = c * (NATOM // LANES) + h
                    totals[i] = totals[i] + sum(hit[i8 : i8 + 8] for i8 in range(0, ROWS, 8))
    rows = [jnp.sum(t, axis=0, keepdims=True) for t in totals]
    moved = jnp.sum(dest_ref[...] * energies, axis=0, keepdims=True)
    rows += [moved[:, h : h + LANES] for h in range(0, dests, LANES)]
    packed = jnp.concatenate(rows, axis=0)
    for i in range(out_ref.shape[0]):
        out_ref[i] = packed


def selector_kernel(width, index_ref, selector_ref):
    first = lax.axis_index("grid") * width
    ids = index_ref[...]
    mine = jnp.logical_and(ids >= first, ids < first + width)
    selector_ref[...] = jnp.where(mine, 1.0, 0.0)


def sum_kernel(copies, arrived_ref, selector_ref, energy_ref, forces_ref):
    me = lax.axis_index("grid")
    total = jnp.sum(arrived_ref[...], axis=0)
    per = NATOM // LANES
    for c in range(3):
        for h in range(per):
            forces_ref[c : c + 1, h * LANES : (h + 1) * LANES] = total[c * per + h : c * per + h + 1]
    width = energy_ref.shape[1]
    first = me * width
    energy = jnp.sum(total[3 * per :] * selector_ref[...], axis=0, keepdims=True)
    turn = lax.rem(LANES - lax.rem(first, LANES), LANES)
    energy = pltpu.roll(jnp.broadcast_to(energy, (8, LANES)), turn, 1)
    energy_ref[...] = energy[0:1, 0:width] * (1.0 / copies)


def swap(array, offset):
    count = lax.axis_size("grid")
    return lax.ppermute(array, "grid", [(i, i ^ offset) for i in range(count)])


STAGES = (((8, 0), (4, 0), (2, 0)), ((12, 8), (10, 8)), ((14, 10), (6, 4)))
PACKS = ((0, 8, 4, 2), (12, 10, 14, 6))


def in_hbm(array):
    return pltpu.with_memory_space_constraint(array, pltpu.HBM)


def spec(space):
    return pl.BlockSpec(memory_space=space)


def params(blocks):
    return pltpu.CompilerParams(vmem_limit_bytes=blocks * 1024 * 1024)


def cost(nominal_us):
    return pl.CostEstimate(
        flops=0, bytes_accessed=int(nominal_us * 3.69e6), transcendentals=0
    )


def f32(*shape):
    return jax.ShapeDtypeStruct(shape, jnp.float32)


def local(density, points, sig_blocks, migration, atom_coords, exponents, shape_coef, func_atom):
    grid_count = lax.axis_size("grid")
    blk_count = lax.axis_size("blk")
    slots, _, point_count = points.shape
    length = sig_blocks.shape[1]
    functions = exponents.shape[0]
    blocks = functions // BLOCK
    dests = grid_count * (slots // 2)
    sizes = [slots // 4, slots // 2, slots // 4]
    starts = [0, slots // 4, slots // 4 * 3]
    slab = density.T
    tied = lax.optimization_barrier
    lists = sig_blocks.T

    table, dest_mask, points, lists, migration = pl.pallas_call(
        table_kernel,
        out_shape=[
            f32(blocks, 8, BLOCK, LANES),
            f32(slots, dests),
            f32(*points.shape),
            jax.ShapeDtypeStruct(lists.shape, jnp.int32),
            jax.ShapeDtypeStruct(migration.shape, jnp.int32),
        ],
        in_specs=[spec(pltpu.HBM)] * 7,
        out_specs=[spec(VMEM)] * 5,
        scratch_shapes=[
            pltpu.SMEM((slots,), jnp.int32),
            pltpu.VMEM((functions,), jnp.int32),
            pltpu.VMEM((functions,), jnp.float32),
            pltpu.VMEM((3, functions), jnp.float32),
            pltpu.VMEM((3, NATOM), jnp.float32),
            pltpu.SemaphoreType.DMA((8,)),
        ],
        compiler_params=params(blocks),
        cost_estimate=cost(4),
        name="param_table",
    )(
        *[
            in_hbm(a)
            for a in (migration, func_atom, exponents, shape_coef, atom_coords, points, lists)
        ]
    )

    tile_shape = jax.ShapeDtypeStruct((functions, BPD * BLOCK), jnp.bfloat16)

    def basis_chunk(c, points, offsets=(), packed=()):
        some = 1 if offsets else 0
        return pl.pallas_call(
            functools.partial(phi_kernel, starts[c], offsets, packed),
            out_shape=[
                jax.ShapeDtypeStruct((sizes[c], length, BLOCK, point_count), jnp.bfloat16),
                f32(sizes[c], BLOCK, point_count),
                f32(sizes[c], BLOCK, point_count),
            ]
            + [tile_shape, jax.ShapeDtypeStruct((len(packed), *slab.shape), slab.dtype)] * some,
            in_specs=[spec(SMEM), spec(SMEM)] + [spec(VMEM)] * (2 + len(offsets)),
            out_specs=[spec(VMEM)] * (3 + 2 * some),
            compiler_params=params(blocks),
            cost_estimate=cost(5),
            name="basis_values",
        )(lists, migration, points, table, *[held[e] for e in offsets])

    held = {0: slab}
    late, slabs = [], []
    if grid_count == 16:
        held.update({e: swap(held[source], e ^ source) for e, source in STAGES[0]})
        first = basis_chunk(0, points)
        held, first, points = tied((held, first, points))
        held.update({e: swap(held[source], e ^ source) for e, source in STAGES[1]})
        *second, tiles, pack = basis_chunk(1, points, PACKS[0], PACKS[0])
        held, second, tiles, pack, points = tied((held, second, tiles, pack, points))
        held.update({e: swap(held[source], e ^ source) for e, source in STAGES[2]})
        crossed = swap(pack, 1)
        third = basis_chunk(2, points)
        held, crossed, third = tied((held, crossed, third))
        pack = pl.pallas_call(
            pack_kernel,
            out_shape=jax.ShapeDtypeStruct((len(PACKS[1]), *slab.shape), slab.dtype),
            in_specs=[spec(VMEM)] * len(PACKS[1]),
            out_specs=spec(VMEM),
            compiler_params=params(blocks),
            name="pack",
        )(*[held[e] for e in PACKS[1]])
        chunks = [first, second, third]
        late = [*PACKS[1], *[tuple(e ^ 1 for e in offsets) for offsets in PACKS]]
        slabs = [*[held[e] for e in PACKS[1]], crossed, swap(pack, 1)]
    else:
        tiles = lax.all_gather(slab, "grid", axis=0, tiled=True)
        chunks = [basis_chunk(i, points) for i in range(len(starts))]
    phis, radials, bases = zip(*chunks)

    some = 1 if late else 0
    chi, rho, *_ = pl.pallas_call(
        functools.partial(rho_kernel, late, starts),
        out_shape=[f32(slots, BLOCK, point_count), f32(slots, point_count)] + [tile_shape] * some,
        in_specs=[spec(SMEM), spec(SMEM)]
        + [spec(VMEM)] * (len(starts) + len(late) + 1),
        out_specs=[spec(VMEM)] * (2 + some),
        input_output_aliases={2 + len(starts) + len(late): 2} if late else {},
        compiler_params=params(blocks),
        cost_estimate=cost(5),
        name="density_at_points",
    )(lists, migration, *phis, *slabs, tiles)

    if blk_count == 2:
        other = lax.ppermute(rho, "blk", [(0, 1), (1, 0)])
    else:
        other = lax.psum(rho, "blk") - rho

    rows = 3 * NATOM // LANES + dests // LANES
    outgoing = pl.pallas_call(
        functools.partial(force_kernel, starts),
        out_shape=f32(blk_count * grid_count, rows, LANES),
        in_specs=[spec(SMEM), spec(SMEM)] + [spec(VMEM)] * (6 + 2 * len(starts)),
        out_specs=spec(VMEM),
        scratch_shapes=[
            pltpu.VMEM((slots, point_count), jnp.float32),
            pltpu.VMEM((BPD, 5, BLOCK, LANES), jnp.float32),
        ],
        compiler_params=params(blocks),
        cost_estimate=cost(5),
        name="forces_and_energies",
    )(lists, migration, points, rho, other, chi, *radials, *bases, table, dest_mask)

    indices = jnp.arange(dests, dtype=jnp.int32).reshape(dests // LANES, LANES)
    outgoing, indices = tied((outgoing, indices))
    arrived = lax.all_to_all(outgoing, ("blk", "grid"), split_axis=0, concat_axis=0, tiled=True)
    selector = pl.pallas_call(
        functools.partial(selector_kernel, dests // grid_count),
        out_shape=f32(dests // LANES, LANES),
        in_specs=[spec(VMEM)],
        out_specs=spec(VMEM),
        compiler_params=params(blocks),
        name="energy_selector",
    )(indices)

    energy, forces = pl.pallas_call(
        functools.partial(sum_kernel, blk_count),
        out_shape=[f32(1, dests // grid_count), f32(3, NATOM)],
        in_specs=[spec(VMEM)] * 2,
        out_specs=[spec(VMEM)] * 2,
        compiler_params=params(blocks),
        name="final_sums",
    )(arrived, selector)
    return (energy.reshape(dests // grid_count), forces)


def solution(mesh):
    in_specs = (
        P("blk", "grid"),
        P("grid", None, None),
        P("grid", None),
        P("grid"),
        P(),
        P(),
        P(),
        P(),
    )
    out_specs = (P("grid"), P())
    return jax.shard_map(local, mesh=mesh, in_specs=in_specs, out_specs=out_specs, check_vma=False)
```

```python
import functools

import jax
import jax.numpy as jnp
from jax import lax
from jax.experimental import pallas as pl
from jax.experimental.pallas import tpu as pltpu
from jax.sharding import PartitionSpec as P

BLOCK = 128
BPD = 6
NATOM = 256
LANES = 128
ROWS = 32
UNROLL = 4

SLATER = 0.7386
RHO_SOFT = 0.05

VMEM = pltpu.MemorySpace.VMEM
SMEM = pltpu.MemorySpace.SMEM


def aligned(start, size):
    return pl.ds(pl.multiple_of(start, size), size)


def live_count(mig_ref):
    slots = mig_ref.shape[0]
    step = 1
    while step * 2 <= slots:
        step *= 2
    count = jnp.int32(0)
    while step:
        more = count + step
        found = mig_ref[jnp.minimum(more, slots) - 1] >= 0
        count = jnp.where(jnp.logical_and(more <= slots, found), more, count)
        step //= 2
    return count


def start_copies(pairs, sems):
    copies = [pltpu.make_async_copy(src, dst, sems.at[i]) for i, (src, dst) in enumerate(pairs)]
    for copy in copies:
        copy.start()
    return copies


def place_slabs(offsets, slabs, tiles):
    me = lax.axis_index("grid")
    depth = slabs[0].shape[-2]

    def place(e, slab):
        tiles[aligned(jnp.bitwise_xor(me, e) * depth, depth), :] = slab

    for e, slab in zip(offsets, slabs):
        if isinstance(e, tuple):
            for i, one in enumerate(e):
                place(one, slab[i])
        else:
            place(e, slab[...])


def pack_kernel(*refs):
    *slabs, out_ref = refs
    for i, slab in enumerate(slabs):
        out_ref[i] = slab[...]


def table_kernel(
    mig_hbm,
    atom_hbm,
    expo_hbm,
    coef_hbm,
    coords_hbm,
    points_hbm,
    lists_hbm,
    table_ref,
    dest_ref,
    points_out,
    lists_out,
    mig_out,
    mig_ref,
    atom_ref,
    expo_ref,
    coef_ref,
    coords_ref,
    sems,
):
    copies = start_copies(
        [
            (mig_hbm, mig_ref),
            (atom_hbm, atom_ref),
            (expo_hbm, expo_ref),
            (coef_hbm, coef_ref),
            (coords_hbm, coords_ref),
            (points_hbm, points_out),
            (lists_hbm, lists_out),
            (mig_hbm, mig_out),
        ],
        sems,
    )
    for copy in copies[:5]:
        copy.wait()
    coords = coords_ref[...]
    high = coords.astype(jnp.bfloat16)
    rest = coords - high.astype(jnp.float32)
    mid = rest.astype(jnp.bfloat16)
    low = (rest - mid.astype(jnp.float32)).astype(jnp.bfloat16)
    blocks = table_ref.shape[0]
    atoms = atom_ref[...].reshape(blocks, BLOCK)
    expos = expo_ref[...].reshape(blocks, BLOCK)

    for k in range(blocks):
        atom = atoms[k : k + 1]
        onehot = jnp.where(
            lax.broadcasted_iota(jnp.int32, (NATOM, BLOCK), 0) == atom, 1.0, 0.0
        ).astype(jnp.bfloat16)
        picked = [
            jnp.dot(part, onehot, preferred_element_type=jnp.float32) for part in (high, mid, low)
        ]
        center = (picked[0] + picked[1]) + picked[2]
        coef = coef_ref[:, k * BLOCK : (k + 1) * BLOCK]
        rows = jnp.concatenate(
            [center, coef, expos[k : k + 1], atom.astype(jnp.float32)], axis=0
        )
        columns = rows.T
        for p in range(8):
            table_ref[k, p] = jnp.broadcast_to(columns[:, p : p + 1], (BLOCK, LANES))

    dest_ids = lax.broadcasted_iota(jnp.int32, (1, dest_ref.shape[1]), 1)
    for s in range(mig_ref.shape[0]):
        dest_ref[s : s + 1, :] = jnp.where(dest_ids == mig_ref[s], 1.0, 0.0)
    for copy in copies[5:]:
        copy.wait()


def chunk_steps(mig_ref, first, size):
    left = jnp.clip(live_count(mig_ref) - first, 0, size)
    return lax.div(left + (UNROLL - 1), UNROLL)


def phi_kernel(first, offsets, lists_ref, mig_ref, points_ref, table_ref, *refs):
    slabs = refs[: len(offsets)]
    phi_ref, radial_ref, basis_ref, *more = refs[len(offsets) :]
    if offsets:
        place_slabs(offsets, slabs, more[0])
    blk = lax.axis_index("blk")
    length = lists_ref.shape[0]
    point_count = points_ref.shape[2]

    def one_slot(s):
        for j in range(length):
            k = lists_ref[lax.rem(blk + j, length), first + s]
            for r in range(0, BLOCK, ROWS):
                sub = slice(r, r + ROWS)
                cx, cy, cz, sx, sy, sz, expo = [table_ref[k, p, sub] for p in range(7)]
                for h in range(0, point_count, LANES):
                    lanes = slice(h, h + LANES)
                    ox = points_ref[first + s, 0:1, lanes] - cx
                    oy = points_ref[first + s, 1:2, lanes] - cy
                    oz = points_ref[first + s, 2:3, lanes] - cz
                    squared = ox * ox + oy * oy + oz * oz
                    radial = jnp.exp(-expo * squared)
                    linear = 1.0 + (sx * ox + sy * oy + sz * oz)
                    basis = linear * radial
                    phi_ref[s, j, sub, lanes] = basis.astype(jnp.bfloat16)
                    if j == 0:
                        radial_ref[s, sub, lanes] = radial
                        basis_ref[s, sub, lanes] = basis

    def some_slots(i, carry):
        for u in range(2):
            one_slot(i * 2 + u)
        return carry

    steps = chunk_steps(mig_ref, first, phi_ref.shape[0]) * (UNROLL // 2)
    lax.fori_loop(0, steps, some_slots, 0)


def rho_kernel(offsets, starts, lists_ref, mig_ref, *refs):
    chunks = len(starts)
    phis = refs[:chunks]
    slabs = refs[chunks : chunks + len(offsets)]
    tiles, chi_ref, rho_ref, *placed = refs[chunks + len(offsets) :]
    if offsets:
        tiles = placed[0]
        place_slabs(offsets, slabs, tiles)
    blk = lax.axis_index("blk")
    length = lists_ref.shape[0]
    rho_ref[...] = jnp.zeros_like(rho_ref)

    for c, phi_ref in enumerate(phis):
        size = phi_ref.shape[0]

        def one_slot(s, first=starts[c], phi_ref=phi_ref):
            slot = first + s
            own = lists_ref[blk, slot]
            cols = aligned((own - blk * BPD) * BLOCK, BLOCK)
            phi = phi_ref[s, 0]
            chi = jnp.dot(
                tiles[aligned(own * BLOCK, BLOCK), cols], phi, preferred_element_type=jnp.float32
            )
            for j in range(1, length):
                k = lists_ref[lax.rem(blk + j, length), slot]
                chi += lax.dot_general(
                    tiles[aligned(k * BLOCK, BLOCK), cols],
                    phi_ref[s, j],
                    (((0,), (0,)), ((), ())),
                    preferred_element_type=jnp.float32,
                )
            chi_ref[slot] = chi
            rho_ref[pl.ds(slot, 1), :] = jnp.sum(
                phi.astype(jnp.float32) * chi, axis=0, keepdims=True
            )

        def some_slots(i, carry, one_slot=one_slot):
            for u in range(UNROLL):
                one_slot(i * UNROLL + u)
            return carry

        lax.fori_loop(0, chunk_steps(mig_ref, starts[c], size), some_slots, 0)


def force_kernel(starts, lists_ref, mig_ref, points_ref, rho_a_ref, rho_b_ref, chi_ref, *refs):
    chunks = len(starts)
    radials = refs[:chunks]
    bases = refs[chunks : 2 * chunks]
    table_ref, dest_ref, out_ref, pot_ref, acc = refs[2 * chunks :]
    blk = lax.axis_index("blk")
    slots, _, point_count = points_ref.shape
    dests = dest_ref.shape[1]
    live = live_count(mig_ref)
    rho = rho_a_ref[...] + rho_b_ref[...]
    weight = points_ref[:, 3, :]
    log_sq = jnp.log(rho * rho + RHO_SOFT * RHO_SOFT)
    pot = weight * (-(4.0 / 3.0) * SLATER) * rho * jnp.exp(log_sq * (-1.0 / 3.0))
    slot_ids = lax.broadcasted_iota(jnp.int32, (slots, 1), 0)
    pot_ref[...] = jnp.where(slot_ids < live, pot, 0.0)
    energies = jnp.sum(weight * -SLATER * jnp.exp(log_sq * (2.0 / 3.0)), axis=1, keepdims=True)
    acc[...] = jnp.zeros_like(acc)

    for c in range(chunks):
        radial_ref, basis_ref = radials[c], bases[c]
        size = radial_ref.shape[0]

        def one_slot(s, first=starts[c], radial_ref=radial_ref, basis_ref=basis_ref):
            slot = first + s
            own = lists_ref[blk, slot] - blk * BPD
            pots = pot_ref[pl.ds(slot, 1), :]
            for r in range(0, BLOCK, ROWS):
                sub = slice(r, r + ROWS)
                sums = None
                for h in range(0, point_count, LANES):
                    lanes = slice(h, h + LANES)
                    u = chi_ref[slot, sub, lanes] * pots[:, lanes]
                    ub = u * basis_ref[s, sub, lanes]
                    terms = (
                        u * radial_ref[s, sub, lanes],
                        ub,
                        ub * points_ref[slot, 0:1, lanes],
                        ub * points_ref[slot, 1:2, lanes],
                        ub * points_ref[slot, 2:3, lanes],
                    )
                    sums = terms if sums is None else [a + b for a, b in zip(sums, terms)]
                for q in range(5):
                    acc[own, q, sub] += sums[q]

        def some_slots(i, carry, one_slot=one_slot):
            for u in range(UNROLL):
                one_slot(i * UNROLL + u)
            return carry

        lax.fori_loop(0, chunk_steps(mig_ref, starts[c], size), some_slots, 0)

    lane_ids = lax.broadcasted_iota(jnp.int32, (1, LANES), 1).astype(jnp.float32)

    totals = [jnp.zeros((8, LANES), jnp.float32)] * (3 * NATOM // LANES)
    for b in range(BPD):
        k = blk * BPD + b
        for r in range(0, BLOCK, ROWS):
            sub = slice(r, r + ROWS)
            parts = [acc[b, q, sub] for q in range(5)]
            doubled = 2.0 * table_ref[k, 6, sub]
            atom = table_ref[k, 7, sub]
            for c in range(3):
                force = table_ref[k, 3 + c, sub] * parts[0] - doubled * (
                    parts[2 + c] - table_ref[k, c, sub] * parts[1]
                )
                column = 2.0 * jnp.sum(force, axis=1, keepdims=True)
                for h in range(NATOM // LANES):
                    hit = jnp.where(atom == lane_ids + float(h * LANES), column, 0.0)
                    i = c * (NATOM // LANES) + h
                    totals[i] = totals[i] + sum(hit[i8 : i8 + 8] for i8 in range(0, ROWS, 8))
    rows = [jnp.sum(t, axis=0, keepdims=True) for t in totals]
    moved = jnp.sum(dest_ref[...] * energies, axis=0, keepdims=True)
    rows += [moved[:, h : h + LANES] for h in range(0, dests, LANES)]
    packed = jnp.concatenate(rows, axis=0)
    for i in range(out_ref.shape[0]):
        out_ref[i] = packed


def sum_kernel(copies, arrived_ref, energy_ref, forces_ref):
    me = lax.axis_index("grid")
    total = jnp.sum(arrived_ref[...], axis=0)
    per = NATOM // LANES
    for c in range(3):
        for h in range(per):
            forces_ref[c : c + 1, h * LANES : (h + 1) * LANES] = total[c * per + h : c * per + h + 1]
    width = energy_ref.shape[1]
    first = me * width
    energy = jnp.zeros((1, LANES), jnp.float32)
    for i in range(3 * per, total.shape[0]):
        chosen = lax.div(first, LANES) == i - 3 * per
        energy = jnp.where(chosen, total[i : i + 1], energy)
    turn = lax.rem(LANES - lax.rem(first, LANES), LANES)
    energy = pltpu.roll(jnp.broadcast_to(energy, (8, LANES)), turn, 1)
    energy_ref[...] = energy[0:1, 0:width] * (1.0 / copies)


def swap(array, offset):
    count = lax.axis_size("grid")
    return lax.ppermute(array, "grid", [(i, i ^ offset) for i in range(count)])


STAGES = (((8, 0), (4, 0), (2, 0)), ((14, 8), (12, 8), (10, 8), (6, 4)))


def in_hbm(array):
    return pltpu.with_memory_space_constraint(array, pltpu.HBM)


def spec(space):
    return pl.BlockSpec(memory_space=space)


def params(blocks):
    return pltpu.CompilerParams(vmem_limit_bytes=blocks * 1024 * 1024)


def cost(nominal_us):
    return pl.CostEstimate(
        flops=0, bytes_accessed=int(nominal_us * 3.69e6), transcendentals=0
    )


def f32(*shape):
    return jax.ShapeDtypeStruct(shape, jnp.float32)


def local(density, points, sig_blocks, migration, atom_coords, exponents, shape_coef, func_atom):
    grid_count = lax.axis_size("grid")
    blk_count = lax.axis_size("blk")
    slots, _, point_count = points.shape
    length = sig_blocks.shape[1]
    functions = exponents.shape[0]
    blocks = functions // BLOCK
    dests = grid_count * (slots // 2)
    sizes = [slots // 4, slots // 4 * 3]
    starts = [0, slots // 4]
    slab = density.T
    tied = lax.optimization_barrier
    lists = sig_blocks.T

    table, dest_mask, points, lists, migration = pl.pallas_call(
        table_kernel,
        out_shape=[
            f32(blocks, 8, BLOCK, LANES),
            f32(slots, dests),
            f32(*points.shape),
            jax.ShapeDtypeStruct(lists.shape, jnp.int32),
            jax.ShapeDtypeStruct(migration.shape, jnp.int32),
        ],
        in_specs=[spec(pltpu.HBM)] * 7,
        out_specs=[spec(VMEM)] * 5,
        scratch_shapes=[
            pltpu.SMEM((slots,), jnp.int32),
            pltpu.VMEM((functions,), jnp.int32),
            pltpu.VMEM((functions,), jnp.float32),
            pltpu.VMEM((3, functions), jnp.float32),
            pltpu.VMEM((3, NATOM), jnp.float32),
            pltpu.SemaphoreType.DMA((8,)),
        ],
        compiler_params=params(blocks),
        cost_estimate=cost(4),
        name="param_table",
    )(
        *[
            in_hbm(a)
            for a in (migration, func_atom, exponents, shape_coef, atom_coords, points, lists)
        ]
    )

    tile_shape = jax.ShapeDtypeStruct((functions, BPD * BLOCK), jnp.bfloat16)

    def basis_chunk(c, points, offsets=()):
        some = 1 if offsets else 0
        return pl.pallas_call(
            functools.partial(phi_kernel, starts[c], offsets),
            out_shape=[
                jax.ShapeDtypeStruct((sizes[c], length, BLOCK, point_count), jnp.bfloat16),
                f32(sizes[c], BLOCK, point_count),
                f32(sizes[c], BLOCK, point_count),
            ]
            + [tile_shape] * some,
            in_specs=[spec(SMEM), spec(SMEM)] + [spec(VMEM)] * (2 + len(offsets)),
            out_specs=[spec(VMEM)] * (3 + some),
            compiler_params=params(blocks),
            cost_estimate=cost(5),
            name="basis_values",
        )(lists, migration, points, table, *[held[e] for e in offsets])

    held = {0: slab}
    late, slabs = [], []
    if grid_count == 16:
        held.update({e: swap(held[source], e ^ source) for e, source in STAGES[0]})
        ready = tuple(held)
        first = basis_chunk(0, points)
        held, first, points = tied((held, first, points))
        held.update({e: swap(held[source], e ^ source) for e, source in STAGES[1]})
        *second, tiles = basis_chunk(1, points, ready)
        held, second, tiles = tied((held, second, tiles))
        everything = tuple(held)
        pack = pl.pallas_call(
            pack_kernel,
            out_shape=jax.ShapeDtypeStruct((len(everything), *slab.shape), slab.dtype),
            in_specs=[spec(VMEM)] * len(everything),
            out_specs=spec(VMEM),
            compiler_params=params(blocks),
            name="pack",
        )(*[held[e] for e in everything])
        chunks = [first, second]
        late = [e for e in everything if e not in ready]
        late.append(tuple(e ^ 1 for e in everything))
        slabs = [*[held[e] for e in late[:-1]], swap(pack, 1)]
    else:
        tiles = lax.all_gather(slab, "grid", axis=0, tiled=True)
        chunks = [basis_chunk(i, points) for i in range(len(starts))]
    phis, radials, bases = zip(*chunks)

    some = 1 if late else 0
    chi, rho, *_ = pl.pallas_call(
        functools.partial(rho_kernel, late, starts),
        out_shape=[f32(slots, BLOCK, point_count), f32(slots, point_count)] + [tile_shape] * some,
        in_specs=[spec(SMEM), spec(SMEM)]
        + [spec(VMEM)] * (len(starts) + len(late) + 1),
        out_specs=[spec(VMEM)] * (2 + some),
        input_output_aliases={2 + len(starts) + len(late): 2} if late else {},
        compiler_params=params(blocks),
        cost_estimate=cost(5),
        name="density_at_points",
    )(lists, migration, *phis, *slabs, tiles)

    if blk_count == 2:
        other = lax.ppermute(rho, "blk", [(0, 1), (1, 0)])
    else:
        other = lax.psum(rho, "blk") - rho

    rows = 3 * NATOM // LANES + dests // LANES
    outgoing = pl.pallas_call(
        functools.partial(force_kernel, starts),
        out_shape=f32(blk_count * grid_count, rows, LANES),
        in_specs=[spec(SMEM), spec(SMEM)] + [spec(VMEM)] * (6 + 2 * len(starts)),
        out_specs=spec(VMEM),
        scratch_shapes=[
            pltpu.VMEM((slots, point_count), jnp.float32),
            pltpu.VMEM((BPD, 5, BLOCK, LANES), jnp.float32),
        ],
        compiler_params=params(blocks),
        cost_estimate=cost(5),
        name="forces_and_energies",
    )(lists, migration, points, rho, other, chi, *radials, *bases, table, dest_mask)

    arrived = lax.all_to_all(outgoing, ("blk", "grid"), split_axis=0, concat_axis=0, tiled=True)

    energy, forces = pl.pallas_call(
        functools.partial(sum_kernel, blk_count),
        out_shape=[f32(1, dests // grid_count), f32(3, NATOM)],
        in_specs=[spec(VMEM)],
        out_specs=[spec(VMEM)] * 2,
        compiler_params=params(blocks),
        name="final_sums",
    )(arrived)
    return (energy.reshape(dests // grid_count), forces)


def solution(mesh):
    in_specs = (
        P("blk", "grid"),
        P("grid", None, None),
        P("grid", None),
        P("grid"),
        P(),
        P(),
        P(),
        P(),
    )
    out_specs = (P("grid"), P())
    return jax.shard_map(local, mesh=mesh, in_specs=in_specs, out_specs=out_specs, check_vma=False)
```

```python
import functools

import jax
import jax.numpy as jnp
from jax import lax
from jax.experimental import pallas as pl
from jax.experimental.pallas import tpu as pltpu
from jax.sharding import PartitionSpec as P

BLOCK = 128
BPD = 6
NATOM = 256
LANES = 128
ROWS = 32
UNROLL = 4

SLATER = 0.7386
RHO_SOFT = 0.05
LOG2E = 1.4426950408889634
MIDDLE = 2.0
REACH = 64.0
PARTS = 48

VMEM = pltpu.MemorySpace.VMEM
SMEM = pltpu.MemorySpace.SMEM


def aligned(start, size):
    return pl.ds(pl.multiple_of(start, size), size)


def live_count(mig_ref):
    slots = mig_ref.shape[0]
    step = 1
    while step * 2 <= slots:
        step *= 2
    count = jnp.int32(0)
    while step:
        more = count + step
        found = mig_ref[jnp.minimum(more, slots) - 1] >= 0
        count = jnp.where(jnp.logical_and(more <= slots, found), more, count)
        step //= 2
    return count


def start_copies(pairs, sems):
    copies = [pltpu.make_async_copy(src, dst, sems.at[i]) for i, (src, dst) in enumerate(pairs)]
    for copy in copies:
        copy.start()
    return copies


def place_slabs(offsets, slabs, tiles):
    me = lax.axis_index("grid")
    depth = slabs[0].shape[-2]

    def place(e, slab):
        tiles[aligned(jnp.bitwise_xor(me, e) * depth, depth), :] = slab

    for e, slab in zip(offsets, slabs):
        if isinstance(e, tuple):
            for i, one in enumerate(e):
                place(one, slab[i])
        else:
            place(e, slab[...])


def pack_kernel(*refs):
    *slabs, out_ref = refs
    for i, slab in enumerate(slabs):
        out_ref[i] = slab[...]


def three_parts(value):
    high = value.astype(jnp.bfloat16).astype(jnp.float32)
    rest = value - high
    mid = rest.astype(jnp.bfloat16).astype(jnp.float32)
    return high, mid, rest - mid


def left_parts(value):
    high, mid, low = three_parts(value)
    return jnp.concatenate([high, high, mid, mid, high, low], axis=0)


def right_parts(value):
    high, mid, low = three_parts(value)
    return jnp.concatenate([high, mid, high, mid, low, high], axis=0)


def table_kernel(
    mig_hbm,
    atom_hbm,
    expo_hbm,
    coef_hbm,
    coords_hbm,
    points_hbm,
    lists_hbm,
    factors_ref,
    table_ref,
    dest_ref,
    points_out,
    lists_out,
    mig_out,
    mig_ref,
    atom_ref,
    expo_ref,
    coef_ref,
    coords_ref,
    sems,
):
    copies = start_copies(
        [
            (mig_hbm, mig_ref),
            (atom_hbm, atom_ref),
            (expo_hbm, expo_ref),
            (coef_hbm, coef_ref),
            (coords_hbm, coords_ref),
            (points_hbm, points_out),
            (lists_hbm, lists_out),
            (mig_hbm, mig_out),
        ],
        sems,
    )
    for copy in copies[:5]:
        copy.wait()
    coords = coords_ref[...]
    high = coords.astype(jnp.bfloat16)
    rest = coords - high.astype(jnp.float32)
    mid = rest.astype(jnp.bfloat16)
    low = (rest - mid.astype(jnp.float32)).astype(jnp.bfloat16)
    blocks = factors_ref.shape[0]
    blk = lax.axis_index("blk")
    atoms = atom_ref[...].reshape(blocks, BLOCK)
    expos = expo_ref[...].reshape(blocks, BLOCK)
    none = jnp.zeros((3, BLOCK), jnp.float32)

    for k in range(blocks):
        atom = atoms[k : k + 1]
        onehot = jnp.where(
            lax.broadcasted_iota(jnp.int32, (NATOM, BLOCK), 0) == atom, 1.0, 0.0
        ).astype(jnp.bfloat16)
        picked = [
            jnp.dot(part, onehot, preferred_element_type=jnp.float32) for part in (high, mid, low)
        ]
        center = (picked[0] + picked[1]) + picked[2]
        coef = coef_ref[:, k * BLOCK : (k + 1) * BLOCK]
        expo = expos[k : k + 1]

        shifted = center - MIDDLE
        scale = expo * LOG2E
        square = jnp.sum(shifted * shifted, axis=0, keepdims=True)
        offset = jnp.sum(coef * shifted, axis=0, keepdims=True)
        power = jnp.concatenate(
            [-scale, (2.0 * scale) * shifted, -scale * square, none], axis=0
        )
        linear = jnp.concatenate([none[0:1], coef, 1.0 - offset, none], axis=0)
        stacked = [left_parts(power), left_parts(linear)]
        stacked.append(jnp.zeros((BLOCK - 2 * PARTS, BLOCK), jnp.float32))
        factors_ref[k] = jnp.concatenate(stacked, axis=0).T.astype(jnp.bfloat16)

        @pl.when(blk == k // BPD)
        def _(k=k, rows=(center, coef, expo, atom)):
            rows = jnp.concatenate([*rows[:3], rows[3].astype(jnp.float32)], axis=0)
            columns = rows.T
            for p in range(8):
                table_ref[k % BPD, p] = jnp.broadcast_to(columns[:, p : p + 1], (BLOCK, LANES))

    dest_ids = lax.broadcasted_iota(jnp.int32, (1, dest_ref.shape[1]), 1)
    for s in range(mig_ref.shape[0]):
        dest_ref[s : s + 1, :] = jnp.where(dest_ids == mig_ref[s], 1.0, 0.0)
    for copy in copies[5:]:
        copy.wait()


def chunk_steps(mig_ref, first, size):
    left = jnp.clip(live_count(mig_ref) - first, 0, size)
    return lax.div(left + (UNROLL - 1), UNROLL)


def phi_kernel(first, offsets, lists_ref, mig_ref, points_ref, factors_ref, *refs):
    slabs = refs[: len(offsets)]
    phi_ref, radial_ref, basis_ref, *more = refs[len(offsets) :]
    if offsets:
        place_slabs(offsets, slabs, more[0])
    blk = lax.axis_index("blk")
    length = lists_ref.shape[0]
    point_count = points_ref.shape[2]

    ones = jnp.ones((1, point_count), jnp.float32)
    none = jnp.zeros((BLOCK - 2 * PARTS, point_count), jnp.float32)
    empty = jnp.zeros((PARTS, point_count), jnp.float32)

    def one_slot(s):
        place = jnp.clip(points_ref[first + s, 0:3, :] - MIDDLE, -REACH, REACH)
        square = jnp.sum(place * place, axis=0, keepdims=True)
        right = right_parts(jnp.concatenate([square, place, ones, none[0:3]], axis=0))
        for_power = jnp.concatenate([right, empty, none], axis=0).astype(jnp.bfloat16)
        for_linear = jnp.concatenate([empty, right, none], axis=0).astype(jnp.bfloat16)
        for j in range(length):
            factors = factors_ref[lists_ref[lax.rem(blk + j, length), first + s]]
            power = jnp.dot(factors, for_power, preferred_element_type=jnp.float32)
            linear = jnp.dot(factors, for_linear, preferred_element_type=jnp.float32)
            radial = jnp.exp2(power)
            basis = linear * radial
            phi_ref[s, j] = basis.astype(jnp.bfloat16)
            if j == 0:
                radial_ref[s] = radial
                basis_ref[s] = basis

    def some_slots(i, carry):
        for u in range(2):
            one_slot(i * 2 + u)
        return carry

    steps = chunk_steps(mig_ref, first, phi_ref.shape[0]) * (UNROLL // 2)
    lax.fori_loop(0, steps, some_slots, 0)


def rho_kernel(offsets, starts, lists_ref, mig_ref, *refs):
    chunks = len(starts)
    phis = refs[:chunks]
    slabs = refs[chunks : chunks + len(offsets)]
    tiles, chi_ref, rho_ref, *placed = refs[chunks + len(offsets) :]
    if offsets:
        tiles = placed[0]
        place_slabs(offsets, slabs, tiles)
    blk = lax.axis_index("blk")
    length = lists_ref.shape[0]
    rho_ref[...] = jnp.zeros_like(rho_ref)

    for c, phi_ref in enumerate(phis):
        size = phi_ref.shape[0]

        def one_slot(s, first=starts[c], phi_ref=phi_ref):
            slot = first + s
            own = lists_ref[blk, slot]
            cols = aligned((own - blk * BPD) * BLOCK, BLOCK)
            phi = phi_ref[s, 0]
            chi = jnp.dot(
                tiles[aligned(own * BLOCK, BLOCK), cols], phi, preferred_element_type=jnp.float32
            )
            for j in range(1, length):
                k = lists_ref[lax.rem(blk + j, length), slot]
                chi += lax.dot_general(
                    tiles[aligned(k * BLOCK, BLOCK), cols],
                    phi_ref[s, j],
                    (((0,), (0,)), ((), ())),
                    preferred_element_type=jnp.float32,
                )
            chi_ref[slot] = chi
            rho_ref[pl.ds(slot, 1), :] = jnp.sum(
                phi.astype(jnp.float32) * chi, axis=0, keepdims=True
            )

        def some_slots(i, carry, one_slot=one_slot):
            for u in range(UNROLL):
                one_slot(i * UNROLL + u)
            return carry

        lax.fori_loop(0, chunk_steps(mig_ref, starts[c], size), some_slots, 0)


def force_kernel(starts, lists_ref, mig_ref, points_ref, rho_a_ref, rho_b_ref, chi_ref, *refs):
    chunks = len(starts)
    radials = refs[:chunks]
    bases = refs[chunks : 2 * chunks]
    table_ref, dest_ref, out_ref, pot_ref, acc = refs[2 * chunks :]
    blk = lax.axis_index("blk")
    slots, _, point_count = points_ref.shape
    dests = dest_ref.shape[1]
    live = live_count(mig_ref)
    rho = rho_a_ref[...] + rho_b_ref[...]
    weight = points_ref[:, 3, :]
    log_sq = jnp.log(rho * rho + RHO_SOFT * RHO_SOFT)
    pot = weight * (-(4.0 / 3.0) * SLATER) * rho * jnp.exp(log_sq * (-1.0 / 3.0))
    slot_ids = lax.broadcasted_iota(jnp.int32, (slots, 1), 0)
    pot_ref[...] = jnp.where(slot_ids < live, pot, 0.0)
    energies = jnp.sum(weight * -SLATER * jnp.exp(log_sq * (2.0 / 3.0)), axis=1, keepdims=True)
    acc[...] = jnp.zeros_like(acc)

    for c in range(chunks):
        radial_ref, basis_ref = radials[c], bases[c]
        size = radial_ref.shape[0]

        def one_slot(s, first=starts[c], radial_ref=radial_ref, basis_ref=basis_ref):
            slot = first + s
            own = lists_ref[blk, slot] - blk * BPD
            pots = pot_ref[pl.ds(slot, 1), :]
            for r in range(0, BLOCK, ROWS):
                sub = slice(r, r + ROWS)
                sums = None
                for h in range(0, point_count, LANES):
                    lanes = slice(h, h + LANES)
                    u = chi_ref[slot, sub, lanes] * pots[:, lanes]
                    ub = u * basis_ref[s, sub, lanes]
                    terms = (
                        u * radial_ref[s, sub, lanes],
                        ub,
                        ub * points_ref[slot, 0:1, lanes],
                        ub * points_ref[slot, 1:2, lanes],
                        ub * points_ref[slot, 2:3, lanes],
                    )
                    sums = terms if sums is None else [a + b for a, b in zip(sums, terms)]
                for q in range(5):
                    acc[own, q, sub] += sums[q]

        def some_slots(i, carry, one_slot=one_slot):
            for u in range(UNROLL):
                one_slot(i * UNROLL + u)
            return carry

        lax.fori_loop(0, chunk_steps(mig_ref, starts[c], size), some_slots, 0)

    lane_ids = lax.broadcasted_iota(jnp.int32, (1, LANES), 1).astype(jnp.float32)

    totals = [jnp.zeros((8, LANES), jnp.float32)] * (3 * NATOM // LANES)
    for b in range(BPD):
        for r in range(0, BLOCK, ROWS):
            sub = slice(r, r + ROWS)
            parts = [acc[b, q, sub] for q in range(5)]
            doubled = 2.0 * table_ref[b, 6, sub]
            atom = table_ref[b, 7, sub]
            for c in range(3):
                force = table_ref[b, 3 + c, sub] * parts[0] - doubled * (
                    parts[2 + c] - table_ref[b, c, sub] * parts[1]
                )
                column = 2.0 * jnp.sum(force, axis=1, keepdims=True)
                for h in range(NATOM // LANES):
                    hit = jnp.where(atom == lane_ids + float(h * LANES), column, 0.0)
                    i = c * (NATOM // LANES) + h
                    totals[i] = totals[i] + sum(hit[i8 : i8 + 8] for i8 in range(0, ROWS, 8))
    rows = [jnp.sum(t, axis=0, keepdims=True) for t in totals]
    moved = jnp.sum(dest_ref[...] * energies, axis=0, keepdims=True)
    rows += [moved[:, h : h + LANES] for h in range(0, dests, LANES)]
    packed = jnp.concatenate(rows, axis=0)
    for i in range(out_ref.shape[0]):
        out_ref[i] = packed


def sum_kernel(copies, arrived_ref, energy_ref, forces_ref):
    me = lax.axis_index("grid")
    total = jnp.sum(arrived_ref[...], axis=0)
    per = NATOM // LANES
    for c in range(3):
        for h in range(per):
            forces_ref[c : c + 1, h * LANES : (h + 1) * LANES] = total[c * per + h : c * per + h + 1]
    width = energy_ref.shape[1]
    first = me * width
    energy = jnp.zeros((1, LANES), jnp.float32)
    for i in range(3 * per, total.shape[0]):
        chosen = lax.div(first, LANES) == i - 3 * per
        energy = jnp.where(chosen, total[i : i + 1], energy)
    turn = lax.rem(LANES - lax.rem(first, LANES), LANES)
    energy = pltpu.roll(jnp.broadcast_to(energy, (8, LANES)), turn, 1)
    energy_ref[...] = energy[0:1, 0:width] * (1.0 / copies)


def swap(array, offset):
    count = lax.axis_size("grid")
    return lax.ppermute(array, "grid", [(i, i ^ offset) for i in range(count)])


STAGES = (((8, 0), (4, 0), (2, 0)), ((14, 8), (12, 8), (10, 8), (6, 4)))


def in_hbm(array):
    return pltpu.with_memory_space_constraint(array, pltpu.HBM)


def spec(space):
    return pl.BlockSpec(memory_space=space)


def params(blocks):
    return pltpu.CompilerParams(vmem_limit_bytes=blocks * 1024 * 1024)


def cost(nominal_us):
    return pl.CostEstimate(
        flops=0, bytes_accessed=int(nominal_us * 3.69e6), transcendentals=0
    )


def f32(*shape):
    return jax.ShapeDtypeStruct(shape, jnp.float32)


def local(density, points, sig_blocks, migration, atom_coords, exponents, shape_coef, func_atom):
    grid_count = lax.axis_size("grid")
    blk_count = lax.axis_size("blk")
    slots, _, point_count = points.shape
    length = sig_blocks.shape[1]
    functions = exponents.shape[0]
    blocks = functions // BLOCK
    dests = grid_count * (slots // 2)
    sizes = [slots // 4, slots // 4 * 3]
    starts = [0, slots // 4]
    slab = density.T
    tied = lax.optimization_barrier
    lists = sig_blocks.T

    factors, table, dest_mask, points, lists, migration = pl.pallas_call(
        table_kernel,
        out_shape=[
            jax.ShapeDtypeStruct((blocks, BLOCK, BLOCK), jnp.bfloat16),
            f32(BPD, 8, BLOCK, LANES),
            f32(slots, dests),
            f32(*points.shape),
            jax.ShapeDtypeStruct(lists.shape, jnp.int32),
            jax.ShapeDtypeStruct(migration.shape, jnp.int32),
        ],
        in_specs=[spec(pltpu.HBM)] * 7,
        out_specs=[spec(VMEM)] * 6,
        scratch_shapes=[
            pltpu.SMEM((slots,), jnp.int32),
            pltpu.VMEM((functions,), jnp.int32),
            pltpu.VMEM((functions,), jnp.float32),
            pltpu.VMEM((3, functions), jnp.float32),
            pltpu.VMEM((3, NATOM), jnp.float32),
            pltpu.SemaphoreType.DMA((8,)),
        ],
        compiler_params=params(blocks),
        cost_estimate=cost(4),
        name="param_table",
    )(
        *[
            in_hbm(a)
            for a in (migration, func_atom, exponents, shape_coef, atom_coords, points, lists)
        ]
    )

    tile_shape = jax.ShapeDtypeStruct((functions, BPD * BLOCK), jnp.bfloat16)

    def basis_chunk(c, points, offsets=()):
        some = 1 if offsets else 0
        return pl.pallas_call(
            functools.partial(phi_kernel, starts[c], offsets),
            out_shape=[
                jax.ShapeDtypeStruct((sizes[c], length, BLOCK, point_count), jnp.bfloat16),
                f32(sizes[c], BLOCK, point_count),
                f32(sizes[c], BLOCK, point_count),
            ]
            + [tile_shape] * some,
            in_specs=[spec(SMEM), spec(SMEM)] + [spec(VMEM)] * (2 + len(offsets)),
            out_specs=[spec(VMEM)] * (3 + some),
            compiler_params=params(blocks),
            cost_estimate=cost(5),
            name="basis_values",
        )(lists, migration, points, factors, *[held[e] for e in offsets])

    held = {0: slab}
    late, slabs = [], []
    if grid_count == 16:
        held.update({e: swap(held[source], e ^ source) for e, source in STAGES[0]})
        ready = tuple(held)
        first = basis_chunk(0, points)
        held, first, points = tied((held, first, points))
        held.update({e: swap(held[source], e ^ source) for e, source in STAGES[1]})
        *second, tiles = basis_chunk(1, points, ready)
        held, second, tiles = tied((held, second, tiles))
        everything = tuple(held)
        pack = pl.pallas_call(
            pack_kernel,
            out_shape=jax.ShapeDtypeStruct((len(everything), *slab.shape), slab.dtype),
            in_specs=[spec(VMEM)] * len(everything),
            out_specs=spec(VMEM),
            compiler_params=params(blocks),
            name="pack",
        )(*[held[e] for e in everything])
        chunks = [first, second]
        late = [e for e in everything if e not in ready]
        late.append(tuple(e ^ 1 for e in everything))
        slabs = [*[held[e] for e in late[:-1]], swap(pack, 1)]
    else:
        tiles = lax.all_gather(slab, "grid", axis=0, tiled=True)
        chunks = [basis_chunk(i, points) for i in range(len(starts))]
    phis, radials, bases = zip(*chunks)

    some = 1 if late else 0
    chi, rho, *_ = pl.pallas_call(
        functools.partial(rho_kernel, late, starts),
        out_shape=[f32(slots, BLOCK, point_count), f32(slots, point_count)] + [tile_shape] * some,
        in_specs=[spec(SMEM), spec(SMEM)]
        + [spec(VMEM)] * (len(starts) + len(late) + 1),
        out_specs=[spec(VMEM)] * (2 + some),
        input_output_aliases={2 + len(starts) + len(late): 2} if late else {},
        compiler_params=params(blocks),
        cost_estimate=cost(5),
        name="density_at_points",
    )(lists, migration, *phis, *slabs, tiles)

    if blk_count == 2:
        other = lax.ppermute(rho, "blk", [(0, 1), (1, 0)])
    else:
        other = lax.psum(rho, "blk") - rho

    rows = 3 * NATOM // LANES + dests // LANES
    outgoing = pl.pallas_call(
        functools.partial(force_kernel, starts),
        out_shape=f32(blk_count * grid_count, rows, LANES),
        in_specs=[spec(SMEM), spec(SMEM)] + [spec(VMEM)] * (6 + 2 * len(starts)),
        out_specs=spec(VMEM),
        scratch_shapes=[
            pltpu.VMEM((slots, point_count), jnp.float32),
            pltpu.VMEM((BPD, 5, BLOCK, LANES), jnp.float32),
        ],
        compiler_params=params(blocks),
        cost_estimate=cost(5),
        name="forces_and_energies",
    )(lists, migration, points, rho, other, chi, *radials, *bases, table, dest_mask)

    arrived = lax.all_to_all(outgoing, ("blk", "grid"), split_axis=0, concat_axis=0, tiled=True)

    energy, forces = pl.pallas_call(
        functools.partial(sum_kernel, blk_count),
        out_shape=[f32(1, dests // grid_count), f32(3, NATOM)],
        in_specs=[spec(VMEM)],
        out_specs=[spec(VMEM)] * 2,
        compiler_params=params(blocks),
        name="final_sums",
    )(arrived)
    return (energy.reshape(dests // grid_count), forces)


def solution(mesh):
    in_specs = (
        P("blk", "grid"),
        P("grid", None, None),
        P("grid", None),
        P("grid"),
        P(),
        P(),
        P(),
        P(),
    )
    out_specs = (P("grid"), P())
    return jax.shard_map(local, mesh=mesh, in_specs=in_specs, out_specs=out_specs, check_vma=False)
```

```python
import functools

import jax
import jax.numpy as jnp
from jax import lax
from jax.experimental import pallas as pl
from jax.experimental.pallas import tpu as pltpu
from jax.sharding import PartitionSpec as P

BLOCK = 128
BPD = 6
NATOM = 256
LANES = 128
ROWS = 32
UNROLL = 4

SLATER = 0.7386
RHO_SOFT = 0.05

VMEM = pltpu.MemorySpace.VMEM
SMEM = pltpu.MemorySpace.SMEM


def aligned(start, size):
    return pl.ds(pl.multiple_of(start, size), size)


def live_count(mig_ref):
    slots = mig_ref.shape[0]
    step = 1
    while step * 2 <= slots:
        step *= 2
    count = jnp.int32(0)
    while step:
        more = count + step
        found = mig_ref[jnp.minimum(more, slots) - 1] >= 0
        count = jnp.where(jnp.logical_and(more <= slots, found), more, count)
        step //= 2
    return count


def start_copies(pairs, sems):
    copies = [pltpu.make_async_copy(src, dst, sems.at[i]) for i, (src, dst) in enumerate(pairs)]
    for copy in copies:
        copy.start()
    return copies


def place_slabs(offsets, slabs, tiles):
    me = lax.axis_index("grid")
    depth = slabs[0].shape[-2]

    def place(e, slab):
        tiles[aligned(jnp.bitwise_xor(me, e) * depth, depth), :] = slab

    for e, slab in zip(offsets, slabs):
        if isinstance(e, tuple):
            for i, one in enumerate(e):
                place(one, slab[i])
        else:
            place(e, slab[...])


def pack_kernel(*refs):
    *slabs, out_ref = refs
    for i, slab in enumerate(slabs):
        out_ref[i] = slab[...]


def table_kernel(
    mig_hbm,
    atom_hbm,
    expo_hbm,
    coef_hbm,
    coords_hbm,
    points_hbm,
    lists_hbm,
    table_ref,
    dest_ref,
    points_out,
    lists_out,
    mig_out,
    mig_ref,
    atom_ref,
    expo_ref,
    coef_ref,
    coords_ref,
    sems,
):
    copies = start_copies(
        [
            (mig_hbm, mig_ref),
            (atom_hbm, atom_ref),
            (expo_hbm, expo_ref),
            (coef_hbm, coef_ref),
            (coords_hbm, coords_ref),
            (points_hbm, points_out),
            (lists_hbm, lists_out),
            (mig_hbm, mig_out),
        ],
        sems,
    )
    for copy in copies[:5]:
        copy.wait()
    coords = coords_ref[...]
    high = coords.astype(jnp.bfloat16)
    rest = coords - high.astype(jnp.float32)
    mid = rest.astype(jnp.bfloat16)
    low = (rest - mid.astype(jnp.float32)).astype(jnp.bfloat16)
    blocks = table_ref.shape[0]
    atoms = atom_ref[...].reshape(blocks, BLOCK)
    expos = expo_ref[...].reshape(blocks, BLOCK)

    for k in range(blocks):
        atom = atoms[k : k + 1]
        onehot = jnp.where(
            lax.broadcasted_iota(jnp.int32, (NATOM, BLOCK), 0) == atom, 1.0, 0.0
        ).astype(jnp.bfloat16)
        picked = [
            jnp.dot(part, onehot, preferred_element_type=jnp.float32) for part in (high, mid, low)
        ]
        center = (picked[0] + picked[1]) + picked[2]
        coef = coef_ref[:, k * BLOCK : (k + 1) * BLOCK]
        rows = jnp.concatenate(
            [center, coef, expos[k : k + 1], atom.astype(jnp.float32)], axis=0
        )
        columns = rows.T
        for p in range(8):
            table_ref[k, p] = jnp.broadcast_to(columns[:, p : p + 1], (BLOCK, LANES))

    dest_ids = lax.broadcasted_iota(jnp.int32, (1, dest_ref.shape[1]), 1)
    for s in range(mig_ref.shape[0]):
        dest_ref[s : s + 1, :] = jnp.where(dest_ids == mig_ref[s], 1.0, 0.0)
    for copy in copies[5:]:
        copy.wait()


def chunk_steps(mig_ref, first, size):
    left = jnp.clip(live_count(mig_ref) - first, 0, size)
    return lax.div(left + (UNROLL - 1), UNROLL)


def phi_kernel(first, offsets, lists_ref, mig_ref, points_ref, table_ref, *refs):
    slabs = refs[: len(offsets)]
    phi_ref, radial_ref, basis_ref, *more = refs[len(offsets) :]
    if first == 0:
        more.pop(0)[...] = jnp.zeros((BPD, 5, BLOCK, LANES), jnp.float32)
    if offsets:
        place_slabs(offsets, slabs, more[0])
    blk = lax.axis_index("blk")
    length = lists_ref.shape[0]
    point_count = points_ref.shape[2]

    def one_slot(s):
        for j in range(length):
            k = lists_ref[lax.rem(blk + j, length), first + s]
            for r in range(0, BLOCK, ROWS):
                sub = slice(r, r + ROWS)
                cx, cy, cz, sx, sy, sz, expo = [table_ref[k, p, sub] for p in range(7)]
                for h in range(0, point_count, LANES):
                    lanes = slice(h, h + LANES)
                    ox = points_ref[first + s, 0:1, lanes] - cx
                    oy = points_ref[first + s, 1:2, lanes] - cy
                    oz = points_ref[first + s, 2:3, lanes] - cz
                    squared = ox * ox + oy * oy + oz * oz
                    radial = jnp.exp(-expo * squared)
                    linear = 1.0 + (sx * ox + sy * oy + sz * oz)
                    basis = linear * radial
                    rows = slice(j * BLOCK + r, j * BLOCK + r + ROWS)
                    phi_ref[s, rows, lanes] = basis.astype(jnp.bfloat16)
                    if j == 0:
                        radial_ref[s, sub, lanes] = radial
                        basis_ref[s, sub, lanes] = basis

    def some_slots(i, carry):
        for u in range(2):
            one_slot(i * 2 + u)
        return carry

    steps = chunk_steps(mig_ref, first, phi_ref.shape[0]) * (UNROLL // 2)
    lax.fori_loop(0, steps, some_slots, 0)


def rho_kernel(offsets, starts, lists_ref, mig_ref, *refs):
    chunks = len(starts)
    phis = refs[:chunks]
    slabs = refs[chunks : chunks + len(offsets)]
    tiles, chi_ref, rho_ref, *placed = refs[chunks + len(offsets) :]
    if offsets:
        tiles = placed[0]
        place_slabs(offsets, slabs, tiles)
    blk = lax.axis_index("blk")
    length = lists_ref.shape[0]
    rho_ref[...] = jnp.zeros_like(rho_ref)

    for c, phi_ref in enumerate(phis):
        size = phi_ref.shape[0]

        def one_slot(s, first=starts[c], phi_ref=phi_ref):
            slot = first + s
            own = lists_ref[blk, slot]
            cols = aligned((own - blk * BPD) * BLOCK, BLOCK)
            left = [tiles[aligned(own * BLOCK, BLOCK), cols]]
            for j in range(1, length):
                k = lists_ref[lax.rem(blk + j, length), slot]
                left.append(tiles[aligned(k * BLOCK, BLOCK), cols].T)
            chi = jnp.dot(
                jnp.concatenate(left, axis=1), phi_ref[s], preferred_element_type=jnp.float32
            )
            phi = phi_ref[s, 0:BLOCK, :]
            chi_ref[slot] = chi
            rho_ref[pl.ds(slot, 1), :] = jnp.sum(
                phi.astype(jnp.float32) * chi, axis=0, keepdims=True
            )

        def some_slots(i, carry, one_slot=one_slot):
            for u in range(UNROLL):
                one_slot(i * UNROLL + u)
            return carry

        lax.fori_loop(0, chunk_steps(mig_ref, starts[c], size), some_slots, 0)


def force_kernel(starts, lists_ref, mig_ref, points_ref, rho_a_ref, rho_b_ref, chi_ref, *refs):
    chunks = len(starts)
    radials = refs[:chunks]
    bases = refs[chunks : 2 * chunks]
    table_ref, dest_ref, _, out_ref, acc, pot_ref = refs[2 * chunks :]
    blk = lax.axis_index("blk")
    slots, _, point_count = points_ref.shape
    dests = dest_ref.shape[1]
    live = live_count(mig_ref)
    rho = rho_a_ref[...] + rho_b_ref[...]
    weight = points_ref[:, 3, :]
    log_sq = jnp.log(rho * rho + RHO_SOFT * RHO_SOFT)
    pot = weight * (-(4.0 / 3.0) * SLATER) * rho * jnp.exp(log_sq * (-1.0 / 3.0))
    slot_ids = lax.broadcasted_iota(jnp.int32, (slots, 1), 0)
    pot_ref[...] = jnp.where(slot_ids < live, pot, 0.0)
    energies = jnp.sum(weight * -SLATER * jnp.exp(log_sq * (2.0 / 3.0)), axis=1, keepdims=True)

    for c in range(chunks):
        radial_ref, basis_ref = radials[c], bases[c]
        size = radial_ref.shape[0]

        def one_slot(s, first=starts[c], radial_ref=radial_ref, basis_ref=basis_ref):
            slot = first + s
            own = lists_ref[blk, slot] - blk * BPD
            pots = pot_ref[pl.ds(slot, 1), :]
            for r in range(0, BLOCK, ROWS):
                sub = slice(r, r + ROWS)
                sums = None
                for h in range(0, point_count, LANES):
                    lanes = slice(h, h + LANES)
                    u = chi_ref[slot, sub, lanes] * pots[:, lanes]
                    ub = u * basis_ref[s, sub, lanes]
                    terms = (
                        u * radial_ref[s, sub, lanes],
                        ub,
                        ub * points_ref[slot, 0:1, lanes],
                        ub * points_ref[slot, 1:2, lanes],
                        ub * points_ref[slot, 2:3, lanes],
                    )
                    sums = terms if sums is None else [a + b for a, b in zip(sums, terms)]
                for q in range(5):
                    acc[own, q, sub] += sums[q]

        def some_slots(i, carry, one_slot=one_slot):
            for u in range(UNROLL):
                one_slot(i * UNROLL + u)
            return carry

        lax.fori_loop(0, chunk_steps(mig_ref, starts[c], size), some_slots, 0)

    lane_ids = lax.broadcasted_iota(jnp.int32, (1, LANES), 1).astype(jnp.float32)

    totals = [jnp.zeros((8, LANES), jnp.float32)] * (3 * NATOM // LANES)
    for b in range(BPD):
        k = blk * BPD + b
        for r in range(0, BLOCK, ROWS):
            sub = slice(r, r + ROWS)
            parts = [acc[b, q, sub] for q in range(5)]
            doubled = 2.0 * table_ref[k, 6, sub]
            atom = table_ref[k, 7, sub]
            for c in range(3):
                force = table_ref[k, 3 + c, sub] * parts[0] - doubled * (
                    parts[2 + c] - table_ref[k, c, sub] * parts[1]
                )
                column = 2.0 * jnp.sum(force, axis=1, keepdims=True)
                for h in range(NATOM // LANES):
                    hit = jnp.where(atom == lane_ids + float(h * LANES), column, 0.0)
                    i = c * (NATOM // LANES) + h
                    totals[i] = totals[i] + sum(hit[i8 : i8 + 8] for i8 in range(0, ROWS, 8))
    rows = [jnp.sum(t, axis=0, keepdims=True) for t in totals]
    moved = jnp.sum(dest_ref[...] * energies, axis=0, keepdims=True)
    rows += [moved[:, h : h + LANES] for h in range(0, dests, LANES)]
    packed = jnp.concatenate(rows, axis=0)
    for i in range(out_ref.shape[0]):
        out_ref[i] = packed


def sum_kernel(copies, arrived_ref, energy_ref, forces_ref):
    me = lax.axis_index("grid")
    total = jnp.sum(arrived_ref[...], axis=0)
    per = NATOM // LANES
    for c in range(3):
        for h in range(per):
            forces_ref[c : c + 1, h * LANES : (h + 1) * LANES] = total[c * per + h : c * per + h + 1]
    width = energy_ref.shape[1]
    first = me * width
    energy = jnp.zeros((1, LANES), jnp.float32)
    for i in range(3 * per, total.shape[0]):
        chosen = lax.div(first, LANES) == i - 3 * per
        energy = jnp.where(chosen, total[i : i + 1], energy)
    turn = lax.rem(LANES - lax.rem(first, LANES), LANES)
    energy = pltpu.roll(jnp.broadcast_to(energy, (8, LANES)), turn, 1)
    energy_ref[...] = energy[0:1, 0:width] * (1.0 / copies)


def swap(array, offset):
    count = lax.axis_size("grid")
    return lax.ppermute(array, "grid", [(i, i ^ offset) for i in range(count)])


FIRST = ((8, 0), (4, 0), (2, 0), (6, 0))
SECOND = ((14, 8), (12, 8), (10, 8))


def in_hbm(array):
    return pltpu.with_memory_space_constraint(array, pltpu.HBM)


def spec(space):
    return pl.BlockSpec(memory_space=space)


def params(blocks):
    return pltpu.CompilerParams(vmem_limit_bytes=blocks * 1024 * 1024)


def cost(nominal_us):
    return pl.CostEstimate(
        flops=0, bytes_accessed=int(nominal_us * 3.69e6), transcendentals=0
    )


def f32(*shape):
    return jax.ShapeDtypeStruct(shape, jnp.float32)


def local(density, points, sig_blocks, migration, atom_coords, exponents, shape_coef, func_atom):
    grid_count = lax.axis_size("grid")
    blk_count = lax.axis_size("blk")
    slots, _, point_count = points.shape
    length = sig_blocks.shape[1]
    functions = exponents.shape[0]
    blocks = functions // BLOCK
    dests = grid_count * (slots // 2)
    sizes = [slots // 4 * 3, slots // 4]
    starts = [0, slots // 4 * 3]
    slab = density.T
    tied = lax.optimization_barrier
    lists = sig_blocks.T

    table, dest_mask, points, lists, migration = pl.pallas_call(
        table_kernel,
        out_shape=[
            f32(blocks, 8, BLOCK, LANES),
            f32(slots, dests),
            f32(*points.shape),
            jax.ShapeDtypeStruct(lists.shape, jnp.int32),
            jax.ShapeDtypeStruct(migration.shape, jnp.int32),
        ],
        in_specs=[spec(pltpu.HBM)] * 7,
        out_specs=[spec(VMEM)] * 5,
        scratch_shapes=[
            pltpu.SMEM((slots,), jnp.int32),
            pltpu.VMEM((functions,), jnp.int32),
            pltpu.VMEM((functions,), jnp.float32),
            pltpu.VMEM((3, functions), jnp.float32),
            pltpu.VMEM((3, NATOM), jnp.float32),
            pltpu.SemaphoreType.DMA((8,)),
        ],
        compiler_params=params(blocks),
        cost_estimate=cost(4),
        name="param_table",
    )(
        *[
            in_hbm(a)
            for a in (migration, func_atom, exponents, shape_coef, atom_coords, points, lists)
        ]
    )

    tile_shape = jax.ShapeDtypeStruct((functions, BPD * BLOCK), jnp.bfloat16)

    def basis_chunk(c, points, offsets=()):
        some = 1 if offsets else 0
        zeros = 1 if c == 0 else 0
        return pl.pallas_call(
            functools.partial(phi_kernel, starts[c], offsets),
            out_shape=[
                jax.ShapeDtypeStruct((sizes[c], length * BLOCK, point_count), jnp.bfloat16),
                f32(sizes[c], BLOCK, point_count),
                f32(sizes[c], BLOCK, point_count),
            ]
            + [f32(BPD, 5, BLOCK, LANES)] * zeros
            + [tile_shape] * some,
            in_specs=[spec(SMEM), spec(SMEM)] + [spec(VMEM)] * (2 + len(offsets)),
            out_specs=[spec(VMEM)] * (3 + zeros + some),
            compiler_params=params(blocks),
            cost_estimate=cost(5),
            name="basis_values",
        )(lists, migration, points, table, *[held[e] for e in offsets])

    held = {0: slab}
    late, slabs = [], []
    if grid_count == 16:
        for e, source in FIRST:
            held[e] = swap(held[source], e ^ source)
        held, points = tied((held, points))
        for e, source in SECOND:
            held[e] = swap(held[source], e ^ source)
        ready = [e for e, _ in ((0, 0), *FIRST)]
        *first, acc, tiles = basis_chunk(0, points, ready)
        held, first, tiles, points = tied((held, first, tiles, points))
        everything = list(held)
        pack = pl.pallas_call(
            pack_kernel,
            out_shape=jax.ShapeDtypeStruct((len(everything), *slab.shape), slab.dtype),
            in_specs=[spec(VMEM)] * len(everything),
            out_specs=spec(VMEM),
            compiler_params=params(blocks),
            name="pack",
        )(*[held[e] for e in everything])
        crossed = swap(pack, 1)
        second = basis_chunk(1, points)
        late = [e for e in everything if e not in ready]
        late.append(tuple(e ^ 1 for e in everything))
        slabs = [*[held[e] for e in late[:-1]], crossed]
    else:
        tiles = lax.all_gather(slab, "grid", axis=0, tiled=True)
        *first, acc = basis_chunk(0, points)
        second = basis_chunk(1, points)
    chunks = [first, second]
    phis, radials, bases = zip(*chunks)

    some = 1 if late else 0
    chi, rho, *_ = pl.pallas_call(
        functools.partial(rho_kernel, late, starts),
        out_shape=[f32(slots, BLOCK, point_count), f32(slots, point_count)] + [tile_shape] * some,
        in_specs=[spec(SMEM), spec(SMEM)]
        + [spec(VMEM)] * (len(starts) + len(late) + 1),
        out_specs=[spec(VMEM)] * (2 + some),
        input_output_aliases={2 + len(starts) + len(late): 2} if late else {},
        compiler_params=params(blocks),
        cost_estimate=cost(5),
        name="density_at_points",
    )(lists, migration, *phis, *slabs, tiles)

    if blk_count == 2:
        other = lax.ppermute(rho, "blk", [(0, 1), (1, 0)])
    else:
        other = lax.psum(rho, "blk") - rho

    rows = 3 * NATOM // LANES + dests // LANES
    outgoing, _ = pl.pallas_call(
        functools.partial(force_kernel, starts),
        out_shape=[f32(blk_count * grid_count, rows, LANES), f32(BPD, 5, BLOCK, LANES)],
        in_specs=[spec(SMEM), spec(SMEM)] + [spec(VMEM)] * (7 + 2 * len(starts)),
        out_specs=[spec(VMEM)] * 2,
        scratch_shapes=[pltpu.VMEM((slots, point_count), jnp.float32)],
        input_output_aliases={8 + 2 * len(starts): 1},
        compiler_params=params(blocks),
        cost_estimate=cost(5),
        name="forces_and_energies",
    )(lists, migration, points, rho, other, chi, *radials, *bases, table, dest_mask, acc)

    arrived = lax.all_to_all(outgoing, ("blk", "grid"), split_axis=0, concat_axis=0, tiled=True)

    energy, forces = pl.pallas_call(
        functools.partial(sum_kernel, blk_count),
        out_shape=[f32(1, dests // grid_count), f32(3, NATOM)],
        in_specs=[spec(VMEM)],
        out_specs=[spec(VMEM)] * 2,
        compiler_params=params(blocks),
        name="final_sums",
    )(arrived)
    return (energy.reshape(dests // grid_count), forces)


def solution(mesh):
    in_specs = (
        P("blk", "grid"),
        P("grid", None, None),
        P("grid", None),
        P("grid"),
        P(),
        P(),
        P(),
        P(),
    )
    out_specs = (P("grid"), P())
    return jax.shard_map(local, mesh=mesh, in_specs=in_specs, out_specs=out_specs, check_vma=False)
```

```python
import functools

import jax
import jax.numpy as jnp
from jax import lax
from jax.experimental import pallas as pl
from jax.experimental.pallas import tpu as pltpu
from jax.sharding import PartitionSpec as P

BLOCK = 128
BPD = 6
NATOM = 256
LANES = 128
ROWS = 32
UNROLL = 4

SLATER = 0.7386
RHO_SOFT = 0.05

VMEM = pltpu.MemorySpace.VMEM
SMEM = pltpu.MemorySpace.SMEM


def aligned(start, size):
    return pl.ds(pl.multiple_of(start, size), size)


def live_count(mig_ref):
    slots = mig_ref.shape[0]
    step = 1
    while step * 2 <= slots:
        step *= 2
    count = jnp.int32(0)
    while step:
        more = count + step
        found = mig_ref[jnp.minimum(more, slots) - 1] >= 0
        count = jnp.where(jnp.logical_and(more <= slots, found), more, count)
        step //= 2
    return count


def start_copies(pairs, sems):
    copies = [pltpu.make_async_copy(src, dst, sems.at[i]) for i, (src, dst) in enumerate(pairs)]
    for copy in copies:
        copy.start()
    return copies


def place_slabs(offsets, slabs, tiles):
    me = lax.axis_index("grid")
    depth = slabs[0].shape[-2]

    def place(e, slab):
        tiles[aligned(jnp.bitwise_xor(me, e) * depth, depth), :] = slab

    for e, slab in zip(offsets, slabs):
        if isinstance(e, tuple):
            for i, one in enumerate(e):
                place(one, slab[i])
        else:
            place(e, slab[...])


def pack_kernel(*refs):
    *slabs, out_ref = refs
    for i, slab in enumerate(slabs):
        out_ref[i] = slab[...]


def table_kernel(
    mig_hbm,
    atom_hbm,
    expo_hbm,
    coef_hbm,
    coords_hbm,
    points_hbm,
    lists_hbm,
    table_ref,
    dest_ref,
    points_out,
    lists_out,
    mig_out,
    mig_ref,
    atom_ref,
    expo_ref,
    coef_ref,
    coords_ref,
    sems,
):
    copies = start_copies(
        [
            (mig_hbm, mig_ref),
            (atom_hbm, atom_ref),
            (expo_hbm, expo_ref),
            (coef_hbm, coef_ref),
            (coords_hbm, coords_ref),
            (points_hbm, points_out),
            (lists_hbm, lists_out),
            (mig_hbm, mig_out),
        ],
        sems,
    )
    for copy in copies[:5]:
        copy.wait()
    coords = coords_ref[...]
    high = coords.astype(jnp.bfloat16)
    rest = coords - high.astype(jnp.float32)
    mid = rest.astype(jnp.bfloat16)
    low = (rest - mid.astype(jnp.float32)).astype(jnp.bfloat16)
    blocks = table_ref.shape[0]
    atoms = atom_ref[...].reshape(blocks, BLOCK)
    expos = expo_ref[...].reshape(blocks, BLOCK)

    for k in range(blocks):
        atom = atoms[k : k + 1]
        onehot = jnp.where(
            lax.broadcasted_iota(jnp.int32, (NATOM, BLOCK), 0) == atom, 1.0, 0.0
        ).astype(jnp.bfloat16)
        picked = [
            jnp.dot(part, onehot, preferred_element_type=jnp.float32) for part in (high, mid, low)
        ]
        center = (picked[0] + picked[1]) + picked[2]
        coef = coef_ref[:, k * BLOCK : (k + 1) * BLOCK]
        rows = jnp.concatenate(
            [center, coef, expos[k : k + 1], atom.astype(jnp.float32)], axis=0
        )
        columns = rows.T
        for p in range(8):
            table_ref[k, p] = jnp.broadcast_to(columns[:, p : p + 1], (BLOCK, LANES))

    dest_ids = lax.broadcasted_iota(jnp.int32, (1, dest_ref.shape[1]), 1)
    for s in range(mig_ref.shape[0]):
        dest_ref[s : s + 1, :] = jnp.where(dest_ids == mig_ref[s], 1.0, 0.0)
    for copy in copies[5:]:
        copy.wait()


def chunk_steps(mig_ref, first, size):
    left = jnp.clip(live_count(mig_ref) - first, 0, size)
    return lax.div(left + (UNROLL - 1), UNROLL)


def phi_kernel(first, offsets, lists_ref, mig_ref, points_ref, table_ref, *refs):
    slabs = refs[: len(offsets)]
    phi_ref, radial_ref, basis_ref, *more = refs[len(offsets) :]
    if first == 0:
        more.pop(0)[...] = jnp.zeros((BPD, 5, BLOCK, LANES), jnp.float32)
    if offsets:
        place_slabs(offsets, slabs, more[0])
    blk = lax.axis_index("blk")
    length = lists_ref.shape[0]
    point_count = points_ref.shape[2]

    def one_slot(s):
        for j in range(length):
            k = lists_ref[lax.rem(blk + j, length), first + s]
            for r in range(0, BLOCK, ROWS):
                sub = slice(r, r + ROWS)
                cx, cy, cz, sx, sy, sz, expo = [table_ref[k, p, sub] for p in range(7)]
                for h in range(0, point_count, LANES):
                    lanes = slice(h, h + LANES)
                    ox = points_ref[first + s, 0:1, lanes] - cx
                    oy = points_ref[first + s, 1:2, lanes] - cy
                    oz = points_ref[first + s, 2:3, lanes] - cz
                    squared = ox * ox + oy * oy + oz * oz
                    radial = jnp.exp(-expo * squared)
                    linear = 1.0 + (sx * ox + sy * oy + sz * oz)
                    basis = linear * radial
                    rows = slice(j * BLOCK + r, j * BLOCK + r + ROWS)
                    phi_ref[s, rows, lanes] = basis.astype(jnp.bfloat16)
                    if j == 0:
                        radial_ref[s, sub, lanes] = radial
                        basis_ref[s, sub, lanes] = basis

    def some_slots(i, carry):
        for u in range(2):
            one_slot(i * 2 + u)
        return carry

    steps = chunk_steps(mig_ref, first, phi_ref.shape[0]) * (UNROLL // 2)
    lax.fori_loop(0, steps, some_slots, 0)


def rho_kernel(offsets, starts, lists_ref, mig_ref, *refs):
    chunks = len(starts)
    phis = refs[:chunks]
    slabs = refs[chunks : chunks + len(offsets)]
    tiles, chi_ref, rho_ref, *placed = refs[chunks + len(offsets) :]
    if offsets:
        tiles = placed[0]
        place_slabs(offsets, slabs, tiles)
    blk = lax.axis_index("blk")
    length = lists_ref.shape[0]
    rho_ref[...] = jnp.zeros_like(rho_ref)

    for c, phi_ref in enumerate(phis):
        size = phi_ref.shape[0]

        def one_slot(s, first=starts[c], phi_ref=phi_ref):
            slot = first + s
            own = lists_ref[blk, slot]
            cols = aligned((own - blk * BPD) * BLOCK, BLOCK)
            left = [tiles[aligned(own * BLOCK, BLOCK), cols]]
            for j in range(1, length):
                k = lists_ref[lax.rem(blk + j, length), slot]
                left.append(tiles[aligned(k * BLOCK, BLOCK), cols].T)
            chi = jnp.dot(
                jnp.concatenate(left, axis=1), phi_ref[s], preferred_element_type=jnp.float32
            )
            phi = phi_ref[s, 0:BLOCK, :]
            chi_ref[slot] = chi
            rho_ref[pl.ds(slot, 1), :] = jnp.sum(
                phi.astype(jnp.float32) * chi, axis=0, keepdims=True
            )

        def some_slots(i, carry, one_slot=one_slot):
            for u in range(UNROLL):
                one_slot(i * UNROLL + u)
            return carry

        lax.fori_loop(0, chunk_steps(mig_ref, starts[c], size), some_slots, 0)


def force_kernel(starts, lists_ref, mig_ref, points_ref, rho_a_ref, rho_b_ref, chi_ref, *refs):
    chunks = len(starts)
    radials = refs[:chunks]
    bases = refs[chunks : 2 * chunks]
    table_ref, dest_ref, _, out_ref, acc, pot_ref = refs[2 * chunks :]
    blk = lax.axis_index("blk")
    slots, _, point_count = points_ref.shape
    dests = dest_ref.shape[1]
    live = live_count(mig_ref)
    rho = rho_a_ref[...] + rho_b_ref[...]
    weight = points_ref[:, 3, :]
    log_sq = jnp.log(rho * rho + RHO_SOFT * RHO_SOFT)
    pot = weight * (-(4.0 / 3.0) * SLATER) * rho * jnp.exp(log_sq * (-1.0 / 3.0))
    slot_ids = lax.broadcasted_iota(jnp.int32, (slots, 1), 0)
    pot_ref[...] = jnp.where(slot_ids < live, pot, 0.0)
    energies = jnp.sum(weight * -SLATER * jnp.exp(log_sq * (2.0 / 3.0)), axis=1, keepdims=True)

    for c in range(chunks):
        radial_ref, basis_ref = radials[c], bases[c]
        size = radial_ref.shape[0]

        def one_slot(s, first=starts[c], radial_ref=radial_ref, basis_ref=basis_ref):
            slot = first + s
            own = lists_ref[blk, slot] - blk * BPD
            pots = pot_ref[pl.ds(slot, 1), :]
            for r in range(0, BLOCK, ROWS):
                sub = slice(r, r + ROWS)
                sums = None
                for h in range(0, point_count, LANES):
                    lanes = slice(h, h + LANES)
                    u = chi_ref[slot, sub, lanes] * pots[:, lanes]
                    ub = u * basis_ref[s, sub, lanes]
                    terms = (
                        u * radial_ref[s, sub, lanes],
                        ub,
                        ub * points_ref[slot, 0:1, lanes],
                        ub * points_ref[slot, 1:2, lanes],
                        ub * points_ref[slot, 2:3, lanes],
                    )
                    sums = terms if sums is None else [a + b for a, b in zip(sums, terms)]
                for q in range(5):
                    acc[own, q, sub] += sums[q]

        def some_slots(i, carry, one_slot=one_slot):
            for u in range(UNROLL):
                one_slot(i * UNROLL + u)
            return carry

        lax.fori_loop(0, chunk_steps(mig_ref, starts[c], size), some_slots, 0)

    lane_ids = lax.broadcasted_iota(jnp.int32, (1, LANES), 1).astype(jnp.float32)

    totals = [jnp.zeros((8, LANES), jnp.float32)] * (3 * NATOM // LANES)
    for b in range(BPD):
        k = blk * BPD + b
        for r in range(0, BLOCK, ROWS):
            sub = slice(r, r + ROWS)
            parts = [acc[b, q, sub] for q in range(5)]
            doubled = 2.0 * table_ref[k, 6, sub]
            atom = table_ref[k, 7, sub]
            for c in range(3):
                force = table_ref[k, 3 + c, sub] * parts[0] - doubled * (
                    parts[2 + c] - table_ref[k, c, sub] * parts[1]
                )
                column = 2.0 * jnp.sum(force, axis=1, keepdims=True)
                for h in range(NATOM // LANES):
                    hit = jnp.where(atom == lane_ids + float(h * LANES), column, 0.0)
                    i = c * (NATOM // LANES) + h
                    totals[i] = totals[i] + sum(hit[i8 : i8 + 8] for i8 in range(0, ROWS, 8))
    rows = [jnp.sum(t, axis=0, keepdims=True) for t in totals]
    moved = jnp.sum(dest_ref[...] * energies, axis=0, keepdims=True)
    rows += [moved[:, h : h + LANES] for h in range(0, dests, LANES)]
    packed = jnp.concatenate(rows, axis=0)
    out_ref[...] = packed


def sum_kernel(copies, arrived_ref, energy_ref, forces_ref):
    me = lax.axis_index("grid")
    total = jnp.sum(arrived_ref[...], axis=0)
    per = NATOM // LANES
    for c in range(3):
        for h in range(per):
            forces_ref[c : c + 1, h * LANES : (h + 1) * LANES] = total[c * per + h : c * per + h + 1]
    width = energy_ref.shape[1]
    first = me * width
    energy = jnp.zeros((1, LANES), jnp.float32)
    for i in range(3 * per, total.shape[0]):
        chosen = lax.div(first, LANES) == i - 3 * per
        energy = jnp.where(chosen, total[i : i + 1], energy)
    turn = lax.rem(LANES - lax.rem(first, LANES), LANES)
    energy = pltpu.roll(jnp.broadcast_to(energy, (8, LANES)), turn, 1)
    energy_ref[...] = energy[0:1, 0:width] * (1.0 / copies)


def swap(array, offset):
    count = lax.axis_size("grid")
    return lax.ppermute(array, "grid", [(i, i ^ offset) for i in range(count)])


FIRST = ((8, 0), (4, 0), (2, 0))
SECOND = ((14, 8), (12, 8), (10, 8), (6, 4))


def in_hbm(array):
    return pltpu.with_memory_space_constraint(array, pltpu.HBM)


def spec(space):
    return pl.BlockSpec(memory_space=space)


def params(blocks):
    return pltpu.CompilerParams(vmem_limit_bytes=blocks * 1024 * 1024)


def cost(nominal_us):
    return pl.CostEstimate(
        flops=0, bytes_accessed=int(nominal_us * 3.69e6), transcendentals=0
    )


def f32(*shape):
    return jax.ShapeDtypeStruct(shape, jnp.float32)


def local(density, points, sig_blocks, migration, atom_coords, exponents, shape_coef, func_atom):
    grid_count = lax.axis_size("grid")
    blk_count = lax.axis_size("blk")
    slots, _, point_count = points.shape
    length = sig_blocks.shape[1]
    functions = exponents.shape[0]
    blocks = functions // BLOCK
    dests = grid_count * (slots // 2)
    sizes = [slots // 4 * 3, slots // 4]
    starts = [0, slots // 4 * 3]
    slab = density.T
    tied = lax.optimization_barrier
    lists = sig_blocks.T

    table, dest_mask, points, lists, migration = pl.pallas_call(
        table_kernel,
        out_shape=[
            f32(blocks, 8, BLOCK, LANES),
            f32(slots, dests),
            f32(*points.shape),
            jax.ShapeDtypeStruct(lists.shape, jnp.int32),
            jax.ShapeDtypeStruct(migration.shape, jnp.int32),
        ],
        in_specs=[spec(pltpu.HBM)] * 7,
        out_specs=[spec(VMEM)] * 5,
        scratch_shapes=[
            pltpu.SMEM((slots,), jnp.int32),
            pltpu.VMEM((functions,), jnp.int32),
            pltpu.VMEM((functions,), jnp.float32),
            pltpu.VMEM((3, functions), jnp.float32),
            pltpu.VMEM((3, NATOM), jnp.float32),
            pltpu.SemaphoreType.DMA((8,)),
        ],
        compiler_params=params(blocks),
        cost_estimate=cost(4),
        name="param_table",
    )(
        *[
            in_hbm(a)
            for a in (migration, func_atom, exponents, shape_coef, atom_coords, points, lists)
        ]
    )

    tile_shape = jax.ShapeDtypeStruct((functions, BPD * BLOCK), jnp.bfloat16)

    def basis_chunk(c, points, offsets=()):
        some = 1 if offsets else 0
        zeros = 1 if c == 0 else 0
        return pl.pallas_call(
            functools.partial(phi_kernel, starts[c], offsets),
            out_shape=[
                jax.ShapeDtypeStruct((sizes[c], length * BLOCK, point_count), jnp.bfloat16),
                f32(sizes[c], BLOCK, point_count),
                f32(sizes[c], BLOCK, point_count),
            ]
            + [f32(BPD, 5, BLOCK, LANES)] * zeros
            + [tile_shape] * some,
            in_specs=[spec(SMEM), spec(SMEM)] + [spec(VMEM)] * (2 + len(offsets)),
            out_specs=[spec(VMEM)] * (3 + zeros + some),
            compiler_params=params(blocks),
            cost_estimate=cost(5),
            name="basis_values",
        )(lists, migration, points, table, *[held[e] for e in offsets])

    held = {0: slab}
    late, slabs = [], []
    if grid_count == 16:
        for e, source in FIRST:
            held[e] = swap(held[source], e ^ source)
        held, points = tied((held, points))
        for e, source in SECOND:
            held[e] = swap(held[source], e ^ source)
        ready = [e for e, _ in ((0, 0), *FIRST)]
        *first, acc, tiles = basis_chunk(0, points, ready)
        held, first, tiles, points = tied((held, first, tiles, points))
        everything = list(held)
        pack = pl.pallas_call(
            pack_kernel,
            out_shape=jax.ShapeDtypeStruct((len(everything), *slab.shape), slab.dtype),
            in_specs=[spec(VMEM)] * len(everything),
            out_specs=spec(VMEM),
            compiler_params=params(blocks),
            name="pack",
        )(*[held[e] for e in everything])
        crossed = swap(pack, 1)
        second = basis_chunk(1, points)
        late = [e for e in everything if e not in ready]
        late.append(tuple(e ^ 1 for e in everything))
        slabs = [*[held[e] for e in late[:-1]], crossed]
    else:
        tiles = lax.all_gather(slab, "grid", axis=0, tiled=True)
        *first, acc = basis_chunk(0, points)
        second = basis_chunk(1, points)
    chunks = [first, second]
    phis, radials, bases = zip(*chunks)

    some = 1 if late else 0
    chi, rho, *_ = pl.pallas_call(
        functools.partial(rho_kernel, late, starts),
        out_shape=[f32(slots, BLOCK, point_count), f32(slots, point_count)] + [tile_shape] * some,
        in_specs=[spec(SMEM), spec(SMEM)]
        + [spec(VMEM)] * (len(starts) + len(late) + 1),
        out_specs=[spec(VMEM)] * (2 + some),
        input_output_aliases={2 + len(starts) + len(late): 2} if late else {},
        compiler_params=params(blocks),
        cost_estimate=cost(5),
        name="density_at_points",
    )(lists, migration, *phis, *slabs, tiles)

    if blk_count == 2:
        other = lax.ppermute(rho, "blk", [(0, 1), (1, 0)])
    else:
        other = lax.psum(rho, "blk") - rho

    rows = 3 * NATOM // LANES + dests // LANES
    outgoing, _ = pl.pallas_call(
        functools.partial(force_kernel, starts),
        out_shape=[f32(rows, LANES), f32(BPD, 5, BLOCK, LANES)],
        in_specs=[spec(SMEM), spec(SMEM)] + [spec(VMEM)] * (7 + 2 * len(starts)),
        out_specs=[spec(VMEM)] * 2,
        scratch_shapes=[pltpu.VMEM((slots, point_count), jnp.float32)],
        input_output_aliases={8 + 2 * len(starts): 1},
        compiler_params=params(blocks),
        cost_estimate=cost(5),
        name="forces_and_energies",
    )(lists, migration, points, rho, other, chi, *radials, *bases, table, dest_mask, acc)

    arrived = lax.all_gather(outgoing, ("blk", "grid"), axis=0, tiled=False)

    energy, forces = pl.pallas_call(
        functools.partial(sum_kernel, blk_count),
        out_shape=[f32(1, dests // grid_count), f32(3, NATOM)],
        in_specs=[spec(VMEM)],
        out_specs=[spec(VMEM)] * 2,
        compiler_params=params(blocks),
        name="final_sums",
    )(arrived)
    return (energy.reshape(dests // grid_count), forces)


def solution(mesh):
    in_specs = (
        P("blk", "grid"),
        P("grid", None, None),
        P("grid", None),
        P("grid"),
        P(),
        P(),
        P(),
        P(),
    )
    out_specs = (P("grid"), P())
    return jax.shard_map(local, mesh=mesh, in_specs=in_specs, out_specs=out_specs, check_vma=False)
```

```python
import functools

import jax
import jax.numpy as jnp
from jax import lax
from jax.experimental import pallas as pl
from jax.experimental.pallas import tpu as pltpu
from jax.sharding import PartitionSpec as P

BLOCK = 128
BPD = 6
NATOM = 256
LANES = 128
ROWS = 32
UNROLL = 4

SLATER = 0.7386
RHO_SOFT = 0.05

VMEM = pltpu.MemorySpace.VMEM
SMEM = pltpu.MemorySpace.SMEM


def aligned(start, size):
    return pl.ds(pl.multiple_of(start, size), size)


def live_count(mig_ref):
    slots = mig_ref.shape[0]
    step = 1
    while step * 2 <= slots:
        step *= 2
    count = jnp.int32(0)
    while step:
        more = count + step
        found = mig_ref[jnp.minimum(more, slots) - 1] >= 0
        count = jnp.where(jnp.logical_and(more <= slots, found), more, count)
        step //= 2
    return count


def start_copies(pairs, sems):
    copies = [pltpu.make_async_copy(src, dst, sems.at[i]) for i, (src, dst) in enumerate(pairs)]
    for copy in copies:
        copy.start()
    return copies


def place_slabs(offsets, slabs, tiles):
    me = lax.axis_index("grid")
    depth = slabs[0].shape[-2]

    def place(e, slab):
        tiles[aligned(jnp.bitwise_xor(me, e) * depth, depth), :] = slab

    for e, slab in zip(offsets, slabs):
        if isinstance(e, tuple):
            for i, one in enumerate(e):
                place(one, slab[i])
        else:
            place(e, slab[...])


def pack_kernel(*refs):
    *slabs, out_ref = refs
    for i, slab in enumerate(slabs):
        out_ref[i] = slab[...]


def table_kernel(
    mig_hbm,
    atom_hbm,
    expo_hbm,
    coef_hbm,
    coords_hbm,
    points_hbm,
    lists_hbm,
    slab_hbm,
    table_ref,
    dest_ref,
    points_out,
    lists_out,
    mig_out,
    slab_out,
    mig_ref,
    atom_ref,
    expo_ref,
    coef_ref,
    coords_ref,
    sems,
):
    copies = start_copies(
        [
            (mig_hbm, mig_ref),
            (atom_hbm, atom_ref),
            (expo_hbm, expo_ref),
            (coef_hbm, coef_ref),
            (coords_hbm, coords_ref),
            (points_hbm, points_out),
            (lists_hbm, lists_out),
            (mig_hbm, mig_out),
            (slab_hbm, slab_out),
        ],
        sems,
    )
    for copy in copies[:5]:
        copy.wait()
    coords = coords_ref[...]
    high = coords.astype(jnp.bfloat16)
    rest = coords - high.astype(jnp.float32)
    mid = rest.astype(jnp.bfloat16)
    low = (rest - mid.astype(jnp.float32)).astype(jnp.bfloat16)
    blocks = table_ref.shape[0]
    atoms = atom_ref[...].reshape(blocks, BLOCK)
    expos = expo_ref[...].reshape(blocks, BLOCK)

    for k in range(blocks):
        atom = atoms[k : k + 1]
        onehot = jnp.where(
            lax.broadcasted_iota(jnp.int32, (NATOM, BLOCK), 0) == atom, 1.0, 0.0
        ).astype(jnp.bfloat16)
        picked = [
            jnp.dot(part, onehot, preferred_element_type=jnp.float32) for part in (high, mid, low)
        ]
        center = (picked[0] + picked[1]) + picked[2]
        coef = coef_ref[:, k * BLOCK : (k + 1) * BLOCK]
        rows = jnp.concatenate(
            [center, coef, expos[k : k + 1], atom.astype(jnp.float32)], axis=0
        )
        columns = rows.T
        for p in range(8):
            table_ref[k, p] = jnp.broadcast_to(columns[:, p : p + 1], (BLOCK, LANES))

    dest_ids = lax.broadcasted_iota(jnp.int32, (1, dest_ref.shape[1]), 1)
    for s in range(mig_ref.shape[0]):
        dest_ref[s : s + 1, :] = jnp.where(dest_ids == mig_ref[s], 1.0, 0.0)
    for copy in copies[5:]:
        copy.wait()


def chunk_steps(mig_ref, first, size):
    left = jnp.clip(live_count(mig_ref) - first, 0, size)
    return lax.div(left + (UNROLL - 1), UNROLL)


def phi_kernel(first, offsets, lists_ref, mig_ref, points_ref, table_ref, *refs):
    slabs = refs[: len(offsets)]
    phi_ref, radial_ref, basis_ref, *more = refs[len(offsets) :]
    if first == 0:
        more.pop(0)[...] = jnp.zeros((BPD, 5, BLOCK, LANES), jnp.float32)
    if offsets:
        place_slabs(offsets, slabs, more[0])
    blk = lax.axis_index("blk")
    length = lists_ref.shape[0]
    point_count = points_ref.shape[2]

    def one_slot(s):
        for j in range(length):
            k = lists_ref[lax.rem(blk + j, length), first + s]
            for r in range(0, BLOCK, ROWS):
                sub = slice(r, r + ROWS)
                cx, cy, cz, sx, sy, sz, expo = [table_ref[k, p, sub] for p in range(7)]
                for h in range(0, point_count, LANES):
                    lanes = slice(h, h + LANES)
                    ox = points_ref[first + s, 0:1, lanes] - cx
                    oy = points_ref[first + s, 1:2, lanes] - cy
                    oz = points_ref[first + s, 2:3, lanes] - cz
                    squared = ox * ox + oy * oy + oz * oz
                    radial = jnp.exp(-expo * squared)
                    linear = 1.0 + (sx * ox + sy * oy + sz * oz)
                    basis = linear * radial
                    rows = slice(j * BLOCK + r, j * BLOCK + r + ROWS)
                    phi_ref[s, rows, lanes] = basis.astype(jnp.bfloat16)
                    if j == 0:
                        radial_ref[s, sub, lanes] = radial
                        basis_ref[s, sub, lanes] = basis

    def some_slots(i, carry):
        for u in range(2):
            one_slot(i * 2 + u)
        return carry

    steps = chunk_steps(mig_ref, first, phi_ref.shape[0]) * (UNROLL // 2)
    lax.fori_loop(0, steps, some_slots, 0)


def rho_kernel(offsets, starts, lists_ref, mig_ref, *refs):
    chunks = len(starts)
    phis = refs[:chunks]
    slabs = refs[chunks : chunks + len(offsets)]
    tiles, chi_ref, rho_ref, *placed = refs[chunks + len(offsets) :]
    if offsets:
        tiles = placed[0]
        place_slabs(offsets, slabs, tiles)
    blk = lax.axis_index("blk")
    length = lists_ref.shape[0]
    rho_ref[...] = jnp.zeros_like(rho_ref)

    for c, phi_ref in enumerate(phis):
        size = phi_ref.shape[0]

        def one_slot(s, first=starts[c], phi_ref=phi_ref):
            slot = first + s
            own = lists_ref[blk, slot]
            cols = aligned((own - blk * BPD) * BLOCK, BLOCK)
            left = [tiles[aligned(own * BLOCK, BLOCK), cols]]
            for j in range(1, length):
                k = lists_ref[lax.rem(blk + j, length), slot]
                left.append(tiles[aligned(k * BLOCK, BLOCK), cols].T)
            chi = jnp.dot(
                jnp.concatenate(left, axis=1), phi_ref[s], preferred_element_type=jnp.float32
            )
            phi = phi_ref[s, 0:BLOCK, :]
            chi_ref[slot] = chi
            rho_ref[pl.ds(slot, 1), :] = jnp.sum(
                phi.astype(jnp.float32) * chi, axis=0, keepdims=True
            )

        def some_slots(i, carry, one_slot=one_slot):
            for u in range(UNROLL):
                one_slot(i * UNROLL + u)
            return carry

        lax.fori_loop(0, chunk_steps(mig_ref, starts[c], size), some_slots, 0)


def force_kernel(starts, lists_ref, mig_ref, points_ref, rho_a_ref, rho_b_ref, chi_ref, *refs):
    chunks = len(starts)
    radials = refs[:chunks]
    bases = refs[chunks : 2 * chunks]
    table_ref, dest_ref, _, out_ref, acc, pot_ref = refs[2 * chunks :]
    blk = lax.axis_index("blk")
    slots, _, point_count = points_ref.shape
    dests = dest_ref.shape[1]
    live = live_count(mig_ref)
    rho = rho_a_ref[...] + rho_b_ref[...]
    weight = points_ref[:, 3, :]
    log_sq = jnp.log(rho * rho + RHO_SOFT * RHO_SOFT)
    pot = weight * (-(4.0 / 3.0) * SLATER) * rho * jnp.exp(log_sq * (-1.0 / 3.0))
    slot_ids = lax.broadcasted_iota(jnp.int32, (slots, 1), 0)
    pot_ref[...] = jnp.where(slot_ids < live, pot, 0.0)
    energies = jnp.sum(weight * -SLATER * jnp.exp(log_sq * (2.0 / 3.0)), axis=1, keepdims=True)

    for c in range(chunks):
        radial_ref, basis_ref = radials[c], bases[c]
        size = radial_ref.shape[0]

        def one_slot(s, first=starts[c], radial_ref=radial_ref, basis_ref=basis_ref):
            slot = first + s
            own = lists_ref[blk, slot] - blk * BPD
            pots = pot_ref[pl.ds(slot, 1), :]
            for r in range(0, BLOCK, ROWS):
                sub = slice(r, r + ROWS)
                sums = None
                for h in range(0, point_count, LANES):
                    lanes = slice(h, h + LANES)
                    u = chi_ref[slot, sub, lanes] * pots[:, lanes]
                    ub = u * basis_ref[s, sub, lanes]
                    terms = (
                        u * radial_ref[s, sub, lanes],
                        ub,
                        ub * points_ref[slot, 0:1, lanes],
                        ub * points_ref[slot, 1:2, lanes],
                        ub * points_ref[slot, 2:3, lanes],
                    )
                    sums = terms if sums is None else [a + b for a, b in zip(sums, terms)]
                for q in range(5):
                    acc[own, q, sub] += sums[q]

        def some_slots(i, carry, one_slot=one_slot):
            for u in range(UNROLL):
                one_slot(i * UNROLL + u)
            return carry

        lax.fori_loop(0, chunk_steps(mig_ref, starts[c], size), some_slots, 0)

    lane_ids = lax.broadcasted_iota(jnp.int32, (1, LANES), 1).astype(jnp.float32)

    totals = [jnp.zeros((8, LANES), jnp.float32)] * (3 * NATOM // LANES)
    for b in range(BPD):
        k = blk * BPD + b
        for r in range(0, BLOCK, ROWS):
            sub = slice(r, r + ROWS)
            parts = [acc[b, q, sub] for q in range(5)]
            doubled = 2.0 * table_ref[k, 6, sub]
            atom = table_ref[k, 7, sub]
            for c in range(3):
                force = table_ref[k, 3 + c, sub] * parts[0] - doubled * (
                    parts[2 + c] - table_ref[k, c, sub] * parts[1]
                )
                column = 2.0 * jnp.sum(force, axis=1, keepdims=True)
                for h in range(NATOM // LANES):
                    hit = jnp.where(atom == lane_ids + float(h * LANES), column, 0.0)
                    i = c * (NATOM // LANES) + h
                    totals[i] = totals[i] + sum(hit[i8 : i8 + 8] for i8 in range(0, ROWS, 8))
    rows = [jnp.sum(t, axis=0, keepdims=True) for t in totals]
    moved = jnp.sum(dest_ref[...] * energies, axis=0, keepdims=True)
    rows += [moved[:, h : h + LANES] for h in range(0, dests, LANES)]
    packed = jnp.concatenate(rows, axis=0)
    for i in range(out_ref.shape[0]):
        out_ref[i] = packed


def sum_kernel(copies, arrived_ref, energy_ref, forces_ref):
    me = lax.axis_index("grid")
    total = jnp.sum(arrived_ref[...], axis=0)
    per = NATOM // LANES
    for c in range(3):
        for h in range(per):
            forces_ref[c : c + 1, h * LANES : (h + 1) * LANES] = total[c * per + h : c * per + h + 1]
    width = energy_ref.shape[1]
    first = me * width
    energy = jnp.zeros((1, LANES), jnp.float32)
    for i in range(3 * per, total.shape[0]):
        chosen = lax.div(first, LANES) == i - 3 * per
        energy = jnp.where(chosen, total[i : i + 1], energy)
    turn = lax.rem(LANES - lax.rem(first, LANES), LANES)
    energy = pltpu.roll(jnp.broadcast_to(energy, (8, LANES)), turn, 1)
    energy_ref[...] = energy[0:1, 0:width] * (1.0 / copies)


def swap(array, offset):
    count = lax.axis_size("grid")
    return lax.ppermute(array, "grid", [(i, i ^ offset) for i in range(count)])


FIRST = ((8, 0), (4, 0), (2, 0))
SECOND = ((14, 8), (12, 8), (10, 8), (6, 4))


def in_hbm(array):
    return pltpu.with_memory_space_constraint(array, pltpu.HBM)


def spec(space):
    return pl.BlockSpec(memory_space=space)


def params(blocks):
    return pltpu.CompilerParams(vmem_limit_bytes=blocks * 1024 * 1024)


def cost(nominal_us):
    return pl.CostEstimate(
        flops=0, bytes_accessed=int(nominal_us * 3.69e6), transcendentals=0
    )


def f32(*shape):
    return jax.ShapeDtypeStruct(shape, jnp.float32)


def local(density, points, sig_blocks, migration, atom_coords, exponents, shape_coef, func_atom):
    grid_count = lax.axis_size("grid")
    blk_count = lax.axis_size("blk")
    slots, _, point_count = points.shape
    length = sig_blocks.shape[1]
    functions = exponents.shape[0]
    blocks = functions // BLOCK
    dests = grid_count * (slots // 2)
    sizes = [slots // 4 * 3, slots // 4]
    starts = [0, slots // 4 * 3]
    slab = density.T
    tied = lax.optimization_barrier
    lists = sig_blocks.T

    table, dest_mask, points, lists, migration, near_slab = pl.pallas_call(
        table_kernel,
        out_shape=[
            f32(blocks, 8, BLOCK, LANES),
            f32(slots, dests),
            f32(*points.shape),
            jax.ShapeDtypeStruct(lists.shape, jnp.int32),
            jax.ShapeDtypeStruct(migration.shape, jnp.int32),
            jax.ShapeDtypeStruct(slab.shape, slab.dtype),
        ],
        in_specs=[spec(pltpu.HBM)] * 8,
        out_specs=[spec(VMEM)] * 6,
        scratch_shapes=[
            pltpu.SMEM((slots,), jnp.int32),
            pltpu.VMEM((functions,), jnp.int32),
            pltpu.VMEM((functions,), jnp.float32),
            pltpu.VMEM((3, functions), jnp.float32),
            pltpu.VMEM((3, NATOM), jnp.float32),
            pltpu.SemaphoreType.DMA((9,)),
        ],
        compiler_params=params(blocks),
        cost_estimate=cost(4),
        name="param_table",
    )(
        *[
            in_hbm(a)
            for a in (
                migration,
                func_atom,
                exponents,
                shape_coef,
                atom_coords,
                points,
                lists,
                slab,
            )
        ]
    )

    tile_shape = jax.ShapeDtypeStruct((functions, BPD * BLOCK), jnp.bfloat16)

    def basis_chunk(c, points, offsets=()):
        some = 1 if offsets else 0
        zeros = 1 if c == 0 else 0
        return pl.pallas_call(
            functools.partial(phi_kernel, starts[c], offsets),
            out_shape=[
                jax.ShapeDtypeStruct((sizes[c], length * BLOCK, point_count), jnp.bfloat16),
                f32(sizes[c], BLOCK, point_count),
                f32(sizes[c], BLOCK, point_count),
            ]
            + [f32(BPD, 5, BLOCK, LANES)] * zeros
            + [tile_shape] * some,
            in_specs=[spec(SMEM), spec(SMEM)] + [spec(VMEM)] * (2 + len(offsets)),
            out_specs=[spec(VMEM)] * (3 + zeros + some),
            compiler_params=params(blocks),
            cost_estimate=cost(5),
            name="basis_values",
        )(lists, migration, points, table, *[held[e] for e in offsets])

    held = {0: slab}
    late, slabs = [], []
    if grid_count == 16:
        for e, source in FIRST:
            held[e] = swap(held[source], e ^ source)
        held[0] = near_slab
        held, points = tied((held, points))
        for e, source in SECOND:
            held[e] = swap(held[source], e ^ source)
        ready = [e for e, _ in ((0, 0), *FIRST)]
        *first, acc, tiles = basis_chunk(0, points, ready)
        held, first, tiles, points = tied((held, first, tiles, points))
        everything = list(held)
        pack = pl.pallas_call(
            pack_kernel,
            out_shape=jax.ShapeDtypeStruct((len(everything), *slab.shape), slab.dtype),
            in_specs=[spec(VMEM)] * len(everything),
            out_specs=spec(VMEM),
            compiler_params=params(blocks),
            name="pack",
        )(*[held[e] for e in everything])
        crossed = swap(pack, 1)
        second = basis_chunk(1, points)
        late = [e for e in everything if e not in ready]
        late.append(tuple(e ^ 1 for e in everything))
        slabs = [*[held[e] for e in late[:-1]], crossed]
    else:
        tiles = lax.all_gather(slab, "grid", axis=0, tiled=True)
        *first, acc = basis_chunk(0, points)
        second = basis_chunk(1, points)
    chunks = [first, second]
    phis, radials, bases = zip(*chunks)

    some = 1 if late else 0
    chi, rho, *_ = pl.pallas_call(
        functools.partial(rho_kernel, late, starts),
        out_shape=[f32(slots, BLOCK, point_count), f32(slots, point_count)] + [tile_shape] * some,
        in_specs=[spec(SMEM), spec(SMEM)]
        + [spec(VMEM)] * (len(starts) + len(late) + 1),
        out_specs=[spec(VMEM)] * (2 + some),
        input_output_aliases={2 + len(starts) + len(late): 2} if late else {},
        compiler_params=params(blocks),
        cost_estimate=cost(5),
        name="density_at_points",
    )(lists, migration, *phis, *slabs, tiles)

    if blk_count == 2:
        other = lax.ppermute(rho, "blk", [(0, 1), (1, 0)])
    else:
        other = lax.psum(rho, "blk") - rho

    rows = 3 * NATOM // LANES + dests // LANES
    outgoing, _ = pl.pallas_call(
        functools.partial(force_kernel, starts),
        out_shape=[f32(blk_count * grid_count, rows, LANES), f32(BPD, 5, BLOCK, LANES)],
        in_specs=[spec(SMEM), spec(SMEM)] + [spec(VMEM)] * (7 + 2 * len(starts)),
        out_specs=[spec(VMEM)] * 2,
        scratch_shapes=[pltpu.VMEM((slots, point_count), jnp.float32)],
        input_output_aliases={8 + 2 * len(starts): 1},
        compiler_params=params(blocks),
        cost_estimate=cost(5),
        name="forces_and_energies",
    )(lists, migration, points, rho, other, chi, *radials, *bases, table, dest_mask, acc)

    arrived = lax.all_to_all(outgoing, ("grid", "blk"), split_axis=0, concat_axis=0, tiled=True)

    energy, forces = pl.pallas_call(
        functools.partial(sum_kernel, blk_count),
        out_shape=[f32(1, dests // grid_count), f32(3, NATOM)],
        in_specs=[spec(VMEM)],
        out_specs=[spec(VMEM)] * 2,
        compiler_params=params(blocks),
        name="final_sums",
    )(arrived)
    return (energy.reshape(dests // grid_count), forces)


def solution(mesh):
    in_specs = (
        P("blk", "grid"),
        P("grid", None, None),
        P("grid", None),
        P("grid"),
        P(),
        P(),
        P(),
        P(),
    )
    out_specs = (P("grid"), P())
    return jax.shard_map(local, mesh=mesh, in_specs=in_specs, out_specs=out_specs, check_vma=False)
```

```python
import functools

import jax
import jax.numpy as jnp
from jax import lax
from jax.experimental import pallas as pl
from jax.experimental.pallas import tpu as pltpu
from jax.sharding import PartitionSpec as P

BLOCK = 128
BPD = 6
NATOM = 256
LANES = 128
ROWS = 32
UNROLL = 4

SLATER = 0.7386
RHO_SOFT = 0.05

VMEM = pltpu.MemorySpace.VMEM
SMEM = pltpu.MemorySpace.SMEM


def aligned(start, size):
    return pl.ds(pl.multiple_of(start, size), size)


def live_count(mig_ref):
    slots = mig_ref.shape[0]
    step = 1
    while step * 2 <= slots:
        step *= 2
    count = jnp.int32(0)
    while step:
        more = count + step
        found = mig_ref[jnp.minimum(more, slots) - 1] >= 0
        count = jnp.where(jnp.logical_and(more <= slots, found), more, count)
        step //= 2
    return count


def start_copies(pairs, sems):
    copies = [pltpu.make_async_copy(src, dst, sems.at[i]) for i, (src, dst) in enumerate(pairs)]
    for copy in copies:
        copy.start()
    return copies


def place_slabs(offsets, slabs, tiles):
    me = lax.axis_index("grid")
    depth = slabs[0].shape[-2]

    def place(e, slab):
        tiles[aligned(jnp.bitwise_xor(me, e) * depth, depth), :] = slab

    for e, slab in zip(offsets, slabs):
        if isinstance(e, tuple):
            for i, one in enumerate(e):
                place(one, slab[i])
        else:
            place(e, slab[...])


def pack_kernel(*refs):
    *slabs, out_ref = refs
    i = 0
    for slab in slabs:
        many = slab.shape[0] if len(slab.shape) == 3 else 1
        out_ref[pl.ds(i, many)] = slab[...].reshape(many, *out_ref.shape[1:])
        i += many


def table_kernel(
    mig_hbm,
    atom_hbm,
    expo_hbm,
    coef_hbm,
    coords_hbm,
    points_hbm,
    lists_hbm,
    slab_hbm,
    table_ref,
    dest_ref,
    points_out,
    lists_out,
    mig_out,
    slab_out,
    mig_ref,
    atom_ref,
    expo_ref,
    coef_ref,
    coords_ref,
    sems,
):
    copies = start_copies(
        [
            (mig_hbm, mig_ref),
            (atom_hbm, atom_ref),
            (expo_hbm, expo_ref),
            (coef_hbm, coef_ref),
            (coords_hbm, coords_ref),
            (points_hbm, points_out),
            (lists_hbm, lists_out),
            (mig_hbm, mig_out),
            (slab_hbm, slab_out),
        ],
        sems,
    )
    for copy in copies[:5]:
        copy.wait()
    coords = coords_ref[...]
    high = coords.astype(jnp.bfloat16)
    rest = coords - high.astype(jnp.float32)
    mid = rest.astype(jnp.bfloat16)
    low = (rest - mid.astype(jnp.float32)).astype(jnp.bfloat16)
    blocks = table_ref.shape[0]
    atoms = atom_ref[...].reshape(blocks, BLOCK)
    expos = expo_ref[...].reshape(blocks, BLOCK)

    for k in range(blocks):
        atom = atoms[k : k + 1]
        onehot = jnp.where(
            lax.broadcasted_iota(jnp.int32, (NATOM, BLOCK), 0) == atom, 1.0, 0.0
        ).astype(jnp.bfloat16)
        picked = [
            jnp.dot(part, onehot, preferred_element_type=jnp.float32) for part in (high, mid, low)
        ]
        center = (picked[0] + picked[1]) + picked[2]
        coef = coef_ref[:, k * BLOCK : (k + 1) * BLOCK]
        rows = jnp.concatenate(
            [center, coef, expos[k : k + 1], atom.astype(jnp.float32)], axis=0
        )
        columns = rows.T
        for p in range(8):
            table_ref[k, p] = jnp.broadcast_to(columns[:, p : p + 1], (BLOCK, LANES))

    dest_ids = lax.broadcasted_iota(jnp.int32, (1, dest_ref.shape[1]), 1)
    for s in range(mig_ref.shape[0]):
        dest_ref[s : s + 1, :] = jnp.where(dest_ids == mig_ref[s], 1.0, 0.0)
    for copy in copies[5:]:
        copy.wait()


def chunk_steps(mig_ref, first, size):
    left = jnp.clip(live_count(mig_ref) - first, 0, size)
    return lax.div(left + (UNROLL - 1), UNROLL)


def phi_kernel(first, offsets, lists_ref, mig_ref, points_ref, table_ref, *refs):
    slabs = refs[: len(offsets)]
    phi_ref, radial_ref, basis_ref, *more = refs[len(offsets) :]
    if first == 0:
        more.pop(0)[...] = jnp.zeros((BPD, 5, BLOCK, LANES), jnp.float32)
    if offsets:
        place_slabs(offsets, slabs, more[0])
    blk = lax.axis_index("blk")
    length = lists_ref.shape[0]
    point_count = points_ref.shape[2]

    def one_slot(s):
        for j in range(length):
            k = lists_ref[lax.rem(blk + j, length), first + s]
            for r in range(0, BLOCK, ROWS):
                sub = slice(r, r + ROWS)
                cx, cy, cz, sx, sy, sz, expo = [table_ref[k, p, sub] for p in range(7)]
                for h in range(0, point_count, LANES):
                    lanes = slice(h, h + LANES)
                    ox = points_ref[first + s, 0:1, lanes] - cx
                    oy = points_ref[first + s, 1:2, lanes] - cy
                    oz = points_ref[first + s, 2:3, lanes] - cz
                    squared = ox * ox + oy * oy + oz * oz
                    radial = jnp.exp(-expo * squared)
                    linear = 1.0 + (sx * ox + sy * oy + sz * oz)
                    basis = linear * radial
                    rows = slice(j * BLOCK + r, j * BLOCK + r + ROWS)
                    phi_ref[s, rows, lanes] = basis.astype(jnp.bfloat16)
                    if j == 0:
                        radial_ref[s, sub, lanes] = radial
                        basis_ref[s, sub, lanes] = basis

    def some_slots(i, carry):
        for u in range(2):
            one_slot(i * 2 + u)
        return carry

    steps = chunk_steps(mig_ref, first, phi_ref.shape[0]) * (UNROLL // 2)
    lax.fori_loop(0, steps, some_slots, 0)


def rho_kernel(offsets, starts, lists_ref, mig_ref, *refs):
    chunks = len(starts)
    phis = refs[:chunks]
    slabs = refs[chunks : chunks + len(offsets)]
    tiles, chi_ref, rho_ref, *placed = refs[chunks + len(offsets) :]
    if offsets:
        tiles = placed[0]
        place_slabs(offsets, slabs, tiles)
    blk = lax.axis_index("blk")
    length = lists_ref.shape[0]
    rho_ref[...] = jnp.zeros_like(rho_ref)

    for c, phi_ref in enumerate(phis):
        size = phi_ref.shape[0]

        def one_slot(s, first=starts[c], phi_ref=phi_ref):
            slot = first + s
            own = lists_ref[blk, slot]
            cols = aligned((own - blk * BPD) * BLOCK, BLOCK)
            left = [tiles[aligned(own * BLOCK, BLOCK), cols]]
            for j in range(1, length):
                k = lists_ref[lax.rem(blk + j, length), slot]
                left.append(tiles[aligned(k * BLOCK, BLOCK), cols].T)
            chi = jnp.dot(
                jnp.concatenate(left, axis=1), phi_ref[s], preferred_element_type=jnp.float32
            )
            phi = phi_ref[s, 0:BLOCK, :]
            chi_ref[slot] = chi
            rho_ref[pl.ds(slot, 1), :] = jnp.sum(
                phi.astype(jnp.float32) * chi, axis=0, keepdims=True
            )

        def some_slots(i, carry, one_slot=one_slot):
            for u in range(UNROLL):
                one_slot(i * UNROLL + u)
            return carry

        lax.fori_loop(0, chunk_steps(mig_ref, starts[c], size), some_slots, 0)


def force_kernel(starts, lists_ref, mig_ref, points_ref, rho_a_ref, rho_b_ref, chi_ref, *refs):
    chunks = len(starts)
    radials = refs[:chunks]
    bases = refs[chunks : 2 * chunks]
    table_ref, dest_ref, _, out_ref, acc, pot_ref = refs[2 * chunks :]
    blk = lax.axis_index("blk")
    slots, _, point_count = points_ref.shape
    dests = dest_ref.shape[1]
    live = live_count(mig_ref)
    rho = rho_a_ref[...] + rho_b_ref[...]
    weight = points_ref[:, 3, :]
    log_sq = jnp.log(rho * rho + RHO_SOFT * RHO_SOFT)
    pot = weight * (-(4.0 / 3.0) * SLATER) * rho * jnp.exp(log_sq * (-1.0 / 3.0))
    slot_ids = lax.broadcasted_iota(jnp.int32, (slots, 1), 0)
    pot_ref[...] = jnp.where(slot_ids < live, pot, 0.0)
    energies = jnp.sum(weight * -SLATER * jnp.exp(log_sq * (2.0 / 3.0)), axis=1, keepdims=True)

    for c in range(chunks):
        radial_ref, basis_ref = radials[c], bases[c]
        size = radial_ref.shape[0]

        def one_slot(s, first=starts[c], radial_ref=radial_ref, basis_ref=basis_ref):
            slot = first + s
            own = lists_ref[blk, slot] - blk * BPD
            pots = pot_ref[pl.ds(slot, 1), :]
            for r in range(0, BLOCK, ROWS):
                sub = slice(r, r + ROWS)
                sums = None
                for h in range(0, point_count, LANES):
                    lanes = slice(h, h + LANES)
                    u = chi_ref[slot, sub, lanes] * pots[:, lanes]
                    ub = u * basis_ref[s, sub, lanes]
                    terms = (
                        u * radial_ref[s, sub, lanes],
                        ub,
                        ub * points_ref[slot, 0:1, lanes],
                        ub * points_ref[slot, 1:2, lanes],
                        ub * points_ref[slot, 2:3, lanes],
                    )
                    sums = terms if sums is None else [a + b for a, b in zip(sums, terms)]
                for q in range(5):
                    acc[own, q, sub] += sums[q]

        def some_slots(i, carry, one_slot=one_slot):
            for u in range(UNROLL):
                one_slot(i * UNROLL + u)
            return carry

        lax.fori_loop(0, chunk_steps(mig_ref, starts[c], size), some_slots, 0)

    lane_ids = lax.broadcasted_iota(jnp.int32, (1, LANES), 1).astype(jnp.float32)

    totals = [jnp.zeros((8, LANES), jnp.float32)] * (3 * NATOM // LANES)
    for b in range(BPD):
        k = blk * BPD + b
        for r in range(0, BLOCK, ROWS):
            sub = slice(r, r + ROWS)
            parts = [acc[b, q, sub] for q in range(5)]
            doubled = 2.0 * table_ref[k, 6, sub]
            atom = table_ref[k, 7, sub]
            for c in range(3):
                force = table_ref[k, 3 + c, sub] * parts[0] - doubled * (
                    parts[2 + c] - table_ref[k, c, sub] * parts[1]
                )
                column = 2.0 * jnp.sum(force, axis=1, keepdims=True)
                for h in range(NATOM // LANES):
                    hit = jnp.where(atom == lane_ids + float(h * LANES), column, 0.0)
                    i = c * (NATOM // LANES) + h
                    totals[i] = totals[i] + sum(hit[i8 : i8 + 8] for i8 in range(0, ROWS, 8))
    rows = [jnp.sum(t, axis=0, keepdims=True) for t in totals]
    moved = jnp.sum(dest_ref[...] * energies, axis=0, keepdims=True)
    rows += [moved[:, h : h + LANES] for h in range(0, dests, LANES)]
    packed = jnp.concatenate(rows, axis=0)
    for i in range(out_ref.shape[0]):
        out_ref[i] = packed


def sum_kernel(copies, arrived_ref, energy_ref, forces_ref):
    me = lax.axis_index("grid")
    total = jnp.sum(arrived_ref[...], axis=0)
    per = NATOM // LANES
    for c in range(3):
        for h in range(per):
            forces_ref[c : c + 1, h * LANES : (h + 1) * LANES] = total[c * per + h : c * per + h + 1]
    width = energy_ref.shape[1]
    first = me * width
    energy = jnp.zeros((1, LANES), jnp.float32)
    for i in range(3 * per, total.shape[0]):
        chosen = lax.div(first, LANES) == i - 3 * per
        energy = jnp.where(chosen, total[i : i + 1], energy)
    turn = lax.rem(LANES - lax.rem(first, LANES), LANES)
    energy = pltpu.roll(jnp.broadcast_to(energy, (8, LANES)), turn, 1)
    energy_ref[...] = energy[0:1, 0:width] * (1.0 / copies)


def swap(array, offset):
    count = lax.axis_size("grid")
    return lax.ppermute(array, "grid", [(i, i ^ offset) for i in range(count)])


FIRST = ((8, 0), (4, 0), (2, 0))
SECOND = ((14, 8), (12, 8))
PAIR = (10, 6)


def in_hbm(array):
    return pltpu.with_memory_space_constraint(array, pltpu.HBM)


def spec(space):
    return pl.BlockSpec(memory_space=space)


def params(blocks):
    return pltpu.CompilerParams(vmem_limit_bytes=blocks * 1024 * 1024)


def cost(nominal_us):
    return pl.CostEstimate(
        flops=0, bytes_accessed=int(nominal_us * 3.69e6), transcendentals=0
    )


def f32(*shape):
    return jax.ShapeDtypeStruct(shape, jnp.float32)


def local(density, points, sig_blocks, migration, atom_coords, exponents, shape_coef, func_atom):
    grid_count = lax.axis_size("grid")
    blk_count = lax.axis_size("blk")
    slots, _, point_count = points.shape
    length = sig_blocks.shape[1]
    functions = exponents.shape[0]
    blocks = functions // BLOCK
    dests = grid_count * (slots // 2)
    sizes = [slots // 4 * 3, slots // 4]
    starts = [0, slots // 4 * 3]
    slab = density.T
    tied = lax.optimization_barrier
    lists = sig_blocks.T

    table, dest_mask, points, lists, migration, near_slab = pl.pallas_call(
        table_kernel,
        out_shape=[
            f32(blocks, 8, BLOCK, LANES),
            f32(slots, dests),
            f32(*points.shape),
            jax.ShapeDtypeStruct(lists.shape, jnp.int32),
            jax.ShapeDtypeStruct(migration.shape, jnp.int32),
            jax.ShapeDtypeStruct(slab.shape, slab.dtype),
        ],
        in_specs=[spec(pltpu.HBM)] * 8,
        out_specs=[spec(VMEM)] * 6,
        scratch_shapes=[
            pltpu.SMEM((slots,), jnp.int32),
            pltpu.VMEM((functions,), jnp.int32),
            pltpu.VMEM((functions,), jnp.float32),
            pltpu.VMEM((3, functions), jnp.float32),
            pltpu.VMEM((3, NATOM), jnp.float32),
            pltpu.SemaphoreType.DMA((9,)),
        ],
        compiler_params=params(blocks),
        cost_estimate=cost(4),
        name="param_table",
    )(
        *[
            in_hbm(a)
            for a in (
                migration,
                func_atom,
                exponents,
                shape_coef,
                atom_coords,
                points,
                lists,
                slab,
            )
        ]
    )

    tile_shape = jax.ShapeDtypeStruct((functions, BPD * BLOCK), jnp.bfloat16)

    def basis_chunk(c, points, offsets=()):
        some = 1 if offsets else 0
        zeros = 1 if c == 0 else 0
        return pl.pallas_call(
            functools.partial(phi_kernel, starts[c], offsets),
            out_shape=[
                jax.ShapeDtypeStruct((sizes[c], length * BLOCK, point_count), jnp.bfloat16),
                f32(sizes[c], BLOCK, point_count),
                f32(sizes[c], BLOCK, point_count),
            ]
            + [f32(BPD, 5, BLOCK, LANES)] * zeros
            + [tile_shape] * some,
            in_specs=[spec(SMEM), spec(SMEM)] + [spec(VMEM)] * (2 + len(offsets)),
            out_specs=[spec(VMEM)] * (3 + zeros + some),
            compiler_params=params(blocks),
            cost_estimate=cost(5),
            name="basis_values",
        )(lists, migration, points, table, *[held[e] for e in offsets])

    def pack(*parts):
        many = sum(part.size for part in parts) // slab.size
        return pl.pallas_call(
            pack_kernel,
            out_shape=jax.ShapeDtypeStruct((many, *slab.shape), slab.dtype),
            in_specs=[spec(VMEM)] * len(parts),
            out_specs=spec(VMEM),
            compiler_params=params(blocks),
            name="pack",
        )(*parts)

    held = {0: slab}
    late, slabs = [], []
    if grid_count == 16:
        for e, source in FIRST:
            held[e] = swap(held[source], e ^ source)
        held[0] = near_slab
        held, points = tied((held, points))
        pair = swap(pack(held[8], held[4]), 2)
        for e, source in SECOND:
            held[e] = swap(held[source], e ^ source)
        ready = [e for e, _ in ((0, 0), *FIRST)]
        *first, acc, tiles = basis_chunk(0, points, ready)
        held, pair, first, tiles, points = tied((held, pair, first, tiles, points))
        crossed = swap(pack(*held.values(), pair), 1)
        second = basis_chunk(1, points)
        rest = [e for e, _ in SECOND]
        late = [*rest, PAIR, tuple(e ^ 1 for e in (*held, *PAIR))]
        slabs = [*[held[e] for e in rest], pair, crossed]
    else:
        tiles = lax.all_gather(slab, "grid", axis=0, tiled=True)
        *first, acc = basis_chunk(0, points)
        second = basis_chunk(1, points)
    chunks = [first, second]
    phis, radials, bases = zip(*chunks)

    some = 1 if late else 0
    chi, rho, *_ = pl.pallas_call(
        functools.partial(rho_kernel, late, starts),
        out_shape=[f32(slots, BLOCK, point_count), f32(slots, point_count)] + [tile_shape] * some,
        in_specs=[spec(SMEM), spec(SMEM)]
        + [spec(VMEM)] * (len(starts) + len(late) + 1),
        out_specs=[spec(VMEM)] * (2 + some),
        input_output_aliases={2 + len(starts) + len(late): 2} if late else {},
        compiler_params=params(blocks),
        cost_estimate=cost(5),
        name="density_at_points",
    )(lists, migration, *phis, *slabs, tiles)

    if blk_count == 2:
        other = lax.ppermute(rho, "blk", [(0, 1), (1, 0)])
    else:
        other = lax.psum(rho, "blk") - rho

    rows = 3 * NATOM // LANES + dests // LANES
    outgoing, _ = pl.pallas_call(
        functools.partial(force_kernel, starts),
        out_shape=[f32(blk_count * grid_count, rows, LANES), f32(BPD, 5, BLOCK, LANES)],
        in_specs=[spec(SMEM), spec(SMEM)] + [spec(VMEM)] * (7 + 2 * len(starts)),
        out_specs=[spec(VMEM)] * 2,
        scratch_shapes=[pltpu.VMEM((slots, point_count), jnp.float32)],
        input_output_aliases={8 + 2 * len(starts): 1},
        compiler_params=params(blocks),
        cost_estimate=cost(5),
        name="forces_and_energies",
    )(lists, migration, points, rho, other, chi, *radials, *bases, table, dest_mask, acc)

    arrived = lax.all_to_all(outgoing, ("blk", "grid"), split_axis=0, concat_axis=0, tiled=True)

    energy, forces = pl.pallas_call(
        functools.partial(sum_kernel, blk_count),
        out_shape=[f32(1, dests // grid_count), f32(3, NATOM)],
        in_specs=[spec(VMEM)],
        out_specs=[spec(VMEM)] * 2,
        compiler_params=params(blocks),
        name="final_sums",
    )(arrived)
    return (energy.reshape(dests // grid_count), forces)


def solution(mesh):
    in_specs = (
        P("blk", "grid"),
        P("grid", None, None),
        P("grid", None),
        P("grid"),
        P(),
        P(),
        P(),
        P(),
    )
    out_specs = (P("grid"), P())
    return jax.shard_map(local, mesh=mesh, in_specs=in_specs, out_specs=out_specs, check_vma=False)
```

```python
import functools

import jax
import jax.numpy as jnp
from jax import lax
from jax.experimental import pallas as pl
from jax.experimental.pallas import tpu as pltpu
from jax.sharding import PartitionSpec as P

BLOCK = 128
BPD = 6
NATOM = 256
LANES = 128
ROWS = 32
UNROLL = 4

SLATER = 0.7386
RHO_SOFT = 0.05

VMEM = pltpu.MemorySpace.VMEM
SMEM = pltpu.MemorySpace.SMEM


def aligned(start, size):
    return pl.ds(pl.multiple_of(start, size), size)


def live_count(mig_ref):
    slots = mig_ref.shape[0]
    step = 1
    while step * 2 <= slots:
        step *= 2
    count = jnp.int32(0)
    while step:
        more = count + step
        found = mig_ref[jnp.minimum(more, slots) - 1] >= 0
        count = jnp.where(jnp.logical_and(more <= slots, found), more, count)
        step //= 2
    return count


def start_copies(pairs, sems):
    copies = [pltpu.make_async_copy(src, dst, sems.at[i]) for i, (src, dst) in enumerate(pairs)]
    for copy in copies:
        copy.start()
    return copies


def place_slabs(offsets, slabs, tiles):
    me = lax.axis_index("grid")
    for e, slab in zip(offsets, slabs):
        if isinstance(e, tuple):
            half = slab.shape[1]
            for i, (one, h) in enumerate(e):
                first = (2 * jnp.bitwise_xor(me, one) + h) * half
                tiles[aligned(first, half), :] = slab[i]
        else:
            depth = slab.shape[0]
            tiles[aligned(jnp.bitwise_xor(me, e) * depth, depth), :] = slab[...]


def pack_kernel(picks, *refs):
    *parts, out_ref = refs
    half = out_ref.shape[1]
    for i, (p, h) in enumerate(picks):
        part = parts[p]
        out_ref[i] = part[h] if len(part.shape) == 3 else part[h * half : (h + 1) * half, :]


def table_kernel(
    mig_hbm,
    atom_hbm,
    expo_hbm,
    coef_hbm,
    coords_hbm,
    points_hbm,
    lists_hbm,
    slab_hbm,
    table_ref,
    dest_ref,
    points_out,
    lists_out,
    mig_out,
    slab_out,
    mig_ref,
    atom_ref,
    expo_ref,
    coef_ref,
    coords_ref,
    sems,
):
    copies = start_copies(
        [
            (mig_hbm, mig_ref),
            (atom_hbm, atom_ref),
            (expo_hbm, expo_ref),
            (coef_hbm, coef_ref),
            (coords_hbm, coords_ref),
            (points_hbm, points_out),
            (lists_hbm, lists_out),
            (mig_hbm, mig_out),
            (slab_hbm, slab_out),
        ],
        sems,
    )
    for copy in copies[:5]:
        copy.wait()
    coords = coords_ref[...]
    high = coords.astype(jnp.bfloat16)
    rest = coords - high.astype(jnp.float32)
    mid = rest.astype(jnp.bfloat16)
    low = (rest - mid.astype(jnp.float32)).astype(jnp.bfloat16)
    blocks = table_ref.shape[0]
    atoms = atom_ref[...].reshape(blocks, BLOCK)
    expos = expo_ref[...].reshape(blocks, BLOCK)

    for k in range(blocks):
        atom = atoms[k : k + 1]
        onehot = jnp.where(
            lax.broadcasted_iota(jnp.int32, (NATOM, BLOCK), 0) == atom, 1.0, 0.0
        ).astype(jnp.bfloat16)
        picked = [
            jnp.dot(part, onehot, preferred_element_type=jnp.float32) for part in (high, mid, low)
        ]
        center = (picked[0] + picked[1]) + picked[2]
        coef = coef_ref[:, k * BLOCK : (k + 1) * BLOCK]
        rows = jnp.concatenate(
            [center, coef, expos[k : k + 1], atom.astype(jnp.float32)], axis=0
        )
        columns = rows.T
        for p in range(8):
            table_ref[k, p] = jnp.broadcast_to(columns[:, p : p + 1], (BLOCK, LANES))

    dest_ids = lax.broadcasted_iota(jnp.int32, (1, dest_ref.shape[1]), 1)
    for s in range(mig_ref.shape[0]):
        dest_ref[s : s + 1, :] = jnp.where(dest_ids == mig_ref[s], 1.0, 0.0)
    for copy in copies[5:]:
        copy.wait()


def chunk_steps(mig_ref, first, size):
    left = jnp.clip(live_count(mig_ref) - first, 0, size)
    return lax.div(left + (UNROLL - 1), UNROLL)


def phi_kernel(first, offsets, lists_ref, mig_ref, points_ref, table_ref, *refs):
    slabs = refs[: len(offsets)]
    phi_ref, radial_ref, basis_ref, *more = refs[len(offsets) :]
    if first == 0:
        more.pop(0)[...] = jnp.zeros((BPD, 5, BLOCK, LANES), jnp.float32)
    if offsets:
        place_slabs(offsets, slabs, more[0])
    blk = lax.axis_index("blk")
    length = lists_ref.shape[0]
    point_count = points_ref.shape[2]

    def one_slot(s):
        for j in range(length):
            k = lists_ref[lax.rem(blk + j, length), first + s]
            for r in range(0, BLOCK, ROWS):
                sub = slice(r, r + ROWS)
                cx, cy, cz, sx, sy, sz, expo = [table_ref[k, p, sub] for p in range(7)]
                for h in range(0, point_count, LANES):
                    lanes = slice(h, h + LANES)
                    ox = points_ref[first + s, 0:1, lanes] - cx
                    oy = points_ref[first + s, 1:2, lanes] - cy
                    oz = points_ref[first + s, 2:3, lanes] - cz
                    squared = ox * ox + oy * oy + oz * oz
                    radial = jnp.exp(-expo * squared)
                    linear = 1.0 + (sx * ox + sy * oy + sz * oz)
                    basis = linear * radial
                    rows = slice(j * BLOCK + r, j * BLOCK + r + ROWS)
                    phi_ref[s, rows, lanes] = basis.astype(jnp.bfloat16)
                    if j == 0:
                        radial_ref[s, sub, lanes] = radial
                        basis_ref[s, sub, lanes] = basis

    def some_slots(i, carry):
        for u in range(2):
            one_slot(i * 2 + u)
        return carry

    steps = chunk_steps(mig_ref, first, phi_ref.shape[0]) * (UNROLL // 2)
    lax.fori_loop(0, steps, some_slots, 0)


def rho_kernel(offsets, starts, lists_ref, mig_ref, *refs):
    chunks = len(starts)
    phis = refs[:chunks]
    slabs = refs[chunks : chunks + len(offsets)]
    tiles, chi_ref, rho_ref, *placed = refs[chunks + len(offsets) :]
    if offsets:
        tiles = placed[0]
        place_slabs(offsets, slabs, tiles)
    blk = lax.axis_index("blk")
    length = lists_ref.shape[0]
    rho_ref[...] = jnp.zeros_like(rho_ref)

    for c, phi_ref in enumerate(phis):
        size = phi_ref.shape[0]

        def one_slot(s, first=starts[c], phi_ref=phi_ref):
            slot = first + s
            own = lists_ref[blk, slot]
            cols = aligned((own - blk * BPD) * BLOCK, BLOCK)
            left = [tiles[aligned(own * BLOCK, BLOCK), cols]]
            for j in range(1, length):
                k = lists_ref[lax.rem(blk + j, length), slot]
                left.append(tiles[aligned(k * BLOCK, BLOCK), cols].T)
            chi = jnp.dot(
                jnp.concatenate(left, axis=1), phi_ref[s], preferred_element_type=jnp.float32
            )
            phi = phi_ref[s, 0:BLOCK, :]
            chi_ref[slot] = chi
            rho_ref[pl.ds(slot, 1), :] = jnp.sum(
                phi.astype(jnp.float32) * chi, axis=0, keepdims=True
            )

        def some_slots(i, carry, one_slot=one_slot):
            for u in range(UNROLL):
                one_slot(i * UNROLL + u)
            return carry

        lax.fori_loop(0, chunk_steps(mig_ref, starts[c], size), some_slots, 0)


def force_kernel(starts, lists_ref, mig_ref, points_ref, rho_a_ref, rho_b_ref, chi_ref, *refs):
    chunks = len(starts)
    radials = refs[:chunks]
    bases = refs[chunks : 2 * chunks]
    table_ref, dest_ref, _, out_ref, acc, pot_ref = refs[2 * chunks :]
    blk = lax.axis_index("blk")
    slots, _, point_count = points_ref.shape
    dests = dest_ref.shape[1]
    live = live_count(mig_ref)
    rho = rho_a_ref[...] + rho_b_ref[...]
    weight = points_ref[:, 3, :]
    log_sq = jnp.log(rho * rho + RHO_SOFT * RHO_SOFT)
    pot = weight * (-(4.0 / 3.0) * SLATER) * rho * jnp.exp(log_sq * (-1.0 / 3.0))
    slot_ids = lax.broadcasted_iota(jnp.int32, (slots, 1), 0)
    pot_ref[...] = jnp.where(slot_ids < live, pot, 0.0)
    energies = jnp.sum(weight * -SLATER * jnp.exp(log_sq * (2.0 / 3.0)), axis=1, keepdims=True)

    for c in range(chunks):
        radial_ref, basis_ref = radials[c], bases[c]
        size = radial_ref.shape[0]

        def one_slot(s, first=starts[c], radial_ref=radial_ref, basis_ref=basis_ref):
            slot = first + s
            own = lists_ref[blk, slot] - blk * BPD
            pots = pot_ref[pl.ds(slot, 1), :]
            for r in range(0, BLOCK, ROWS):
                sub = slice(r, r + ROWS)
                sums = None
                for h in range(0, point_count, LANES):
                    lanes = slice(h, h + LANES)
                    u = chi_ref[slot, sub, lanes] * pots[:, lanes]
                    ub = u * basis_ref[s, sub, lanes]
                    terms = (
                        u * radial_ref[s, sub, lanes],
                        ub,
                        ub * points_ref[slot, 0:1, lanes],
                        ub * points_ref[slot, 1:2, lanes],
                        ub * points_ref[slot, 2:3, lanes],
                    )
                    sums = terms if sums is None else [a + b for a, b in zip(sums, terms)]
                for q in range(5):
                    acc[own, q, sub] += sums[q]

        def some_slots(i, carry, one_slot=one_slot):
            for u in range(UNROLL):
                one_slot(i * UNROLL + u)
            return carry

        lax.fori_loop(0, chunk_steps(mig_ref, starts[c], size), some_slots, 0)

    lane_ids = lax.broadcasted_iota(jnp.int32, (1, LANES), 1).astype(jnp.float32)

    totals = [jnp.zeros((8, LANES), jnp.float32)] * (3 * NATOM // LANES)
    for b in range(BPD):
        k = blk * BPD + b
        for r in range(0, BLOCK, ROWS):
            sub = slice(r, r + ROWS)
            parts = [acc[b, q, sub] for q in range(5)]
            doubled = 2.0 * table_ref[k, 6, sub]
            atom = table_ref[k, 7, sub]
            for c in range(3):
                force = table_ref[k, 3 + c, sub] * parts[0] - doubled * (
                    parts[2 + c] - table_ref[k, c, sub] * parts[1]
                )
                column = 2.0 * jnp.sum(force, axis=1, keepdims=True)
                for h in range(NATOM // LANES):
                    hit = jnp.where(atom == lane_ids + float(h * LANES), column, 0.0)
                    i = c * (NATOM // LANES) + h
                    totals[i] = totals[i] + sum(hit[i8 : i8 + 8] for i8 in range(0, ROWS, 8))
    rows = [jnp.sum(t, axis=0, keepdims=True) for t in totals]
    moved = jnp.sum(dest_ref[...] * energies, axis=0, keepdims=True)
    rows += [moved[:, h : h + LANES] for h in range(0, dests, LANES)]
    packed = jnp.concatenate(rows, axis=0)
    for i in range(out_ref.shape[0]):
        out_ref[i] = packed


def sum_kernel(copies, arrived_ref, energy_ref, forces_ref):
    me = lax.axis_index("grid")
    total = jnp.sum(arrived_ref[...], axis=0)
    per = NATOM // LANES
    for c in range(3):
        for h in range(per):
            forces_ref[c : c + 1, h * LANES : (h + 1) * LANES] = total[c * per + h : c * per + h + 1]
    width = energy_ref.shape[1]
    first = me * width
    energy = jnp.zeros((1, LANES), jnp.float32)
    for i in range(3 * per, total.shape[0]):
        chosen = lax.div(first, LANES) == i - 3 * per
        energy = jnp.where(chosen, total[i : i + 1], energy)
    turn = lax.rem(LANES - lax.rem(first, LANES), LANES)
    energy = pltpu.roll(jnp.broadcast_to(energy, (8, LANES)), turn, 1)
    energy_ref[...] = energy[0:1, 0:width] * (1.0 / copies)


def swap(array, offset):
    count = lax.axis_size("grid")
    return lax.ppermute(array, "grid", [(i, i ^ offset) for i in range(count)])


FIRST = (8, 4, 2)
OVER_X = ((10, 0), (10, 1), (6, 0))
OVER_Z = ((12, 0), (12, 1), (6, 1))


def in_hbm(array):
    return pltpu.with_memory_space_constraint(array, pltpu.HBM)


def spec(space):
    return pl.BlockSpec(memory_space=space)


def params(blocks):
    return pltpu.CompilerParams(vmem_limit_bytes=blocks * 1024 * 1024)


def cost(nominal_us):
    return pl.CostEstimate(
        flops=0, bytes_accessed=int(nominal_us * 3.69e6), transcendentals=0
    )


def f32(*shape):
    return jax.ShapeDtypeStruct(shape, jnp.float32)


def local(density, points, sig_blocks, migration, atom_coords, exponents, shape_coef, func_atom):
    grid_count = lax.axis_size("grid")
    blk_count = lax.axis_size("blk")
    slots, _, point_count = points.shape
    length = sig_blocks.shape[1]
    functions = exponents.shape[0]
    blocks = functions // BLOCK
    dests = grid_count * (slots // 2)
    sizes = [slots // 4 * 3, slots // 4]
    starts = [0, slots // 4 * 3]
    slab = density.T
    tied = lax.optimization_barrier
    lists = sig_blocks.T

    table, dest_mask, points, lists, migration, near_slab = pl.pallas_call(
        table_kernel,
        out_shape=[
            f32(blocks, 8, BLOCK, LANES),
            f32(slots, dests),
            f32(*points.shape),
            jax.ShapeDtypeStruct(lists.shape, jnp.int32),
            jax.ShapeDtypeStruct(migration.shape, jnp.int32),
            jax.ShapeDtypeStruct(slab.shape, slab.dtype),
        ],
        in_specs=[spec(pltpu.HBM)] * 8,
        out_specs=[spec(VMEM)] * 6,
        scratch_shapes=[
            pltpu.SMEM((slots,), jnp.int32),
            pltpu.VMEM((functions,), jnp.int32),
            pltpu.VMEM((functions,), jnp.float32),
            pltpu.VMEM((3, functions), jnp.float32),
            pltpu.VMEM((3, NATOM), jnp.float32),
            pltpu.SemaphoreType.DMA((9,)),
        ],
        compiler_params=params(blocks),
        cost_estimate=cost(4),
        name="param_table",
    )(
        *[
            in_hbm(a)
            for a in (
                migration,
                func_atom,
                exponents,
                shape_coef,
                atom_coords,
                points,
                lists,
                slab,
            )
        ]
    )

    tile_shape = jax.ShapeDtypeStruct((functions, BPD * BLOCK), jnp.bfloat16)

    def basis_chunk(c, points, offsets=()):
        some = 1 if offsets else 0
        zeros = 1 if c == 0 else 0
        return pl.pallas_call(
            functools.partial(phi_kernel, starts[c], offsets),
            out_shape=[
                jax.ShapeDtypeStruct((sizes[c], length * BLOCK, point_count), jnp.bfloat16),
                f32(sizes[c], BLOCK, point_count),
                f32(sizes[c], BLOCK, point_count),
            ]
            + [f32(BPD, 5, BLOCK, LANES)] * zeros
            + [tile_shape] * some,
            in_specs=[spec(SMEM), spec(SMEM)] + [spec(VMEM)] * (2 + len(offsets)),
            out_specs=[spec(VMEM)] * (3 + zeros + some),
            compiler_params=params(blocks),
            cost_estimate=cost(5),
            name="basis_values",
        )(lists, migration, points, table, *[held[e] for e in offsets])

    def pack(parts, picks):
        return pl.pallas_call(
            functools.partial(pack_kernel, picks),
            out_shape=jax.ShapeDtypeStruct(
                (len(picks), slab.shape[0] // 2, slab.shape[1]), slab.dtype
            ),
            in_specs=[spec(VMEM)] * len(parts),
            out_specs=spec(VMEM),
            compiler_params=params(blocks),
            name="pack",
        )(*parts)

    held = {0: slab}
    late, slabs = [], []
    if grid_count == 16:
        for e in FIRST:
            held[e] = swap(slab, e)
        held[0] = near_slab
        held, points = tied((held, points))
        ready = list(held)
        over_x = swap(pack((held[8], held[4]), ((0, 0), (0, 1), (1, 0))), 2)
        over_z = swap(pack((held[8], held[2]), ((0, 0), (0, 1), (1, 1))), 4)
        across = swap(held[8], 6)
        *first, acc, tiles = basis_chunk(0, points, ready)
        held, across, over_x, over_z, first, tiles, points = tied(
            (held, across, over_x, over_z, first, tiles, points)
        )
        parts = [*held.values(), across, over_x, over_z]
        wholes = [(e, h) for e in (*held, 14) for h in range(2)]
        picks = [(p, h) for p in range(len(held) + 1) for h in range(2)]
        picks += [(len(held) + 1 + p, h) for p in range(2) for h in range(3)]
        crossed = swap(pack(parts, picks), 1)
        second = basis_chunk(1, points)
        late = [14, OVER_X, OVER_Z, tuple((e ^ 1, h) for e, h in (*wholes, *OVER_X, *OVER_Z))]
        slabs = [across, over_x, over_z, crossed]
    else:
        tiles = lax.all_gather(slab, "grid", axis=0, tiled=True)
        *first, acc = basis_chunk(0, points)
        second = basis_chunk(1, points)
    chunks = [first, second]
    phis, radials, bases = zip(*chunks)

    some = 1 if late else 0
    chi, rho, *_ = pl.pallas_call(
        functools.partial(rho_kernel, late, starts),
        out_shape=[f32(slots, BLOCK, point_count), f32(slots, point_count)] + [tile_shape] * some,
        in_specs=[spec(SMEM), spec(SMEM)]
        + [spec(VMEM)] * (len(starts) + len(late) + 1),
        out_specs=[spec(VMEM)] * (2 + some),
        input_output_aliases={2 + len(starts) + len(late): 2} if late else {},
        compiler_params=params(blocks),
        cost_estimate=cost(5),
        name="density_at_points",
    )(lists, migration, *phis, *slabs, tiles)

    if blk_count == 2:
        other = lax.ppermute(rho, "blk", [(0, 1), (1, 0)])
    else:
        other = lax.psum(rho, "blk") - rho

    rows = 3 * NATOM // LANES + dests // LANES
    outgoing, _ = pl.pallas_call(
        functools.partial(force_kernel, starts),
        out_shape=[f32(blk_count * grid_count, rows, LANES), f32(BPD, 5, BLOCK, LANES)],
        in_specs=[spec(SMEM), spec(SMEM)] + [spec(VMEM)] * (7 + 2 * len(starts)),
        out_specs=[spec(VMEM)] * 2,
        scratch_shapes=[pltpu.VMEM((slots, point_count), jnp.float32)],
        input_output_aliases={8 + 2 * len(starts): 1},
        compiler_params=params(blocks),
        cost_estimate=cost(5),
        name="forces_and_energies",
    )(lists, migration, points, rho, other, chi, *radials, *bases, table, dest_mask, acc)

    arrived = lax.all_to_all(outgoing, ("blk", "grid"), split_axis=0, concat_axis=0, tiled=True)

    energy, forces = pl.pallas_call(
        functools.partial(sum_kernel, blk_count),
        out_shape=[f32(1, dests // grid_count), f32(3, NATOM)],
        in_specs=[spec(VMEM)],
        out_specs=[spec(VMEM)] * 2,
        compiler_params=params(blocks),
        name="final_sums",
    )(arrived)
    return (energy.reshape(dests // grid_count), forces)


def solution(mesh):
    in_specs = (
        P("blk", "grid"),
        P("grid", None, None),
        P("grid", None),
        P("grid"),
        P(),
        P(),
        P(),
        P(),
    )
    out_specs = (P("grid"), P())
    return jax.shard_map(local, mesh=mesh, in_specs=in_specs, out_specs=out_specs, check_vma=False)
```

```python
import functools

import jax
import jax.numpy as jnp
from jax import lax
from jax.experimental import pallas as pl
from jax.experimental.pallas import tpu as pltpu
from jax.sharding import PartitionSpec as P

BLOCK = 128
BPD = 6
NATOM = 256
LANES = 128
ROWS = 32
UNROLL = 4

SLATER = 0.7386
RHO_SOFT = 0.05

VMEM = pltpu.MemorySpace.VMEM
SMEM = pltpu.MemorySpace.SMEM


def aligned(start, size):
    return pl.ds(pl.multiple_of(start, size), size)


def live_count(ints_ref):
    row = ints_ref.shape[0] - 1
    slots = ints_ref.shape[1]
    step = 1
    while step * 2 <= slots:
        step *= 2
    count = jnp.int32(0)
    while step:
        more = count + step
        found = ints_ref[row, jnp.minimum(more, slots) - 1] >= 0
        count = jnp.where(jnp.logical_and(more <= slots, found), more, count)
        step //= 2
    return count


def start_copies(pairs, sems):
    copies = [pltpu.make_async_copy(src, dst, sems.at[i]) for i, (src, dst) in enumerate(pairs)]
    for copy in copies:
        copy.start()
    return copies


def place_slabs(offsets, slabs, tiles):
    me = lax.axis_index("grid")
    for e, slab in zip(offsets, slabs):
        if isinstance(e, tuple):
            half = slab.shape[1]
            for i, (one, h) in enumerate(e):
                first = (2 * jnp.bitwise_xor(me, one) + h) * half
                tiles[aligned(first, half), :] = slab[i]
        else:
            depth = slab.shape[0]
            tiles[aligned(jnp.bitwise_xor(me, e) * depth, depth), :] = slab[...]


def pack_kernel(picks, *refs):
    *parts, out_ref = refs
    half = out_ref.shape[1]
    for i, (p, h) in enumerate(picks):
        part = parts[p]
        out_ref[i] = part[h] if len(part.shape) == 3 else part[h * half : (h + 1) * half, :]


def share_slots(own_ints, other_ints, own_points, other_points, points_out, ints_out, dest_ref):
    rows, slots = own_ints.shape
    core = lax.rem(lax.axis_index("grid"), 2)
    own, other = live_count(own_ints), live_count(other_ints)
    count0 = jnp.where(core == 0, own, other)
    half = lax.div(own + other + 1, 2)
    base = jnp.where(core == 0, 0, half)
    count = jnp.where(core == 0, half, own + other - half)
    lanes = lax.broadcasted_iota(jnp.int32, (1, slots), 1)
    dest_ids = lax.broadcasted_iota(jnp.int32, (1, dest_ref.shape[1]), 1)
    kept = [jnp.zeros((1, slots), jnp.int32)] * rows
    for v in range(slots):
        from0 = base + v < count0
        slot = jnp.clip(base + v - jnp.where(from0, 0, count0), 0, slots - 1)
        mine = from0 == (core == 0)
        points_out[v] = jnp.where(mine, own_points[slot], other_points[slot])
        values = [jnp.where(mine, own_ints[i, slot], other_ints[i, slot]) for i in range(rows)]
        values[-1] = jnp.where(v < count, values[-1], -1)
        kept = [jnp.where(lanes == v, value, row) for value, row in zip(values, kept)]
        dest_ref[v : v + 1, :] = jnp.where(dest_ids == values[-1], 1.0, 0.0)
    ints_out[...] = jnp.concatenate(kept, axis=0)


def table_kernel(
    own_ints,
    other_ints,
    other_points,
    atom_hbm,
    expo_hbm,
    coef_hbm,
    coords_hbm,
    points_hbm,
    slab_hbm,
    table_ref,
    dest_ref,
    points_out,
    ints_out,
    slab_out,
    own_points,
    atom_ref,
    expo_ref,
    coef_ref,
    coords_ref,
    sems,
):
    copies = start_copies(
        [
            (atom_hbm, atom_ref),
            (expo_hbm, expo_ref),
            (coef_hbm, coef_ref),
            (coords_hbm, coords_ref),
            (points_hbm, own_points),
            (slab_hbm, slab_out),
        ],
        sems,
    )
    for copy in copies[:5]:
        copy.wait()
    share_slots(own_ints, other_ints, own_points, other_points, points_out, ints_out, dest_ref)
    coords = coords_ref[...]
    high = coords.astype(jnp.bfloat16)
    rest = coords - high.astype(jnp.float32)
    mid = rest.astype(jnp.bfloat16)
    low = (rest - mid.astype(jnp.float32)).astype(jnp.bfloat16)
    blocks = table_ref.shape[0]
    atoms = atom_ref[...].reshape(blocks, BLOCK)
    expos = expo_ref[...].reshape(blocks, BLOCK)

    for k in range(blocks):
        atom = atoms[k : k + 1]
        onehot = jnp.where(
            lax.broadcasted_iota(jnp.int32, (NATOM, BLOCK), 0) == atom, 1.0, 0.0
        ).astype(jnp.bfloat16)
        picked = [
            jnp.dot(part, onehot, preferred_element_type=jnp.float32) for part in (high, mid, low)
        ]
        center = (picked[0] + picked[1]) + picked[2]
        coef = coef_ref[:, k * BLOCK : (k + 1) * BLOCK]
        rows = jnp.concatenate(
            [center, coef, expos[k : k + 1], atom.astype(jnp.float32)], axis=0
        )
        columns = rows.T
        for p in range(8):
            table_ref[k, p] = jnp.broadcast_to(columns[:, p : p + 1], (BLOCK, LANES))

    for copy in copies[5:]:
        copy.wait()


def chunk_steps(ints_ref, first, size):
    left = jnp.clip(live_count(ints_ref) - first, 0, size)
    return lax.div(left + (UNROLL - 1), UNROLL)


def phi_kernel(first, offsets, ints_ref, points_ref, table_ref, *refs):
    slabs = refs[: len(offsets)]
    phi_ref, radial_ref, basis_ref, *more = refs[len(offsets) :]
    if first == 0:
        more.pop(0)[...] = jnp.zeros((BPD, 5, BLOCK, LANES), jnp.float32)
    if offsets:
        place_slabs(offsets, slabs, more[0])
    blk = lax.axis_index("blk")
    length = ints_ref.shape[0] - 1
    point_count = points_ref.shape[2]

    def one_slot(s):
        for j in range(length):
            k = ints_ref[lax.rem(blk + j, length), first + s]
            for r in range(0, BLOCK, ROWS):
                sub = slice(r, r + ROWS)
                cx, cy, cz, sx, sy, sz, expo = [table_ref[k, p, sub] for p in range(7)]
                for h in range(0, point_count, LANES):
                    lanes = slice(h, h + LANES)
                    ox = points_ref[first + s, 0:1, lanes] - cx
                    oy = points_ref[first + s, 1:2, lanes] - cy
                    oz = points_ref[first + s, 2:3, lanes] - cz
                    squared = ox * ox + oy * oy + oz * oz
                    radial = jnp.exp(-expo * squared)
                    linear = 1.0 + (sx * ox + sy * oy + sz * oz)
                    basis = linear * radial
                    rows = slice(j * BLOCK + r, j * BLOCK + r + ROWS)
                    phi_ref[s, rows, lanes] = basis.astype(jnp.bfloat16)
                    if j == 0:
                        radial_ref[s, sub, lanes] = radial
                        basis_ref[s, sub, lanes] = basis

    def some_slots(i, carry):
        for u in range(2):
            one_slot(i * 2 + u)
        return carry

    steps = chunk_steps(ints_ref, first, phi_ref.shape[0]) * (UNROLL // 2)
    lax.fori_loop(0, steps, some_slots, 0)


def rho_kernel(offsets, starts, ints_ref, *refs):
    chunks = len(starts)
    phis = refs[:chunks]
    slabs = refs[chunks : chunks + len(offsets)]
    tiles, chi_ref, rho_ref, *placed = refs[chunks + len(offsets) :]
    if offsets:
        tiles = placed[0]
        place_slabs(offsets, slabs, tiles)
    blk = lax.axis_index("blk")
    length = ints_ref.shape[0] - 1
    rho_ref[...] = jnp.zeros_like(rho_ref)

    for c, phi_ref in enumerate(phis):
        size = phi_ref.shape[0]

        def one_slot(s, first=starts[c], phi_ref=phi_ref):
            slot = first + s
            own = ints_ref[blk, slot]
            cols = aligned((own - blk * BPD) * BLOCK, BLOCK)
            left = [tiles[aligned(own * BLOCK, BLOCK), cols]]
            for j in range(1, length):
                k = ints_ref[lax.rem(blk + j, length), slot]
                left.append(tiles[aligned(k * BLOCK, BLOCK), cols].T)
            chi = jnp.dot(
                jnp.concatenate(left, axis=1), phi_ref[s], preferred_element_type=jnp.float32
            )
            phi = phi_ref[s, 0:BLOCK, :]
            chi_ref[slot] = chi
            rho_ref[pl.ds(slot, 1), :] = jnp.sum(
                phi.astype(jnp.float32) * chi, axis=0, keepdims=True
            )

        def some_slots(i, carry, one_slot=one_slot):
            for u in range(UNROLL):
                one_slot(i * UNROLL + u)
            return carry

        lax.fori_loop(0, chunk_steps(ints_ref, starts[c], size), some_slots, 0)


def force_kernel(starts, ints_ref, points_ref, rho_a_ref, rho_b_ref, chi_ref, *refs):
    chunks = len(starts)
    radials = refs[:chunks]
    bases = refs[chunks : 2 * chunks]
    table_ref, dest_ref, _, out_ref, acc, pot_ref = refs[2 * chunks :]
    blk = lax.axis_index("blk")
    slots, _, point_count = points_ref.shape
    dests = dest_ref.shape[1]
    live = live_count(ints_ref)
    rho = rho_a_ref[...] + rho_b_ref[...]
    weight = points_ref[:, 3, :]
    log_sq = jnp.log(rho * rho + RHO_SOFT * RHO_SOFT)
    pot = weight * (-(4.0 / 3.0) * SLATER) * rho * jnp.exp(log_sq * (-1.0 / 3.0))
    slot_ids = lax.broadcasted_iota(jnp.int32, (slots, 1), 0)
    pot_ref[...] = jnp.where(slot_ids < live, pot, 0.0)
    energies = jnp.sum(weight * -SLATER * jnp.exp(log_sq * (2.0 / 3.0)), axis=1, keepdims=True)

    for c in range(chunks):
        radial_ref, basis_ref = radials[c], bases[c]
        size = radial_ref.shape[0]

        def one_slot(s, first=starts[c], radial_ref=radial_ref, basis_ref=basis_ref):
            slot = first + s
            own = ints_ref[blk, slot] - blk * BPD
            pots = pot_ref[pl.ds(slot, 1), :]
            for r in range(0, BLOCK, ROWS):
                sub = slice(r, r + ROWS)
                sums = None
                for h in range(0, point_count, LANES):
                    lanes = slice(h, h + LANES)
                    u = chi_ref[slot, sub, lanes] * pots[:, lanes]
                    ub = u * basis_ref[s, sub, lanes]
                    terms = (
                        u * radial_ref[s, sub, lanes],
                        ub,
                        ub * points_ref[slot, 0:1, lanes],
                        ub * points_ref[slot, 1:2, lanes],
                        ub * points_ref[slot, 2:3, lanes],
                    )
                    sums = terms if sums is None else [a + b for a, b in zip(sums, terms)]
                for q in range(5):
                    acc[own, q, sub] += sums[q]

        def some_slots(i, carry, one_slot=one_slot):
            for u in range(UNROLL):
                one_slot(i * UNROLL + u)
            return carry

        lax.fori_loop(0, chunk_steps(ints_ref, starts[c], size), some_slots, 0)

    lane_ids = lax.broadcasted_iota(jnp.int32, (1, LANES), 1).astype(jnp.float32)

    totals = [jnp.zeros((8, LANES), jnp.float32)] * (3 * NATOM // LANES)
    for b in range(BPD):
        k = blk * BPD + b
        for r in range(0, BLOCK, ROWS):
            sub = slice(r, r + ROWS)
            parts = [acc[b, q, sub] for q in range(5)]
            doubled = 2.0 * table_ref[k, 6, sub]
            atom = table_ref[k, 7, sub]
            for c in range(3):
                force = table_ref[k, 3 + c, sub] * parts[0] - doubled * (
                    parts[2 + c] - table_ref[k, c, sub] * parts[1]
                )
                column = 2.0 * jnp.sum(force, axis=1, keepdims=True)
                for h in range(NATOM // LANES):
                    hit = jnp.where(atom == lane_ids + float(h * LANES), column, 0.0)
                    i = c * (NATOM // LANES) + h
                    totals[i] = totals[i] + sum(hit[i8 : i8 + 8] for i8 in range(0, ROWS, 8))
    rows = [jnp.sum(t, axis=0, keepdims=True) for t in totals]
    moved = jnp.sum(dest_ref[...] * energies, axis=0, keepdims=True)
    rows += [moved[:, h : h + LANES] for h in range(0, dests, LANES)]
    packed = jnp.concatenate(rows, axis=0)
    for i in range(out_ref.shape[0]):
        out_ref[i] = packed


def sum_kernel(copies, arrived_ref, energy_ref, forces_ref):
    me = lax.axis_index("grid")
    total = jnp.sum(arrived_ref[...], axis=0)
    per = NATOM // LANES
    for c in range(3):
        for h in range(per):
            forces_ref[c : c + 1, h * LANES : (h + 1) * LANES] = total[c * per + h : c * per + h + 1]
    width = energy_ref.shape[1]
    first = me * width
    energy = jnp.zeros((1, LANES), jnp.float32)
    for i in range(3 * per, total.shape[0]):
        chosen = lax.div(first, LANES) == i - 3 * per
        energy = jnp.where(chosen, total[i : i + 1], energy)
    turn = lax.rem(LANES - lax.rem(first, LANES), LANES)
    energy = pltpu.roll(jnp.broadcast_to(energy, (8, LANES)), turn, 1)
    energy_ref[...] = energy[0:1, 0:width] * (1.0 / copies)


def swap(array, offset):
    count = lax.axis_size("grid")
    return lax.ppermute(array, "grid", [(i, i ^ offset) for i in range(count)])


FIRST = (8, 4, 2)
OVER_X = ((10, 0), (10, 1), (6, 0))
OVER_Z = ((12, 0), (12, 1), (6, 1))


def in_hbm(array):
    return pltpu.with_memory_space_constraint(array, pltpu.HBM)


def spec(space):
    return pl.BlockSpec(memory_space=space)


def params(blocks):
    return pltpu.CompilerParams(vmem_limit_bytes=blocks * 1024 * 1024)


def cost(nominal_us):
    return pl.CostEstimate(
        flops=0, bytes_accessed=int(nominal_us * 3.69e6), transcendentals=0
    )


def f32(*shape):
    return jax.ShapeDtypeStruct(shape, jnp.float32)


def local(density, points, sig_blocks, migration, atom_coords, exponents, shape_coef, func_atom):
    grid_count = lax.axis_size("grid")
    blk_count = lax.axis_size("blk")
    slots, _, point_count = points.shape
    length = sig_blocks.shape[1]
    functions = exponents.shape[0]
    blocks = functions // BLOCK
    dests = grid_count * (slots // 2)
    sizes = [slots // 4 * 3, slots // 4]
    starts = [0, slots // 4 * 3]
    tied = lax.optimization_barrier

    slab = density.T
    held = {0: slab}
    if grid_count == 16:
        for e in FIRST:
            held[e] = swap(slab, e)
    ints = jnp.concatenate([sig_blocks.T, migration[None]], axis=0)
    table, dest_mask, points, ints, near_slab = pl.pallas_call(
        table_kernel,
        out_shape=[
            f32(blocks, 8, BLOCK, LANES),
            f32(slots, dests),
            f32(*points.shape),
            jax.ShapeDtypeStruct(ints.shape, jnp.int32),
            jax.ShapeDtypeStruct(slab.shape, slab.dtype),
        ],
        in_specs=[spec(SMEM)] * 2 + [spec(VMEM)] + [spec(pltpu.HBM)] * 6,
        out_specs=[spec(VMEM)] * 5,
        scratch_shapes=[
            pltpu.VMEM(points.shape, jnp.float32),
            pltpu.VMEM((functions,), jnp.int32),
            pltpu.VMEM((functions,), jnp.float32),
            pltpu.VMEM((3, functions), jnp.float32),
            pltpu.VMEM((3, NATOM), jnp.float32),
            pltpu.SemaphoreType.DMA((6,)),
        ],
        compiler_params=params(blocks),
        cost_estimate=cost(4),
        name="param_table",
    )(
        ints,
        swap(ints, 1),
        swap(points, 1),
        *[in_hbm(a) for a in (func_atom, exponents, shape_coef, atom_coords, points, slab)],
    )

    tile_shape = jax.ShapeDtypeStruct((functions, BPD * BLOCK), jnp.bfloat16)

    def basis_chunk(c, points, offsets=()):
        some = 1 if offsets else 0
        zeros = 1 if c == 0 else 0
        return pl.pallas_call(
            functools.partial(phi_kernel, starts[c], offsets),
            out_shape=[
                jax.ShapeDtypeStruct((sizes[c], length * BLOCK, point_count), jnp.bfloat16),
                f32(sizes[c], BLOCK, point_count),
                f32(sizes[c], BLOCK, point_count),
            ]
            + [f32(BPD, 5, BLOCK, LANES)] * zeros
            + [tile_shape] * some,
            in_specs=[spec(SMEM)] + [spec(VMEM)] * (2 + len(offsets)),
            out_specs=[spec(VMEM)] * (3 + zeros + some),
            compiler_params=params(blocks),
            cost_estimate=cost(5),
            name="basis_values",
        )(ints, points, table, *[held[e] for e in offsets])

    def pack(parts, picks):
        return pl.pallas_call(
            functools.partial(pack_kernel, picks),
            out_shape=jax.ShapeDtypeStruct(
                (len(picks), slab.shape[0] // 2, slab.shape[1]), slab.dtype
            ),
            in_specs=[spec(VMEM)] * len(parts),
            out_specs=spec(VMEM),
            compiler_params=params(blocks),
            name="pack",
        )(*parts)

    late, slabs = [], []
    if grid_count == 16:
        held[0] = near_slab
        held, points = tied((held, points))
        ready = list(held)
        over_x = swap(pack((held[8], held[4]), ((0, 0), (0, 1), (1, 0))), 2)
        over_z = swap(pack((held[8], held[2]), ((0, 0), (0, 1), (1, 1))), 4)
        across = swap(held[8], 6)
        *first, acc, tiles = basis_chunk(0, points, ready)
        held, across, over_x, over_z, first, tiles, points = tied(
            (held, across, over_x, over_z, first, tiles, points)
        )
        parts = [*held.values(), across, over_x, over_z]
        wholes = [(e, h) for e in (*held, 14) for h in range(2)]
        picks = [(p, h) for p in range(len(held) + 1) for h in range(2)]
        picks += [(len(held) + 1 + p, h) for p in range(2) for h in range(3)]
        crossed = swap(pack(parts, picks), 1)
        second = basis_chunk(1, points)
        late = [14, OVER_X, OVER_Z, tuple((e ^ 1, h) for e, h in (*wholes, *OVER_X, *OVER_Z))]
        slabs = [across, over_x, over_z, crossed]
    else:
        tiles = lax.all_gather(slab, "grid", axis=0, tiled=True)
        *first, acc = basis_chunk(0, points)
        second = basis_chunk(1, points)
    chunks = [first, second]
    phis, radials, bases = zip(*chunks)

    some = 1 if late else 0
    chi, rho, *_ = pl.pallas_call(
        functools.partial(rho_kernel, late, starts),
        out_shape=[f32(slots, BLOCK, point_count), f32(slots, point_count)] + [tile_shape] * some,
        in_specs=[spec(SMEM)] + [spec(VMEM)] * (len(starts) + len(late) + 1),
        out_specs=[spec(VMEM)] * (2 + some),
        input_output_aliases={1 + len(starts) + len(late): 2} if late else {},
        compiler_params=params(blocks),
        cost_estimate=cost(5),
        name="density_at_points",
    )(ints, *phis, *slabs, tiles)

    if blk_count == 2:
        other = lax.ppermute(rho, "blk", [(0, 1), (1, 0)])
    else:
        other = lax.psum(rho, "blk") - rho

    rows = 3 * NATOM // LANES + dests // LANES
    outgoing, _ = pl.pallas_call(
        functools.partial(force_kernel, starts),
        out_shape=[f32(blk_count * grid_count, rows, LANES), f32(BPD, 5, BLOCK, LANES)],
        in_specs=[spec(SMEM)] + [spec(VMEM)] * (7 + 2 * len(starts)),
        out_specs=[spec(VMEM)] * 2,
        scratch_shapes=[pltpu.VMEM((slots, point_count), jnp.float32)],
        input_output_aliases={7 + 2 * len(starts): 1},
        compiler_params=params(blocks),
        cost_estimate=cost(5),
        name="forces_and_energies",
    )(ints, points, rho, other, chi, *radials, *bases, table, dest_mask, acc)

    arrived = lax.all_to_all(outgoing, ("blk", "grid"), split_axis=0, concat_axis=0, tiled=True)

    energy, forces = pl.pallas_call(
        functools.partial(sum_kernel, blk_count),
        out_shape=[f32(1, dests // grid_count), f32(3, NATOM)],
        in_specs=[spec(VMEM)],
        out_specs=[spec(VMEM)] * 2,
        compiler_params=params(blocks),
        name="final_sums",
    )(arrived)
    return (energy.reshape(dests // grid_count), forces)


def solution(mesh):
    in_specs = (
        P("blk", "grid"),
        P("grid", None, None),
        P("grid", None),
        P("grid"),
        P(),
        P(),
        P(),
        P(),
    )
    out_specs = (P("grid"), P())
    return jax.shard_map(local, mesh=mesh, in_specs=in_specs, out_specs=out_specs, check_vma=False)
```

```python
import functools

import jax
import jax.numpy as jnp
from jax import lax
from jax.experimental import pallas as pl
from jax.experimental.pallas import tpu as pltpu
from jax.sharding import PartitionSpec as P

BLOCK = 128
BPD = 6
NATOM = 256
LANES = 128
ROWS = 32
UNROLL = 4

SLATER = 0.7386
RHO_SOFT = 0.05

VMEM = pltpu.MemorySpace.VMEM
SMEM = pltpu.MemorySpace.SMEM


def aligned(start, size):
    return pl.ds(pl.multiple_of(start, size), size)


def live_count(ints_ref):
    row = ints_ref.shape[0] - 1
    slots = ints_ref.shape[1]
    step = 1
    while step * 2 <= slots:
        step *= 2
    count = jnp.int32(0)
    while step:
        more = count + step
        found = ints_ref[row, jnp.minimum(more, slots) - 1] >= 0
        count = jnp.where(jnp.logical_and(more <= slots, found), more, count)
        step //= 2
    return count


def start_copies(pairs, sems):
    copies = [pltpu.make_async_copy(src, dst, sems.at[i]) for i, (src, dst) in enumerate(pairs)]
    for copy in copies:
        copy.start()
    return copies


def place_slabs(offsets, slabs, tiles):
    me = lax.axis_index("grid")
    for e, slab in zip(offsets, slabs):
        if isinstance(e, tuple):
            half = slab.shape[1]
            for i, (one, h) in enumerate(e):
                first = (2 * jnp.bitwise_xor(me, one) + h) * half
                tiles[aligned(first, half), :] = slab[i]
        else:
            depth = slab.shape[0]
            tiles[aligned(jnp.bitwise_xor(me, e) * depth, depth), :] = slab[...]


def pack_kernel(picks, *refs):
    *parts, out_ref = refs
    half = out_ref.shape[1]
    for i, (p, h) in enumerate(picks):
        part = parts[p]
        out_ref[i] = part[h] if len(part.shape) == 3 else part[h * half : (h + 1) * half, :]


def share_kernel(own_ints, other_ints, own_points, other_points, points_out, ints_out, dest_ref):
    rows, slots = own_ints.shape
    core = lax.rem(lax.axis_index("grid"), 2)
    own, other = live_count(own_ints), live_count(other_ints)
    count0 = jnp.where(core == 0, own, other)
    half = lax.div(own + other + 1, 2)
    base = jnp.where(core == 0, 0, half)
    count = jnp.where(core == 0, half, own + other - half)
    lanes = lax.broadcasted_iota(jnp.int32, (1, slots), 1)
    dest_ids = lax.broadcasted_iota(jnp.int32, (1, dest_ref.shape[1]), 1)
    kept = [jnp.zeros((1, slots), jnp.int32)] * rows
    for v in range(slots):
        from0 = base + v < count0
        slot = jnp.clip(base + v - jnp.where(from0, 0, count0), 0, slots - 1)
        mine = from0 == (core == 0)
        points_out[v] = jnp.where(mine, own_points[slot], other_points[slot])
        values = [jnp.where(mine, own_ints[i, slot], other_ints[i, slot]) for i in range(rows)]
        values[-1] = jnp.where(v < count, values[-1], -1)
        kept = [jnp.where(lanes == v, value, row) for value, row in zip(values, kept)]
        dest_ref[v : v + 1, :] = jnp.where(dest_ids == values[-1], 1.0, 0.0)
    ints_out[...] = jnp.concatenate(kept, axis=0)


def table_kernel(
    atom_hbm,
    expo_hbm,
    coef_hbm,
    coords_hbm,
    points_hbm,
    slab_hbm,
    table_ref,
    points_out,
    slab_out,
    atom_ref,
    expo_ref,
    coef_ref,
    coords_ref,
    sems,
):
    copies = start_copies(
        [
            (atom_hbm, atom_ref),
            (expo_hbm, expo_ref),
            (coef_hbm, coef_ref),
            (coords_hbm, coords_ref),
            (points_hbm, points_out),
            (slab_hbm, slab_out),
        ],
        sems,
    )
    for copy in copies[:4]:
        copy.wait()
    coords = coords_ref[...]
    high = coords.astype(jnp.bfloat16)
    rest = coords - high.astype(jnp.float32)
    mid = rest.astype(jnp.bfloat16)
    low = (rest - mid.astype(jnp.float32)).astype(jnp.bfloat16)
    blocks = table_ref.shape[0]
    atoms = atom_ref[...].reshape(blocks, BLOCK)
    expos = expo_ref[...].reshape(blocks, BLOCK)

    for k in range(blocks):
        atom = atoms[k : k + 1]
        onehot = jnp.where(
            lax.broadcasted_iota(jnp.int32, (NATOM, BLOCK), 0) == atom, 1.0, 0.0
        ).astype(jnp.bfloat16)
        picked = [
            jnp.dot(part, onehot, preferred_element_type=jnp.float32) for part in (high, mid, low)
        ]
        center = (picked[0] + picked[1]) + picked[2]
        coef = coef_ref[:, k * BLOCK : (k + 1) * BLOCK]
        rows = jnp.concatenate(
            [center, coef, expos[k : k + 1], atom.astype(jnp.float32)], axis=0
        )
        columns = rows.T
        for p in range(8):
            table_ref[k, p] = jnp.broadcast_to(columns[:, p : p + 1], (BLOCK, LANES))

    for copy in copies[4:]:
        copy.wait()


def chunk_steps(ints_ref, first, size):
    left = jnp.clip(live_count(ints_ref) - first, 0, size)
    return lax.div(left + (UNROLL - 1), UNROLL)


def phi_kernel(first, offsets, ints_ref, points_ref, table_ref, *refs):
    slabs = refs[: len(offsets)]
    phi_ref, radial_ref, basis_ref, *more = refs[len(offsets) :]
    if first == 0:
        more.pop(0)[...] = jnp.zeros((BPD, 5, BLOCK, LANES), jnp.float32)
    if offsets:
        place_slabs(offsets, slabs, more[0])
    blk = lax.axis_index("blk")
    length = ints_ref.shape[0] - 1
    point_count = points_ref.shape[2]

    def one_slot(s):
        for j in range(length):
            k = ints_ref[lax.rem(blk + j, length), first + s]
            for r in range(0, BLOCK, ROWS):
                sub = slice(r, r + ROWS)
                cx, cy, cz, sx, sy, sz, expo = [table_ref[k, p, sub] for p in range(7)]
                for h in range(0, point_count, LANES):
                    lanes = slice(h, h + LANES)
                    ox = points_ref[first + s, 0:1, lanes] - cx
                    oy = points_ref[first + s, 1:2, lanes] - cy
                    oz = points_ref[first + s, 2:3, lanes] - cz
                    squared = ox * ox + oy * oy + oz * oz
                    radial = jnp.exp(-expo * squared)
                    linear = 1.0 + (sx * ox + sy * oy + sz * oz)
                    basis = linear * radial
                    rows = slice(j * BLOCK + r, j * BLOCK + r + ROWS)
                    phi_ref[s, rows, lanes] = basis.astype(jnp.bfloat16)
                    if j == 0:
                        radial_ref[s, sub, lanes] = radial
                        basis_ref[s, sub, lanes] = basis

    def some_slots(i, carry):
        for u in range(2):
            one_slot(i * 2 + u)
        return carry

    steps = chunk_steps(ints_ref, first, phi_ref.shape[0]) * (UNROLL // 2)
    lax.fori_loop(0, steps, some_slots, 0)


def rho_kernel(offsets, starts, ints_ref, *refs):
    chunks = len(starts)
    phis = refs[:chunks]
    slabs = refs[chunks : chunks + len(offsets)]
    tiles, chi_ref, rho_ref, *placed = refs[chunks + len(offsets) :]
    if offsets:
        tiles = placed[0]
        place_slabs(offsets, slabs, tiles)
    blk = lax.axis_index("blk")
    length = ints_ref.shape[0] - 1
    rho_ref[...] = jnp.zeros_like(rho_ref)

    for c, phi_ref in enumerate(phis):
        size = phi_ref.shape[0]

        def one_slot(s, first=starts[c], phi_ref=phi_ref):
            slot = first + s
            own = ints_ref[blk, slot]
            cols = aligned((own - blk * BPD) * BLOCK, BLOCK)
            left = [tiles[aligned(own * BLOCK, BLOCK), cols]]
            for j in range(1, length):
                k = ints_ref[lax.rem(blk + j, length), slot]
                left.append(tiles[aligned(k * BLOCK, BLOCK), cols].T)
            chi = jnp.dot(
                jnp.concatenate(left, axis=1), phi_ref[s], preferred_element_type=jnp.float32
            )
            phi = phi_ref[s, 0:BLOCK, :]
            chi_ref[slot] = chi
            rho_ref[pl.ds(slot, 1), :] = jnp.sum(
                phi.astype(jnp.float32) * chi, axis=0, keepdims=True
            )

        def some_slots(i, carry, one_slot=one_slot):
            for u in range(UNROLL):
                one_slot(i * UNROLL + u)
            return carry

        lax.fori_loop(0, chunk_steps(ints_ref, starts[c], size), some_slots, 0)


def force_kernel(starts, ints_ref, points_ref, rho_a_ref, rho_b_ref, chi_ref, *refs):
    chunks = len(starts)
    radials = refs[:chunks]
    bases = refs[chunks : 2 * chunks]
    table_ref, dest_ref, _, out_ref, acc, pot_ref = refs[2 * chunks :]
    blk = lax.axis_index("blk")
    slots, _, point_count = points_ref.shape
    dests = dest_ref.shape[1]
    live = live_count(ints_ref)
    rho = rho_a_ref[...] + rho_b_ref[...]
    weight = points_ref[:, 3, :]
    log_sq = jnp.log(rho * rho + RHO_SOFT * RHO_SOFT)
    pot = weight * (-(4.0 / 3.0) * SLATER) * rho * jnp.exp(log_sq * (-1.0 / 3.0))
    slot_ids = lax.broadcasted_iota(jnp.int32, (slots, 1), 0)
    pot_ref[...] = jnp.where(slot_ids < live, pot, 0.0)
    energies = jnp.sum(weight * -SLATER * jnp.exp(log_sq * (2.0 / 3.0)), axis=1, keepdims=True)

    for c in range(chunks):
        radial_ref, basis_ref = radials[c], bases[c]
        size = radial_ref.shape[0]

        def one_slot(s, first=starts[c], radial_ref=radial_ref, basis_ref=basis_ref):
            slot = first + s
            own = ints_ref[blk, slot] - blk * BPD
            pots = pot_ref[pl.ds(slot, 1), :]
            for r in range(0, BLOCK, ROWS):
                sub = slice(r, r + ROWS)
                sums = None
                for h in range(0, point_count, LANES):
                    lanes = slice(h, h + LANES)
                    u = chi_ref[slot, sub, lanes] * pots[:, lanes]
                    ub = u * basis_ref[s, sub, lanes]
                    terms = (
                        u * radial_ref[s, sub, lanes],
                        ub,
                        ub * points_ref[slot, 0:1, lanes],
                        ub * points_ref[slot, 1:2, lanes],
                        ub * points_ref[slot, 2:3, lanes],
                    )
                    sums = terms if sums is None else [a + b for a, b in zip(sums, terms)]
                for q in range(5):
                    acc[own, q, sub] += sums[q]

        def some_slots(i, carry, one_slot=one_slot):
            for u in range(UNROLL):
                one_slot(i * UNROLL + u)
            return carry

        lax.fori_loop(0, chunk_steps(ints_ref, starts[c], size), some_slots, 0)

    lane_ids = lax.broadcasted_iota(jnp.int32, (1, LANES), 1).astype(jnp.float32)

    totals = [jnp.zeros((8, LANES), jnp.float32)] * (3 * NATOM // LANES)
    for b in range(BPD):
        k = blk * BPD + b
        for r in range(0, BLOCK, ROWS):
            sub = slice(r, r + ROWS)
            parts = [acc[b, q, sub] for q in range(5)]
            doubled = 2.0 * table_ref[k, 6, sub]
            atom = table_ref[k, 7, sub]
            for c in range(3):
                force = table_ref[k, 3 + c, sub] * parts[0] - doubled * (
                    parts[2 + c] - table_ref[k, c, sub] * parts[1]
                )
                column = 2.0 * jnp.sum(force, axis=1, keepdims=True)
                for h in range(NATOM // LANES):
                    hit = jnp.where(atom == lane_ids + float(h * LANES), column, 0.0)
                    i = c * (NATOM // LANES) + h
                    totals[i] = totals[i] + sum(hit[i8 : i8 + 8] for i8 in range(0, ROWS, 8))
    rows = [jnp.sum(t, axis=0, keepdims=True) for t in totals]
    moved = jnp.sum(dest_ref[...] * energies, axis=0, keepdims=True)
    rows += [moved[:, h : h + LANES] for h in range(0, dests, LANES)]
    packed = jnp.concatenate(rows, axis=0)
    for i in range(out_ref.shape[0]):
        out_ref[i] = packed


def sum_kernel(copies, arrived_ref, energy_ref, forces_ref):
    me = lax.axis_index("grid")
    total = jnp.sum(arrived_ref[...], axis=0)
    per = NATOM // LANES
    for c in range(3):
        for h in range(per):
            forces_ref[c : c + 1, h * LANES : (h + 1) * LANES] = total[c * per + h : c * per + h + 1]
    width = energy_ref.shape[1]
    first = me * width
    energy = jnp.zeros((1, LANES), jnp.float32)
    for i in range(3 * per, total.shape[0]):
        chosen = lax.div(first, LANES) == i - 3 * per
        energy = jnp.where(chosen, total[i : i + 1], energy)
    turn = lax.rem(LANES - lax.rem(first, LANES), LANES)
    energy = pltpu.roll(jnp.broadcast_to(energy, (8, LANES)), turn, 1)
    energy_ref[...] = energy[0:1, 0:width] * (1.0 / copies)


def swap(array, offset):
    count = lax.axis_size("grid")
    return lax.ppermute(array, "grid", [(i, i ^ offset) for i in range(count)])


FIRST = (8, 4, 2)
OVER_X = ((10, 0), (10, 1), (6, 0))
OVER_Z = ((12, 0), (12, 1), (6, 1))


def in_hbm(array):
    return pltpu.with_memory_space_constraint(array, pltpu.HBM)


def spec(space):
    return pl.BlockSpec(memory_space=space)


def params(blocks):
    return pltpu.CompilerParams(vmem_limit_bytes=blocks * 1024 * 1024)


def cost(nominal_us):
    return pl.CostEstimate(
        flops=0, bytes_accessed=int(nominal_us * 3.69e6), transcendentals=0
    )


def f32(*shape):
    return jax.ShapeDtypeStruct(shape, jnp.float32)


def local(density, points, sig_blocks, migration, atom_coords, exponents, shape_coef, func_atom):
    grid_count = lax.axis_size("grid")
    blk_count = lax.axis_size("blk")
    slots, _, point_count = points.shape
    length = sig_blocks.shape[1]
    functions = exponents.shape[0]
    blocks = functions // BLOCK
    dests = grid_count * (slots // 2)
    sizes = [slots // 4 * 3, slots // 4]
    starts = [0, slots // 4 * 3]
    tied = lax.optimization_barrier

    slab = density.T
    held = {0: slab}
    if grid_count == 16:
        for e in FIRST:
            held[e] = swap(slab, e)
    ints = jnp.concatenate([sig_blocks.T, migration[None]], axis=0)
    other_ints, other_points = swap(ints, 1), swap(points, 1)
    table, points, near_slab = pl.pallas_call(
        table_kernel,
        out_shape=[
            f32(blocks, 8, BLOCK, LANES),
            f32(*points.shape),
            jax.ShapeDtypeStruct(slab.shape, slab.dtype),
        ],
        in_specs=[spec(pltpu.HBM)] * 6,
        out_specs=[spec(VMEM)] * 3,
        scratch_shapes=[
            pltpu.VMEM((functions,), jnp.int32),
            pltpu.VMEM((functions,), jnp.float32),
            pltpu.VMEM((3, functions), jnp.float32),
            pltpu.VMEM((3, NATOM), jnp.float32),
            pltpu.SemaphoreType.DMA((6,)),
        ],
        compiler_params=params(blocks),
        cost_estimate=cost(4),
        name="param_table",
    )(*[in_hbm(a) for a in (func_atom, exponents, shape_coef, atom_coords, points, slab)])

    def share(other_ints, other_points):
        return pl.pallas_call(
            share_kernel,
            out_shape=[
                f32(*points.shape),
                jax.ShapeDtypeStruct(ints.shape, jnp.int32),
                f32(slots, dests),
            ],
            in_specs=[spec(SMEM)] * 2 + [spec(VMEM)] * 2,
            out_specs=[spec(VMEM)] * 3,
            compiler_params=params(blocks),
            cost_estimate=cost(1),
            name="shared_slots",
        )(ints, other_ints, points, other_points)

    tile_shape = jax.ShapeDtypeStruct((functions, BPD * BLOCK), jnp.bfloat16)

    def basis_chunk(c, points, ints, offsets=()):
        some = 1 if offsets else 0
        zeros = 1 if c == 0 else 0
        return pl.pallas_call(
            functools.partial(phi_kernel, starts[c], offsets),
            out_shape=[
                jax.ShapeDtypeStruct((sizes[c], length * BLOCK, point_count), jnp.bfloat16),
                f32(sizes[c], BLOCK, point_count),
                f32(sizes[c], BLOCK, point_count),
            ]
            + [f32(BPD, 5, BLOCK, LANES)] * zeros
            + [tile_shape] * some,
            in_specs=[spec(SMEM)] + [spec(VMEM)] * (2 + len(offsets)),
            out_specs=[spec(VMEM)] * (3 + zeros + some),
            compiler_params=params(blocks),
            cost_estimate=cost(5),
            name="basis_values",
        )(ints, points, table, *[held[e] for e in offsets])

    def pack(parts, picks):
        return pl.pallas_call(
            functools.partial(pack_kernel, picks),
            out_shape=jax.ShapeDtypeStruct(
                (len(picks), slab.shape[0] // 2, slab.shape[1]), slab.dtype
            ),
            in_specs=[spec(VMEM)] * len(parts),
            out_specs=spec(VMEM),
            compiler_params=params(blocks),
            name="pack",
        )(*parts)

    late, slabs = [], []
    if grid_count == 16:
        held[0] = near_slab
        held, other_ints, other_points, table = tied((held, other_ints, other_points, table))
        ready = list(held)
        over_x = swap(pack((held[8], held[4]), ((0, 0), (0, 1), (1, 0))), 2)
        over_z = swap(pack((held[8], held[2]), ((0, 0), (0, 1), (1, 1))), 4)
        across = swap(held[8], 6)
        points, ints, dest_mask = share(other_ints, other_points)
        *first, acc, tiles = basis_chunk(0, points, ints, ready)
        held, across, over_x, over_z, first, tiles, points = tied(
            (held, across, over_x, over_z, first, tiles, points)
        )
        parts = [*held.values(), across, over_x, over_z]
        wholes = [(e, h) for e in (*held, 14) for h in range(2)]
        picks = [(p, h) for p in range(len(held) + 1) for h in range(2)]
        picks += [(len(held) + 1 + p, h) for p in range(2) for h in range(3)]
        crossed = swap(pack(parts, picks), 1)
        second = basis_chunk(1, points, ints)
        late = [14, OVER_X, OVER_Z, tuple((e ^ 1, h) for e, h in (*wholes, *OVER_X, *OVER_Z))]
        slabs = [across, over_x, over_z, crossed]
    else:
        tiles = lax.all_gather(slab, "grid", axis=0, tiled=True)
        points, ints, dest_mask = share(other_ints, other_points)
        *first, acc = basis_chunk(0, points, ints)
        second = basis_chunk(1, points, ints)
    chunks = [first, second]
    phis, radials, bases = zip(*chunks)

    some = 1 if late else 0
    chi, rho, *_ = pl.pallas_call(
        functools.partial(rho_kernel, late, starts),
        out_shape=[f32(slots, BLOCK, point_count), f32(slots, point_count)] + [tile_shape] * some,
        in_specs=[spec(SMEM)] + [spec(VMEM)] * (len(starts) + len(late) + 1),
        out_specs=[spec(VMEM)] * (2 + some),
        input_output_aliases={1 + len(starts) + len(late): 2} if late else {},
        compiler_params=params(blocks),
        cost_estimate=cost(5),
        name="density_at_points",
    )(ints, *phis, *slabs, tiles)

    if blk_count == 2:
        other = lax.ppermute(rho, "blk", [(0, 1), (1, 0)])
    else:
        other = lax.psum(rho, "blk") - rho

    rows = 3 * NATOM // LANES + dests // LANES
    outgoing, _ = pl.pallas_call(
        functools.partial(force_kernel, starts),
        out_shape=[f32(blk_count * grid_count, rows, LANES), f32(BPD, 5, BLOCK, LANES)],
        in_specs=[spec(SMEM)] + [spec(VMEM)] * (7 + 2 * len(starts)),
        out_specs=[spec(VMEM)] * 2,
        scratch_shapes=[pltpu.VMEM((slots, point_count), jnp.float32)],
        input_output_aliases={7 + 2 * len(starts): 1},
        compiler_params=params(blocks),
        cost_estimate=cost(5),
        name="forces_and_energies",
    )(ints, points, rho, other, chi, *radials, *bases, table, dest_mask, acc)

    arrived = lax.all_to_all(outgoing, ("blk", "grid"), split_axis=0, concat_axis=0, tiled=True)

    energy, forces = pl.pallas_call(
        functools.partial(sum_kernel, blk_count),
        out_shape=[f32(1, dests // grid_count), f32(3, NATOM)],
        in_specs=[spec(VMEM)],
        out_specs=[spec(VMEM)] * 2,
        compiler_params=params(blocks),
        name="final_sums",
    )(arrived)
    return (energy.reshape(dests // grid_count), forces)


def solution(mesh):
    in_specs = (
        P("blk", "grid"),
        P("grid", None, None),
        P("grid", None),
        P("grid"),
        P(),
        P(),
        P(),
        P(),
    )
    out_specs = (P("grid"), P())
    return jax.shard_map(local, mesh=mesh, in_specs=in_specs, out_specs=out_specs, check_vma=False)
```

```python
import functools

import jax
import jax.numpy as jnp
from jax import lax
from jax.experimental import pallas as pl
from jax.experimental.pallas import tpu as pltpu
from jax.sharding import PartitionSpec as P

BLOCK = 128
BPD = 6
NATOM = 256
LANES = 128
ROWS = 32
UNROLL = 4

SLATER = 0.7386
RHO_SOFT = 0.05

VMEM = pltpu.MemorySpace.VMEM
SMEM = pltpu.MemorySpace.SMEM


def aligned(start, size):
    return pl.ds(pl.multiple_of(start, size), size)


def live_count(ints_ref):
    row = ints_ref.shape[0] - 1
    slots = ints_ref.shape[1]
    step = 1
    while step * 2 <= slots:
        step *= 2
    count = jnp.int32(0)
    while step:
        more = count + step
        found = ints_ref[row, jnp.minimum(more, slots) - 1] >= 0
        count = jnp.where(jnp.logical_and(more <= slots, found), more, count)
        step //= 2
    return count


def start_copies(pairs, sems):
    copies = [pltpu.make_async_copy(src, dst, sems.at[i]) for i, (src, dst) in enumerate(pairs)]
    for copy in copies:
        copy.start()
    return copies


def place_slabs(offsets, slabs, tiles):
    me = lax.axis_index("grid")
    for e, slab in zip(offsets, slabs):
        if isinstance(e, tuple):
            half = slab.shape[1]
            for i, (one, h) in enumerate(e):
                first = (2 * jnp.bitwise_xor(me, one) + h) * half
                tiles[aligned(first, half), :] = slab[i]
        else:
            depth = slab.shape[0]
            tiles[aligned(jnp.bitwise_xor(me, e) * depth, depth), :] = slab[...]


def pack_kernel(picks, *refs):
    *parts, out_ref = refs
    half = out_ref.shape[1]
    for i, (p, h) in enumerate(picks):
        part = parts[p]
        out_ref[i] = part[h] if len(part.shape) == 3 else part[h * half : (h + 1) * half, :]


def share_kernel(own_ints, other_ints, own_points, other_points, points_out, ints_out, dest_ref):
    rows, slots = own_ints.shape
    core = lax.rem(lax.axis_index("grid"), 2)
    own, other = live_count(own_ints), live_count(other_ints)
    count0 = jnp.where(core == 0, own, other)
    half = lax.div(own + other + 1, 2)
    base = jnp.where(core == 0, 0, half)
    count = jnp.where(core == 0, half, own + other - half)
    lanes = lax.broadcasted_iota(jnp.int32, (1, slots), 1)
    dest_ids = lax.broadcasted_iota(jnp.int32, (1, dest_ref.shape[1]), 1)
    kept = [jnp.zeros((1, slots), jnp.int32)] * rows
    for v in range(slots):
        from0 = base + v < count0
        slot = jnp.clip(base + v - jnp.where(from0, 0, count0), 0, slots - 1)
        mine = from0 == (core == 0)
        points_out[v] = jnp.where(mine, own_points[slot], other_points[slot])
        values = [jnp.where(mine, own_ints[i, slot], other_ints[i, slot]) for i in range(rows)]
        values[-1] = jnp.where(v < count, values[-1], -1)
        kept = [jnp.where(lanes == v, value, row) for value, row in zip(values, kept)]
        dest_ref[v : v + 1, :] = jnp.where(dest_ids == values[-1], 1.0, 0.0)
    ints_out[...] = jnp.concatenate(kept, axis=0)


def table_kernel(
    atom_hbm,
    expo_hbm,
    coef_hbm,
    coords_hbm,
    points_hbm,
    slab_hbm,
    table_ref,
    points_out,
    slab_out,
    atom_ref,
    expo_ref,
    coef_ref,
    coords_ref,
    sems,
):
    copies = start_copies(
        [
            (atom_hbm, atom_ref),
            (expo_hbm, expo_ref),
            (coef_hbm, coef_ref),
            (coords_hbm, coords_ref),
            (points_hbm, points_out),
            (slab_hbm, slab_out),
        ],
        sems,
    )
    for copy in copies[:4]:
        copy.wait()
    coords = coords_ref[...]
    high = coords.astype(jnp.bfloat16)
    rest = coords - high.astype(jnp.float32)
    mid = rest.astype(jnp.bfloat16)
    low = (rest - mid.astype(jnp.float32)).astype(jnp.bfloat16)
    blocks = table_ref.shape[0]
    atoms = atom_ref[...].reshape(blocks, BLOCK)
    expos = expo_ref[...].reshape(blocks, BLOCK)

    for k in range(blocks):
        atom = atoms[k : k + 1]
        onehot = jnp.where(
            lax.broadcasted_iota(jnp.int32, (NATOM, BLOCK), 0) == atom, 1.0, 0.0
        ).astype(jnp.bfloat16)
        picked = [
            jnp.dot(part, onehot, preferred_element_type=jnp.float32) for part in (high, mid, low)
        ]
        center = (picked[0] + picked[1]) + picked[2]
        coef = coef_ref[:, k * BLOCK : (k + 1) * BLOCK]
        rows = jnp.concatenate(
            [center, coef, expos[k : k + 1], atom.astype(jnp.float32)], axis=0
        )
        columns = rows.T
        for p in range(8):
            table_ref[k, p] = jnp.broadcast_to(columns[:, p : p + 1], (BLOCK, LANES))

    for copy in copies[4:]:
        copy.wait()


def chunk_steps(ints_ref, first, size):
    left = jnp.clip(live_count(ints_ref) - first, 0, size)
    return lax.div(left + (UNROLL - 1), UNROLL)


def phi_kernel(first, offsets, ints_ref, points_ref, table_ref, *refs):
    slabs = refs[: len(offsets)]
    phi_ref, radial_ref, basis_ref, *more = refs[len(offsets) :]
    if first == 0:
        more.pop(0)[...] = jnp.zeros((BPD, 5, BLOCK, LANES), jnp.float32)
    if offsets:
        place_slabs(offsets, slabs, more[0])
    blk = lax.axis_index("blk")
    length = ints_ref.shape[0] - 1
    point_count = points_ref.shape[2]

    def one_slot(s):
        for j in range(length):
            k = ints_ref[lax.rem(blk + j, length), first + s]
            for r in range(0, BLOCK, ROWS):
                sub = slice(r, r + ROWS)
                cx, cy, cz, sx, sy, sz, expo = [table_ref[k, p, sub] for p in range(7)]
                for h in range(0, point_count, LANES):
                    lanes = slice(h, h + LANES)
                    ox = points_ref[first + s, 0:1, lanes] - cx
                    oy = points_ref[first + s, 1:2, lanes] - cy
                    oz = points_ref[first + s, 2:3, lanes] - cz
                    squared = ox * ox + oy * oy + oz * oz
                    radial = jnp.exp(-expo * squared)
                    linear = 1.0 + (sx * ox + sy * oy + sz * oz)
                    basis = linear * radial
                    rows = slice(j * BLOCK + r, j * BLOCK + r + ROWS)
                    phi_ref[s, rows, lanes] = basis.astype(jnp.bfloat16)
                    if j == 0:
                        radial_ref[s, sub, lanes] = radial
                        basis_ref[s, sub, lanes] = basis

    def some_slots(i, carry):
        for u in range(2):
            one_slot(i * 2 + u)
        return carry

    steps = chunk_steps(ints_ref, first, phi_ref.shape[0]) * (UNROLL // 2)
    lax.fori_loop(0, steps, some_slots, 0)


def rho_kernel(offsets, starts, ints_ref, *refs):
    chunks = len(starts)
    phis = refs[:chunks]
    slabs = refs[chunks : chunks + len(offsets)]
    tiles, chi_ref, rho_ref, *placed = refs[chunks + len(offsets) :]
    if offsets:
        tiles = placed[0]
        place_slabs(offsets, slabs, tiles)
    blk = lax.axis_index("blk")
    length = ints_ref.shape[0] - 1
    rho_ref[...] = jnp.zeros_like(rho_ref)

    for c, phi_ref in enumerate(phis):
        size = phi_ref.shape[0]

        def one_slot(s, first=starts[c], phi_ref=phi_ref):
            slot = first + s
            own = ints_ref[blk, slot]
            cols = aligned((own - blk * BPD) * BLOCK, BLOCK)
            left = [tiles[aligned(own * BLOCK, BLOCK), cols]]
            for j in range(1, length):
                k = ints_ref[lax.rem(blk + j, length), slot]
                left.append(tiles[aligned(k * BLOCK, BLOCK), cols].T)
            chi = jnp.dot(
                jnp.concatenate(left, axis=1), phi_ref[s], preferred_element_type=jnp.float32
            )
            phi = phi_ref[s, 0:BLOCK, :]
            chi_ref[slot] = chi
            rho_ref[pl.ds(slot, 1), :] = jnp.sum(
                phi.astype(jnp.float32) * chi, axis=0, keepdims=True
            )

        def some_slots(i, carry, one_slot=one_slot):
            for u in range(UNROLL):
                one_slot(i * UNROLL + u)
            return carry

        lax.fori_loop(0, chunk_steps(ints_ref, starts[c], size), some_slots, 0)


def force_kernel(starts, ints_ref, points_ref, rho_a_ref, rho_b_ref, chi_ref, *refs):
    chunks = len(starts)
    radials = refs[:chunks]
    bases = refs[chunks : 2 * chunks]
    table_ref, dest_ref, _, out_ref, acc, pot_ref = refs[2 * chunks :]
    blk = lax.axis_index("blk")
    slots, _, point_count = points_ref.shape
    dests = dest_ref.shape[1]
    live = live_count(ints_ref)
    rho = rho_a_ref[...] + rho_b_ref[...]
    weight = points_ref[:, 3, :]
    log_sq = jnp.log(rho * rho + RHO_SOFT * RHO_SOFT)
    pot = weight * (-(4.0 / 3.0) * SLATER) * rho * jnp.exp(log_sq * (-1.0 / 3.0))
    slot_ids = lax.broadcasted_iota(jnp.int32, (slots, 1), 0)
    pot_ref[...] = jnp.where(slot_ids < live, pot, 0.0)
    energies = jnp.sum(weight * -SLATER * jnp.exp(log_sq * (2.0 / 3.0)), axis=1, keepdims=True)

    for c in range(chunks):
        radial_ref, basis_ref = radials[c], bases[c]
        size = radial_ref.shape[0]

        def one_slot(s, first=starts[c], radial_ref=radial_ref, basis_ref=basis_ref):
            slot = first + s
            own = ints_ref[blk, slot] - blk * BPD
            pots = pot_ref[pl.ds(slot, 1), :]
            for r in range(0, BLOCK, ROWS):
                sub = slice(r, r + ROWS)
                sums = None
                for h in range(0, point_count, LANES):
                    lanes = slice(h, h + LANES)
                    u = chi_ref[slot, sub, lanes] * pots[:, lanes]
                    ub = u * basis_ref[s, sub, lanes]
                    terms = (
                        u * radial_ref[s, sub, lanes],
                        ub,
                        ub * points_ref[slot, 0:1, lanes],
                        ub * points_ref[slot, 1:2, lanes],
                        ub * points_ref[slot, 2:3, lanes],
                    )
                    sums = terms if sums is None else [a + b for a, b in zip(sums, terms)]
                for q in range(5):
                    acc[own, q, sub] += sums[q]

        def some_slots(i, carry, one_slot=one_slot):
            for u in range(UNROLL):
                one_slot(i * UNROLL + u)
            return carry

        lax.fori_loop(0, chunk_steps(ints_ref, starts[c], size), some_slots, 0)

    lane_ids = lax.broadcasted_iota(jnp.int32, (1, LANES), 1).astype(jnp.float32)

    totals = [jnp.zeros((8, LANES), jnp.float32)] * (3 * NATOM // LANES)
    for b in range(BPD):
        k = blk * BPD + b
        for r in range(0, BLOCK, ROWS):
            sub = slice(r, r + ROWS)
            parts = [acc[b, q, sub] for q in range(5)]
            doubled = 2.0 * table_ref[k, 6, sub]
            atom = table_ref[k, 7, sub]
            for c in range(3):
                force = table_ref[k, 3 + c, sub] * parts[0] - doubled * (
                    parts[2 + c] - table_ref[k, c, sub] * parts[1]
                )
                column = 2.0 * jnp.sum(force, axis=1, keepdims=True)
                for h in range(NATOM // LANES):
                    hit = jnp.where(atom == lane_ids + float(h * LANES), column, 0.0)
                    i = c * (NATOM // LANES) + h
                    totals[i] = totals[i] + sum(hit[i8 : i8 + 8] for i8 in range(0, ROWS, 8))
    rows = [jnp.sum(t, axis=0, keepdims=True) for t in totals]
    moved = jnp.sum(dest_ref[...] * energies, axis=0, keepdims=True)
    rows += [moved[:, h : h + LANES] for h in range(0, dests, LANES)]
    packed = jnp.concatenate(rows, axis=0)
    for i in range(out_ref.shape[0]):
        out_ref[i] = packed


def sum_kernel(copies, arrived_ref, energy_ref, forces_ref):
    me = lax.axis_index("grid")
    total = jnp.sum(arrived_ref[...], axis=0)
    per = NATOM // LANES
    for c in range(3):
        for h in range(per):
            forces_ref[c : c + 1, h * LANES : (h + 1) * LANES] = total[c * per + h : c * per + h + 1]
    width = energy_ref.shape[1]
    first = me * width
    energy = jnp.zeros((1, LANES), jnp.float32)
    for i in range(3 * per, total.shape[0]):
        chosen = lax.div(first, LANES) == i - 3 * per
        energy = jnp.where(chosen, total[i : i + 1], energy)
    turn = lax.rem(LANES - lax.rem(first, LANES), LANES)
    energy = pltpu.roll(jnp.broadcast_to(energy, (8, LANES)), turn, 1)
    energy_ref[...] = energy[0:1, 0:width] * (1.0 / copies)


def swap(array, offset):
    count = lax.axis_size("grid")
    return lax.ppermute(array, "grid", [(i, i ^ offset) for i in range(count)])


FIRST = (8, 4, 2)
OVER_X = ((10, 0), (10, 1), (6, 0))
OVER_Z = ((12, 0), (12, 1), (6, 1))


def in_hbm(array):
    return pltpu.with_memory_space_constraint(array, pltpu.HBM)


def spec(space):
    return pl.BlockSpec(memory_space=space)


def params(blocks):
    return pltpu.CompilerParams(vmem_limit_bytes=blocks * 1024 * 1024)


def cost(nominal_us):
    return pl.CostEstimate(
        flops=0, bytes_accessed=int(nominal_us * 3.69e6), transcendentals=0
    )


def f32(*shape):
    return jax.ShapeDtypeStruct(shape, jnp.float32)


def local(density, points, sig_blocks, migration, atom_coords, exponents, shape_coef, func_atom):
    grid_count = lax.axis_size("grid")
    blk_count = lax.axis_size("blk")
    slots, _, point_count = points.shape
    length = sig_blocks.shape[1]
    functions = exponents.shape[0]
    blocks = functions // BLOCK
    dests = grid_count * (slots // 2)
    sizes = [slots // 4 * 3, slots // 4]
    starts = [0, slots // 4 * 3]
    tied = lax.optimization_barrier

    slab = density.T
    held = {0: slab}
    if grid_count == 16:
        for e in FIRST:
            held[e] = swap(slab, e)
    ints = jnp.concatenate([sig_blocks.T, migration[None]], axis=0)
    other_ints, other_points = swap(ints, 1), swap(points, 1)
    table, points, near_slab = pl.pallas_call(
        table_kernel,
        out_shape=[
            f32(blocks, 8, BLOCK, LANES),
            f32(*points.shape),
            jax.ShapeDtypeStruct(slab.shape, slab.dtype),
        ],
        in_specs=[spec(pltpu.HBM)] * 6,
        out_specs=[spec(VMEM)] * 3,
        scratch_shapes=[
            pltpu.VMEM((functions,), jnp.int32),
            pltpu.VMEM((functions,), jnp.float32),
            pltpu.VMEM((3, functions), jnp.float32),
            pltpu.VMEM((3, NATOM), jnp.float32),
            pltpu.SemaphoreType.DMA((6,)),
        ],
        compiler_params=params(blocks),
        cost_estimate=cost(4),
        name="param_table",
    )(*[in_hbm(a) for a in (func_atom, exponents, shape_coef, atom_coords, points, slab)])

    def share(other_ints, other_points):
        return pl.pallas_call(
            share_kernel,
            out_shape=[
                f32(*points.shape),
                jax.ShapeDtypeStruct(ints.shape, jnp.int32),
                f32(slots, dests),
            ],
            in_specs=[spec(SMEM)] * 2 + [spec(VMEM)] * 2,
            out_specs=[spec(VMEM)] * 3,
            compiler_params=params(blocks),
            cost_estimate=cost(1),
            name="shared_slots",
        )(ints, other_ints, points, other_points)

    tile_shape = jax.ShapeDtypeStruct((functions, BPD * BLOCK), jnp.bfloat16)

    def basis_chunk(c, points, ints, offsets=()):
        some = 1 if offsets else 0
        zeros = 1 if c == 0 else 0
        return pl.pallas_call(
            functools.partial(phi_kernel, starts[c], offsets),
            out_shape=[
                jax.ShapeDtypeStruct((sizes[c], length * BLOCK, point_count), jnp.bfloat16),
                f32(sizes[c], BLOCK, point_count),
                f32(sizes[c], BLOCK, point_count),
            ]
            + [f32(BPD, 5, BLOCK, LANES)] * zeros
            + [tile_shape] * some,
            in_specs=[spec(SMEM)] + [spec(VMEM)] * (2 + len(offsets)),
            out_specs=[spec(VMEM)] * (3 + zeros + some),
            compiler_params=params(blocks),
            cost_estimate=cost(5),
            name="basis_values",
        )(ints, points, table, *[held[e] for e in offsets])

    def pack(parts, picks):
        return pl.pallas_call(
            functools.partial(pack_kernel, picks),
            out_shape=jax.ShapeDtypeStruct(
                (len(picks), slab.shape[0] // 2, slab.shape[1]), slab.dtype
            ),
            in_specs=[spec(VMEM)] * len(parts),
            out_specs=spec(VMEM),
            compiler_params=params(blocks),
            name="pack",
        )(*parts)

    late, slabs = [], []
    if grid_count == 16:
        held[0] = near_slab
        held, other_ints, other_points, table = tied((held, other_ints, other_points, table))
        ready = list(held)
        over_x = swap(pack((held[8], held[4]), ((0, 0), (0, 1), (1, 0))), 2)
        over_z = swap(pack((held[8], held[2]), ((0, 0), (0, 1), (1, 1))), 4)
        across = swap(held[8], 6)
        early = tuple((e ^ 1, h) for e in ready for h in range(2))
        picks = [(p, h) for p in range(len(ready)) for h in range(2)]
        crossed_early = swap(pack([held[e] for e in ready], picks), 1)
        points, ints, dest_mask = share(other_ints, other_points)
        *first, acc, tiles = basis_chunk(0, points, ints, ready)
        held, across, over_x, over_z, first, tiles, points = tied(
            (held, across, over_x, over_z, first, tiles, points)
        )
        halves = [(p, h) for p in range(3) for h in range(3)]
        crossed = swap(pack((across, over_x, over_z), [(0, 0), (0, 1), *halves[3:]]), 1)
        second = basis_chunk(1, points, ints)
        pieces = ((14, 0), (14, 1), *OVER_X, *OVER_Z)
        late = [14, OVER_X, OVER_Z, tuple((e ^ 1, h) for e, h in pieces), early]
        slabs = [across, over_x, over_z, crossed, crossed_early]
    else:
        tiles = lax.all_gather(slab, "grid", axis=0, tiled=True)
        points, ints, dest_mask = share(other_ints, other_points)
        *first, acc = basis_chunk(0, points, ints)
        second = basis_chunk(1, points, ints)
    chunks = [first, second]
    phis, radials, bases = zip(*chunks)

    some = 1 if late else 0
    chi, rho, *_ = pl.pallas_call(
        functools.partial(rho_kernel, late, starts),
        out_shape=[f32(slots, BLOCK, point_count), f32(slots, point_count)] + [tile_shape] * some,
        in_specs=[spec(SMEM)] + [spec(VMEM)] * (len(starts) + len(late) + 1),
        out_specs=[spec(VMEM)] * (2 + some),
        input_output_aliases={1 + len(starts) + len(late): 2} if late else {},
        compiler_params=params(blocks),
        cost_estimate=cost(5),
        name="density_at_points",
    )(ints, *phis, *slabs, tiles)

    if blk_count == 2:
        other = lax.ppermute(rho, "blk", [(0, 1), (1, 0)])
    else:
        other = lax.psum(rho, "blk") - rho

    rows = 3 * NATOM // LANES + dests // LANES
    outgoing, _ = pl.pallas_call(
        functools.partial(force_kernel, starts),
        out_shape=[f32(blk_count * grid_count, rows, LANES), f32(BPD, 5, BLOCK, LANES)],
        in_specs=[spec(SMEM)] + [spec(VMEM)] * (7 + 2 * len(starts)),
        out_specs=[spec(VMEM)] * 2,
        scratch_shapes=[pltpu.VMEM((slots, point_count), jnp.float32)],
        input_output_aliases={7 + 2 * len(starts): 1},
        compiler_params=params(blocks),
        cost_estimate=cost(5),
        name="forces_and_energies",
    )(ints, points, rho, other, chi, *radials, *bases, table, dest_mask, acc)

    arrived = lax.all_to_all(outgoing, ("blk", "grid"), split_axis=0, concat_axis=0, tiled=True)

    energy, forces = pl.pallas_call(
        functools.partial(sum_kernel, blk_count),
        out_shape=[f32(1, dests // grid_count), f32(3, NATOM)],
        in_specs=[spec(VMEM)],
        out_specs=[spec(VMEM)] * 2,
        compiler_params=params(blocks),
        name="final_sums",
    )(arrived)
    return (energy.reshape(dests // grid_count), forces)


def solution(mesh):
    in_specs = (
        P("blk", "grid"),
        P("grid", None, None),
        P("grid", None),
        P("grid"),
        P(),
        P(),
        P(),
        P(),
    )
    out_specs = (P("grid"), P())
    return jax.shard_map(local, mesh=mesh, in_specs=in_specs, out_specs=out_specs, check_vma=False)
```

```python
import functools

import jax
import jax.numpy as jnp
from jax import lax
from jax.experimental import pallas as pl
from jax.experimental.pallas import tpu as pltpu
from jax.sharding import PartitionSpec as P

BLOCK = 128
BPD = 6
NATOM = 256
LANES = 128
ROWS = 32
UNROLL = 4

SLATER = 0.7386
RHO_SOFT = 0.05

VMEM = pltpu.MemorySpace.VMEM
SMEM = pltpu.MemorySpace.SMEM


def aligned(start, size):
    return pl.ds(pl.multiple_of(start, size), size)


def live_count(ints_ref):
    row = ints_ref.shape[0] - 1
    slots = ints_ref.shape[1]
    step = 1
    while step * 2 <= slots:
        step *= 2
    count = jnp.int32(0)
    while step:
        more = count + step
        found = ints_ref[row, jnp.minimum(more, slots) - 1] >= 0
        count = jnp.where(jnp.logical_and(more <= slots, found), more, count)
        step //= 2
    return count


def start_copies(pairs, sems):
    copies = [pltpu.make_async_copy(src, dst, sems.at[i]) for i, (src, dst) in enumerate(pairs)]
    for copy in copies:
        copy.start()
    return copies


def place_slabs(offsets, slabs, tiles):
    me = lax.axis_index("grid")
    for e, slab in zip(offsets, slabs):
        if isinstance(e, tuple):
            half = slab.shape[1]
            for i, (one, h) in enumerate(e):
                first = (2 * jnp.bitwise_xor(me, one) + h) * half
                tiles[aligned(first, half), :] = slab[i]
        else:
            depth = slab.shape[0]
            tiles[aligned(jnp.bitwise_xor(me, e) * depth, depth), :] = slab[...]


def pack_kernel(picks, *refs):
    *parts, out_ref = refs
    half = out_ref.shape[1]
    for i, (p, h) in enumerate(picks):
        part = parts[p]
        out_ref[i] = part[h] if len(part.shape) == 3 else part[h * half : (h + 1) * half, :]


def share_kernel(own_ints, other_ints, own_points, other_points, points_out, ints_out, dest_ref):
    rows, slots = own_ints.shape
    core = lax.rem(lax.axis_index("grid"), 2)
    own, other = live_count(own_ints), live_count(other_ints)
    count0 = jnp.where(core == 0, own, other)
    half = lax.div(own + other + 1, 2)
    base = jnp.where(core == 0, 0, half)
    count = jnp.where(core == 0, half, own + other - half)
    lanes = lax.broadcasted_iota(jnp.int32, (1, slots), 1)
    dest_ids = lax.broadcasted_iota(jnp.int32, (1, dest_ref.shape[1]), 1)
    kept = [jnp.zeros((1, slots), jnp.int32)] * rows
    for v in range(slots):
        from0 = base + v < count0
        slot = jnp.clip(base + v - jnp.where(from0, 0, count0), 0, slots - 1)
        mine = from0 == (core == 0)
        points_out[v] = jnp.where(mine, own_points[slot], other_points[slot])
        values = [jnp.where(mine, own_ints[i, slot], other_ints[i, slot]) for i in range(rows)]
        values[-1] = jnp.where(v < count, values[-1], -1)
        kept = [jnp.where(lanes == v, value, row) for value, row in zip(values, kept)]
        dest_ref[v : v + 1, :] = jnp.where(dest_ids == values[-1], 1.0, 0.0)
    ints_out[...] = jnp.concatenate(kept, axis=0)


def table_kernel(
    atom_hbm,
    expo_hbm,
    coef_hbm,
    coords_hbm,
    points_hbm,
    slab_hbm,
    table_ref,
    points_out,
    slab_out,
    atom_ref,
    expo_ref,
    coef_ref,
    coords_ref,
    sems,
):
    copies = start_copies(
        [
            (atom_hbm, atom_ref),
            (expo_hbm, expo_ref),
            (coef_hbm, coef_ref),
            (coords_hbm, coords_ref),
            (points_hbm, points_out),
            (slab_hbm, slab_out),
        ],
        sems,
    )
    for copy in copies[:4]:
        copy.wait()
    coords = coords_ref[...]
    high = coords.astype(jnp.bfloat16)
    rest = coords - high.astype(jnp.float32)
    mid = rest.astype(jnp.bfloat16)
    low = (rest - mid.astype(jnp.float32)).astype(jnp.bfloat16)
    blocks = table_ref.shape[0]
    atoms = atom_ref[...].reshape(blocks, BLOCK)
    expos = expo_ref[...].reshape(blocks, BLOCK)

    for k in range(blocks):
        atom = atoms[k : k + 1]
        onehot = jnp.where(
            lax.broadcasted_iota(jnp.int32, (NATOM, BLOCK), 0) == atom, 1.0, 0.0
        ).astype(jnp.bfloat16)
        picked = [
            jnp.dot(part, onehot, preferred_element_type=jnp.float32) for part in (high, mid, low)
        ]
        center = (picked[0] + picked[1]) + picked[2]
        coef = coef_ref[:, k * BLOCK : (k + 1) * BLOCK]
        rows = jnp.concatenate(
            [center, coef, expos[k : k + 1], atom.astype(jnp.float32)], axis=0
        )
        columns = rows.T
        for p in range(8):
            table_ref[k, p] = jnp.broadcast_to(columns[:, p : p + 1], (BLOCK, LANES))

    for copy in copies[4:]:
        copy.wait()


def chunk_steps(ints_ref, first, size):
    left = jnp.clip(live_count(ints_ref) - first, 0, size)
    return lax.div(left + (UNROLL - 1), UNROLL)


def phi_kernel(first, offsets, ints_ref, points_ref, table_ref, *refs):
    slabs = refs[: len(offsets)]
    phi_ref, radial_ref, basis_ref, *more = refs[len(offsets) :]
    if first == 0:
        more.pop(0)[...] = jnp.zeros((BPD, 5, BLOCK, LANES), jnp.float32)
    if offsets:
        place_slabs(offsets, slabs, more[0])
    blk = lax.axis_index("blk")
    length = ints_ref.shape[0] - 1
    point_count = points_ref.shape[2]

    def one_slot(s):
        for j in range(length):
            k = ints_ref[lax.rem(blk + j, length), first + s]
            for r in range(0, BLOCK, ROWS):
                sub = slice(r, r + ROWS)
                cx, cy, cz, sx, sy, sz, expo = [table_ref[k, p, sub] for p in range(7)]
                for h in range(0, point_count, LANES):
                    lanes = slice(h, h + LANES)
                    ox = points_ref[first + s, 0:1, lanes] - cx
                    oy = points_ref[first + s, 1:2, lanes] - cy
                    oz = points_ref[first + s, 2:3, lanes] - cz
                    squared = ox * ox + oy * oy + oz * oz
                    radial = jnp.exp(-expo * squared)
                    linear = 1.0 + (sx * ox + sy * oy + sz * oz)
                    basis = linear * radial
                    rows = slice(j * BLOCK + r, j * BLOCK + r + ROWS)
                    phi_ref[s, rows, lanes] = basis.astype(jnp.bfloat16)
                    if j == 0:
                        radial_ref[s, sub, lanes] = radial
                        basis_ref[s, sub, lanes] = basis

    def some_slots(i, carry):
        for u in range(2):
            one_slot(i * 2 + u)
        return carry

    steps = chunk_steps(ints_ref, first, phi_ref.shape[0]) * (UNROLL // 2)
    lax.fori_loop(0, steps, some_slots, 0)


def rho_kernel(offsets, starts, ints_ref, *refs):
    chunks = len(starts)
    phis = refs[:chunks]
    slabs = refs[chunks : chunks + len(offsets)]
    tiles, chi_ref, rho_ref, *placed = refs[chunks + len(offsets) :]
    if offsets:
        tiles = placed[0]
        place_slabs(offsets, slabs, tiles)
    blk = lax.axis_index("blk")
    length = ints_ref.shape[0] - 1
    rho_ref[...] = jnp.zeros_like(rho_ref)

    for c, phi_ref in enumerate(phis):
        size = phi_ref.shape[0]

        def one_slot(s, first=starts[c], phi_ref=phi_ref):
            slot = first + s
            own = ints_ref[blk, slot]
            cols = aligned((own - blk * BPD) * BLOCK, BLOCK)
            left = [tiles[aligned(own * BLOCK, BLOCK), cols]]
            for j in range(1, length):
                k = ints_ref[lax.rem(blk + j, length), slot]
                left.append(tiles[aligned(k * BLOCK, BLOCK), cols].T)
            chi = jnp.dot(
                jnp.concatenate(left, axis=1), phi_ref[s], preferred_element_type=jnp.float32
            )
            phi = phi_ref[s, 0:BLOCK, :]
            chi_ref[slot] = chi
            rho_ref[pl.ds(slot, 1), :] = jnp.sum(
                phi.astype(jnp.float32) * chi, axis=0, keepdims=True
            )

        def some_slots(i, carry, one_slot=one_slot):
            for u in range(UNROLL):
                one_slot(i * UNROLL + u)
            return carry

        lax.fori_loop(0, chunk_steps(ints_ref, starts[c], size), some_slots, 0)


def force_kernel(starts, ints_ref, points_ref, rho_a_ref, rho_b_ref, chi_ref, *refs):
    chunks = len(starts)
    radials = refs[:chunks]
    bases = refs[chunks : 2 * chunks]
    table_ref, dest_ref, _, out_ref, acc, pot_ref = refs[2 * chunks :]
    blk = lax.axis_index("blk")
    slots, _, point_count = points_ref.shape
    dests = dest_ref.shape[1]
    live = live_count(ints_ref)
    rho = rho_a_ref[...] + rho_b_ref[...]
    weight = points_ref[:, 3, :]
    log_sq = jnp.log(rho * rho + RHO_SOFT * RHO_SOFT)
    pot = weight * (-(4.0 / 3.0) * SLATER) * rho * jnp.exp(log_sq * (-1.0 / 3.0))
    slot_ids = lax.broadcasted_iota(jnp.int32, (slots, 1), 0)
    pot_ref[...] = jnp.where(slot_ids < live, pot, 0.0)
    energies = jnp.sum(weight * -SLATER * jnp.exp(log_sq * (2.0 / 3.0)), axis=1, keepdims=True)

    for c in range(chunks):
        radial_ref, basis_ref = radials[c], bases[c]
        size = radial_ref.shape[0]

        def one_slot(s, first=starts[c], radial_ref=radial_ref, basis_ref=basis_ref):
            slot = first + s
            own = ints_ref[blk, slot] - blk * BPD
            pots = pot_ref[pl.ds(slot, 1), :]
            for r in range(0, BLOCK, ROWS):
                sub = slice(r, r + ROWS)
                sums = None
                for h in range(0, point_count, LANES):
                    lanes = slice(h, h + LANES)
                    u = chi_ref[slot, sub, lanes] * pots[:, lanes]
                    ub = u * basis_ref[s, sub, lanes]
                    terms = (
                        u * radial_ref[s, sub, lanes],
                        ub,
                        ub * points_ref[slot, 0:1, lanes],
                        ub * points_ref[slot, 1:2, lanes],
                        ub * points_ref[slot, 2:3, lanes],
                    )
                    sums = terms if sums is None else [a + b for a, b in zip(sums, terms)]
                for q in range(5):
                    acc[own, q, sub] += sums[q]

        def some_slots(i, carry, one_slot=one_slot):
            for u in range(UNROLL):
                one_slot(i * UNROLL + u)
            return carry

        lax.fori_loop(0, chunk_steps(ints_ref, starts[c], size), some_slots, 0)

    lane_ids = lax.broadcasted_iota(jnp.int32, (1, LANES), 1).astype(jnp.float32)

    totals = [jnp.zeros((8, LANES), jnp.float32)] * (3 * NATOM // LANES)
    for b in range(BPD):
        k = blk * BPD + b
        for r in range(0, BLOCK, ROWS):
            sub = slice(r, r + ROWS)
            parts = [acc[b, q, sub] for q in range(5)]
            doubled = 2.0 * table_ref[k, 6, sub]
            atom = table_ref[k, 7, sub]
            for c in range(3):
                force = table_ref[k, 3 + c, sub] * parts[0] - doubled * (
                    parts[2 + c] - table_ref[k, c, sub] * parts[1]
                )
                column = 2.0 * jnp.sum(force, axis=1, keepdims=True)
                for h in range(NATOM // LANES):
                    hit = jnp.where(atom == lane_ids + float(h * LANES), column, 0.0)
                    i = c * (NATOM // LANES) + h
                    totals[i] = totals[i] + sum(hit[i8 : i8 + 8] for i8 in range(0, ROWS, 8))
    rows = [jnp.sum(t, axis=0, keepdims=True) for t in totals]
    moved = jnp.sum(dest_ref[...] * energies, axis=0, keepdims=True)
    rows += [moved[:, h : h + LANES] for h in range(0, dests, LANES)]
    packed = jnp.concatenate(rows, axis=0)
    if len(out_ref.shape) == 2:
        out_ref[...] = packed
    else:
        for i in range(out_ref.shape[0]):
            out_ref[i] = packed


def group_total(refs):
    parts = [ref[...] for ref in refs]
    while len(parts) > 1:
        parts = [a + b for a, b in zip(parts[::2], parts[1::2])]
    return parts[0]


def group_kernel(*refs):
    *parts, out_ref = refs
    out_ref[...] = group_total(parts)


def sum_kernel(copies, *refs):
    *arrived, energy_ref, forces_ref = refs
    me = lax.axis_index("grid")
    if len(arrived) == 1:
        total = jnp.sum(arrived[0][...], axis=0)
    else:
        total = group_total(arrived)
    per = NATOM // LANES
    for c in range(3):
        for h in range(per):
            forces_ref[c : c + 1, h * LANES : (h + 1) * LANES] = total[c * per + h : c * per + h + 1]
    width = energy_ref.shape[1]
    first = me * width
    energy = jnp.zeros((1, LANES), jnp.float32)
    for i in range(3 * per, total.shape[0]):
        chosen = lax.div(first, LANES) == i - 3 * per
        energy = jnp.where(chosen, total[i : i + 1], energy)
    turn = lax.rem(LANES - lax.rem(first, LANES), LANES)
    energy = pltpu.roll(jnp.broadcast_to(energy, (8, LANES)), turn, 1)
    energy_ref[...] = energy[0:1, 0:width] * (1.0 / copies)


def swap(array, offset):
    count = lax.axis_size("grid")
    return lax.ppermute(array, "grid", [(i, i ^ offset) for i in range(count)])


FIRST = (8, 4, 2)
OVER_X = ((10, 0), (10, 1), (6, 0))
OVER_Z = ((12, 0), (12, 1), (6, 1))


def in_hbm(array):
    return pltpu.with_memory_space_constraint(array, pltpu.HBM)


def spec(space):
    return pl.BlockSpec(memory_space=space)


def params(blocks):
    return pltpu.CompilerParams(vmem_limit_bytes=blocks * 1024 * 1024)


def cost(nominal_us):
    return pl.CostEstimate(
        flops=0, bytes_accessed=int(nominal_us * 3.69e6), transcendentals=0
    )


def f32(*shape):
    return jax.ShapeDtypeStruct(shape, jnp.float32)


def local(density, points, sig_blocks, migration, atom_coords, exponents, shape_coef, func_atom):
    grid_count = lax.axis_size("grid")
    blk_count = lax.axis_size("blk")
    slots, _, point_count = points.shape
    length = sig_blocks.shape[1]
    functions = exponents.shape[0]
    blocks = functions // BLOCK
    dests = grid_count * (slots // 2)
    sizes = [slots // 4 * 3, slots // 4]
    starts = [0, slots // 4 * 3]
    tied = lax.optimization_barrier

    slab = density.T
    held = {0: slab}
    if grid_count == 16:
        for e in FIRST:
            held[e] = swap(slab, e)
    ints = jnp.concatenate([sig_blocks.T, migration[None]], axis=0)
    other_ints, other_points = swap(ints, 1), swap(points, 1)
    table, points, near_slab = pl.pallas_call(
        table_kernel,
        out_shape=[
            f32(blocks, 8, BLOCK, LANES),
            f32(*points.shape),
            jax.ShapeDtypeStruct(slab.shape, slab.dtype),
        ],
        in_specs=[spec(pltpu.HBM)] * 6,
        out_specs=[spec(VMEM)] * 3,
        scratch_shapes=[
            pltpu.VMEM((functions,), jnp.int32),
            pltpu.VMEM((functions,), jnp.float32),
            pltpu.VMEM((3, functions), jnp.float32),
            pltpu.VMEM((3, NATOM), jnp.float32),
            pltpu.SemaphoreType.DMA((6,)),
        ],
        compiler_params=params(blocks),
        cost_estimate=cost(4),
        name="param_table",
    )(*[in_hbm(a) for a in (func_atom, exponents, shape_coef, atom_coords, points, slab)])

    def share(other_ints, other_points):
        return pl.pallas_call(
            share_kernel,
            out_shape=[
                f32(*points.shape),
                jax.ShapeDtypeStruct(ints.shape, jnp.int32),
                f32(slots, dests),
            ],
            in_specs=[spec(SMEM)] * 2 + [spec(VMEM)] * 2,
            out_specs=[spec(VMEM)] * 3,
            compiler_params=params(blocks),
            cost_estimate=cost(1),
            name="shared_slots",
        )(ints, other_ints, points, other_points)

    tile_shape = jax.ShapeDtypeStruct((functions, BPD * BLOCK), jnp.bfloat16)

    def basis_chunk(c, points, ints, offsets=()):
        some = 1 if offsets else 0
        zeros = 1 if c == 0 else 0
        return pl.pallas_call(
            functools.partial(phi_kernel, starts[c], offsets),
            out_shape=[
                jax.ShapeDtypeStruct((sizes[c], length * BLOCK, point_count), jnp.bfloat16),
                f32(sizes[c], BLOCK, point_count),
                f32(sizes[c], BLOCK, point_count),
            ]
            + [f32(BPD, 5, BLOCK, LANES)] * zeros
            + [tile_shape] * some,
            in_specs=[spec(SMEM)] + [spec(VMEM)] * (2 + len(offsets)),
            out_specs=[spec(VMEM)] * (3 + zeros + some),
            compiler_params=params(blocks),
            cost_estimate=cost(5),
            name="basis_values",
        )(ints, points, table, *[held[e] for e in offsets])

    def pack(parts, picks):
        return pl.pallas_call(
            functools.partial(pack_kernel, picks),
            out_shape=jax.ShapeDtypeStruct(
                (len(picks), slab.shape[0] // 2, slab.shape[1]), slab.dtype
            ),
            in_specs=[spec(VMEM)] * len(parts),
            out_specs=spec(VMEM),
            compiler_params=params(blocks),
            name="pack",
        )(*parts)

    late, slabs = [], []
    if grid_count == 16:
        held[0] = near_slab
        held, other_ints, other_points, table = tied((held, other_ints, other_points, table))
        ready = list(held)
        over_x = swap(pack((held[8], held[4]), ((0, 0), (0, 1), (1, 0))), 2)
        over_z = swap(pack((held[8], held[2]), ((0, 0), (0, 1), (1, 1))), 4)
        across = swap(held[8], 6)
        early = tuple((e ^ 1, h) for e in ready for h in range(2))
        picks = [(p, h) for p in range(len(ready)) for h in range(2)]
        crossed_early = swap(pack([held[e] for e in ready], picks), 1)
        points, ints, dest_mask = share(other_ints, other_points)
        *first, acc, tiles = basis_chunk(0, points, ints, ready)
        held, across, over_x, over_z, first, tiles, points = tied(
            (held, across, over_x, over_z, first, tiles, points)
        )
        halves = [(p, h) for p in range(3) for h in range(3)]
        crossed = swap(pack((across, over_x, over_z), [(0, 0), (0, 1), *halves[3:]]), 1)
        second = basis_chunk(1, points, ints)
        pieces = ((14, 0), (14, 1), *OVER_X, *OVER_Z)
        late = [14, OVER_X, OVER_Z, tuple((e ^ 1, h) for e, h in pieces), early]
        slabs = [across, over_x, over_z, crossed, crossed_early]
    else:
        tiles = lax.all_gather(slab, "grid", axis=0, tiled=True)
        points, ints, dest_mask = share(other_ints, other_points)
        *first, acc = basis_chunk(0, points, ints)
        second = basis_chunk(1, points, ints)
    chunks = [first, second]
    phis, radials, bases = zip(*chunks)

    some = 1 if late else 0
    chi, rho, *_ = pl.pallas_call(
        functools.partial(rho_kernel, late, starts),
        out_shape=[f32(slots, BLOCK, point_count), f32(slots, point_count)] + [tile_shape] * some,
        in_specs=[spec(SMEM)] + [spec(VMEM)] * (len(starts) + len(late) + 1),
        out_specs=[spec(VMEM)] * (2 + some),
        input_output_aliases={1 + len(starts) + len(late): 2} if late else {},
        compiler_params=params(blocks),
        cost_estimate=cost(5),
        name="density_at_points",
    )(ints, *phis, *slabs, tiles)

    if blk_count == 2:
        other = lax.ppermute(rho, "blk", [(0, 1), (1, 0)])
    else:
        other = lax.psum(rho, "blk") - rho

    rows = 3 * NATOM // LANES + dests // LANES
    grouped = (blk_count, grid_count) == (2, 16)
    outgoing, _ = pl.pallas_call(
        functools.partial(force_kernel, starts),
        out_shape=[
            f32(rows, LANES) if grouped else f32(blk_count * grid_count, rows, LANES),
            f32(BPD, 5, BLOCK, LANES),
        ],
        in_specs=[spec(SMEM)] + [spec(VMEM)] * (7 + 2 * len(starts)),
        out_specs=[spec(VMEM)] * 2,
        scratch_shapes=[pltpu.VMEM((slots, point_count), jnp.float32)],
        input_output_aliases={7 + 2 * len(starts): 1},
        compiler_params=params(blocks),
        cost_estimate=cost(5),
        name="forces_and_energies",
    )(ints, points, rho, other, chi, *radials, *bases, table, dest_mask, acc)

    if grouped:
        def exchanged(part, offsets):
            pairs = [[(i, i ^ e) for i in range(blk_count * grid_count)] for e in offsets]
            return [part] + [lax.ppermute(part, ("blk", "grid"), perm) for perm in pairs]

        arrived = [outgoing]
        for offsets in ((1, grid_count, grid_count + 1), (2, 4, 6), (8,)):
            if len(arrived) > 1:
                outgoing = pl.pallas_call(
                    group_kernel,
                    out_shape=f32(rows, LANES),
                    in_specs=[spec(VMEM)] * len(arrived),
                    out_specs=spec(VMEM),
                    compiler_params=params(blocks),
                    name="group_sums",
                )(*arrived)
            arrived = exchanged(outgoing, offsets)
    else:
        arrived = [
            lax.all_to_all(outgoing, ("blk", "grid"), split_axis=0, concat_axis=0, tiled=True)
        ]

    energy, forces = pl.pallas_call(
        functools.partial(sum_kernel, blk_count),
        out_shape=[f32(1, dests // grid_count), f32(3, NATOM)],
        in_specs=[spec(VMEM)] * len(arrived),
        out_specs=[spec(VMEM)] * 2,
        compiler_params=params(blocks),
        name="final_sums",
    )(*arrived)
    return (energy.reshape(dests // grid_count), forces)


def solution(mesh):
    in_specs = (
        P("blk", "grid"),
        P("grid", None, None),
        P("grid", None),
        P("grid"),
        P(),
        P(),
        P(),
        P(),
    )
    out_specs = (P("grid"), P())
    return jax.shard_map(local, mesh=mesh, in_specs=in_specs, out_specs=out_specs, check_vma=False)
```

```python
import functools

import jax
import jax.numpy as jnp
from jax import lax
from jax.experimental import pallas as pl
from jax.experimental.pallas import tpu as pltpu
from jax.sharding import PartitionSpec as P

BLOCK = 128
BPD = 6
NATOM = 256
LANES = 128
ROWS = 32
UNROLL = 4

SLATER = 0.7386
RHO_SOFT = 0.05

VMEM = pltpu.MemorySpace.VMEM
SMEM = pltpu.MemorySpace.SMEM


def aligned(start, size):
    return pl.ds(pl.multiple_of(start, size), size)


def live_count(ints_ref):
    row = ints_ref.shape[0] - 1
    slots = ints_ref.shape[1]
    step = 1
    while step * 2 <= slots:
        step *= 2
    count = jnp.int32(0)
    while step:
        more = count + step
        found = ints_ref[row, jnp.minimum(more, slots) - 1] >= 0
        count = jnp.where(jnp.logical_and(more <= slots, found), more, count)
        step //= 2
    return count


def start_copies(pairs, sems):
    copies = [pltpu.make_async_copy(src, dst, sems.at[i]) for i, (src, dst) in enumerate(pairs)]
    for copy in copies:
        copy.start()
    return copies


def place_slabs(offsets, slabs, tiles):
    me = lax.axis_index("grid")
    for e, slab in zip(offsets, slabs):
        if isinstance(e, tuple):
            half = slab.shape[1]
            for i, (one, h) in enumerate(e):
                first = (2 * jnp.bitwise_xor(me, one) + h) * half
                tiles[aligned(first, half), :] = slab[i]
        else:
            depth = slab.shape[0]
            tiles[aligned(jnp.bitwise_xor(me, e) * depth, depth), :] = slab[...]


def pack_kernel(picks, *refs):
    *parts, out_ref = refs
    half = out_ref.shape[1]
    for i, (p, h) in enumerate(picks):
        part = parts[p]
        out_ref[i] = part[h] if len(part.shape) == 3 else part[h * half : (h + 1) * half, :]


def share_kernel(own_ints, other_ints, own_points, other_points, points_out, ints_out, dest_ref):
    rows, slots = own_ints.shape
    core = lax.rem(lax.axis_index("grid"), 2)
    own, other = live_count(own_ints), live_count(other_ints)
    count0 = jnp.where(core == 0, own, other)
    half = lax.div(own + other + 1, 2)
    base = jnp.where(core == 0, 0, half)
    count = jnp.where(core == 0, half, own + other - half)
    lanes = lax.broadcasted_iota(jnp.int32, (1, slots), 1)
    dest_ids = lax.broadcasted_iota(jnp.int32, (1, dest_ref.shape[1]), 1)
    kept = [jnp.zeros((1, slots), jnp.int32)] * rows
    for v in range(slots):
        from0 = base + v < count0
        slot = jnp.clip(base + v - jnp.where(from0, 0, count0), 0, slots - 1)
        mine = from0 == (core == 0)
        points_out[v] = jnp.where(mine, own_points[slot], other_points[slot])
        values = [jnp.where(mine, own_ints[i, slot], other_ints[i, slot]) for i in range(rows)]
        values[-1] = jnp.where(v < count, values[-1], -1)
        kept = [jnp.where(lanes == v, value, row) for value, row in zip(values, kept)]
        dest_ref[v : v + 1, :] = jnp.where(dest_ids == values[-1], 1.0, 0.0)
    ints_out[...] = jnp.concatenate(kept, axis=0)


def table_kernel(
    atom_hbm,
    expo_hbm,
    coef_hbm,
    coords_hbm,
    points_hbm,
    slab_hbm,
    table_ref,
    points_out,
    slab_out,
    atom_ref,
    expo_ref,
    coef_ref,
    coords_ref,
    sems,
):
    copies = start_copies(
        [
            (atom_hbm, atom_ref),
            (expo_hbm, expo_ref),
            (coef_hbm, coef_ref),
            (coords_hbm, coords_ref),
            (points_hbm, points_out),
            (slab_hbm, slab_out),
        ],
        sems,
    )
    for copy in copies[:4]:
        copy.wait()
    coords = coords_ref[...]
    high = coords.astype(jnp.bfloat16)
    rest = coords - high.astype(jnp.float32)
    mid = rest.astype(jnp.bfloat16)
    low = (rest - mid.astype(jnp.float32)).astype(jnp.bfloat16)
    blocks = table_ref.shape[0]
    atoms = atom_ref[...].reshape(blocks, BLOCK)
    expos = expo_ref[...].reshape(blocks, BLOCK)

    for k in range(blocks):
        atom = atoms[k : k + 1]
        onehot = jnp.where(
            lax.broadcasted_iota(jnp.int32, (NATOM, BLOCK), 0) == atom, 1.0, 0.0
        ).astype(jnp.bfloat16)
        picked = [
            jnp.dot(part, onehot, preferred_element_type=jnp.float32) for part in (high, mid, low)
        ]
        center = (picked[0] + picked[1]) + picked[2]
        coef = coef_ref[:, k * BLOCK : (k + 1) * BLOCK]
        rows = jnp.concatenate(
            [center, coef, expos[k : k + 1], atom.astype(jnp.float32)], axis=0
        )
        columns = rows.T
        for p in range(8):
            table_ref[k, p] = jnp.broadcast_to(columns[:, p : p + 1], (BLOCK, LANES))

    for copy in copies[4:]:
        copy.wait()


def chunk_steps(ints_ref, first, size):
    left = jnp.clip(live_count(ints_ref) - first, 0, size)
    return lax.div(left + (UNROLL - 1), UNROLL)


def phi_kernel(first, offsets, ints_ref, points_ref, table_ref, *refs):
    slabs = refs[: len(offsets)]
    outputs = 3 + (1 if first == 0 else 0) + (1 if offsets else 0)
    phi_ref, radial_ref, basis_ref, *more = refs[len(refs) - outputs :]
    if first == 0:
        more.pop(0)[...] = jnp.zeros((BPD, 5, BLOCK, LANES), jnp.float32)
    if offsets:
        place_slabs(offsets, slabs, more[0])
    blk = lax.axis_index("blk")
    length = ints_ref.shape[0] - 1
    point_count = points_ref.shape[2]

    def one_slot(s):
        for j in range(length):
            k = ints_ref[lax.rem(blk + j, length), first + s]
            for r in range(0, BLOCK, ROWS):
                sub = slice(r, r + ROWS)
                cx, cy, cz, sx, sy, sz, expo = [table_ref[k, p, sub] for p in range(7)]
                for h in range(0, point_count, LANES):
                    lanes = slice(h, h + LANES)
                    ox = points_ref[first + s, 0:1, lanes] - cx
                    oy = points_ref[first + s, 1:2, lanes] - cy
                    oz = points_ref[first + s, 2:3, lanes] - cz
                    squared = ox * ox + oy * oy + oz * oz
                    radial = jnp.exp(-expo * squared)
                    linear = 1.0 + (sx * ox + sy * oy + sz * oz)
                    basis = linear * radial
                    rows = slice(j * BLOCK + r, j * BLOCK + r + ROWS)
                    phi_ref[s, rows, lanes] = basis.astype(jnp.bfloat16)
                    if j == 0:
                        radial_ref[s, sub, lanes] = radial
                        basis_ref[s, sub, lanes] = basis

    def some_slots(i, carry):
        for u in range(2):
            one_slot(i * 2 + u)
        return carry

    steps = chunk_steps(ints_ref, first, phi_ref.shape[0]) * (UNROLL // 2)
    lax.fori_loop(0, steps, some_slots, 0)


def rho_kernel(offsets, starts, ints_ref, *refs):
    chunks = len(starts)
    phis = refs[:chunks]
    slabs = refs[chunks : chunks + len(offsets)]
    tiles, chi_ref, rho_ref, *placed = refs[chunks + len(offsets) :]
    if offsets:
        tiles = placed[0]
        place_slabs(offsets, slabs, tiles)
    blk = lax.axis_index("blk")
    length = ints_ref.shape[0] - 1
    rho_ref[...] = jnp.zeros_like(rho_ref)

    for c, phi_ref in enumerate(phis):
        size = phi_ref.shape[0]

        def one_slot(s, first=starts[c], phi_ref=phi_ref):
            slot = first + s
            own = ints_ref[blk, slot]
            cols = aligned((own - blk * BPD) * BLOCK, BLOCK)
            left = [tiles[aligned(own * BLOCK, BLOCK), cols]]
            for j in range(1, length):
                k = ints_ref[lax.rem(blk + j, length), slot]
                left.append(tiles[aligned(k * BLOCK, BLOCK), cols].T)
            chi = jnp.dot(
                jnp.concatenate(left, axis=1), phi_ref[s], preferred_element_type=jnp.float32
            )
            phi = phi_ref[s, 0:BLOCK, :]
            chi_ref[slot] = chi
            rho_ref[pl.ds(slot, 1), :] = jnp.sum(
                phi.astype(jnp.float32) * chi, axis=0, keepdims=True
            )

        def some_slots(i, carry, one_slot=one_slot):
            for u in range(UNROLL):
                one_slot(i * UNROLL + u)
            return carry

        lax.fori_loop(0, chunk_steps(ints_ref, starts[c], size), some_slots, 0)


def force_kernel(starts, ints_ref, points_ref, rho_a_ref, rho_b_ref, chi_ref, *refs):
    chunks = len(starts)
    radials = refs[:chunks]
    bases = refs[chunks : 2 * chunks]
    table_ref, dest_ref, _, out_ref, acc, pot_ref = refs[2 * chunks :]
    blk = lax.axis_index("blk")
    slots, _, point_count = points_ref.shape
    dests = dest_ref.shape[1]
    live = live_count(ints_ref)
    rho = rho_a_ref[...] + rho_b_ref[...]
    weight = points_ref[:, 3, :]
    log_sq = jnp.log(rho * rho + RHO_SOFT * RHO_SOFT)
    pot = weight * (-(4.0 / 3.0) * SLATER) * rho * jnp.exp(log_sq * (-1.0 / 3.0))
    slot_ids = lax.broadcasted_iota(jnp.int32, (slots, 1), 0)
    pot_ref[...] = jnp.where(slot_ids < live, pot, 0.0)
    energies = jnp.sum(weight * -SLATER * jnp.exp(log_sq * (2.0 / 3.0)), axis=1, keepdims=True)

    for c in range(chunks):
        radial_ref, basis_ref = radials[c], bases[c]
        size = radial_ref.shape[0]

        def one_slot(s, first=starts[c], radial_ref=radial_ref, basis_ref=basis_ref):
            slot = first + s
            own = ints_ref[blk, slot] - blk * BPD
            pots = pot_ref[pl.ds(slot, 1), :]
            for r in range(0, BLOCK, ROWS):
                sub = slice(r, r + ROWS)
                sums = None
                for h in range(0, point_count, LANES):
                    lanes = slice(h, h + LANES)
                    u = chi_ref[slot, sub, lanes] * pots[:, lanes]
                    ub = u * basis_ref[s, sub, lanes]
                    terms = (
                        u * radial_ref[s, sub, lanes],
                        ub,
                        ub * points_ref[slot, 0:1, lanes],
                        ub * points_ref[slot, 1:2, lanes],
                        ub * points_ref[slot, 2:3, lanes],
                    )
                    sums = terms if sums is None else [a + b for a, b in zip(sums, terms)]
                for q in range(5):
                    acc[own, q, sub] += sums[q]

        def some_slots(i, carry, one_slot=one_slot):
            for u in range(UNROLL):
                one_slot(i * UNROLL + u)
            return carry

        lax.fori_loop(0, chunk_steps(ints_ref, starts[c], size), some_slots, 0)

    lane_ids = lax.broadcasted_iota(jnp.int32, (1, LANES), 1).astype(jnp.float32)

    totals = [jnp.zeros((8, LANES), jnp.float32)] * (3 * NATOM // LANES)
    for b in range(BPD):
        k = blk * BPD + b
        for r in range(0, BLOCK, ROWS):
            sub = slice(r, r + ROWS)
            parts = [acc[b, q, sub] for q in range(5)]
            doubled = 2.0 * table_ref[k, 6, sub]
            atom = table_ref[k, 7, sub]
            for c in range(3):
                force = table_ref[k, 3 + c, sub] * parts[0] - doubled * (
                    parts[2 + c] - table_ref[k, c, sub] * parts[1]
                )
                column = 2.0 * jnp.sum(force, axis=1, keepdims=True)
                for h in range(NATOM // LANES):
                    hit = jnp.where(atom == lane_ids + float(h * LANES), column, 0.0)
                    i = c * (NATOM // LANES) + h
                    totals[i] = totals[i] + sum(hit[i8 : i8 + 8] for i8 in range(0, ROWS, 8))
    rows = [jnp.sum(t, axis=0, keepdims=True) for t in totals]
    moved = jnp.sum(dest_ref[...] * energies, axis=0, keepdims=True)
    rows += [moved[:, h : h + LANES] for h in range(0, dests, LANES)]
    packed = jnp.concatenate(rows, axis=0)
    for i in range(out_ref.shape[0]):
        out_ref[i] = packed


def sum_kernel(copies, arrived_ref, energy_ref, forces_ref):
    me = lax.axis_index("grid")
    total = jnp.sum(arrived_ref[...], axis=0)
    per = NATOM // LANES
    for c in range(3):
        for h in range(per):
            forces_ref[c : c + 1, h * LANES : (h + 1) * LANES] = total[c * per + h : c * per + h + 1]
    width = energy_ref.shape[1]
    first = me * width
    energy = jnp.zeros((1, LANES), jnp.float32)
    for i in range(3 * per, total.shape[0]):
        chosen = lax.div(first, LANES) == i - 3 * per
        energy = jnp.where(chosen, total[i : i + 1], energy)
    turn = lax.rem(LANES - lax.rem(first, LANES), LANES)
    energy = pltpu.roll(jnp.broadcast_to(energy, (8, LANES)), turn, 1)
    energy_ref[...] = energy[0:1, 0:width] * (1.0 / copies)


def swap(array, offset):
    count = lax.axis_size("grid")
    return lax.ppermute(array, "grid", [(i, i ^ offset) for i in range(count)])


FIRST = (8, 4, 2)
OVER_X = ((10, 0), (10, 1), (6, 0))
OVER_Z = ((12, 0), (12, 1), (6, 1))


def in_hbm(array):
    return pltpu.with_memory_space_constraint(array, pltpu.HBM)


def spec(space):
    return pl.BlockSpec(memory_space=space)


def params(blocks):
    return pltpu.CompilerParams(vmem_limit_bytes=blocks * 1024 * 1024)


def cost(nominal_us):
    return pl.CostEstimate(
        flops=0, bytes_accessed=int(nominal_us * 3.69e6), transcendentals=0
    )


def f32(*shape):
    return jax.ShapeDtypeStruct(shape, jnp.float32)


def local(density, points, sig_blocks, migration, atom_coords, exponents, shape_coef, func_atom):
    grid_count = lax.axis_size("grid")
    blk_count = lax.axis_size("blk")
    slots, _, point_count = points.shape
    length = sig_blocks.shape[1]
    functions = exponents.shape[0]
    blocks = functions // BLOCK
    dests = grid_count * (slots // 2)
    sizes = [slots // 8 * 7, slots // 8]
    starts = [0, slots // 8 * 7]
    tied = lax.optimization_barrier

    slab = density.T
    held = {0: slab}
    if grid_count == 16:
        for e in FIRST:
            held[e] = swap(slab, e)
    ints = jnp.concatenate([sig_blocks.T, migration[None]], axis=0)
    other_ints, other_points = swap(ints, 1), swap(points, 1)
    table, points, near_slab = pl.pallas_call(
        table_kernel,
        out_shape=[
            f32(blocks, 8, BLOCK, LANES),
            f32(*points.shape),
            jax.ShapeDtypeStruct(slab.shape, slab.dtype),
        ],
        in_specs=[spec(pltpu.HBM)] * 6,
        out_specs=[spec(VMEM)] * 3,
        scratch_shapes=[
            pltpu.VMEM((functions,), jnp.int32),
            pltpu.VMEM((functions,), jnp.float32),
            pltpu.VMEM((3, functions), jnp.float32),
            pltpu.VMEM((3, NATOM), jnp.float32),
            pltpu.SemaphoreType.DMA((6,)),
        ],
        compiler_params=params(blocks),
        cost_estimate=cost(4),
        name="param_table",
    )(*[in_hbm(a) for a in (func_atom, exponents, shape_coef, atom_coords, points, slab)])

    def share(other_ints, other_points):
        return pl.pallas_call(
            share_kernel,
            out_shape=[
                f32(*points.shape),
                jax.ShapeDtypeStruct(ints.shape, jnp.int32),
                f32(slots, dests),
            ],
            in_specs=[spec(SMEM)] * 2 + [spec(VMEM)] * 2,
            out_specs=[spec(VMEM)] * 3,
            compiler_params=params(blocks),
            cost_estimate=cost(1),
            name="shared_slots",
        )(ints, other_ints, points, other_points)

    tile_shape = jax.ShapeDtypeStruct((functions, BPD * BLOCK), jnp.bfloat16)

    def basis_chunk(c, points, ints, offsets=(), slabs=(), tiles=()):
        some = 1 if offsets else 0
        zeros = 1 if c == 0 else 0
        inputs = [ints, points, table, *slabs, *tiles]
        return pl.pallas_call(
            functools.partial(phi_kernel, starts[c], offsets),
            out_shape=[
                jax.ShapeDtypeStruct((sizes[c], length * BLOCK, point_count), jnp.bfloat16),
                f32(sizes[c], BLOCK, point_count),
                f32(sizes[c], BLOCK, point_count),
            ]
            + [f32(BPD, 5, BLOCK, LANES)] * zeros
            + [tile_shape] * some,
            in_specs=[spec(SMEM)] + [spec(VMEM)] * (len(inputs) - 1),
            out_specs=[spec(VMEM)] * (3 + zeros + some),
            input_output_aliases={len(inputs) - 1: 3 + zeros} if tiles else {},
            compiler_params=params(blocks),
            cost_estimate=cost(5),
            name="basis_values",
        )(*inputs)

    def pack(parts, picks):
        return pl.pallas_call(
            functools.partial(pack_kernel, picks),
            out_shape=jax.ShapeDtypeStruct(
                (len(picks), slab.shape[0] // 2, slab.shape[1]), slab.dtype
            ),
            in_specs=[spec(VMEM)] * len(parts),
            out_specs=spec(VMEM),
            compiler_params=params(blocks),
            name="pack",
        )(*parts)

    late, slabs = [], []
    if grid_count == 16:
        held[0] = near_slab
        held, other_ints, other_points, table = tied((held, other_ints, other_points, table))
        ready = list(held)
        over_x = swap(pack((held[8], held[4]), ((0, 0), (0, 1), (1, 0))), 2)
        over_z = swap(pack((held[8], held[2]), ((0, 0), (0, 1), (1, 1))), 4)
        across = swap(held[8], 6)
        early = tuple((e ^ 1, h) for e in ready for h in range(2))
        picks = [(p, h) for p in range(len(ready)) for h in range(2)]
        crossed_early = swap(pack([held[e] for e in ready], picks), 1)
        points, ints, dest_mask = share(other_ints, other_points)
        *first, acc, tiles = basis_chunk(0, points, ints, ready, [held[e] for e in ready])
        held, across, over_x, over_z, first, tiles, points = tied(
            (held, across, over_x, over_z, first, tiles, points)
        )
        halves = [(p, h) for p in range(3) for h in range(3)]
        crossed = swap(pack((across, over_x, over_z), [(0, 0), (0, 1), *halves[3:]]), 1)
        placed = [14, OVER_X, OVER_Z, early]
        *second, tiles = basis_chunk(
            1, points, ints, placed, [across, over_x, over_z, crossed_early], [tiles]
        )
        pieces = ((14, 0), (14, 1), *OVER_X, *OVER_Z)
        late = [tuple((e ^ 1, h) for e, h in pieces)]
        slabs = [crossed]
    else:
        tiles = lax.all_gather(slab, "grid", axis=0, tiled=True)
        points, ints, dest_mask = share(other_ints, other_points)
        *first, acc = basis_chunk(0, points, ints)
        second = basis_chunk(1, points, ints)
    chunks = [first, second]
    phis, radials, bases = zip(*chunks)

    some = 1 if late else 0
    chi, rho, *_ = pl.pallas_call(
        functools.partial(rho_kernel, late, starts),
        out_shape=[f32(slots, BLOCK, point_count), f32(slots, point_count)] + [tile_shape] * some,
        in_specs=[spec(SMEM)] + [spec(VMEM)] * (len(starts) + len(late) + 1),
        out_specs=[spec(VMEM)] * (2 + some),
        input_output_aliases={1 + len(starts) + len(late): 2} if late else {},
        compiler_params=params(blocks),
        cost_estimate=cost(5),
        name="density_at_points",
    )(ints, *phis, *slabs, tiles)

    if blk_count == 2:
        other = lax.ppermute(rho, "blk", [(0, 1), (1, 0)])
    else:
        other = lax.psum(rho, "blk") - rho

    rows = 3 * NATOM // LANES + dests // LANES
    outgoing, _ = pl.pallas_call(
        functools.partial(force_kernel, starts),
        out_shape=[f32(blk_count * grid_count, rows, LANES), f32(BPD, 5, BLOCK, LANES)],
        in_specs=[spec(SMEM)] + [spec(VMEM)] * (7 + 2 * len(starts)),
        out_specs=[spec(VMEM)] * 2,
        scratch_shapes=[pltpu.VMEM((slots, point_count), jnp.float32)],
        input_output_aliases={7 + 2 * len(starts): 1},
        compiler_params=params(blocks),
        cost_estimate=cost(5),
        name="forces_and_energies",
    )(ints, points, rho, other, chi, *radials, *bases, table, dest_mask, acc)

    arrived = lax.all_to_all(outgoing, ("blk", "grid"), split_axis=0, concat_axis=0, tiled=True)

    energy, forces = pl.pallas_call(
        functools.partial(sum_kernel, blk_count),
        out_shape=[f32(1, dests // grid_count), f32(3, NATOM)],
        in_specs=[spec(VMEM)],
        out_specs=[spec(VMEM)] * 2,
        compiler_params=params(blocks),
        name="final_sums",
    )(arrived)
    return (energy.reshape(dests // grid_count), forces)


def solution(mesh):
    in_specs = (
        P("blk", "grid"),
        P("grid", None, None),
        P("grid", None),
        P("grid"),
        P(),
        P(),
        P(),
        P(),
    )
    out_specs = (P("grid"), P())
    return jax.shard_map(local, mesh=mesh, in_specs=in_specs, out_specs=out_specs, check_vma=False)
```

```python
import functools

import jax
import jax.numpy as jnp
from jax import lax
from jax.experimental import pallas as pl
from jax.experimental.pallas import tpu as pltpu
from jax.sharding import PartitionSpec as P

BLOCK = 128
BPD = 6
NATOM = 256
LANES = 128
ROWS = 32
UNROLL = 4

SLATER = 0.7386
RHO_SOFT = 0.05

VMEM = pltpu.MemorySpace.VMEM
SMEM = pltpu.MemorySpace.SMEM


def aligned(start, size):
    return pl.ds(pl.multiple_of(start, size), size)


def live_count(ints_ref):
    row = ints_ref.shape[0] - 1
    slots = ints_ref.shape[1]
    step = 1
    while step * 2 <= slots:
        step *= 2
    count = jnp.int32(0)
    while step:
        more = count + step
        found = ints_ref[row, jnp.minimum(more, slots) - 1] >= 0
        count = jnp.where(jnp.logical_and(more <= slots, found), more, count)
        step //= 2
    return count


def start_copies(pairs, sems):
    copies = [pltpu.make_async_copy(src, dst, sems.at[i]) for i, (src, dst) in enumerate(pairs)]
    for copy in copies:
        copy.start()
    return copies


def place_slabs(offsets, slabs, tiles):
    me = lax.axis_index("grid")
    for e, slab in zip(offsets, slabs):
        if isinstance(e, tuple):
            half = slab.shape[1]
            for i, (one, h) in enumerate(e):
                first = (2 * jnp.bitwise_xor(me, one) + h) * half
                tiles[aligned(first, half), :] = slab[i]
        else:
            depth = slab.shape[0]
            tiles[aligned(jnp.bitwise_xor(me, e) * depth, depth), :] = slab[...]


def pack_kernel(picks, *refs):
    *parts, out_ref = refs
    half = out_ref.shape[1]
    for i, (p, h) in enumerate(picks):
        part = parts[p]
        out_ref[i] = part[h] if len(part.shape) == 3 else part[h * half : (h + 1) * half, :]


def share_kernel(own_ints, other_ints, own_points, other_points, points_out, ints_out, dest_ref):
    rows, slots = own_ints.shape
    core = lax.rem(lax.axis_index("grid"), 2)
    own, other = live_count(own_ints), live_count(other_ints)
    count0 = jnp.where(core == 0, own, other)
    half = lax.div(own + other + 1, 2)
    base = jnp.where(core == 0, 0, half)
    count = jnp.where(core == 0, half, own + other - half)
    lanes = lax.broadcasted_iota(jnp.int32, (1, slots), 1)
    dest_ids = lax.broadcasted_iota(jnp.int32, (1, dest_ref.shape[1]), 1)
    kept = [jnp.zeros((1, slots), jnp.int32)] * rows
    for v in range(slots):
        from0 = base + v < count0
        slot = jnp.clip(base + v - jnp.where(from0, 0, count0), 0, slots - 1)
        mine = from0 == (core == 0)
        points_out[v] = jnp.where(mine, own_points[slot], other_points[slot])
        values = [jnp.where(mine, own_ints[i, slot], other_ints[i, slot]) for i in range(rows)]
        values[-1] = jnp.where(v < count, values[-1], -1)
        kept = [jnp.where(lanes == v, value, row) for value, row in zip(values, kept)]
        dest_ref[v : v + 1, :] = jnp.where(dest_ids == values[-1], 1.0, 0.0)
    ints_out[...] = jnp.concatenate(kept, axis=0)


def table_kernel(
    atom_hbm,
    expo_hbm,
    coef_hbm,
    coords_hbm,
    points_hbm,
    slab_hbm,
    table_ref,
    points_out,
    slab_out,
    atom_ref,
    expo_ref,
    coef_ref,
    coords_ref,
    sems,
):
    copies = start_copies(
        [
            (atom_hbm, atom_ref),
            (expo_hbm, expo_ref),
            (coef_hbm, coef_ref),
            (coords_hbm, coords_ref),
            (points_hbm, points_out),
            (slab_hbm, slab_out),
        ],
        sems,
    )
    for copy in copies[:4]:
        copy.wait()
    coords = coords_ref[...]
    high = coords.astype(jnp.bfloat16)
    rest = coords - high.astype(jnp.float32)
    mid = rest.astype(jnp.bfloat16)
    low = (rest - mid.astype(jnp.float32)).astype(jnp.bfloat16)
    blocks = table_ref.shape[0]
    atoms = atom_ref[...].reshape(blocks, BLOCK)
    expos = expo_ref[...].reshape(blocks, BLOCK)

    for k in range(blocks):
        atom = atoms[k : k + 1]
        onehot = jnp.where(
            lax.broadcasted_iota(jnp.int32, (NATOM, BLOCK), 0) == atom, 1.0, 0.0
        ).astype(jnp.bfloat16)
        picked = [
            jnp.dot(part, onehot, preferred_element_type=jnp.float32) for part in (high, mid, low)
        ]
        center = (picked[0] + picked[1]) + picked[2]
        coef = coef_ref[:, k * BLOCK : (k + 1) * BLOCK]
        rows = jnp.concatenate(
            [center, coef, expos[k : k + 1], atom.astype(jnp.float32)], axis=0
        )
        columns = rows.T
        for p in range(8):
            table_ref[k, p] = jnp.broadcast_to(columns[:, p : p + 1], (BLOCK, LANES))

    for copy in copies[4:]:
        copy.wait()


def chunk_steps(ints_ref, first, size):
    left = jnp.clip(live_count(ints_ref) - first, 0, size)
    return lax.div(left + (UNROLL - 1), UNROLL)


def phi_kernel(first, offsets, ints_ref, points_ref, table_ref, *refs):
    slabs = refs[: len(offsets)]
    outputs = 3 + (1 if first == 0 else 0) + (1 if offsets else 0)
    phi_ref, radial_ref, basis_ref, *more = refs[len(refs) - outputs :]
    if first == 0:
        more.pop(0)[...] = jnp.zeros((2, BPD, 5, BLOCK, LANES), jnp.float32)
    if offsets:
        place_slabs(offsets, slabs, more[0])
    blk = lax.axis_index("blk")
    length = ints_ref.shape[0] - 1
    point_count = points_ref.shape[2]

    def one_slot(s):
        for j in range(length):
            k = ints_ref[lax.rem(blk + j, length), first + s]
            for r in range(0, BLOCK, ROWS):
                sub = slice(r, r + ROWS)
                cx, cy, cz, sx, sy, sz, expo = [table_ref[k, p, sub] for p in range(7)]
                for h in range(0, point_count, LANES):
                    lanes = slice(h, h + LANES)
                    ox = points_ref[first + s, 0:1, lanes] - cx
                    oy = points_ref[first + s, 1:2, lanes] - cy
                    oz = points_ref[first + s, 2:3, lanes] - cz
                    squared = ox * ox + oy * oy + oz * oz
                    radial = jnp.exp(-expo * squared)
                    linear = 1.0 + (sx * ox + sy * oy + sz * oz)
                    basis = linear * radial
                    rows = slice(j * BLOCK + r, j * BLOCK + r + ROWS)
                    phi_ref[s, rows, lanes] = basis.astype(jnp.bfloat16)
                    if j == 0:
                        radial_ref[s, sub, lanes] = radial
                        basis_ref[s, sub, lanes] = basis

    def some_slots(i, carry):
        for u in range(2):
            one_slot(i * 2 + u)
        return carry

    steps = chunk_steps(ints_ref, first, phi_ref.shape[0]) * (UNROLL // 2)
    lax.fori_loop(0, steps, some_slots, 0)


def rho_kernel(offsets, starts, ints_ref, *refs):
    chunks = len(starts)
    phis = refs[:chunks]
    slabs = refs[chunks : chunks + len(offsets)]
    tiles, chi_ref, rho_ref, *placed = refs[chunks + len(offsets) :]
    if offsets:
        tiles = placed[0]
        place_slabs(offsets, slabs, tiles)
    blk = lax.axis_index("blk")
    length = ints_ref.shape[0] - 1
    rho_ref[...] = jnp.zeros_like(rho_ref)

    for c, phi_ref in enumerate(phis):
        size = phi_ref.shape[0]

        def one_slot(s, first=starts[c], phi_ref=phi_ref):
            slot = first + s
            own = ints_ref[blk, slot]
            cols = aligned((own - blk * BPD) * BLOCK, BLOCK)
            left = [tiles[aligned(own * BLOCK, BLOCK), cols]]
            for j in range(1, length):
                k = ints_ref[lax.rem(blk + j, length), slot]
                left.append(tiles[aligned(k * BLOCK, BLOCK), cols].T)
            chi = jnp.dot(
                jnp.concatenate(left, axis=1), phi_ref[s], preferred_element_type=jnp.float32
            )
            phi = phi_ref[s, 0:BLOCK, :]
            chi_ref[slot] = chi
            rho_ref[pl.ds(slot, 1), :] = jnp.sum(
                phi.astype(jnp.float32) * chi, axis=0, keepdims=True
            )

        def some_slots(i, carry, one_slot=one_slot):
            for u in range(UNROLL):
                one_slot(i * UNROLL + u)
            return carry

        lax.fori_loop(0, chunk_steps(ints_ref, starts[c], size), some_slots, 0)


def force_kernel(starts, ints_ref, points_ref, rho_a_ref, rho_b_ref, chi_ref, *refs):
    chunks = len(starts)
    radials = refs[:chunks]
    bases = refs[chunks : 2 * chunks]
    table_ref, dest_ref, _, out_ref, acc, pot_ref = refs[2 * chunks :]
    blk = lax.axis_index("blk")
    slots, _, point_count = points_ref.shape
    dests = dest_ref.shape[1]
    live = live_count(ints_ref)
    rho = rho_a_ref[...] + rho_b_ref[...]
    weight = points_ref[:, 3, :]
    log_sq = jnp.log(rho * rho + RHO_SOFT * RHO_SOFT)
    pot = weight * (-(4.0 / 3.0) * SLATER) * rho * jnp.exp(log_sq * (-1.0 / 3.0))
    slot_ids = lax.broadcasted_iota(jnp.int32, (slots, 1), 0)
    pot_ref[...] = jnp.where(slot_ids < live, pot, 0.0)
    energies = jnp.sum(weight * -SLATER * jnp.exp(log_sq * (2.0 / 3.0)), axis=1, keepdims=True)

    for c in range(chunks):
        radial_ref, basis_ref = radials[c], bases[c]
        size = radial_ref.shape[0]

        def one_slot(s, side, first=starts[c], radial_ref=radial_ref, basis_ref=basis_ref):
            slot = first + s
            own = ints_ref[blk, slot] - blk * BPD
            pots = pot_ref[pl.ds(slot, 1), :]
            for r in range(0, BLOCK, ROWS):
                sub = slice(r, r + ROWS)
                sums = None
                for h in range(0, point_count, LANES):
                    lanes = slice(h, h + LANES)
                    u = chi_ref[slot, sub, lanes] * pots[:, lanes]
                    ub = u * basis_ref[s, sub, lanes]
                    terms = (
                        u * radial_ref[s, sub, lanes],
                        ub,
                        ub * points_ref[slot, 0:1, lanes],
                        ub * points_ref[slot, 1:2, lanes],
                        ub * points_ref[slot, 2:3, lanes],
                    )
                    sums = terms if sums is None else [a + b for a, b in zip(sums, terms)]
                for q in range(5):
                    acc[side, own, q, sub] += sums[q]

        def some_slots(i, carry, one_slot=one_slot):
            for u in range(UNROLL):
                one_slot(i * UNROLL + u, u % 2)
            return carry

        lax.fori_loop(0, chunk_steps(ints_ref, starts[c], size), some_slots, 0)

    lane_ids = lax.broadcasted_iota(jnp.int32, (1, LANES), 1).astype(jnp.float32)

    totals = [jnp.zeros((8, LANES), jnp.float32)] * (3 * NATOM // LANES)
    for b in range(BPD):
        k = blk * BPD + b
        for r in range(0, BLOCK, ROWS):
            sub = slice(r, r + ROWS)
            parts = [acc[0, b, q, sub] + acc[1, b, q, sub] for q in range(5)]
            doubled = 2.0 * table_ref[k, 6, sub]
            atom = table_ref[k, 7, sub]
            for c in range(3):
                force = table_ref[k, 3 + c, sub] * parts[0] - doubled * (
                    parts[2 + c] - table_ref[k, c, sub] * parts[1]
                )
                column = 2.0 * jnp.sum(force, axis=1, keepdims=True)
                for h in range(NATOM // LANES):
                    hit = jnp.where(atom == lane_ids + float(h * LANES), column, 0.0)
                    i = c * (NATOM // LANES) + h
                    totals[i] = totals[i] + sum(hit[i8 : i8 + 8] for i8 in range(0, ROWS, 8))
    rows = [jnp.sum(t, axis=0, keepdims=True) for t in totals]
    moved = jnp.sum(dest_ref[...] * energies, axis=0, keepdims=True)
    rows += [moved[:, h : h + LANES] for h in range(0, dests, LANES)]
    packed = jnp.concatenate(rows, axis=0)
    for i in range(out_ref.shape[0]):
        out_ref[i] = packed


def sum_kernel(copies, arrived_ref, energy_ref, forces_ref):
    me = lax.axis_index("grid")
    total = jnp.sum(arrived_ref[...], axis=0)
    per = NATOM // LANES
    for c in range(3):
        for h in range(per):
            forces_ref[c : c + 1, h * LANES : (h + 1) * LANES] = total[c * per + h : c * per + h + 1]
    width = energy_ref.shape[1]
    first = me * width
    energy = jnp.zeros((1, LANES), jnp.float32)
    for i in range(3 * per, total.shape[0]):
        chosen = lax.div(first, LANES) == i - 3 * per
        energy = jnp.where(chosen, total[i : i + 1], energy)
    turn = lax.rem(LANES - lax.rem(first, LANES), LANES)
    energy = pltpu.roll(jnp.broadcast_to(energy, (8, LANES)), turn, 1)
    energy_ref[...] = energy[0:1, 0:width] * (1.0 / copies)


def swap(array, offset):
    count = lax.axis_size("grid")
    return lax.ppermute(array, "grid", [(i, i ^ offset) for i in range(count)])


FIRST = (8, 4, 2)
OVER_X = ((10, 0), (10, 1), (6, 0))
OVER_Z = ((12, 0), (12, 1), (6, 1))


def in_hbm(array):
    return pltpu.with_memory_space_constraint(array, pltpu.HBM)


def spec(space):
    return pl.BlockSpec(memory_space=space)


def params(blocks):
    return pltpu.CompilerParams(vmem_limit_bytes=blocks * 1024 * 1024)


def cost(nominal_us):
    return pl.CostEstimate(
        flops=0, bytes_accessed=int(nominal_us * 3.69e6), transcendentals=0
    )


def f32(*shape):
    return jax.ShapeDtypeStruct(shape, jnp.float32)


def local(density, points, sig_blocks, migration, atom_coords, exponents, shape_coef, func_atom):
    grid_count = lax.axis_size("grid")
    blk_count = lax.axis_size("blk")
    slots, _, point_count = points.shape
    length = sig_blocks.shape[1]
    functions = exponents.shape[0]
    blocks = functions // BLOCK
    dests = grid_count * (slots // 2)
    sizes = [slots // 8 * 7, slots // 8]
    starts = [0, slots // 8 * 7]
    tied = lax.optimization_barrier

    slab = density.T
    held = {0: slab}
    if grid_count == 16:
        for e in FIRST:
            held[e] = swap(slab, e)
    ints = jnp.concatenate([sig_blocks.T, migration[None]], axis=0)
    other_ints, other_points = swap(ints, 1), swap(points, 1)
    table, points, near_slab = pl.pallas_call(
        table_kernel,
        out_shape=[
            f32(blocks, 8, BLOCK, LANES),
            f32(*points.shape),
            jax.ShapeDtypeStruct(slab.shape, slab.dtype),
        ],
        in_specs=[spec(pltpu.HBM)] * 6,
        out_specs=[spec(VMEM)] * 3,
        scratch_shapes=[
            pltpu.VMEM((functions,), jnp.int32),
            pltpu.VMEM((functions,), jnp.float32),
            pltpu.VMEM((3, functions), jnp.float32),
            pltpu.VMEM((3, NATOM), jnp.float32),
            pltpu.SemaphoreType.DMA((6,)),
        ],
        compiler_params=params(blocks),
        cost_estimate=cost(4),
        name="param_table",
    )(*[in_hbm(a) for a in (func_atom, exponents, shape_coef, atom_coords, points, slab)])

    def share(other_ints, other_points):
        return pl.pallas_call(
            share_kernel,
            out_shape=[
                f32(*points.shape),
                jax.ShapeDtypeStruct(ints.shape, jnp.int32),
                f32(slots, dests),
            ],
            in_specs=[spec(SMEM)] * 2 + [spec(VMEM)] * 2,
            out_specs=[spec(VMEM)] * 3,
            compiler_params=params(blocks),
            cost_estimate=cost(1),
            name="shared_slots",
        )(ints, other_ints, points, other_points)

    tile_shape = jax.ShapeDtypeStruct((functions, BPD * BLOCK), jnp.bfloat16)

    def basis_chunk(c, points, ints, offsets=(), slabs=(), tiles=()):
        some = 1 if offsets else 0
        zeros = 1 if c == 0 else 0
        inputs = [ints, points, table, *slabs, *tiles]
        return pl.pallas_call(
            functools.partial(phi_kernel, starts[c], offsets),
            out_shape=[
                jax.ShapeDtypeStruct((sizes[c], length * BLOCK, point_count), jnp.bfloat16),
                f32(sizes[c], BLOCK, point_count),
                f32(sizes[c], BLOCK, point_count),
            ]
            + [f32(2, BPD, 5, BLOCK, LANES)] * zeros
            + [tile_shape] * some,
            in_specs=[spec(SMEM)] + [spec(VMEM)] * (len(inputs) - 1),
            out_specs=[spec(VMEM)] * (3 + zeros + some),
            input_output_aliases={len(inputs) - 1: 3 + zeros} if tiles else {},
            compiler_params=params(blocks),
            cost_estimate=cost(5),
            name="basis_values",
        )(*inputs)

    def pack(parts, picks):
        return pl.pallas_call(
            functools.partial(pack_kernel, picks),
            out_shape=jax.ShapeDtypeStruct(
                (len(picks), slab.shape[0] // 2, slab.shape[1]), slab.dtype
            ),
            in_specs=[spec(VMEM)] * len(parts),
            out_specs=spec(VMEM),
            compiler_params=params(blocks),
            name="pack",
        )(*parts)

    late, slabs = [], []
    if grid_count == 16:
        held[0] = near_slab
        held, other_ints, other_points, table = tied((held, other_ints, other_points, table))
        ready = list(held)
        over_x = swap(pack((held[8], held[4]), ((0, 0), (0, 1), (1, 0))), 2)
        over_z = swap(pack((held[8], held[2]), ((0, 0), (0, 1), (1, 1))), 4)
        across = swap(held[8], 6)
        early = tuple((e ^ 1, h) for e in ready for h in range(2))
        picks = [(p, h) for p in range(len(ready)) for h in range(2)]
        crossed_early = swap(pack([held[e] for e in ready], picks), 1)
        points, ints, dest_mask = share(other_ints, other_points)
        *first, acc, tiles = basis_chunk(0, points, ints, ready, [held[e] for e in ready])
        held, across, over_x, over_z, first, tiles, points = tied(
            (held, across, over_x, over_z, first, tiles, points)
        )
        halves = [(p, h) for p in range(3) for h in range(3)]
        crossed = swap(pack((across, over_x, over_z), [(0, 0), (0, 1), *halves[3:]]), 1)
        placed = [14, OVER_X, OVER_Z, early]
        *second, tiles = basis_chunk(
            1, points, ints, placed, [across, over_x, over_z, crossed_early], [tiles]
        )
        pieces = ((14, 0), (14, 1), *OVER_X, *OVER_Z)
        late = [tuple((e ^ 1, h) for e, h in pieces)]
        slabs = [crossed]
    else:
        tiles = lax.all_gather(slab, "grid", axis=0, tiled=True)
        points, ints, dest_mask = share(other_ints, other_points)
        *first, acc = basis_chunk(0, points, ints)
        second = basis_chunk(1, points, ints)
    chunks = [first, second]
    phis, radials, bases = zip(*chunks)

    some = 1 if late else 0
    chi, rho, *_ = pl.pallas_call(
        functools.partial(rho_kernel, late, starts),
        out_shape=[f32(slots, BLOCK, point_count), f32(slots, point_count)] + [tile_shape] * some,
        in_specs=[spec(SMEM)] + [spec(VMEM)] * (len(starts) + len(late) + 1),
        out_specs=[spec(VMEM)] * (2 + some),
        input_output_aliases={1 + len(starts) + len(late): 2} if late else {},
        compiler_params=params(blocks),
        cost_estimate=cost(5),
        name="density_at_points",
    )(ints, *phis, *slabs, tiles)

    if blk_count == 2:
        other = lax.ppermute(rho, "blk", [(0, 1), (1, 0)])
    else:
        other = lax.psum(rho, "blk") - rho

    rows = 3 * NATOM // LANES + dests // LANES
    outgoing, _ = pl.pallas_call(
        functools.partial(force_kernel, starts),
        out_shape=[f32(blk_count * grid_count, rows, LANES), f32(2, BPD, 5, BLOCK, LANES)],
        in_specs=[spec(SMEM)] + [spec(VMEM)] * (7 + 2 * len(starts)),
        out_specs=[spec(VMEM)] * 2,
        scratch_shapes=[pltpu.VMEM((slots, point_count), jnp.float32)],
        input_output_aliases={7 + 2 * len(starts): 1},
        compiler_params=params(blocks),
        cost_estimate=cost(5),
        name="forces_and_energies",
    )(ints, points, rho, other, chi, *radials, *bases, table, dest_mask, acc)

    arrived = lax.all_to_all(outgoing, ("blk", "grid"), split_axis=0, concat_axis=0, tiled=True)

    energy, forces = pl.pallas_call(
        functools.partial(sum_kernel, blk_count),
        out_shape=[f32(1, dests // grid_count), f32(3, NATOM)],
        in_specs=[spec(VMEM)],
        out_specs=[spec(VMEM)] * 2,
        compiler_params=params(blocks),
        name="final_sums",
    )(arrived)
    return (energy.reshape(dests // grid_count), forces)


def solution(mesh):
    in_specs = (
        P("blk", "grid"),
        P("grid", None, None),
        P("grid", None),
        P("grid"),
        P(),
        P(),
        P(),
        P(),
    )
    out_specs = (P("grid"), P())
    return jax.shard_map(local, mesh=mesh, in_specs=in_specs, out_specs=out_specs, check_vma=False)
```

```python
import functools

import jax
import jax.numpy as jnp
from jax import lax
from jax.experimental import pallas as pl
from jax.experimental.pallas import tpu as pltpu
from jax.sharding import PartitionSpec as P

BLOCK = 128
BPD = 6
NATOM = 256
LANES = 128
ROWS = 16
UNROLL = 4

SLATER = 0.7386
RHO_SOFT = 0.05

VMEM = pltpu.MemorySpace.VMEM
SMEM = pltpu.MemorySpace.SMEM


def aligned(start, size):
    return pl.ds(pl.multiple_of(start, size), size)


def live_count(ints_ref):
    row = ints_ref.shape[0] - 1
    slots = ints_ref.shape[1]
    step = 1
    while step * 2 <= slots:
        step *= 2
    count = jnp.int32(0)
    while step:
        more = count + step
        found = ints_ref[row, jnp.minimum(more, slots) - 1] >= 0
        count = jnp.where(jnp.logical_and(more <= slots, found), more, count)
        step //= 2
    return count


def start_copies(pairs, sems):
    copies = [pltpu.make_async_copy(src, dst, sems.at[i]) for i, (src, dst) in enumerate(pairs)]
    for copy in copies:
        copy.start()
    return copies


def place_slabs(offsets, slabs, tiles):
    me = lax.axis_index("grid")
    for e, slab in zip(offsets, slabs):
        if isinstance(e, tuple):
            half = slab.shape[1]
            for i, (one, h) in enumerate(e):
                first = (2 * jnp.bitwise_xor(me, one) + h) * half
                tiles[aligned(first, half), :] = slab[i]
        else:
            depth = slab.shape[0]
            tiles[aligned(jnp.bitwise_xor(me, e) * depth, depth), :] = slab[...]


def pack_kernel(picks, *refs):
    *parts, out_ref = refs
    half = out_ref.shape[1]
    for i, (p, h) in enumerate(picks):
        part = parts[p]
        out_ref[i] = part[h] if len(part.shape) == 3 else part[h * half : (h + 1) * half, :]


def share_kernel(own_ints, other_ints, own_points, other_points, points_out, ints_out, dest_ref):
    rows, slots = own_ints.shape
    core = lax.rem(lax.axis_index("grid"), 2)
    own, other = live_count(own_ints), live_count(other_ints)
    count0 = jnp.where(core == 0, own, other)
    half = lax.div(own + other + 1, 2)
    base = jnp.where(core == 0, 0, half)
    count = jnp.where(core == 0, half, own + other - half)
    lanes = lax.broadcasted_iota(jnp.int32, (1, slots), 1)
    dest_ids = lax.broadcasted_iota(jnp.int32, (1, dest_ref.shape[1]), 1)
    kept = [jnp.zeros((1, slots), jnp.int32)] * rows
    for v in range(slots):
        from0 = base + v < count0
        slot = jnp.clip(base + v - jnp.where(from0, 0, count0), 0, slots - 1)
        mine = from0 == (core == 0)
        points_out[v] = jnp.where(mine, own_points[slot], other_points[slot])
        values = [jnp.where(mine, own_ints[i, slot], other_ints[i, slot]) for i in range(rows)]
        values[-1] = jnp.where(v < count, values[-1], -1)
        kept = [jnp.where(lanes == v, value, row) for value, row in zip(values, kept)]
        dest_ref[v : v + 1, :] = jnp.where(dest_ids == values[-1], 1.0, 0.0)
    ints_out[...] = jnp.concatenate(kept, axis=0)


def table_kernel(
    atom_hbm,
    expo_hbm,
    coef_hbm,
    coords_hbm,
    points_hbm,
    slab_hbm,
    table_ref,
    points_out,
    slab_out,
    atom_ref,
    expo_ref,
    coef_ref,
    coords_ref,
    sems,
):
    copies = start_copies(
        [
            (atom_hbm, atom_ref),
            (expo_hbm, expo_ref),
            (coef_hbm, coef_ref),
            (coords_hbm, coords_ref),
            (points_hbm, points_out),
            (slab_hbm, slab_out),
        ],
        sems,
    )
    for copy in copies[:4]:
        copy.wait()
    coords = coords_ref[...]
    high = coords.astype(jnp.bfloat16)
    rest = coords - high.astype(jnp.float32)
    mid = rest.astype(jnp.bfloat16)
    low = (rest - mid.astype(jnp.float32)).astype(jnp.bfloat16)
    blocks = table_ref.shape[0]
    atoms = atom_ref[...].reshape(blocks, BLOCK)
    expos = expo_ref[...].reshape(blocks, BLOCK)

    for k in range(blocks):
        atom = atoms[k : k + 1]
        onehot = jnp.where(
            lax.broadcasted_iota(jnp.int32, (NATOM, BLOCK), 0) == atom, 1.0, 0.0
        ).astype(jnp.bfloat16)
        picked = [
            jnp.dot(part, onehot, preferred_element_type=jnp.float32) for part in (high, mid, low)
        ]
        center = (picked[0] + picked[1]) + picked[2]
        coef = coef_ref[:, k * BLOCK : (k + 1) * BLOCK]
        rows = jnp.concatenate(
            [center, coef, expos[k : k + 1], atom.astype(jnp.float32)], axis=0
        )
        columns = rows.T
        for p in range(8):
            table_ref[k, p] = jnp.broadcast_to(columns[:, p : p + 1], (BLOCK, LANES))

    for copy in copies[4:]:
        copy.wait()


def chunk_steps(ints_ref, first, size):
    left = jnp.clip(live_count(ints_ref) - first, 0, size)
    return lax.div(left + (UNROLL - 1), UNROLL)


def phi_kernel(first, offsets, ints_ref, points_ref, table_ref, *refs):
    slabs = refs[: len(offsets)]
    outputs = 3 + (1 if first == 0 else 0) + (1 if offsets else 0)
    phi_ref, radial_ref, basis_ref, *more = refs[len(refs) - outputs :]
    if first == 0:
        more.pop(0)[...] = jnp.zeros((BPD, 5, BLOCK, LANES), jnp.float32)
    if offsets:
        place_slabs(offsets, slabs, more[0])
    blk = lax.axis_index("blk")
    length = ints_ref.shape[0] - 1
    point_count = points_ref.shape[2]

    def one_slot(s):
        for j in range(length):
            k = ints_ref[lax.rem(blk + j, length), first + s]
            for r in range(0, BLOCK, ROWS):
                sub = slice(r, r + ROWS)
                cx, cy, cz, sx, sy, sz, expo = [table_ref[k, p, sub] for p in range(7)]
                for h in range(0, point_count, LANES):
                    lanes = slice(h, h + LANES)
                    ox = points_ref[first + s, 0:1, lanes] - cx
                    oy = points_ref[first + s, 1:2, lanes] - cy
                    oz = points_ref[first + s, 2:3, lanes] - cz
                    squared = ox * ox + oy * oy + oz * oz
                    radial = jnp.exp(-expo * squared)
                    linear = 1.0 + (sx * ox + sy * oy + sz * oz)
                    basis = linear * radial
                    rows = slice(j * BLOCK + r, j * BLOCK + r + ROWS)
                    phi_ref[s, rows, lanes] = basis.astype(jnp.bfloat16)
                    if j == 0:
                        radial_ref[s, sub, lanes] = radial
                        basis_ref[s, sub, lanes] = basis

    def some_slots(i, carry):
        for u in range(2):
            one_slot(i * 2 + u)
        return carry

    steps = chunk_steps(ints_ref, first, phi_ref.shape[0]) * (UNROLL // 2)
    lax.fori_loop(0, steps, some_slots, 0)


def rho_kernel(offsets, starts, ints_ref, *refs):
    chunks = len(starts)
    phis = refs[:chunks]
    slabs = refs[chunks : chunks + len(offsets)]
    tiles, chi_ref, rho_ref, *placed = refs[chunks + len(offsets) :]
    if offsets:
        tiles = placed[0]
        place_slabs(offsets, slabs, tiles)
    blk = lax.axis_index("blk")
    length = ints_ref.shape[0] - 1
    rho_ref[...] = jnp.zeros_like(rho_ref)

    for c, phi_ref in enumerate(phis):
        size = phi_ref.shape[0]

        def one_slot(s, first=starts[c], phi_ref=phi_ref):
            slot = first + s
            own = ints_ref[blk, slot]
            cols = aligned((own - blk * BPD) * BLOCK, BLOCK)
            left = [tiles[aligned(own * BLOCK, BLOCK), cols]]
            for j in range(1, length):
                k = ints_ref[lax.rem(blk + j, length), slot]
                left.append(tiles[aligned(k * BLOCK, BLOCK), cols].T)
            chi = jnp.dot(
                jnp.concatenate(left, axis=1), phi_ref[s], preferred_element_type=jnp.float32
            )
            phi = phi_ref[s, 0:BLOCK, :]
            chi_ref[slot] = chi
            rho_ref[pl.ds(slot, 1), :] = jnp.sum(
                phi.astype(jnp.float32) * chi, axis=0, keepdims=True
            )

        def some_slots(i, carry, one_slot=one_slot):
            for u in range(UNROLL):
                one_slot(i * UNROLL + u)
            return carry

        lax.fori_loop(0, chunk_steps(ints_ref, starts[c], size), some_slots, 0)


def force_kernel(starts, ints_ref, points_ref, rho_a_ref, rho_b_ref, chi_ref, *refs):
    chunks = len(starts)
    radials = refs[:chunks]
    bases = refs[chunks : 2 * chunks]
    table_ref, dest_ref, _, out_ref, acc, pot_ref = refs[2 * chunks :]
    blk = lax.axis_index("blk")
    slots, _, point_count = points_ref.shape
    dests = dest_ref.shape[1]
    live = live_count(ints_ref)
    rho = rho_a_ref[...] + rho_b_ref[...]
    weight = points_ref[:, 3, :]
    log_sq = jnp.log(rho * rho + RHO_SOFT * RHO_SOFT)
    pot = weight * (-(4.0 / 3.0) * SLATER) * rho * jnp.exp(log_sq * (-1.0 / 3.0))
    slot_ids = lax.broadcasted_iota(jnp.int32, (slots, 1), 0)
    pot_ref[...] = jnp.where(slot_ids < live, pot, 0.0)
    energies = jnp.sum(weight * -SLATER * jnp.exp(log_sq * (2.0 / 3.0)), axis=1, keepdims=True)

    for c in range(chunks):
        radial_ref, basis_ref = radials[c], bases[c]
        size = radial_ref.shape[0]

        def one_slot(s, first=starts[c], radial_ref=radial_ref, basis_ref=basis_ref):
            slot = first + s
            own = ints_ref[blk, slot] - blk * BPD
            pots = pot_ref[pl.ds(slot, 1), :]
            for r in range(0, BLOCK, ROWS):
                sub = slice(r, r + ROWS)
                sums = None
                for h in range(0, point_count, LANES):
                    lanes = slice(h, h + LANES)
                    u = chi_ref[slot, sub, lanes] * pots[:, lanes]
                    ub = u * basis_ref[s, sub, lanes]
                    terms = (
                        u * radial_ref[s, sub, lanes],
                        ub,
                        ub * points_ref[slot, 0:1, lanes],
                        ub * points_ref[slot, 1:2, lanes],
                        ub * points_ref[slot, 2:3, lanes],
                    )
                    sums = terms if sums is None else [a + b for a, b in zip(sums, terms)]
                for q in range(5):
                    acc[own, q, sub] += sums[q]

        def some_slots(i, carry, one_slot=one_slot):
            for u in range(UNROLL):
                one_slot(i * UNROLL + u)
            return carry

        lax.fori_loop(0, chunk_steps(ints_ref, starts[c], size), some_slots, 0)

    lane_ids = lax.broadcasted_iota(jnp.int32, (1, LANES), 1).astype(jnp.float32)

    totals = [jnp.zeros((8, LANES), jnp.float32)] * (3 * NATOM // LANES)
    for b in range(BPD):
        k = blk * BPD + b
        for r in range(0, BLOCK, ROWS):
            sub = slice(r, r + ROWS)
            parts = [acc[b, q, sub] for q in range(5)]
            doubled = 2.0 * table_ref[k, 6, sub]
            atom = table_ref[k, 7, sub]
            for c in range(3):
                force = table_ref[k, 3 + c, sub] * parts[0] - doubled * (
                    parts[2 + c] - table_ref[k, c, sub] * parts[1]
                )
                column = 2.0 * jnp.sum(force, axis=1, keepdims=True)
                for h in range(NATOM // LANES):
                    hit = jnp.where(atom == lane_ids + float(h * LANES), column, 0.0)
                    i = c * (NATOM // LANES) + h
                    totals[i] = totals[i] + sum(hit[i8 : i8 + 8] for i8 in range(0, ROWS, 8))
    rows = [jnp.sum(t, axis=0, keepdims=True) for t in totals]
    moved = jnp.sum(dest_ref[...] * energies, axis=0, keepdims=True)
    rows += [moved[:, h : h + LANES] for h in range(0, dests, LANES)]
    packed = jnp.concatenate(rows, axis=0)
    for i in range(out_ref.shape[0]):
        out_ref[i] = packed


def sum_kernel(copies, arrived_ref, energy_ref, forces_ref):
    me = lax.axis_index("grid")
    total = jnp.sum(arrived_ref[...], axis=0)
    per = NATOM // LANES
    for c in range(3):
        for h in range(per):
            forces_ref[c : c + 1, h * LANES : (h + 1) * LANES] = total[c * per + h : c * per + h + 1]
    width = energy_ref.shape[1]
    first = me * width
    energy = jnp.zeros((1, LANES), jnp.float32)
    for i in range(3 * per, total.shape[0]):
        chosen = lax.div(first, LANES) == i - 3 * per
        energy = jnp.where(chosen, total[i : i + 1], energy)
    turn = lax.rem(LANES - lax.rem(first, LANES), LANES)
    energy = pltpu.roll(jnp.broadcast_to(energy, (8, LANES)), turn, 1)
    energy_ref[...] = energy[0:1, 0:width] * (1.0 / copies)


def swap(array, offset):
    count = lax.axis_size("grid")
    return lax.ppermute(array, "grid", [(i, i ^ offset) for i in range(count)])


FIRST = (8, 4, 2)
OVER_X = ((10, 0), (10, 1), (6, 0))
OVER_Z = ((12, 0), (12, 1), (6, 1))


def in_hbm(array):
    return pltpu.with_memory_space_constraint(array, pltpu.HBM)


def spec(space):
    return pl.BlockSpec(memory_space=space)


def params(blocks):
    return pltpu.CompilerParams(vmem_limit_bytes=blocks * 1024 * 1024)


def cost(nominal_us):
    return pl.CostEstimate(
        flops=0, bytes_accessed=int(nominal_us * 3.69e6), transcendentals=0
    )


def f32(*shape):
    return jax.ShapeDtypeStruct(shape, jnp.float32)


def local(density, points, sig_blocks, migration, atom_coords, exponents, shape_coef, func_atom):
    grid_count = lax.axis_size("grid")
    blk_count = lax.axis_size("blk")
    slots, _, point_count = points.shape
    length = sig_blocks.shape[1]
    functions = exponents.shape[0]
    blocks = functions // BLOCK
    dests = grid_count * (slots // 2)
    sizes = [slots // 8 * 7, slots // 8]
    starts = [0, slots // 8 * 7]
    tied = lax.optimization_barrier

    slab = density.T
    held = {0: slab}
    if grid_count == 16:
        for e in FIRST:
            held[e] = swap(slab, e)
    ints = jnp.concatenate([sig_blocks.T, migration[None]], axis=0)
    other_ints, other_points = swap(ints, 1), swap(points, 1)
    table, points, near_slab = pl.pallas_call(
        table_kernel,
        out_shape=[
            f32(blocks, 8, BLOCK, LANES),
            f32(*points.shape),
            jax.ShapeDtypeStruct(slab.shape, slab.dtype),
        ],
        in_specs=[spec(pltpu.HBM)] * 6,
        out_specs=[spec(VMEM)] * 3,
        scratch_shapes=[
            pltpu.VMEM((functions,), jnp.int32),
            pltpu.VMEM((functions,), jnp.float32),
            pltpu.VMEM((3, functions), jnp.float32),
            pltpu.VMEM((3, NATOM), jnp.float32),
            pltpu.SemaphoreType.DMA((6,)),
        ],
        compiler_params=params(blocks),
        cost_estimate=cost(4),
        name="param_table",
    )(*[in_hbm(a) for a in (func_atom, exponents, shape_coef, atom_coords, points, slab)])

    def share(other_ints, other_points):
        return pl.pallas_call(
            share_kernel,
            out_shape=[
                f32(*points.shape),
                jax.ShapeDtypeStruct(ints.shape, jnp.int32),
                f32(slots, dests),
            ],
            in_specs=[spec(SMEM)] * 2 + [spec(VMEM)] * 2,
            out_specs=[spec(VMEM)] * 3,
            compiler_params=params(blocks),
            cost_estimate=cost(1),
            name="shared_slots",
        )(ints, other_ints, points, other_points)

    tile_shape = jax.ShapeDtypeStruct((functions, BPD * BLOCK), jnp.bfloat16)

    def basis_chunk(c, points, ints, offsets=(), slabs=(), tiles=()):
        some = 1 if offsets else 0
        zeros = 1 if c == 0 else 0
        inputs = [ints, points, table, *slabs, *tiles]
        return pl.pallas_call(
            functools.partial(phi_kernel, starts[c], offsets),
            out_shape=[
                jax.ShapeDtypeStruct((sizes[c], length * BLOCK, point_count), jnp.bfloat16),
                f32(sizes[c], BLOCK, point_count),
                f32(sizes[c], BLOCK, point_count),
            ]
            + [f32(BPD, 5, BLOCK, LANES)] * zeros
            + [tile_shape] * some,
            in_specs=[spec(SMEM)] + [spec(VMEM)] * (len(inputs) - 1),
            out_specs=[spec(VMEM)] * (3 + zeros + some),
            input_output_aliases={len(inputs) - 1: 3 + zeros} if tiles else {},
            compiler_params=params(blocks),
            cost_estimate=cost(5),
            name="basis_values",
        )(*inputs)

    def pack(parts, picks):
        return pl.pallas_call(
            functools.partial(pack_kernel, picks),
            out_shape=jax.ShapeDtypeStruct(
                (len(picks), slab.shape[0] // 2, slab.shape[1]), slab.dtype
            ),
            in_specs=[spec(VMEM)] * len(parts),
            out_specs=spec(VMEM),
            compiler_params=params(blocks),
            name="pack",
        )(*parts)

    late, slabs = [], []
    if grid_count == 16:
        held[0] = near_slab
        held, other_ints, other_points, table = tied((held, other_ints, other_points, table))
        ready = list(held)
        over_x = swap(pack((held[8], held[4]), ((0, 0), (0, 1), (1, 0))), 2)
        over_z = swap(pack((held[8], held[2]), ((0, 0), (0, 1), (1, 1))), 4)
        across = swap(held[8], 6)
        early = tuple((e ^ 1, h) for e in ready for h in range(2))
        picks = [(p, h) for p in range(len(ready)) for h in range(2)]
        crossed_early = swap(pack([held[e] for e in ready], picks), 1)
        points, ints, dest_mask = share(other_ints, other_points)
        *first, acc, tiles = basis_chunk(0, points, ints, ready, [held[e] for e in ready])
        held, across, over_x, over_z, first, tiles, points = tied(
            (held, across, over_x, over_z, first, tiles, points)
        )
        halves = [(p, h) for p in range(3) for h in range(3)]
        crossed = swap(pack((across, over_x, over_z), [(0, 0), (0, 1), *halves[3:]]), 1)
        placed = [14, OVER_X, OVER_Z, early]
        *second, tiles = basis_chunk(
            1, points, ints, placed, [across, over_x, over_z, crossed_early], [tiles]
        )
        pieces = ((14, 0), (14, 1), *OVER_X, *OVER_Z)
        late = [tuple((e ^ 1, h) for e, h in pieces)]
        slabs = [crossed]
    else:
        tiles = lax.all_gather(slab, "grid", axis=0, tiled=True)
        points, ints, dest_mask = share(other_ints, other_points)
        *first, acc = basis_chunk(0, points, ints)
        second = basis_chunk(1, points, ints)
    chunks = [first, second]
    phis, radials, bases = zip(*chunks)

    some = 1 if late else 0
    chi, rho, *_ = pl.pallas_call(
        functools.partial(rho_kernel, late, starts),
        out_shape=[f32(slots, BLOCK, point_count), f32(slots, point_count)] + [tile_shape] * some,
        in_specs=[spec(SMEM)] + [spec(VMEM)] * (len(starts) + len(late) + 1),
        out_specs=[spec(VMEM)] * (2 + some),
        input_output_aliases={1 + len(starts) + len(late): 2} if late else {},
        compiler_params=params(blocks),
        cost_estimate=cost(5),
        name="density_at_points",
    )(ints, *phis, *slabs, tiles)

    if blk_count == 2:
        other = lax.ppermute(rho, "blk", [(0, 1), (1, 0)])
    else:
        other = lax.psum(rho, "blk") - rho

    rows = 3 * NATOM // LANES + dests // LANES
    outgoing, _ = pl.pallas_call(
        functools.partial(force_kernel, starts),
        out_shape=[f32(blk_count * grid_count, rows, LANES), f32(BPD, 5, BLOCK, LANES)],
        in_specs=[spec(SMEM)] + [spec(VMEM)] * (7 + 2 * len(starts)),
        out_specs=[spec(VMEM)] * 2,
        scratch_shapes=[pltpu.VMEM((slots, point_count), jnp.float32)],
        input_output_aliases={7 + 2 * len(starts): 1},
        compiler_params=params(blocks),
        cost_estimate=cost(5),
        name="forces_and_energies",
    )(ints, points, rho, other, chi, *radials, *bases, table, dest_mask, acc)

    arrived = lax.all_to_all(outgoing, ("blk", "grid"), split_axis=0, concat_axis=0, tiled=True)

    energy, forces = pl.pallas_call(
        functools.partial(sum_kernel, blk_count),
        out_shape=[f32(1, dests // grid_count), f32(3, NATOM)],
        in_specs=[spec(VMEM)],
        out_specs=[spec(VMEM)] * 2,
        compiler_params=params(blocks),
        name="final_sums",
    )(arrived)
    return (energy.reshape(dests // grid_count), forces)


def solution(mesh):
    in_specs = (
        P("blk", "grid"),
        P("grid", None, None),
        P("grid", None),
        P("grid"),
        P(),
        P(),
        P(),
        P(),
    )
    out_specs = (P("grid"), P())
    return jax.shard_map(local, mesh=mesh, in_specs=in_specs, out_specs=out_specs, check_vma=False)
```

```python
import functools

import jax
import jax.numpy as jnp
from jax import lax
from jax.experimental import pallas as pl
from jax.experimental.pallas import tpu as pltpu
from jax.sharding import PartitionSpec as P

BLOCK = 128
BPD = 6
NATOM = 256
LANES = 128
ROWS = 32
UNROLL = 2

SLATER = 0.7386
RHO_SOFT = 0.05

VMEM = pltpu.MemorySpace.VMEM
SMEM = pltpu.MemorySpace.SMEM


def aligned(start, size):
    return pl.ds(pl.multiple_of(start, size), size)


def live_count(ints_ref):
    row = ints_ref.shape[0] - 1
    slots = ints_ref.shape[1]
    step = 1
    while step * 2 <= slots:
        step *= 2
    count = jnp.int32(0)
    while step:
        more = count + step
        found = ints_ref[row, jnp.minimum(more, slots) - 1] >= 0
        count = jnp.where(jnp.logical_and(more <= slots, found), more, count)
        step //= 2
    return count


def start_copies(pairs, sems):
    copies = [pltpu.make_async_copy(src, dst, sems.at[i]) for i, (src, dst) in enumerate(pairs)]
    for copy in copies:
        copy.start()
    return copies


def place_slabs(offsets, slabs, tiles):
    me = lax.axis_index("grid")
    for e, slab in zip(offsets, slabs):
        if isinstance(e, tuple):
            half = slab.shape[1]
            for i, (one, h) in enumerate(e):
                first = (2 * jnp.bitwise_xor(me, one) + h) * half
                tiles[aligned(first, half), :] = slab[i]
        else:
            depth = slab.shape[0]
            tiles[aligned(jnp.bitwise_xor(me, e) * depth, depth), :] = slab[...]


def pack_kernel(picks, *refs):
    *parts, out_ref = refs
    half = out_ref.shape[1]
    for i, (p, h) in enumerate(picks):
        part = parts[p]
        out_ref[i] = part[h] if len(part.shape) == 3 else part[h * half : (h + 1) * half, :]


def share_kernel(own_ints, other_ints, own_points, other_points, points_out, ints_out, dest_ref):
    rows, slots = own_ints.shape
    core = lax.rem(lax.axis_index("grid"), 2)
    own, other = live_count(own_ints), live_count(other_ints)
    count0 = jnp.where(core == 0, own, other)
    half = lax.div(own + other + 1, 2)
    base = jnp.where(core == 0, 0, half)
    count = jnp.where(core == 0, half, own + other - half)
    lanes = lax.broadcasted_iota(jnp.int32, (1, slots), 1)
    dest_ids = lax.broadcasted_iota(jnp.int32, (1, dest_ref.shape[1]), 1)
    kept = [jnp.zeros((1, slots), jnp.int32)] * rows
    for v in range(slots):
        from0 = base + v < count0
        slot = jnp.clip(base + v - jnp.where(from0, 0, count0), 0, slots - 1)
        mine = from0 == (core == 0)
        points_out[v] = jnp.where(mine, own_points[slot], other_points[slot])
        values = [jnp.where(mine, own_ints[i, slot], other_ints[i, slot]) for i in range(rows)]
        values[-1] = jnp.where(v < count, values[-1], -1)
        kept = [jnp.where(lanes == v, value, row) for value, row in zip(values, kept)]
        dest_ref[v : v + 1, :] = jnp.where(dest_ids == values[-1], 1.0, 0.0)
    ints_out[...] = jnp.concatenate(kept, axis=0)


def table_kernel(
    atom_hbm,
    expo_hbm,
    coef_hbm,
    coords_hbm,
    points_hbm,
    slab_hbm,
    table_ref,
    points_out,
    slab_out,
    atom_ref,
    expo_ref,
    coef_ref,
    coords_ref,
    sems,
):
    copies = start_copies(
        [
            (atom_hbm, atom_ref),
            (expo_hbm, expo_ref),
            (coef_hbm, coef_ref),
            (coords_hbm, coords_ref),
            (points_hbm, points_out),
            (slab_hbm, slab_out),
        ],
        sems,
    )
    for copy in copies[:4]:
        copy.wait()
    coords = coords_ref[...]
    high = coords.astype(jnp.bfloat16)
    rest = coords - high.astype(jnp.float32)
    mid = rest.astype(jnp.bfloat16)
    low = (rest - mid.astype(jnp.float32)).astype(jnp.bfloat16)
    blocks = table_ref.shape[0]
    atoms = atom_ref[...].reshape(blocks, BLOCK)
    expos = expo_ref[...].reshape(blocks, BLOCK)

    for k in range(blocks):
        atom = atoms[k : k + 1]
        onehot = jnp.where(
            lax.broadcasted_iota(jnp.int32, (NATOM, BLOCK), 0) == atom, 1.0, 0.0
        ).astype(jnp.bfloat16)
        picked = [
            jnp.dot(part, onehot, preferred_element_type=jnp.float32) for part in (high, mid, low)
        ]
        center = (picked[0] + picked[1]) + picked[2]
        coef = coef_ref[:, k * BLOCK : (k + 1) * BLOCK]
        rows = jnp.concatenate(
            [center, coef, expos[k : k + 1], atom.astype(jnp.float32)], axis=0
        )
        columns = rows.T
        for p in range(8):
            table_ref[k, p] = jnp.broadcast_to(columns[:, p : p + 1], (BLOCK, LANES))

    for copy in copies[4:]:
        copy.wait()


def chunk_steps(ints_ref, first, size):
    left = jnp.clip(live_count(ints_ref) - first, 0, size)
    return lax.div(left + (UNROLL - 1), UNROLL)


def phi_kernel(first, offsets, ints_ref, points_ref, table_ref, *refs):
    slabs = refs[: len(offsets)]
    outputs = 3 + (1 if first == 0 else 0) + (1 if offsets else 0)
    phi_ref, radial_ref, basis_ref, *more = refs[len(refs) - outputs :]
    if first == 0:
        more.pop(0)[...] = jnp.zeros((BPD, 5, BLOCK, LANES), jnp.float32)
    if offsets:
        place_slabs(offsets, slabs, more[0])
    blk = lax.axis_index("blk")
    length = ints_ref.shape[0] - 1
    point_count = points_ref.shape[2]

    def one_slot(s):
        for j in range(length):
            k = ints_ref[lax.rem(blk + j, length), first + s]
            for r in range(0, BLOCK, ROWS):
                sub = slice(r, r + ROWS)
                cx, cy, cz, sx, sy, sz, expo = [table_ref[k, p, sub] for p in range(7)]
                for h in range(0, point_count, LANES):
                    lanes = slice(h, h + LANES)
                    ox = points_ref[first + s, 0:1, lanes] - cx
                    oy = points_ref[first + s, 1:2, lanes] - cy
                    oz = points_ref[first + s, 2:3, lanes] - cz
                    squared = ox * ox + oy * oy + oz * oz
                    radial = jnp.exp(-expo * squared)
                    linear = 1.0 + (sx * ox + sy * oy + sz * oz)
                    basis = linear * radial
                    rows = slice(j * BLOCK + r, j * BLOCK + r + ROWS)
                    phi_ref[s, rows, lanes] = basis.astype(jnp.bfloat16)
                    if j == 0:
                        radial_ref[s, sub, lanes] = radial
                        basis_ref[s, sub, lanes] = basis

    def some_slots(i, carry):
        for u in range(2):
            one_slot(i * 2 + u)
        return carry

    steps = chunk_steps(ints_ref, first, phi_ref.shape[0]) * (UNROLL // 2)
    lax.fori_loop(0, steps, some_slots, 0)


def rho_kernel(offsets, starts, ints_ref, *refs):
    chunks = len(starts)
    phis = refs[:chunks]
    slabs = refs[chunks : chunks + len(offsets)]
    tiles, chi_ref, rho_ref, *placed = refs[chunks + len(offsets) :]
    if offsets:
        tiles = placed[0]
        place_slabs(offsets, slabs, tiles)
    blk = lax.axis_index("blk")
    length = ints_ref.shape[0] - 1
    rho_ref[...] = jnp.zeros_like(rho_ref)

    for c, phi_ref in enumerate(phis):
        size = phi_ref.shape[0]

        def one_slot(s, first=starts[c], phi_ref=phi_ref):
            slot = first + s
            own = ints_ref[blk, slot]
            cols = aligned((own - blk * BPD) * BLOCK, BLOCK)
            left = [tiles[aligned(own * BLOCK, BLOCK), cols]]
            for j in range(1, length):
                k = ints_ref[lax.rem(blk + j, length), slot]
                left.append(tiles[aligned(k * BLOCK, BLOCK), cols].T)
            chi = jnp.dot(
                jnp.concatenate(left, axis=1), phi_ref[s], preferred_element_type=jnp.float32
            )
            phi = phi_ref[s, 0:BLOCK, :]
            chi_ref[slot] = chi
            rho_ref[pl.ds(slot, 1), :] = jnp.sum(
                phi.astype(jnp.float32) * chi, axis=0, keepdims=True
            )

        def some_slots(i, carry, one_slot=one_slot):
            for u in range(UNROLL):
                one_slot(i * UNROLL + u)
            return carry

        lax.fori_loop(0, chunk_steps(ints_ref, starts[c], size), some_slots, 0)


def force_kernel(starts, ints_ref, points_ref, rho_a_ref, rho_b_ref, chi_ref, *refs):
    chunks = len(starts)
    radials = refs[:chunks]
    bases = refs[chunks : 2 * chunks]
    table_ref, dest_ref, _, out_ref, acc, pot_ref = refs[2 * chunks :]
    blk = lax.axis_index("blk")
    slots, _, point_count = points_ref.shape
    dests = dest_ref.shape[1]
    live = live_count(ints_ref)
    rho = rho_a_ref[...] + rho_b_ref[...]
    weight = points_ref[:, 3, :]
    log_sq = jnp.log(rho * rho + RHO_SOFT * RHO_SOFT)
    pot = weight * (-(4.0 / 3.0) * SLATER) * rho * jnp.exp(log_sq * (-1.0 / 3.0))
    slot_ids = lax.broadcasted_iota(jnp.int32, (slots, 1), 0)
    pot_ref[...] = jnp.where(slot_ids < live, pot, 0.0)
    energies = jnp.sum(weight * -SLATER * jnp.exp(log_sq * (2.0 / 3.0)), axis=1, keepdims=True)

    for c in range(chunks):
        radial_ref, basis_ref = radials[c], bases[c]
        size = radial_ref.shape[0]

        def one_slot(s, first=starts[c], radial_ref=radial_ref, basis_ref=basis_ref):
            slot = first + s
            own = ints_ref[blk, slot] - blk * BPD
            pots = pot_ref[pl.ds(slot, 1), :]
            for r in range(0, BLOCK, ROWS):
                sub = slice(r, r + ROWS)
                sums = None
                for h in range(0, point_count, LANES):
                    lanes = slice(h, h + LANES)
                    u = chi_ref[slot, sub, lanes] * pots[:, lanes]
                    ub = u * basis_ref[s, sub, lanes]
                    terms = (
                        u * radial_ref[s, sub, lanes],
                        ub,
                        ub * points_ref[slot, 0:1, lanes],
                        ub * points_ref[slot, 1:2, lanes],
                        ub * points_ref[slot, 2:3, lanes],
                    )
                    sums = terms if sums is None else [a + b for a, b in zip(sums, terms)]
                for q in range(5):
                    acc[own, q, sub] += sums[q]

        def some_slots(i, carry, one_slot=one_slot):
            for u in range(UNROLL):
                one_slot(i * UNROLL + u)
            return carry

        lax.fori_loop(0, chunk_steps(ints_ref, starts[c], size), some_slots, 0)

    lane_ids = lax.broadcasted_iota(jnp.int32, (1, LANES), 1).astype(jnp.float32)

    totals = [jnp.zeros((8, LANES), jnp.float32)] * (3 * NATOM // LANES)
    for b in range(BPD):
        k = blk * BPD + b
        for r in range(0, BLOCK, ROWS):
            sub = slice(r, r + ROWS)
            parts = [acc[b, q, sub] for q in range(5)]
            doubled = 2.0 * table_ref[k, 6, sub]
            atom = table_ref[k, 7, sub]
            for c in range(3):
                force = table_ref[k, 3 + c, sub] * parts[0] - doubled * (
                    parts[2 + c] - table_ref[k, c, sub] * parts[1]
                )
                column = 2.0 * jnp.sum(force, axis=1, keepdims=True)
                for h in range(NATOM // LANES):
                    hit = jnp.where(atom == lane_ids + float(h * LANES), column, 0.0)
                    i = c * (NATOM // LANES) + h
                    totals[i] = totals[i] + sum(hit[i8 : i8 + 8] for i8 in range(0, ROWS, 8))
    rows = [jnp.sum(t, axis=0, keepdims=True) for t in totals]
    moved = jnp.sum(dest_ref[...] * energies, axis=0, keepdims=True)
    rows += [moved[:, h : h + LANES] for h in range(0, dests, LANES)]
    packed = jnp.concatenate(rows, axis=0)
    for i in range(out_ref.shape[0]):
        out_ref[i] = packed


def sum_kernel(copies, arrived_ref, energy_ref, forces_ref):
    me = lax.axis_index("grid")
    total = jnp.sum(arrived_ref[...], axis=0)
    per = NATOM // LANES
    for c in range(3):
        for h in range(per):
            forces_ref[c : c + 1, h * LANES : (h + 1) * LANES] = total[c * per + h : c * per + h + 1]
    width = energy_ref.shape[1]
    first = me * width
    energy = jnp.zeros((1, LANES), jnp.float32)
    for i in range(3 * per, total.shape[0]):
        chosen = lax.div(first, LANES) == i - 3 * per
        energy = jnp.where(chosen, total[i : i + 1], energy)
    turn = lax.rem(LANES - lax.rem(first, LANES), LANES)
    energy = pltpu.roll(jnp.broadcast_to(energy, (8, LANES)), turn, 1)
    energy_ref[...] = energy[0:1, 0:width] * (1.0 / copies)


def swap(array, offset):
    count = lax.axis_size("grid")
    return lax.ppermute(array, "grid", [(i, i ^ offset) for i in range(count)])


FIRST = (8, 4, 2)
OVER_X = ((10, 0), (10, 1), (6, 0))
OVER_Z = ((12, 0), (12, 1), (6, 1))


def in_hbm(array):
    return pltpu.with_memory_space_constraint(array, pltpu.HBM)


def spec(space):
    return pl.BlockSpec(memory_space=space)


def params(blocks):
    return pltpu.CompilerParams(vmem_limit_bytes=blocks * 1024 * 1024)


def cost(nominal_us):
    return pl.CostEstimate(
        flops=0, bytes_accessed=int(nominal_us * 3.69e6), transcendentals=0
    )


def f32(*shape):
    return jax.ShapeDtypeStruct(shape, jnp.float32)


def local(density, points, sig_blocks, migration, atom_coords, exponents, shape_coef, func_atom):
    grid_count = lax.axis_size("grid")
    blk_count = lax.axis_size("blk")
    slots, _, point_count = points.shape
    length = sig_blocks.shape[1]
    functions = exponents.shape[0]
    blocks = functions // BLOCK
    dests = grid_count * (slots // 2)
    sizes = [slots // 8 * 7, slots // 8]
    starts = [0, slots // 8 * 7]
    tied = lax.optimization_barrier

    slab = density.T
    held = {0: slab}
    if grid_count == 16:
        for e in FIRST:
            held[e] = swap(slab, e)
    ints = jnp.concatenate([sig_blocks.T, migration[None]], axis=0)
    other_ints, other_points = swap(ints, 1), swap(points, 1)
    table, points, near_slab = pl.pallas_call(
        table_kernel,
        out_shape=[
            f32(blocks, 8, BLOCK, LANES),
            f32(*points.shape),
            jax.ShapeDtypeStruct(slab.shape, slab.dtype),
        ],
        in_specs=[spec(pltpu.HBM)] * 6,
        out_specs=[spec(VMEM)] * 3,
        scratch_shapes=[
            pltpu.VMEM((functions,), jnp.int32),
            pltpu.VMEM((functions,), jnp.float32),
            pltpu.VMEM((3, functions), jnp.float32),
            pltpu.VMEM((3, NATOM), jnp.float32),
            pltpu.SemaphoreType.DMA((6,)),
        ],
        compiler_params=params(blocks),
        cost_estimate=cost(4),
        name="param_table",
    )(*[in_hbm(a) for a in (func_atom, exponents, shape_coef, atom_coords, points, slab)])

    def share(other_ints, other_points):
        return pl.pallas_call(
            share_kernel,
            out_shape=[
                f32(*points.shape),
                jax.ShapeDtypeStruct(ints.shape, jnp.int32),
                f32(slots, dests),
            ],
            in_specs=[spec(SMEM)] * 2 + [spec(VMEM)] * 2,
            out_specs=[spec(VMEM)] * 3,
            compiler_params=params(blocks),
            cost_estimate=cost(1),
            name="shared_slots",
        )(ints, other_ints, points, other_points)

    tile_shape = jax.ShapeDtypeStruct((functions, BPD * BLOCK), jnp.bfloat16)

    def basis_chunk(c, points, ints, offsets=(), slabs=(), tiles=()):
        some = 1 if offsets else 0
        zeros = 1 if c == 0 else 0
        inputs = [ints, points, table, *slabs, *tiles]
        return pl.pallas_call(
            functools.partial(phi_kernel, starts[c], offsets),
            out_shape=[
                jax.ShapeDtypeStruct((sizes[c], length * BLOCK, point_count), jnp.bfloat16),
                f32(sizes[c], BLOCK, point_count),
                f32(sizes[c], BLOCK, point_count),
            ]
            + [f32(BPD, 5, BLOCK, LANES)] * zeros
            + [tile_shape] * some,
            in_specs=[spec(SMEM)] + [spec(VMEM)] * (len(inputs) - 1),
            out_specs=[spec(VMEM)] * (3 + zeros + some),
            input_output_aliases={len(inputs) - 1: 3 + zeros} if tiles else {},
            compiler_params=params(blocks),
            cost_estimate=cost(5),
            name="basis_values",
        )(*inputs)

    def pack(parts, picks):
        return pl.pallas_call(
            functools.partial(pack_kernel, picks),
            out_shape=jax.ShapeDtypeStruct(
                (len(picks), slab.shape[0] // 2, slab.shape[1]), slab.dtype
            ),
            in_specs=[spec(VMEM)] * len(parts),
            out_specs=spec(VMEM),
            compiler_params=params(blocks),
            name="pack",
        )(*parts)

    late, slabs = [], []
    if grid_count == 16:
        held[0] = near_slab
        held, other_ints, other_points, table = tied((held, other_ints, other_points, table))
        ready = list(held)
        over_x = swap(pack((held[8], held[4]), ((0, 0), (0, 1), (1, 0))), 2)
        over_z = swap(pack((held[8], held[2]), ((0, 0), (0, 1), (1, 1))), 4)
        across = swap(held[8], 6)
        early = tuple((e ^ 1, h) for e in ready for h in range(2))
        picks = [(p, h) for p in range(len(ready)) for h in range(2)]
        crossed_early = swap(pack([held[e] for e in ready], picks), 1)
        points, ints, dest_mask = share(other_ints, other_points)
        *first, acc, tiles = basis_chunk(0, points, ints, ready, [held[e] for e in ready])
        held, across, over_x, over_z, first, tiles, points = tied(
            (held, across, over_x, over_z, first, tiles, points)
        )
        halves = [(p, h) for p in range(3) for h in range(3)]
        crossed = swap(pack((across, over_x, over_z), [(0, 0), (0, 1), *halves[3:]]), 1)
        placed = [14, OVER_X, OVER_Z, early]
        *second, tiles = basis_chunk(
            1, points, ints, placed, [across, over_x, over_z, crossed_early], [tiles]
        )
        pieces = ((14, 0), (14, 1), *OVER_X, *OVER_Z)
        late = [tuple((e ^ 1, h) for e, h in pieces)]
        slabs = [crossed]
    else:
        tiles = lax.all_gather(slab, "grid", axis=0, tiled=True)
        points, ints, dest_mask = share(other_ints, other_points)
        *first, acc = basis_chunk(0, points, ints)
        second = basis_chunk(1, points, ints)
    chunks = [first, second]
    phis, radials, bases = zip(*chunks)

    some = 1 if late else 0
    chi, rho, *_ = pl.pallas_call(
        functools.partial(rho_kernel, late, starts),
        out_shape=[f32(slots, BLOCK, point_count), f32(slots, point_count)] + [tile_shape] * some,
        in_specs=[spec(SMEM)] + [spec(VMEM)] * (len(starts) + len(late) + 1),
        out_specs=[spec(VMEM)] * (2 + some),
        input_output_aliases={1 + len(starts) + len(late): 2} if late else {},
        compiler_params=params(blocks),
        cost_estimate=cost(5),
        name="density_at_points",
    )(ints, *phis, *slabs, tiles)

    if blk_count == 2:
        other = lax.ppermute(rho, "blk", [(0, 1), (1, 0)])
    else:
        other = lax.psum(rho, "blk") - rho

    rows = 3 * NATOM // LANES + dests // LANES
    outgoing, _ = pl.pallas_call(
        functools.partial(force_kernel, starts),
        out_shape=[f32(blk_count * grid_count, rows, LANES), f32(BPD, 5, BLOCK, LANES)],
        in_specs=[spec(SMEM)] + [spec(VMEM)] * (7 + 2 * len(starts)),
        out_specs=[spec(VMEM)] * 2,
        scratch_shapes=[pltpu.VMEM((slots, point_count), jnp.float32)],
        input_output_aliases={7 + 2 * len(starts): 1},
        compiler_params=params(blocks),
        cost_estimate=cost(5),
        name="forces_and_energies",
    )(ints, points, rho, other, chi, *radials, *bases, table, dest_mask, acc)

    arrived = lax.all_to_all(outgoing, ("blk", "grid"), split_axis=0, concat_axis=0, tiled=True)

    energy, forces = pl.pallas_call(
        functools.partial(sum_kernel, blk_count),
        out_shape=[f32(1, dests // grid_count), f32(3, NATOM)],
        in_specs=[spec(VMEM)],
        out_specs=[spec(VMEM)] * 2,
        compiler_params=params(blocks),
        name="final_sums",
    )(arrived)
    return (energy.reshape(dests // grid_count), forces)


def solution(mesh):
    in_specs = (
        P("blk", "grid"),
        P("grid", None, None),
        P("grid", None),
        P("grid"),
        P(),
        P(),
        P(),
        P(),
    )
    out_specs = (P("grid"), P())
    return jax.shard_map(local, mesh=mesh, in_specs=in_specs, out_specs=out_specs, check_vma=False)
```
